32 devices in a mesh: dp: 16 (over z, y, x), tensor: 2 (over core).
Axes of the slice: x: 2, y: 2, z: 4, core: 2. Of those that a mesh axis runs over, the one named last changes fastest.
Arguments:
- clips: bfloat16 [16, 1569, 768], P('dp'), may hold values from -6 to 6
- cotangent: bfloat16 [16, 1569, 768], P('dp'), may hold values from -6 to 6
- live: int32 [16], P('dp'), may hold values 0 or 1
- time_gain: float32 [768], replicated, may hold values from 0.25 to 1.75
- time_shift: float32 [768], replicated, may hold values from -3 to 3
- time_inproj: bfloat16 [768, 3, 768], P(None, None, 'tensor'), may hold values from -0.21875 to 0.21875
- time_inbias: float32 [2, 768], P(None, 'tensor'), may hold values from -3 to 3
- time_outproj: bfloat16 [768, 768], P('tensor'), may hold values from -0.625 to 0.625
- time_outbias: float32 [768], replicated, may hold values from -3 to 3
- time_mixer: bfloat16 [768, 768], P('tensor'), may hold values from -0.21875 to 0.21875
- time_mixbias: float32 [768], replicated, may hold values from -3 to 3
- space_gain: float32 [768], replicated, may hold values from 0.25 to 1.75
- space_shift: float32 [768], replicated, may hold values from -3 to 3
- space_inproj: bfloat16 [768, 3, 768], P(None, None, 'tensor'), may hold values from -0.21875 to 0.21875
- space_inbias: float32 [2, 768], P(None, 'tensor'), may hold values from -3 to 3
- space_outproj: bfloat16 [768, 768], P('tensor'), may hold values from -1.75 to 1.75
- space_outbias: float32 [768], replicated, may hold values from -4 to 4
- feed_gain: float32 [768], replicated, may hold values from 0.25 to 1.75
- feed_shift: float32 [768], replicated, may hold values from -3 to 3
- feed_upward: bfloat16 [768, 3072], P(None, 'tensor'), may hold values from -0.21875 to 0.21875
- feed_upbias: float32 [3072], P('tensor'), may hold values from -3 to 3
- feed_down: bfloat16 [3072, 768], P('tensor'), may hold values from -0.15625 to 0.15625
- feed_downbias: float32 [768], replicated, may hold values from -4 to 4
Outputs:
- mixed: bfloat16 [16, 1569, 768], P('dp')
- grad_clips: bfloat16 [16, 1569, 768], P('dp')
- grad_time_gain: float32 [768], P('dp')
- grad_time_shift: float32 [768], P('dp')
- grad_time_inproj: float32 [768, 3, 768], P('dp', None, 'tensor')
- grad_time_inbias: float32 [2, 768], P(None, ('tensor', 'dp'))
- grad_time_outproj: float32 [768, 768], P('tensor', 'dp')
- grad_time_outbias: float32 [768], P('dp')
- grad_time_mixer: float32 [768, 768], P('tensor', 'dp')
- grad_time_mixbias: float32 [768], P('dp')
- grad_space_gain: float32 [768], P('dp')
- grad_space_shift: float32 [768], P('dp')
- grad_space_inproj: float32 [768, 3, 768], P('dp', None, 'tensor')
- grad_space_inbias: float32 [2, 768], P(None, ('tensor', 'dp'))
- grad_space_outproj: float32 [768, 768], P('tensor', 'dp')
- grad_space_outbias: float32 [768], P('dp')
- grad_feed_gain: float32 [768], P('dp')
- grad_feed_shift: float32 [768], P('dp')
- grad_feed_upward: float32 [768, 3072], P('dp', 'tensor')
- grad_feed_upbias: float32 [3072], P(('tensor', 'dp'))
- grad_feed_down: float32 [3072, 768], P('tensor', 'dp')
- grad_feed_downbias: float32 [768], P('dp')
The draws below stay inside these ranges and needn't reach their ends.
Inputs may be any that keep to these rules, and one draw needn't show every extreme that they name: `live`: 1 where the data group holds a clip, 0 where its slot is empty.
All inputs are finite; a program needn't handle non-finite values.
Results may differ from the reference program's by a relative error of at most 0.03.
Values may be sent and summed in bfloat16 or wider, within the bound.
No kernel may reach another device: no remote copies, remote signals or barrier semaphores. Data moves between devices by JAX's collectives and lax.ppermute only.
A program may use at most 256 MiB of HBM per device.

```python
import jax
import jax.numpy as jnp
from jax import lax

D = 768
HEAD = 64
FF = 3072
FRAMES = 8
PLACES = 196
TOK = 1569
CLIPS = 16
N_TENSOR = 2


def plant(entries, own_key, smallest, top_value):
    shape = entries.shape
    place = [jax.random.randint(jax.random.fold_in(own_key, axis), (), 0, shape[axis]) for axis in range(len(shape))]
    entries = entries.at[tuple(place)].set(smallest)
    longest = shape.index(max(shape))
    place[longest] = (place[longest] + 1) % shape[longest]
    return entries.at[tuple(place)].set(top_value)


def strengthened(drawn, key, source, target, parts, factor):
    owner, partner = [(jnp.arange(drawn.shape[position]) // (drawn.shape[position] // parts)).reshape([-1 if axis == position else 1 for axis in range(drawn.ndim)]) for position in (source, target)]
    chosen = jax.random.permutation(key, parts)[partner]
    strong = (owner == chosen) | (owner == (partner + parts // 2) % parts)
    return jnp.where(strong, factor * drawn, drawn)


def level_of(key, shape, cuts, low, largest):
    def one(axis_at, blocks):
        heights = jax.random.uniform(jax.random.fold_in(jax.random.fold_in(key, 6), axis_at), (blocks,), jnp.float32, low / len(cuts), largest / len(cuts))
        return jnp.repeat(jnp.exp(heights), shape[axis_at] // blocks).reshape((-1,) + (1,) * (len(shape) - axis_at - 1))

    level = one(*cuts[0])
    for cut in cuts[1:]:
        level = level * one(*cut)
    return level


def noise(key, dims, scale, bound, shards=(), kind=jnp.bfloat16):
    array = jax.random.normal(key, dims, jnp.float32) * scale
    if len(shards) > 0:
        array = level_of(key, dims, shards, -0.22, 0.18) * array
    return jnp.clip(array, min=-bound, max=bound).astype(kind)


def noise_with(key, shape, scale, most, shards, heavy, kind=jnp.bfloat16):
    array = scale * jax.random.normal(key, shape, jnp.float32)
    if shards:
        array = array * level_of(key, shape, shards, -0.22, 0.18)
    return jnp.clip(strengthened(array, jax.random.fold_in(key, 3), *heavy), -most, most).astype(kind)


def setup_inputs(seed: int = 0) -> dict:
    arg_keys = jax.random.split(jax.random.key(seed), 24)
    clips = noise_with(arg_keys[0], (CLIPS, TOK, D), 1.0, 6.0, ((0, 16),), (0, 2, 16, 2.0))
    cotangent = noise(arg_keys[1], (CLIPS, TOK, D), 1.0, 6.0, ((0, 16),))
    live = plant((jax.random.randint(arg_keys[2], (CLIPS,), 0, 2) < 1).astype(jnp.int32), jax.random.fold_in(arg_keys[2], 1), 0, 1)
    time_gain = jnp.clip(1.0 + 0.15 * jax.random.normal(arg_keys[3], (D,), jnp.float32), 0.25, 1.75)
    time_shift = noise(arg_keys[4], (D,), 0.3, 3.0, (), jnp.float32)
    time_inproj = noise(arg_keys[5], (D, 3, D), D ** -0.5, 0.21875, ((2, 2),))
    time_inbias = noise(arg_keys[6], (2, D), 0.5, 3.0, ((1, 2),), jnp.float32)
    time_outproj = noise(arg_keys[7], (D, D), (D // 8) ** -0.5, 0.625, ((0, 2),))
    time_outbias = noise(arg_keys[8], (D,), 0.3, 3.0, (), jnp.float32)
    time_mixer = noise(arg_keys[9], (D, D), D ** -0.5, 0.21875, ((0, 2),))
    time_mixbias = noise(arg_keys[10], (D,), 0.3, 3.0, (), jnp.float32)
    space_gain = jnp.clip(1.0 + 0.15 * jax.random.normal(arg_keys[11], (D,), jnp.float32), 0.25, 1.75)
    space_shift = noise(arg_keys[12], (D,), 0.3, 3.0, (), jnp.float32)
    space_inproj = noise(arg_keys[13], (D, 3, D), D ** -0.5, 0.21875, ((2, 2),))
    space_inbias = noise(arg_keys[14], (2, D), 0.5, 3.0, ((1, 2),), jnp.float32)
    space_outproj = noise(arg_keys[15], (D, D), (D // 64) ** -0.5, 1.75, ((0, 2),))
    space_outbias = noise(arg_keys[16], (D,), 0.65, 4.0, (), jnp.float32)
    feed_gain = jnp.clip(1.0 + 0.15 * jax.random.normal(arg_keys[17], (D,), jnp.float32), 0.25, 1.75)
    feed_shift = noise(arg_keys[18], (D,), 0.3, 3.0, (), jnp.float32)
    feed_upward = noise(arg_keys[19], (D, FF), D ** -0.5, 0.21875, ((1, 2),))
    feed_upbias = noise(arg_keys[20], (FF,), 0.5, 3.0, ((0, 2),), jnp.float32)
    feed_down = noise(arg_keys[21], (FF, D), (FF // 2) ** -0.5, 0.15625, ((0, 2),))
    feed_downbias = noise(arg_keys[22], (D,), 1.0, 4.0, (), jnp.float32)
    return dict(clips=clips, cotangent=cotangent, live=live, time_gain=time_gain, time_shift=time_shift, time_inproj=time_inproj, time_inbias=time_inbias, time_outproj=time_outproj, time_outbias=time_outbias, time_mixer=time_mixer, time_mixbias=time_mixbias, space_gain=space_gain, space_shift=space_shift, space_inproj=space_inproj, space_inbias=space_inbias, space_outproj=space_outproj, space_outbias=space_outbias, feed_gain=feed_gain, feed_shift=feed_shift, feed_upward=feed_upward, feed_upbias=feed_upbias, feed_down=feed_down, feed_downbias=feed_downbias)


@jax.custom_vjp
def low(v):
    return lax.optimization_barrier(v.astype(jnp.bfloat16)).astype(jnp.float32)

@jax.custom_vjp
def low_back(v):
    return v

def low_keep(v):
    return (low(v), None)

def low_pass(kept, grad):
    return (grad,)

def back_keep(v):
    return (v, None)

def back_low(kept, grad):
    return (low(grad),)
low.defvjp(low_keep, low_pass)
low_back.defvjp(back_keep, back_low)
HIGHEST = lax.Precision.HIGHEST

def layer_norm(field, gain, shift):
    center = field - lax.optimization_barrier(jnp.mean(field, axis=-1, keepdims=True))
    spread_sq = lax.optimization_barrier(jnp.mean(center * center, axis=-1, keepdims=True))
    return center * lax.rsqrt(spread_sq + 1e-06) * gain + shift

def spread(field):
    rounded = low(field)
    return jnp.broadcast_to(rounded, (N_TENSOR,) + rounded.shape)

def attend(grouped, inproj, inbias):
    width = inproj.shape[0]
    share = width // N_TENSOR
    linear = jnp.einsum('gald,dcgk->cgalk', grouped, inproj.reshape(width, 3, N_TENSOR, share), precision=HIGHEST)
    biases = inbias.reshape(2, N_TENSOR, 1, 1, share)
    query = low_back(low((linear[0] + biases[0]) * HEAD ** (-0.5)))
    keys = low_back(low(linear[1]))
    values = low_back(low(linear[2] + biases[1]))
    split = query.shape[:-1] + (share // HEAD, HEAD)
    query = query.reshape(split)
    keys = keys.reshape(split)
    values = values.reshape(split)
    scores = low_back(jnp.einsum('galhe,gamhe->gahlm', query, keys, precision=HIGHEST))
    probs = low(jax.nn.softmax(scores, axis=-1))
    mixed = jnp.einsum('gahlm,gamhe->galhe', probs, values, precision=HIGHEST)
    return low_back(low(mixed)).reshape(grouped.shape[:-1] + (share,))

def grouped_product(mixed, weight):
    share = mixed.shape[-1]
    return jnp.einsum('g...k,gkd->g...d', mixed, weight.reshape(N_TENSOR, share, weight.shape[1]), precision=HIGHEST)

def block(params, source):
    time_gain, time_shift, time_inproj, time_inbias, time_outproj, time_outbias, time_mixer, time_mixbias, space_gain, space_shift, space_inproj, space_inbias, space_outproj, space_outbias, feed_gain, feed_shift, feed_upward, feed_upbias, feed_down, feed_downbias = params
    width = source.shape[-1]
    share = width // N_TENSOR
    class_row = source[0]
    grid = source[1:].reshape(PLACES, FRAMES, width)
    t_mixed = attend(spread(layer_norm(grid, time_gain, time_shift)), time_inproj, time_inbias)
    t_proj = lax.optimization_barrier(jnp.sum(grouped_product(t_mixed, time_outproj), axis=0))
    mixer_in = low_back(low(t_proj + time_outbias))
    mixer_groups = jnp.moveaxis(mixer_in.reshape(PLACES, FRAMES, N_TENSOR, share), 2, 0)
    time_branch = low_back(lax.optimization_barrier(jnp.sum(grouped_product(mixer_groups, time_mixer), axis=0))) + time_mixbias
    after_time = grid + time_branch
    space_in = jnp.concatenate([jnp.broadcast_to(class_row, (FRAMES, 1, width)), jnp.transpose(after_time, (1, 0, 2))], axis=1)
    s_mixed = attend(spread(layer_norm(space_in, space_gain, space_shift)), space_inproj, space_inbias)
    space_branch = low_back(lax.optimization_barrier(jnp.sum(grouped_product(s_mixed, space_outproj), axis=0))) + space_outbias
    class_after = class_row + lax.optimization_barrier(jnp.mean(space_branch[:, 0], axis=0))
    grid_after = after_time + jnp.transpose(space_branch[:, 1:], (1, 0, 2))
    mid_rows = jnp.concatenate([class_after[None], grid_after.reshape(PLACES * FRAMES, width)], axis=0)
    feed_in = spread(layer_norm(mid_rows, feed_gain, feed_shift))
    units = feed_upward.shape[1] // N_TENSOR
    hidden_pre = low_back(jnp.einsum('gtd,dgf->gtf', feed_in, feed_upward.reshape(width, N_TENSOR, units), precision=HIGHEST) + feed_upbias.reshape(N_TENSOR, 1, units))
    hidden_act = low(jax.nn.gelu(hidden_pre, approximate=False))
    feed_branch = low_back(lax.optimization_barrier(jnp.sum(grouped_product(hidden_act, feed_down), axis=0))) + feed_downbias
    return mid_rows + feed_branch

def reference(clips, cotangent, live, time_gain, time_shift, time_inproj, time_inbias, time_outproj, time_outbias, time_mixer, time_mixbias, space_gain, space_shift, space_inproj, space_inbias, space_outproj, space_outbias, feed_gain, feed_shift, feed_upward, feed_upbias, feed_down, feed_downbias):
    params = tuple((member.astype(jnp.float32) for member in (time_gain, time_shift, time_inproj, time_inbias, time_outproj, time_outbias, time_mixer, time_mixbias, space_gain, space_shift, space_inproj, space_inbias, space_outproj, space_outbias, feed_gain, feed_shift, feed_upward, feed_upbias, feed_down, feed_downbias)))

    def per_clip(totals, inputs):
        source, grad_in, present = inputs

        def forward(weights, field):
            return block(weights, field) * present
        output, pull = jax.vjp(forward, params, source.astype(jnp.float32))
        grads, d_source = pull(grad_in.astype(jnp.float32))
        totals = jax.tree.map(lambda total_sum, addend: total_sum + addend, totals, grads)
        return (totals, (output.astype(jnp.bfloat16), d_source.astype(jnp.bfloat16)))
    zeros = jax.tree.map(jnp.zeros_like, params)
    totals, outputs = lax.scan(per_clip, zeros, (clips, cotangent, live.astype(jnp.float32)))
    return (outputs[0], outputs[1], totals[0], totals[1], totals[2], totals[3], totals[4], totals[5], totals[6], totals[7], totals[8], totals[9], totals[10], totals[11], totals[12], totals[13], totals[14], totals[15], totals[16], totals[17], totals[18], totals[19])
```

```python
import jax
import jax.numpy as jnp
from jax import lax
from jax.sharding import PartitionSpec as P

HEAD = 64
FRAMES = 8
PLACES = 196


def layer_norm(field, gain, shift):
    center = field - jnp.mean(field, axis=-1, keepdims=True)
    spread_sq = jnp.mean(center * center, axis=-1, keepdims=True)
    return center * lax.rsqrt(spread_sq + 1e-06) * gain + shift


def norm_back(field, gain, shift, grad):
    _, pull = jax.vjp(layer_norm, field, gain, shift)
    return pull(grad)


def heads_of(field):
    return field.reshape(field.shape[:-1] + (field.shape[-1] // HEAD, HEAD))


def merge_heads(field):
    return field.reshape(field.shape[:-2] + (field.shape[-2] * field.shape[-1],))


def swap_tensor(field):
    size = lax.axis_size("tensor")
    return lax.ppermute(field, "tensor", [(i, i ^ 1) for i in range(size)])


def branch_total(terms):
    low = terms.astype(jnp.bfloat16)
    other = swap_tensor(low)
    return low.astype(jnp.float32) + other.astype(jnp.float32)


def add_low(left, right):
    return (left.astype(jnp.float32) + right.astype(jnp.float32)).astype(jnp.bfloat16)


def halve(field, axis, bit, size, keep_bit):
    keep = lax.dynamic_index_in_dim(field, keep_bit, axis, keepdims=False)
    send = lax.dynamic_index_in_dim(field, 1 - keep_bit, axis, keepdims=False)
    got = lax.ppermute(send, "dp", [(i, i ^ bit) for i in range(size)])
    return add_low(keep, got)


def line_total(field, stride, size):
    count = field.shape[0]
    place = (lax.axis_index("dp") // stride) % count
    def at(offset):
        return lax.dynamic_index_in_dim(field, jnp.clip(place + offset, 0, count - 1), 0, keepdims=False)
    up = at(count - 1)
    down = at(1 - count)
    for step in range(1, count):
        ups = [(i, i + stride) for i in range(size) if (i // stride) % count < step and (i // stride) % count + 1 < count]
        downs = [(i, i - stride) for i in range(size) if (i // stride) % count > count - 1 - step]
        got_up = lax.ppermute(up, "dp", ups)
        got_down = lax.ppermute(down, "dp", downs)
        if step < count - 1:
            up = add_low(at(count - 1 - step), got_up)
            down = add_low(at(step + 1 - count), got_down)
    return (at(0).astype(jnp.float32) + got_up.astype(jnp.float32)) + got_down.astype(jnp.float32)


def dp_totals(first, second):
    size = lax.axis_size("dp")
    me = lax.axis_index("dp")
    if size == 16:
        def split(field):
            return field.reshape((4, 2, 2) + field.shape[1:])
        x_bit = me % 2
        y_bit = (me // 2) % 2
        first = halve(split(first), 2, 1, size, x_bit)
        second = halve(split(second), 1, 2, size, y_bit)
        first = halve(first, 1, 2, size, y_bit)
        second = halve(second, 1, 1, size, x_bit)
        return line_total(first, 4, size), line_total(second, 4, size)
    out = []
    for field in (first, second):
        span = size // 2
        while span >= 1:
            field = field.reshape((2, span) + field.shape[1:])
            field = halve(field, 0, span, size, (me // span) % 2)
            span //= 2
        out.append(field[0].astype(jnp.float32))
    return tuple(out)


def input_total(terms):
    return branch_total(terms)


def project_heads(normed, inproj, inbias, scale):
    linear = jnp.einsum("bld,dck->cblk", normed, inproj, preferred_element_type=jnp.float32)
    query = ((linear[0] + inbias[0]) * scale).astype(jnp.bfloat16)
    keys = linear[1].astype(jnp.bfloat16)
    values = (linear[2] + inbias[1]).astype(jnp.bfloat16)
    return (heads_of(query), heads_of(keys), heads_of(values))


def attend_forward(query, keys, values):
    scores = jnp.einsum("bihe,bjhe->bhij", query, keys, preferred_element_type=jnp.float32)
    peak = jnp.max(scores, axis=-1, keepdims=True)
    expon = jnp.exp(scores - peak)
    totals = jnp.sum(expon, axis=-1, keepdims=True)
    logsum = peak + jnp.log(totals)
    probs = (expon / totals).astype(jnp.bfloat16)
    mixed = jnp.einsum("bhij,bjhe->bihe", probs, values, preferred_element_type=jnp.float32)
    return (mixed.astype(jnp.bfloat16), logsum)


def attend_backward(query, keys, values, logsum, d_mixed):
    scores = jnp.einsum("bihe,bjhe->bhij", query, keys, preferred_element_type=jnp.float32)
    probs = jnp.exp(scores - logsum)
    d_values = jnp.einsum(
        "bhij,bihe->bjhe", probs.astype(jnp.bfloat16), d_mixed, preferred_element_type=jnp.float32
    )
    d_probs = jnp.einsum("bihe,bjhe->bhij", d_mixed, values, preferred_element_type=jnp.float32)
    inner = jnp.sum(probs * d_probs, axis=-1, keepdims=True)
    d_scores = (probs * (d_probs - inner)).astype(jnp.bfloat16)
    d_query = jnp.einsum("bhij,bjhe->bihe", d_scores, keys, preferred_element_type=jnp.float32)
    d_keys = jnp.einsum("bhij,bihe->bjhe", d_scores, query, preferred_element_type=jnp.float32)
    return (d_query, d_keys, d_values)


def inproj_back(d_query, d_keys, d_values, normed, inproj, scale):
    query_low = merge_heads(d_query).astype(jnp.bfloat16) * scale
    keys_low = merge_heads(d_keys).astype(jnp.bfloat16)
    values_low = merge_heads(d_values).astype(jnp.bfloat16)
    stacked = jnp.stack([query_low, keys_low, values_low])
    grad_inproj = jnp.einsum("bld,cblk->dck", normed, stacked, preferred_element_type=jnp.float32)
    grad_inbias = jnp.stack(
        [
            jnp.sum(query_low.astype(jnp.float32), axis=(0, 1)),
            jnp.sum(values_low.astype(jnp.float32), axis=(0, 1)),
        ]
    )
    terms = jnp.einsum("cblk,dck->bld", stacked, inproj, preferred_element_type=jnp.float32)
    summed = input_total(terms.reshape(-1, terms.shape[-1])).reshape(terms.shape)
    return (grad_inproj, grad_inbias, summed)


def time_project(normed, inproj, inbias, scale):
    linear = jnp.einsum("pfd,dck->cfkp", normed, inproj, preferred_element_type=jnp.float32)
    split = (linear.shape[1], linear.shape[2] // HEAD, HEAD, linear.shape[3])
    query = ((linear[0] + inbias[0][:, None]) * scale).astype(jnp.bfloat16).reshape(split)
    keys = linear[1].astype(jnp.bfloat16).reshape(split)
    values = (linear[2] + inbias[1][:, None]).astype(jnp.bfloat16).reshape(split)
    return (query, keys, values)


def time_forward(query, keys, values):
    scores = jnp.einsum("ihep,jhep->hijp", query, keys, preferred_element_type=jnp.float32)
    peak = jnp.max(scores, axis=2, keepdims=True)
    expon = jnp.exp(scores - peak)
    totals = jnp.sum(expon, axis=2, keepdims=True)
    logsum = peak + jnp.log(totals)
    probs = (expon / totals).astype(jnp.bfloat16)
    mixed = jnp.einsum("hijp,jhep->ihep", probs, values, preferred_element_type=jnp.float32)
    return (mixed.astype(jnp.bfloat16), logsum)


def time_backward(query, keys, values, logsum, d_mixed):
    scores = jnp.einsum("ihep,jhep->hijp", query, keys, preferred_element_type=jnp.float32)
    probs = jnp.exp(scores - logsum)
    d_values = jnp.einsum(
        "hijp,ihep->jhep", probs.astype(jnp.bfloat16), d_mixed, preferred_element_type=jnp.float32
    )
    d_probs = jnp.einsum("ihep,jhep->hijp", d_mixed, values, preferred_element_type=jnp.float32)
    inner = jnp.sum(probs * d_probs, axis=2, keepdims=True)
    d_scores = (probs * (d_probs - inner)).astype(jnp.bfloat16)
    d_query = jnp.einsum("hijp,jhep->ihep", d_scores, keys, preferred_element_type=jnp.float32)
    d_keys = jnp.einsum("hijp,ihep->jhep", d_scores, query, preferred_element_type=jnp.float32)
    return (d_query, d_keys, d_values)


def time_inproj_back(d_query, d_keys, d_values, normed, inproj, scale):
    flat = (d_query.shape[0], d_query.shape[1] * d_query.shape[2], d_query.shape[3])
    query_low = d_query.reshape(flat).astype(jnp.bfloat16) * scale
    keys_low = d_keys.reshape(flat).astype(jnp.bfloat16)
    values_low = d_values.reshape(flat).astype(jnp.bfloat16)
    stacked = jnp.stack([query_low, keys_low, values_low])
    grad_inproj = jnp.einsum("pfd,cfkp->dck", normed, stacked, preferred_element_type=jnp.float32)
    grad_inbias = jnp.stack(
        [
            jnp.sum(query_low.astype(jnp.float32), axis=(0, 2)),
            jnp.sum(values_low.astype(jnp.float32), axis=(0, 2)),
        ]
    )
    terms = jnp.einsum("cfkp,dck->pfd", stacked, inproj, preferred_element_type=jnp.float32)
    summed = input_total(terms.reshape(-1, terms.shape[-1])).reshape(terms.shape)
    return (grad_inproj, grad_inbias, summed)


def local(
    clips,
    cotangent,
    live,
    time_gain,
    time_shift,
    time_inproj,
    time_inbias,
    time_outproj,
    time_outbias,
    time_mixer,
    time_mixbias,
    space_gain,
    space_shift,
    space_inproj,
    space_inbias,
    space_outproj,
    space_outbias,
    feed_gain,
    feed_shift,
    feed_upward,
    feed_upbias,
    feed_down,
    feed_downbias,
):
    scale = HEAD ** (-0.5)
    width = clips.shape[2]
    half = width // lax.axis_size("tensor")
    tensor_rank = lax.axis_index("tensor")
    weight_live = live.astype(jnp.float32)[0]
    source = clips[0].astype(jnp.float32)
    class_row = source[0]
    grid_rows = source[1:].reshape(PLACES, FRAMES, width)
    time_normed = layer_norm(grid_rows, time_gain, time_shift).astype(jnp.bfloat16)
    t_query, t_keys, t_values = time_project(time_normed, time_inproj, time_inbias, scale)
    t_mixed, t_logsum = time_forward(t_query, t_keys, t_values)
    t_flat = jnp.transpose(t_mixed, (3, 0, 1, 2)).reshape(PLACES * FRAMES, half)
    proj_terms = jnp.dot(t_flat, time_outproj, preferred_element_type=jnp.float32)
    proj_low = proj_terms.astype(jnp.bfloat16)
    kept = lax.dynamic_slice_in_dim(proj_low, tensor_rank * half, half, 1)
    sent = lax.dynamic_slice_in_dim(proj_low, (1 - tensor_rank) * half, half, 1)
    proj_half = kept.astype(jnp.float32) + swap_tensor(sent).astype(jnp.float32)
    bias_half = lax.dynamic_slice_in_dim(time_outbias, tensor_rank * half, half)
    mixer_in = (proj_half + bias_half).astype(jnp.bfloat16)
    time_branch = (
        branch_total(jnp.dot(mixer_in, time_mixer, preferred_element_type=jnp.float32))
        + time_mixbias
    )
    after_time = grid_rows.reshape(PLACES * FRAMES, width) + time_branch
    frame_rows = jnp.transpose(after_time.reshape(PLACES, FRAMES, width), (1, 0, 2))
    space_in = jnp.concatenate(
        [jnp.broadcast_to(class_row, (FRAMES, 1, width)), frame_rows], axis=1
    )
    space_normed = layer_norm(space_in, space_gain, space_shift).astype(jnp.bfloat16)
    s_query, s_keys, s_values = project_heads(space_normed, space_inproj, space_inbias, scale)
    s_mixed, s_logsum = attend_forward(s_query, s_keys, s_values)
    s_flat = merge_heads(s_mixed).reshape(FRAMES * (PLACES + 1), half)
    space_terms = jnp.dot(s_flat, space_outproj, preferred_element_type=jnp.float32)
    space_branch = branch_total(space_terms).reshape(FRAMES, PLACES + 1, width) + space_outbias
    class_after = class_row + jnp.mean(space_branch[:, 0], axis=0)
    grid_after = after_time + jnp.transpose(space_branch[:, 1:], (1, 0, 2)).reshape(
        PLACES * FRAMES, width
    )
    mid_rows = jnp.concatenate([class_after[None], grid_after], axis=0)
    feed_normed = layer_norm(mid_rows, feed_gain, feed_shift).astype(jnp.bfloat16)
    hidden_pre = jnp.dot(feed_normed, feed_upward, preferred_element_type=jnp.float32) + feed_upbias
    hidden_act = jax.nn.gelu(hidden_pre, approximate=False).astype(jnp.bfloat16)
    feed_branch = (
        branch_total(jnp.dot(hidden_act, feed_down, preferred_element_type=jnp.float32))
        + feed_downbias
    )
    result = ((mid_rows + feed_branch) * weight_live).astype(jnp.bfloat16)
    grad_out = cotangent[0].astype(jnp.float32) * weight_live
    grad_low = grad_out.astype(jnp.bfloat16)
    g_feed_downbias = jnp.sum(grad_out, axis=0)
    g_feed_down = jnp.einsum("tf,td->df", hidden_act, grad_low, preferred_element_type=jnp.float32)
    d_act = jnp.einsum("td,fd->tf", grad_low, feed_down, preferred_element_type=jnp.float32)
    _, gelu_pull = jax.vjp(lambda field: jax.nn.gelu(field, approximate=False), hidden_pre)
    d_pre = gelu_pull(d_act)[0].astype(jnp.bfloat16)
    g_feed_upbias = jnp.sum(d_pre.astype(jnp.float32), axis=0)
    g_feed_upward = jnp.einsum("td,tf->df", feed_normed, d_pre, preferred_element_type=jnp.float32)
    d_feed_normed = input_total(
        jnp.einsum("tf,df->td", d_pre, feed_upward, preferred_element_type=jnp.float32)
    )
    d_mid_ln, g_feed_gain, g_feed_shift = norm_back(mid_rows, feed_gain, feed_shift, d_feed_normed)
    d_mid = grad_out + d_mid_ln
    d_space = jnp.concatenate(
        [
            jnp.broadcast_to(d_mid[0] / FRAMES, (FRAMES, 1, width)),
            jnp.transpose(d_mid[1:].reshape(PLACES, FRAMES, width), (1, 0, 2)),
        ],
        axis=1,
    )
    g_space_outbias = jnp.sum(d_space, axis=(0, 1))
    d_space_low = d_space.reshape(FRAMES * (PLACES + 1), width).astype(jnp.bfloat16)
    g_space_outproj = jnp.einsum(
        "rk,rd->dk", s_flat, d_space_low, preferred_element_type=jnp.float32
    )
    d_s_mixed = jnp.einsum(
        "rd,kd->rk", d_space_low, space_outproj, preferred_element_type=jnp.float32
    )
    d_s_mixed = heads_of(d_s_mixed.astype(jnp.bfloat16).reshape(FRAMES, PLACES + 1, half))
    s_dquery, s_dkeys, s_dvalues = attend_backward(s_query, s_keys, s_values, s_logsum, d_s_mixed)
    g_space_inproj, g_space_inbias, d_space_normed = inproj_back(
        s_dquery, s_dkeys, s_dvalues, space_normed, space_inproj, scale
    )
    d_space_in, g_space_gain, g_space_shift = norm_back(
        space_in, space_gain, space_shift, d_space_normed
    )
    d_class = d_mid[0] + jnp.sum(d_space_in[:, 0], axis=0)
    d_grid = d_mid[1:] + jnp.transpose(d_space_in[:, 1:], (1, 0, 2)).reshape(PLACES * FRAMES, width)
    g_time_mixbias = jnp.sum(d_grid, axis=0)
    d_grid_low = d_grid.astype(jnp.bfloat16)
    g_time_mixer = jnp.einsum("rk,rd->dk", mixer_in, d_grid_low, preferred_element_type=jnp.float32)
    d_mixer_half = jnp.einsum(
        "rd,kd->rk", d_grid_low, time_mixer, preferred_element_type=jnp.float32
    ).astype(jnp.bfloat16)
    d_mixer_peer = swap_tensor(d_mixer_half)
    d_mixer_in = jnp.where(
        tensor_rank == 0,
        jnp.concatenate([d_mixer_half, d_mixer_peer], axis=1),
        jnp.concatenate([d_mixer_peer, d_mixer_half], axis=1),
    )
    g_time_outbias = jnp.sum(d_mixer_in.astype(jnp.float32), axis=0)
    g_time_outproj = jnp.einsum("rk,rd->dk", t_flat, d_mixer_in, preferred_element_type=jnp.float32)
    d_t_mixed = jnp.einsum(
        "rd,kd->rk", d_mixer_in, time_outproj, preferred_element_type=jnp.float32
    )
    d_t_mixed = d_t_mixed.astype(jnp.bfloat16).reshape(PLACES, FRAMES, half // HEAD, HEAD)
    d_t_mixed = jnp.transpose(d_t_mixed, (1, 2, 3, 0))
    t_dquery, t_dkeys, t_dvalues = time_backward(t_query, t_keys, t_values, t_logsum, d_t_mixed)
    g_time_inproj, g_time_inbias, d_time_normed = time_inproj_back(
        t_dquery, t_dkeys, t_dvalues, time_normed, time_inproj, scale
    )
    d_grid_ln, g_time_gain, g_time_shift = norm_back(
        grid_rows, time_gain, time_shift, d_time_normed
    )
    d_source = jnp.concatenate(
        [d_class[None], d_grid + d_grid_ln.reshape(PLACES * FRAMES, width)], axis=0
    )
    low = lambda field: field.astype(jnp.bfloat16)
    dests = lax.axis_size("dp")
    by_dest = lambda field: low(field).reshape(dests, width // dests, -1)
    feed_up_sum, feed_down_sum = dp_totals(by_dest(g_feed_upward), by_dest(g_feed_down))
    space_first = low(g_space_inproj[:, :2]).reshape(width, 2 * half)
    space_second = jnp.concatenate([low(g_space_inproj[:, 2]), low(g_space_outproj)], axis=1)
    space_a, space_b = dp_totals(by_dest(space_first), by_dest(space_second))
    vectors = [
        g_time_gain, g_time_shift, g_time_outbias, g_time_mixbias, g_space_gain, g_space_shift,
        g_space_outbias, g_feed_gain, g_feed_shift, g_feed_downbias, g_time_inbias[0], g_time_inbias[1],
        g_space_inbias[0], g_space_inbias[1], g_feed_upbias,
    ]
    packed = jnp.concatenate([low(v).reshape(dests, -1) for v in vectors], axis=1)
    share = packed.shape[1]
    rows = width // dests
    packed = jnp.pad(packed, ((0, 0), (0, -share % (2 * half)))).reshape(dests, -1, 2 * half)
    time_first = by_dest(g_time_inproj.reshape(width, 3 * half))
    time_second = jnp.concatenate([low(g_time_outproj), low(g_time_mixer)], axis=1).reshape(dests, rows, -1)
    time_second = jnp.concatenate([time_second, packed], axis=1)
    time_a, time_b = dp_totals(time_first, time_second)
    flat = time_b[rows:].reshape(-1)
    pieces = []
    at = 0
    for v in vectors:
        count = v.shape[0] // dests
        pieces.append(flat[at : at + count])
        at += count
    settled = (
        pieces[0],
        pieces[1],
        time_a.reshape(rows, 3, half),
        jnp.stack([pieces[10], pieces[11]]),
        time_b[:rows, :half].T,
        pieces[2],
        time_b[:rows, half:].T,
        pieces[3],
        pieces[4],
        pieces[5],
        jnp.concatenate([space_a, space_b[:, :half]], axis=1).reshape(rows, 3, half),
        jnp.stack([pieces[12], pieces[13]]),
        space_b[:, half:].T,
        pieces[6],
        pieces[7],
        pieces[8],
        feed_up_sum,
        pieces[14],
        feed_down_sum.T,
        pieces[9],
    )
    return (result[None], d_source.astype(jnp.bfloat16)[None]) + settled


def solution(mesh):
    in_specs = (
        P("dp", None, None),
        P("dp", None, None),
        P("dp"),
        P(),
        P(),
        P(None, None, "tensor"),
        P(None, "tensor"),
        P("tensor", None),
        P(),
        P("tensor", None),
        P(),
        P(),
        P(),
        P(None, None, "tensor"),
        P(None, "tensor"),
        P("tensor", None),
        P(),
        P(),
        P(),
        P(None, "tensor"),
        P("tensor"),
        P("tensor", None),
        P(),
    )
    out_specs = (
        P("dp", None, None),
        P("dp", None, None),
        P("dp"),
        P("dp"),
        P("dp", None, "tensor"),
        P(None, ("tensor", "dp")),
        P("tensor", "dp"),
        P("dp"),
        P("tensor", "dp"),
        P("dp"),
        P("dp"),
        P("dp"),
        P("dp", None, "tensor"),
        P(None, ("tensor", "dp")),
        P("tensor", "dp"),
        P("dp"),
        P("dp"),
        P("dp"),
        P("dp", "tensor"),
        P(("tensor", "dp")),
        P("tensor", "dp"),
        P("dp"),
    )
    return jax.shard_map(local, mesh=mesh, in_specs=in_specs, out_specs=out_specs, check_vma=False)
```

```python
import functools

import jax
import jax.numpy as jnp
from jax import lax
from jax.experimental import pallas as pl
from jax.experimental.pallas import tpu as pltpu
from jax.sharding import PartitionSpec as P

HEAD = 64
FRAMES = 8
PLACES = 196
BLOCK = 16
ROWS = 208
BLOCKS = ROWS // BLOCK
PAIR = 2
EPS = 1e-06
LOW = jnp.bfloat16
VMEM_BYTES = 56 * 1024 * 1024


def dot(left, right):
    return jnp.dot(left, right, preferred_element_type=jnp.float32)


def dot_last(left, right):
    return lax.dot_general(left, right, (((1,), (1,)), ((), ())), preferred_element_type=jnp.float32)


def normed(field):
    center = field - jnp.mean(field, axis=-1, keepdims=True)
    spread_sq = jnp.mean(center * center, axis=-1, keepdims=True)
    inverse = lax.rsqrt(spread_sq + EPS)
    return center * inverse, inverse


def normed_back(unit, inverse, grad_unit):
    first = jnp.mean(grad_unit, axis=-1, keepdims=True)
    second = jnp.mean(grad_unit * unit, axis=-1, keepdims=True)
    return (grad_unit - first - unit * second) * inverse


def flat(field):
    return field.reshape((field.shape[0] * field.shape[1],) + field.shape[2:])


def wide(field):
    return field.astype(jnp.float32)


def iota(shape, axis):
    return lax.broadcasted_iota(jnp.int32, shape, axis)


def column_sum(field):
    return jnp.sum(field, axis=0, keepdims=True)


def call(kernel, grid, in_specs, out_specs, out_shapes, scratch, flops, args):
    moved = sum(a.size * a.dtype.itemsize for a in args) + sum(o.size * o.dtype.itemsize for o in out_shapes)
    return pl.pallas_call(
        kernel,
        grid=grid,
        in_specs=in_specs,
        out_specs=out_specs,
        out_shape=out_shapes,
        scratch_shapes=scratch,
        compiler_params=pltpu.CompilerParams(vmem_limit_bytes=VMEM_BYTES),
        cost_estimate=pl.CostEstimate(flops=int(flops), bytes_accessed=int(moved), transcendentals=0),
    )(*args)


def whole(array):
    zeros = (0,) * array.ndim
    return pl.BlockSpec(array.shape, lambda *at: zeros)


def shape(dims, kind=LOW):
    return jax.ShapeDtypeStruct(dims, kind)


def to_frames(rows, block):
    count = FRAMES * BLOCK
    at = iota((count, count + BLOCK), 0)
    source = 1 + FRAMES * (at % BLOCK) + at // BLOCK
    pick = jnp.where(source == iota((count, count + BLOCK), 1), 1.0, 0.0).astype(LOW)
    return dot(pick, rows)


def to_tokens(rows):
    count = FRAMES * BLOCK
    at = iota((count, count), 1)
    target = 1 + FRAMES * (at % BLOCK) + at // BLOCK
    pick = jnp.where(target == iota((count, count), 0), 1.0, 0.0).astype(LOW)
    return dot(pick, rows)


def fill_rows(source, tokens):
    count = tokens.shape[0]
    even = count // BLOCK * BLOCK
    source[0:even] = tokens[0:even]
    source[even:] = jnp.zeros((source.shape[0] - even, source.shape[1]), source.dtype)
    left = wide(tokens[even:count])
    tail = jnp.zeros((BLOCK, source.shape[1]), jnp.float32)
    for row in range(count - even):
        tail = tail + jnp.where(iota(tail.shape, 0) == row, left[row : row + 1], 0.0)
    source[even : even + BLOCK] = tail.astype(source.dtype)


def frame_rows(source, block, class_row, class_frames):
    count = FRAMES * BLOCK
    rows = to_frames(source[pl.ds(pl.multiple_of(block * count, count), count + BLOCK), :], block)
    at = iota((count, 1), 0)
    is_class = (block * BLOCK + at % BLOCK == PLACES) & (at // BLOCK < class_frames)
    return rows + jnp.where(is_class, class_row, 0.0)


def time_forward_kernel(
    clips, gain, shift, inproj, inbias, outproj, x_out, norm_out, qkv_out, probs_out, mixed_out, part_out, source
):
    half = outproj.shape[0]
    fill_rows(source, clips)
    class_row = wide(clips[0:1])

    def first(block, carry):
        rows = frame_rows(source, block, class_row, FRAMES)
        unit, _ = normed(rows)
        at = pl.ds(pl.multiple_of(block * BLOCK, BLOCK), BLOCK)
        x_out[:, at, :] = rows.astype(LOW).reshape(FRAMES, BLOCK, rows.shape[1])
        norm_out[:, at, :] = (unit * gain[...] + shift[...]).astype(LOW).reshape(FRAMES, BLOCK, rows.shape[1])
        return carry

    lax.fori_loop(0, BLOCKS, first, 0)

    def second(step, carry):
        at = pl.ds(step * PAIR, PAIR)
        linear = dot(flat(norm_out[at]), inproj[...])
        qkv_out[at] = heads_low(linear, inbias, half).reshape(PAIR, ROWS, 3 * half)
        return carry

    lax.fori_loop(0, FRAMES // PAIR, second, 0)
    count = FRAMES * BLOCK
    same = iota((count, count), 0) % BLOCK == iota((count, count), 1) % BLOCK

    def third(block, carry):
        at = pl.ds(pl.multiple_of(block * BLOCK, BLOCK), BLOCK)
        mixed = attend(flat(qkv_out[:, at, :]), same, lambda head, probs: probs_out.__setitem__((block, head), probs))
        mixed_out[:, at, :] = mixed.reshape(FRAMES, BLOCK, half)
        return carry

    lax.fori_loop(0, BLOCKS, third, 0)

    def fourth(step, carry):
        at = pl.ds(step * PAIR, PAIR)
        part = dot(flat(mixed_out[at]), outproj[...]).astype(LOW)
        part_out[at] = part.reshape(PAIR, ROWS, part.shape[1])
        return carry

    lax.fori_loop(0, FRAMES // PAIR, fourth, 0)


def heads_low(linear, inbias, half):
    query = ((linear[:, :half] + inbias[0:1]) * HEAD ** (-0.5)).astype(LOW)
    keys = linear[:, half : 2 * half].astype(LOW)
    values = (linear[:, 2 * half :] + inbias[1:2]).astype(LOW)
    return jnp.concatenate([query, keys, values], axis=1)


def beside(field_t, head):
    own = field_t[HEAD * head : HEAD * (head + 1)]
    none = jnp.zeros_like(own)
    return jnp.concatenate([own, none] if head % 2 == 0 else [none, own], axis=0)


def pair_of(field, head):
    start = head // 2 * 2 * HEAD
    return field[:, start : start + 2 * HEAD]


def attend(qkv, allowed, keep):
    half = qkv.shape[1] // 3
    query_t = qkv[:, :half].T
    keys = qkv[:, half : 2 * half]
    values_t = qkv[:, 2 * half :].T
    mixed_t = []
    for head in range(half // HEAD):
        scores = dot(pair_of(keys, head), beside(query_t, head))
        scores = jnp.where(allowed, scores, -1e30)
        expon = jnp.exp(scores - jnp.max(scores, axis=0, keepdims=True))
        probs = (expon * (1.0 / column_sum(expon))).astype(LOW)
        keep(head, probs)
        mixed_t.append(dot(values_t[HEAD * head : HEAD * (head + 1)], probs))
    return jnp.concatenate(mixed_t, axis=0).T.astype(LOW)


def attend_back(qkv, probs_of, d_mixed):
    half = qkv.shape[1] // 3
    query = qkv[:, :half]
    keys = qkv[:, half : 2 * half]
    keys_t = keys.T
    values = qkv[:, 2 * half :]
    d_mixed_t = d_mixed.T
    rows = qkv.shape[0]
    lane = iota((rows, 2 * HEAD), 1) < HEAD
    d_query_t = []
    d_keys = []
    d_values = []
    for head in range(half // HEAD):
        probs_low = probs_of(head)
        probs = wide(probs_low)
        d_probs = dot(pair_of(values, head), beside(d_mixed_t, head))
        inner = column_sum(probs * d_probs)
        d_scores = (probs * (d_probs - inner)).astype(LOW)
        d_values.append(dot(probs_low, pair_of(d_mixed, head)))
        d_keys.append(dot(d_scores, pair_of(query, head)))
        d_query_t.append(dot(keys_t[HEAD * head : HEAD * (head + 1)], d_scores))

    def paired(fields):
        return [jnp.where(lane, fields[at], fields[at + 1]) for at in range(0, len(fields), 2)]

    d_query = (jnp.concatenate(d_query_t, axis=0).T).astype(LOW) * HEAD ** (-0.5)
    return jnp.concatenate([d_query] + [d.astype(LOW) for d in paired(d_keys) + paired(d_values)], axis=1)


def time_forward(clips, gain, shift, inproj, inbias, outproj):
    tokens, width = clips.shape
    half = outproj.shape[0]
    heads = half // HEAD
    count = FRAMES * BLOCK
    args = (clips, gain, shift, inproj, inbias, outproj)
    outs = [
        shape((FRAMES, ROWS, width)),
        shape((FRAMES, ROWS, width)),
        shape((FRAMES, ROWS, 3 * half)),
        shape((BLOCKS, heads, count, count)),
        shape((FRAMES, ROWS, half)),
        shape((FRAMES, ROWS, width)),
    ]
    rows = FRAMES * ROWS
    return call(
        time_forward_kernel,
        (1,),
        [whole(a) for a in args],
        [whole(o) for o in outs],
        outs,
        [pltpu.VMEM((BLOCKS * count + BLOCK, width), LOW)],
        2 * rows * width * half * 5,
        args,
    )


def cotangent_kernel(cotangent, live, out, total, source):
    fill_rows(source, cotangent)
    present = live[0, 0]
    class_row = wide(cotangent[0:1])

    def first(block, carry):
        rows = frame_rows(source, block, class_row, 1) * present
        at = pl.ds(pl.multiple_of(block * BLOCK, BLOCK), BLOCK)
        out[:, at, :] = rows.astype(LOW).reshape(FRAMES, BLOCK, rows.shape[1])
        return carry + column_sum(rows)

    total[...] = lax.fori_loop(0, BLOCKS, first, jnp.zeros(total.shape, jnp.float32))


def cotangent_frames(cotangent, live):
    tokens, width = cotangent.shape
    args = (cotangent, live)
    outs = [shape((FRAMES, ROWS, width)), shape((1, width), jnp.float32)]
    return call(
        cotangent_kernel,
        (1,),
        [whole(cotangent), pl.BlockSpec(memory_space=pltpu.SMEM)],
        [whole(o) for o in outs],
        outs,
        [pltpu.VMEM((BLOCKS * FRAMES * BLOCK + BLOCK, width), LOW)],
        2 * FRAMES * ROWS * 128 * width,
        args,
    )


def place_of(shape_of):
    return iota(shape_of, 0) % ROWS


def space_forward_kernel(
    own, other, x, outbias, mixer, mixbias, gain, shift, inproj, inbias, outproj,
    mixer_out, after_out, norm_out, qkv_out, probs_out, mixed_out, part_out,
):
    half = outproj.shape[0]
    width = outproj.shape[1]

    def spread(field):
        return field.astype(LOW).reshape(PAIR, ROWS, field.shape[1])

    mixer_in = (wide(flat(own[...])) + wide(flat(other[...])) + outbias[...]).astype(LOW)
    mixer_out[...] = spread(mixer_in)
    branch = dot(mixer_in, mixer[...]) + mixbias[...]
    after = wide(flat(x[...])) + jnp.where(place_of((PAIR * ROWS, 1)) < PLACES, branch, 0.0)
    after_out[...] = spread(after)
    unit, _ = normed(after)
    norm = (unit * gain[...] + shift[...]).astype(LOW)
    norm_out[...] = spread(norm)
    qkv = heads_low(dot(norm, inproj[...]), inbias, half)
    qkv_out[...] = spread(qkv)
    allowed = iota((ROWS, ROWS), 0) <= PLACES
    for frame in range(PAIR):

        def keep(head, probs, frame=frame):
            probs_out[frame, head] = probs

        mixed_out[frame] = attend(qkv[frame * ROWS : (frame + 1) * ROWS], allowed, keep)
    part_out[...] = spread(dot(flat(mixed_out[...]), outproj[...]))


def pairs(array):
    rest = (0,) * (array.ndim - 1)
    return pl.BlockSpec((PAIR,) + array.shape[1:], lambda at: (at,) + rest)


def space_forward(own, other, x, outbias, mixer, mixbias, gain, shift, inproj, inbias, outproj):
    width = x.shape[2]
    half = outproj.shape[0]
    heads = half // HEAD
    args = (own, other, x, outbias, mixer, mixbias, gain, shift, inproj, inbias, outproj)
    outs = [
        shape((FRAMES, ROWS, width)),
        shape((FRAMES, ROWS, width)),
        shape((FRAMES, ROWS, width)),
        shape((FRAMES, ROWS, 3 * half)),
        shape((FRAMES, heads, ROWS, ROWS)),
        shape((FRAMES, ROWS, half)),
        shape((FRAMES, ROWS, width)),
    ]
    return call(
        space_forward_kernel,
        (FRAMES // PAIR,),
        [pairs(a) for a in args[:3]] + [whole(a) for a in args[3:]],
        [pairs(o) for o in outs],
        outs,
        [],
        2 * FRAMES * ROWS * width * half * 8,
        args,
    )


def last_block(count):
    return lambda array: pl.BlockSpec((count, BLOCK, array.shape[2]), lambda at: (0, BLOCKS - 1, 0))


CLASS_AT = PLACES - (BLOCKS - 1) * BLOCK


def feed_kernel(
    own, other, after, cot, own_last, other_last, after_last, outbias, gain, shift, upward, upbias, down,
    mid_out, norm_out, act_out, dpre_out, part_out, dnorm_out, upbias_out,
):
    step = pl.program_id(0)
    units = upward.shape[1]
    width = upward.shape[0]

    def spread(field):
        return field.astype(LOW).reshape(PAIR, ROWS, field.shape[1])

    class_branch = wide(own_last[...]) + wide(other_last[...])
    class_branch = jnp.sum(class_branch, axis=0)[CLASS_AT : CLASS_AT + 1] * (1.0 / FRAMES) + outbias[...]
    at = iota((PAIR * ROWS, 1), 0)
    branch = wide(flat(own[...])) + wide(flat(other[...])) + outbias[...]
    is_class = (at == PLACES) & (step == 0)
    mid = jnp.where(at % ROWS < PLACES, wide(flat(after[...])) + branch, 0.0)
    mid = mid + jnp.where(is_class, wide(after_last[0])[CLASS_AT : CLASS_AT + 1] + class_branch, 0.0)
    mid_out[...] = spread(mid)
    unit, _ = normed(mid)
    norm = (unit * gain[...] + shift[...]).astype(LOW)
    norm_out[...] = spread(norm)
    grad = flat(cot[...])
    part = jnp.zeros((PAIR * ROWS, width), jnp.float32)
    d_norm = jnp.zeros((PAIR * ROWS, width), jnp.float32)
    share = 512

    @pl.when(step == 0)
    def _():
        upbias_out[...] = jnp.zeros(upbias_out.shape, jnp.float32)

    for start in range(0, units, share):
        cols = slice(start, start + share)
        pre = dot(norm, upward[:, cols]) + upbias[:, cols]
        cumulative = 0.5 * (1.0 + lax.erf(pre * 0.5**0.5))
        slope = cumulative + pre * jnp.exp(-0.5 * pre * pre) * 0.3989422804014327
        act = (pre * cumulative).astype(LOW)
        act_out[:, :, cols] = spread(act)
        d_pre = (dot_last(grad, down[cols]) * slope).astype(LOW)
        dpre_out[:, :, cols] = spread(d_pre)
        upbias_out[:, cols] += column_sum(wide(d_pre))
        part = part + dot(act, down[cols])
        d_norm = d_norm + dot_last(d_pre, upward[:, cols])
    part_out[...] = spread(part)
    dnorm_out[...] = spread(d_norm)


def feed(own, other, after, cot, outbias, gain, shift, upward, upbias, down):
    width, units = upward.shape
    args = (own, other, after, cot, own, other, after, outbias, gain, shift, upward, upbias, down)
    outs = [
        shape((FRAMES, ROWS, width)),
        shape((FRAMES, ROWS, width)),
        shape((FRAMES, ROWS, units)),
        shape((FRAMES, ROWS, units)),
        shape((FRAMES, ROWS, width)),
        shape((FRAMES, ROWS, width)),
        shape((1, units), jnp.float32),
    ]
    tail = last_block(FRAMES)
    return call(
        feed_kernel,
        (FRAMES // PAIR,),
        [pairs(a) for a in args[:4]] + [tail(a) for a in args[4:7]] + [whole(a) for a in args[7:]],
        [pairs(o) for o in outs[:6]] + [whole(outs[6])],
        outs,
        [],
        2 * FRAMES * ROWS * width * units * 4,
        args,
    )


def space_backward_kernel(
    own, other, mid, cot, qkv, probs, own_last, other_last, mid_last, cot_last, gain, outproj, inproj,
    dspace_out, back_out, part_out, dclass_out, gain_out, shift_out, outbias_out, inbias_out,
):
    step = pl.program_id(0)
    half = outproj.shape[0]

    def spread(field):
        return field.astype(LOW).reshape(PAIR, ROWS, field.shape[1])

    def back(own_part, other_part, mid_part, cot_part):
        d_norm = wide(own_part) + wide(other_part)
        unit, inverse = normed(wide(mid_part))
        return wide(cot_part) + normed_back(unit, inverse, d_norm * gain[...]), d_norm, d_norm * unit

    d_class = back(own_last[0], other_last[0], mid_last[0], cot_last[0])[0][CLASS_AT : CLASS_AT + 1]
    d_mid, d_shift, d_gain = back(flat(own[...]), flat(other[...]), flat(mid[...]), flat(cot[...]))
    place = place_of((PAIR * ROWS, 1))
    d_space = jnp.where(place < PLACES, d_mid, jnp.where(place == PLACES, d_class * (1.0 / FRAMES), 0.0))

    @pl.when(step == 0)
    def _():
        dclass_out[...] = d_class
        for ref in (gain_out, shift_out, outbias_out, inbias_out):
            ref[...] = jnp.zeros(ref.shape, jnp.float32)

    gain_out[...] += column_sum(d_gain)
    shift_out[...] += column_sum(d_shift)
    outbias_out[...] += column_sum(d_space)
    d_low = d_space.astype(LOW)
    dspace_out[...] = spread(d_low)
    d_mixed = dot_last(d_low, outproj[...]).astype(LOW)
    for frame in range(PAIR):
        rows = slice(frame * ROWS, (frame + 1) * ROWS)
        back_out[frame] = attend_back(qkv[frame], lambda head, frame=frame: probs[frame, head], d_mixed[rows])
    backs = flat(back_out[...])
    inbias_out[...] += column_sum(wide(backs))
    part_out[...] = spread(dot_last(backs, inproj[...]))


def space_backward(own, other, mid, cot, qkv, probs, gain, outproj, inproj):
    width = mid.shape[2]
    half = outproj.shape[0]
    args = (own, other, mid, cot, qkv, probs, own, other, mid, cot, gain, outproj, inproj)
    outs = [
        shape((FRAMES, ROWS, width)),
        shape((FRAMES, ROWS, 3 * half)),
        shape((FRAMES, ROWS, width)),
        shape((1, width), jnp.float32),
        shape((1, width), jnp.float32),
        shape((1, width), jnp.float32),
        shape((1, width), jnp.float32),
        shape((1, 3 * half), jnp.float32),
    ]
    tail = last_block(1)
    return call(
        space_backward_kernel,
        (FRAMES // PAIR,),
        [pairs(a) for a in args[:6]] + [tail(a) for a in args[6:10]] + [whole(a) for a in args[10:]],
        [pairs(o) for o in outs[:3]] + [whole(o) for o in outs[3:]],
        outs,
        [],
        2 * FRAMES * ROWS * width * half * 6,
        args,
    )


def time_backward_kernel(
    own, other, after, dspace, dclass, qkv, probs, gain, mixer, outproj, inproj,
    dgrid_out, dmixer_out, back_out, part_out, dsource_out, gain_out, shift_out, mixbias_out, outbias_out, inbias_out,
    d_mixed,
):
    half = outproj.shape[0]
    width = outproj.shape[1]
    dsource_out[...] = dclass[...]
    for ref in (gain_out, shift_out, mixbias_out, outbias_out, inbias_out):
        ref[...] = jnp.zeros(ref.shape, jnp.float32)

    def first(step, carry):
        at = pl.ds(step * PAIR, PAIR)

        def put(ref, field):
            ref[at] = field.astype(LOW).reshape(PAIR, ROWS, field.shape[1])

        d_norm = wide(flat(own[at])) + wide(flat(other[at]))
        unit, inverse = normed(wide(flat(after[at])))
        gain_out[...] += column_sum(d_norm * unit)
        shift_out[...] += column_sum(d_norm)
        d_space_in = normed_back(unit, inverse, d_norm * gain[...])
        place = place_of((PAIR * ROWS, 1))
        dsource_out[...] += column_sum(jnp.where(place == PLACES, d_space_in, 0.0))
        d_grid = jnp.where(place < PLACES, d_space_in + wide(flat(dspace[at])), 0.0)
        mixbias_out[...] += column_sum(d_grid)
        d_low = d_grid.astype(LOW)
        put(dgrid_out, d_low)
        d_mixer = dot_last(d_low, mixer[...]).astype(LOW)
        put(dmixer_out, d_mixer)
        outbias_out[...] += column_sum(wide(d_mixer))
        put(d_mixed, dot_last(d_mixer, outproj[...]))
        return carry

    lax.fori_loop(0, FRAMES // PAIR, first, 0)

    def second(block, carry):
        at = pl.ds(pl.multiple_of(block * BLOCK, BLOCK), BLOCK)
        backs = attend_back(flat(qkv[:, at, :]), lambda head: probs[block, head], flat(d_mixed[:, at, :]))
        back_out[:, at, :] = backs.reshape(FRAMES, BLOCK, 3 * half)
        return carry

    lax.fori_loop(0, BLOCKS, second, 0)

    def third(step, carry):
        at = pl.ds(step * PAIR, PAIR)
        backs = flat(back_out[at])
        inbias_out[...] += column_sum(wide(backs))
        part_out[at] = dot_last(backs, inproj[...]).astype(LOW).reshape(PAIR, ROWS, width)
        return carry

    lax.fori_loop(0, FRAMES // PAIR, third, 0)


def time_backward(own, other, after, dspace, dclass, qkv, probs, gain, mixer, outproj, inproj):
    width = after.shape[2]
    half = outproj.shape[0]
    args = (own, other, after, dspace, dclass, qkv, probs, gain, mixer, outproj, inproj)
    outs = [
        shape((FRAMES, ROWS, width)),
        shape((FRAMES, ROWS, width)),
        shape((FRAMES, ROWS, 3 * half)),
        shape((FRAMES, ROWS, width)),
        shape((1, width), jnp.float32),
        shape((1, width), jnp.float32),
        shape((1, width), jnp.float32),
        shape((1, width), jnp.float32),
        shape((1, width), jnp.float32),
        shape((1, 3 * half), jnp.float32),
    ]
    return call(
        time_backward_kernel,
        (1,),
        [whole(a) for a in args],
        [whole(o) for o in outs],
        outs,
        [pltpu.VMEM((FRAMES, ROWS, half), LOW)],
        2 * FRAMES * ROWS * width * half * 8,
        args,
    )


def blocks(array):
    return pl.BlockSpec((FRAMES, BLOCK, array.shape[2]), lambda at: (0, at, 0))


def put_tokens(out, rows, carry):
    low = rows.astype(LOW)
    moved = to_tokens(low)
    out[...] = jnp.where(iota((rows.shape[0], 1), 0) == 0, carry[...], moved).astype(out.dtype)
    carry[...] = rows[rows.shape[0] - 1 :].astype(LOW).astype(jnp.float32)


def source_kernel(own, other, x, dgrid, dsource, gain, out, gain_out, shift_out, carry):
    block = pl.program_id(0)

    @pl.when(block == 0)
    def _():
        carry[...] = dsource[...]
        gain_out[...] = jnp.zeros(gain_out.shape, jnp.float32)
        shift_out[...] = jnp.zeros(shift_out.shape, jnp.float32)

    d_norm = wide(flat(own[...])) + wide(flat(other[...]))
    unit, inverse = normed(wide(flat(x[...])))
    gain_out[...] += column_sum(d_norm * unit)
    shift_out[...] += column_sum(d_norm)
    rows = wide(flat(dgrid[...])) + normed_back(unit, inverse, d_norm * gain[...])
    put_tokens(out, rows, carry)


def source_gradient(own, other, x, dgrid, dsource, gain, tokens):
    width = x.shape[2]
    args = (own, other, x, dgrid, dsource, gain)
    outs = [shape((tokens, width)), shape((1, width), jnp.float32), shape((1, width), jnp.float32)]
    out_block = pl.BlockSpec((FRAMES * BLOCK, width), lambda at: (at, 0))
    return call(
        source_kernel,
        (BLOCKS,),
        [blocks(a) for a in args[:4]] + [whole(a) for a in args[4:]],
        [out_block] + [whole(o) for o in outs[1:]],
        outs,
        [pltpu.VMEM((1, width), jnp.float32)],
        2 * FRAMES * ROWS * 128 * width,
        args,
    )


def result_kernel(own, other, mid, own_last, other_last, mid_last, bias, live, out, carry):
    present = live[0, 0]

    def rows_of(own_part, other_part, mid_part):
        return (wide(mid_part) + wide(own_part) + wide(other_part) + bias[...]) * present

    @pl.when(pl.program_id(0) == 0)
    def _():
        carry[...] = rows_of(own_last[0], other_last[0], mid_last[0])[CLASS_AT : CLASS_AT + 1]

    put_tokens(out, rows_of(flat(own[...]), flat(other[...]), flat(mid[...])), carry)


def result_tokens(own, other, mid, bias, live, tokens):
    width = mid.shape[2]
    args = (own, other, mid, own, other, mid, bias, live)
    tail = last_block(1)
    return call(
        result_kernel,
        (BLOCKS,),
        [blocks(a) for a in args[:3]] + [tail(a) for a in args[3:6]]
        + [whole(bias), pl.BlockSpec(memory_space=pltpu.SMEM)],
        [pl.BlockSpec((FRAMES * BLOCK, width), lambda at: (at, 0))],
        [shape((tokens, width))],
        [pltpu.VMEM((1, width), jnp.float32)],
        2 * FRAMES * ROWS * 128 * width,
        args,
    )[0]


def swap_tensor(field):
    size = lax.axis_size("tensor")
    return lax.ppermute(field, "tensor", [(i, i ^ 1) for i in range(size)])


def add_low(left, right):
    return (left.astype(jnp.float32) + right.astype(jnp.float32)).astype(jnp.bfloat16)


def halve(field, axis, bit, size, keep_bit):
    keep = lax.dynamic_index_in_dim(field, keep_bit, axis, keepdims=False)
    send = lax.dynamic_index_in_dim(field, 1 - keep_bit, axis, keepdims=False)
    got = lax.ppermute(send, "dp", [(i, i ^ bit) for i in range(size)])
    return add_low(keep, got)


def line_total(field, stride, size):
    count = field.shape[0]
    place = (lax.axis_index("dp") // stride) % count
    def at(offset):
        return lax.dynamic_index_in_dim(field, jnp.clip(place + offset, 0, count - 1), 0, keepdims=False)
    up = at(count - 1)
    down = at(1 - count)
    for step in range(1, count):
        ups = [(i, i + stride) for i in range(size) if (i // stride) % count < step and (i // stride) % count + 1 < count]
        downs = [(i, i - stride) for i in range(size) if (i // stride) % count > count - 1 - step]
        got_up = lax.ppermute(up, "dp", ups)
        got_down = lax.ppermute(down, "dp", downs)
        if step < count - 1:
            up = add_low(at(count - 1 - step), got_up)
            down = add_low(at(step + 1 - count), got_down)
    return (at(0).astype(jnp.float32) + got_up.astype(jnp.float32)) + got_down.astype(jnp.float32)


def dp_totals(first, second):
    size = lax.axis_size("dp")
    me = lax.axis_index("dp")
    if size == 16:
        def split(field):
            return field.reshape((4, 2, 2) + field.shape[1:])
        x_bit = me % 2
        y_bit = (me // 2) % 2
        first = halve(split(first), 2, 1, size, x_bit)
        second = halve(split(second), 1, 2, size, y_bit)
        first = halve(first, 1, 2, size, y_bit)
        second = halve(second, 1, 1, size, x_bit)
        return line_total(first, 4, size), line_total(second, 4, size)
    out = []
    for field in (first, second):
        span = size // 2
        while span >= 1:
            field = field.reshape((2, span) + field.shape[1:])
            field = halve(field, 0, span, size, (me // span) % 2)
            span //= 2
        out.append(field[0].astype(jnp.float32))
    return tuple(out)


def grad_of(left, right):
    return lax.dot_general(
        left.reshape(-1, left.shape[2]),
        right.reshape(-1, right.shape[2]),
        (((0,), (0,)), ((), ())),
        preferred_element_type=jnp.float32,
    ).astype(LOW)


def local(
    clips,
    cotangent,
    live,
    time_gain,
    time_shift,
    time_inproj,
    time_inbias,
    time_outproj,
    time_outbias,
    time_mixer,
    time_mixbias,
    space_gain,
    space_shift,
    space_inproj,
    space_inbias,
    space_outproj,
    space_outbias,
    feed_gain,
    feed_shift,
    feed_upward,
    feed_upbias,
    feed_down,
    feed_downbias,
):
    tokens, width = clips.shape[1:]
    half = time_outproj.shape[0]
    tensor_rank = lax.axis_index("tensor")
    present = live.astype(jnp.float32).reshape(1, 1)
    row = lambda vector: vector.reshape(1, -1)
    time_in = time_inproj.reshape(width, 3 * half)
    space_in = space_inproj.reshape(width, 3 * half)
    mixer_other = swap_tensor(time_mixer)
    mixer = jnp.where(
        tensor_rank == 0,
        jnp.concatenate([time_mixer, mixer_other], axis=0),
        jnp.concatenate([mixer_other, time_mixer], axis=0),
    )
    x, t_norm, t_qkv, t_probs, t_mixed, t_part = time_forward(
        clips[0], row(time_gain), row(time_shift), time_in, time_inbias, time_outproj
    )
    cot, g_downbias = cotangent_frames(cotangent[0], present)
    mixer_in, after, s_norm, s_qkv, s_probs, s_mixed, s_part = space_forward(
        t_part, swap_tensor(t_part), x, row(time_outbias), mixer, row(time_mixbias), row(space_gain),
        row(space_shift), space_in, space_inbias, space_outproj,
    )
    mid, f_norm, act, d_pre, f_part, df_part, g_upbias = feed(
        s_part, swap_tensor(s_part), after, cot, row(space_outbias), row(feed_gain), row(feed_shift), feed_upward,
        row(feed_upbias), feed_down,
    )
    g_up = grad_of(f_norm, d_pre)
    g_down = grad_of(cot, act)
    d_space, s_back, ds_part, d_class, g_feed_gain, g_feed_shift, g_space_outbias, g_space_inbias = space_backward(
        df_part, swap_tensor(df_part), mid, cot, s_qkv, s_probs, row(feed_gain), space_outproj, space_in
    )
    g_space_in = grad_of(s_norm, s_back)
    g_space_out = grad_of(d_space, s_mixed)
    (
        d_grid, d_mixer, t_back, dt_part, d_source, g_space_gain, g_space_shift, g_mixbias, g_outbias, g_time_inbias,
    ) = time_backward(
        ds_part, swap_tensor(ds_part), after, d_space, d_class, t_qkv, t_probs, row(space_gain), mixer, time_outproj,
        time_in,
    )
    mixer_half = lax.dynamic_slice_in_dim(mixer_in, tensor_rank * half, half, 2)
    g_mixer = grad_of(d_grid, mixer_half)
    g_time_out = grad_of(d_mixer, t_mixed)
    g_time_in = grad_of(t_norm, t_back)
    result = result_tokens(f_part, swap_tensor(f_part), mid, row(feed_downbias), present, tokens)
    grad_clips, g_time_gain, g_time_shift = source_gradient(
        dt_part, swap_tensor(dt_part), x, d_grid, d_source, row(time_gain), tokens
    )

    dests = lax.axis_size("dp")
    share = width // dests
    by_dest = lambda field: field.astype(LOW).reshape(dests, share, -1)
    up_sum, down_sum = dp_totals(by_dest(g_up), by_dest(g_down))
    space_a, space_b = dp_totals(
        by_dest(g_space_in[:, : 2 * half]),
        by_dest(jnp.concatenate([g_space_in[:, 2 * half :], g_space_out], axis=1)),
    )
    vectors = [
        g_time_gain, g_time_shift, g_outbias, g_mixbias, g_space_gain, g_space_shift, g_space_outbias, g_feed_gain,
        g_feed_shift, g_downbias, g_time_inbias[:, :half], g_time_inbias[:, 2 * half :], g_space_inbias[:, :half],
        g_space_inbias[:, 2 * half :], g_upbias,
    ]
    packed = jnp.concatenate([v.astype(LOW).reshape(dests, -1) for v in vectors], axis=1)
    packed = jnp.pad(packed, ((0, 0), (0, -packed.shape[1] % (2 * half)))).reshape(dests, -1, 2 * half)
    time_b = jnp.concatenate([g_time_out, g_mixer], axis=1).reshape(dests, share, 2 * half)
    time_a, time_b = dp_totals(by_dest(g_time_in), jnp.concatenate([time_b, packed], axis=1))
    loose = time_b[share:].reshape(-1)
    pieces = []
    at = 0
    for v in vectors:
        count = v.size // dests
        pieces.append(loose[at : at + count])
        at += count
    settled = (
        pieces[0],
        pieces[1],
        time_a.reshape(share, 3, half),
        jnp.stack([pieces[10], pieces[11]]),
        time_b[:share, :half].T,
        pieces[2],
        time_b[:share, half:].T,
        pieces[3],
        pieces[4],
        pieces[5],
        jnp.concatenate([space_a, space_b[:, :half]], axis=1).reshape(share, 3, half),
        jnp.stack([pieces[12], pieces[13]]),
        space_b[:, half:].T,
        pieces[6],
        pieces[7],
        pieces[8],
        up_sum,
        pieces[14],
        down_sum.T,
        pieces[9],
    )
    return (result[None], grad_clips[None]) + settled


def solution(mesh):
    in_specs = (
        P("dp", None, None),
        P("dp", None, None),
        P("dp"),
        P(),
        P(),
        P(None, None, "tensor"),
        P(None, "tensor"),
        P("tensor", None),
        P(),
        P("tensor", None),
        P(),
        P(),
        P(),
        P(None, None, "tensor"),
        P(None, "tensor"),
        P("tensor", None),
        P(),
        P(),
        P(),
        P(None, "tensor"),
        P("tensor"),
        P("tensor", None),
        P(),
    )
    out_specs = (
        P("dp", None, None),
        P("dp", None, None),
        P("dp"),
        P("dp"),
        P("dp", None, "tensor"),
        P(None, ("tensor", "dp")),
        P("tensor", "dp"),
        P("dp"),
        P("tensor", "dp"),
        P("dp"),
        P("dp"),
        P("dp"),
        P("dp", None, "tensor"),
        P(None, ("tensor", "dp")),
        P("tensor", "dp"),
        P("dp"),
        P("dp"),
        P("dp"),
        P("dp", "tensor"),
        P(("tensor", "dp")),
        P("tensor", "dp"),
        P("dp"),
    )
    return jax.shard_map(local, mesh=mesh, in_specs=in_specs, out_specs=out_specs, check_vma=False)
```

```python
import functools

import jax
import jax.numpy as jnp
from jax import lax
from jax.experimental import pallas as pl
from jax.experimental.pallas import tpu as pltpu
from jax.sharding import PartitionSpec as P

HEAD = 64
FRAMES = 8
PLACES = 196
BLOCK = 16
ROWS = 208
BLOCKS = ROWS // BLOCK
PAIR = 2
EPS = 1e-06
LOW = jnp.bfloat16
VMEM_BYTES = 56 * 1024 * 1024


def dot(left, right):
    return jnp.dot(left, right, preferred_element_type=jnp.float32)


def dot_last(left, right):
    return lax.dot_general(left, right, (((1,), (1,)), ((), ())), preferred_element_type=jnp.float32)


def normed(field):
    center = field - jnp.mean(field, axis=-1, keepdims=True)
    spread_sq = jnp.mean(center * center, axis=-1, keepdims=True)
    inverse = lax.rsqrt(spread_sq + EPS)
    return center * inverse, inverse


def normed_back(unit, inverse, grad_unit):
    first = jnp.mean(grad_unit, axis=-1, keepdims=True)
    second = jnp.mean(grad_unit * unit, axis=-1, keepdims=True)
    return (grad_unit - first - unit * second) * inverse


def flat(field):
    return field.reshape((field.shape[0] * field.shape[1],) + field.shape[2:])


def wide(field):
    return field.astype(jnp.float32)


def iota(shape, axis):
    return lax.broadcasted_iota(jnp.int32, shape, axis)


def column_sum(field):
    return jnp.sum(field, axis=0, keepdims=True)


def call(kernel, grid, in_specs, out_specs, out_shapes, scratch, flops, args):
    moved = sum(a.size * a.dtype.itemsize for a in args) + sum(o.size * o.dtype.itemsize for o in out_shapes)
    return pl.pallas_call(
        kernel,
        grid=grid,
        in_specs=in_specs,
        out_specs=out_specs,
        out_shape=out_shapes,
        scratch_shapes=scratch,
        compiler_params=pltpu.CompilerParams(vmem_limit_bytes=VMEM_BYTES),
        cost_estimate=pl.CostEstimate(flops=int(flops), bytes_accessed=int(moved), transcendentals=0),
    )(*args)


def whole(array):
    zeros = (0,) * array.ndim
    return pl.BlockSpec(array.shape, lambda *at: zeros)


def shape(dims, kind=LOW):
    return jax.ShapeDtypeStruct(dims, kind)


def to_frames(rows, block):
    count = FRAMES * BLOCK
    at = iota((count, count + BLOCK), 0)
    source = 1 + FRAMES * (at % BLOCK) + at // BLOCK
    pick = jnp.where(source == iota((count, count + BLOCK), 1), 1.0, 0.0).astype(LOW)
    return dot(pick, rows)


def to_tokens(rows):
    count = FRAMES * BLOCK
    at = iota((count, count), 1)
    target = 1 + FRAMES * (at % BLOCK) + at // BLOCK
    pick = jnp.where(target == iota((count, count), 0), 1.0, 0.0).astype(LOW)
    return dot(pick, rows)


def fill_rows(source, tokens):
    count = tokens.shape[0]
    even = count // BLOCK * BLOCK
    source[0:even] = tokens[0:even]
    source[even:] = jnp.zeros((source.shape[0] - even, source.shape[1]), source.dtype)
    left = wide(tokens[even:count])
    tail = jnp.zeros((BLOCK, source.shape[1]), jnp.float32)
    for row in range(count - even):
        tail = tail + jnp.where(iota(tail.shape, 0) == row, left[row : row + 1], 0.0)
    source[even : even + BLOCK] = tail.astype(source.dtype)


def frame_rows(source, block, class_row, class_frames):
    count = FRAMES * BLOCK
    rows = to_frames(source[pl.ds(pl.multiple_of(block * count, count), count + BLOCK), :], block)
    at = iota((count, 1), 0)
    is_class = (block * BLOCK + at % BLOCK == PLACES) & (at // BLOCK < class_frames)
    return rows + jnp.where(is_class, class_row, 0.0)


def time_forward_kernel(
    clips, gain, shift, inproj, inbias, outproj, x_out, norm_out, qkv_out, probs_out, mixed_out, part_out, source
):
    half = outproj.shape[0]
    fill_rows(source, clips)
    class_row = wide(clips[0:1])

    def first(block, carry):
        rows = frame_rows(source, block, class_row, FRAMES)
        unit, _ = normed(rows)
        at = pl.ds(pl.multiple_of(block * BLOCK, BLOCK), BLOCK)
        x_out[:, at, :] = rows.astype(LOW).reshape(FRAMES, BLOCK, rows.shape[1])
        norm_out[:, at, :] = (unit * vector(gain) + vector(shift)).astype(LOW).reshape(FRAMES, BLOCK, rows.shape[1])
        return carry

    lax.fori_loop(0, BLOCKS, first, 0)

    def second(step, carry):
        at = pl.ds(step * PAIR, PAIR)
        linear = dot(flat(norm_out[at]), inproj[...])
        qkv_out[at] = heads_low(linear, inbias, half).reshape(PAIR, ROWS, 3 * half)
        return carry

    lax.fori_loop(0, FRAMES // PAIR, second, 0)
    count = FRAMES * BLOCK
    same = iota((count, count), 0) % BLOCK == iota((count, count), 1) % BLOCK

    def third(block, carry):
        at = pl.ds(pl.multiple_of(block * BLOCK, BLOCK), BLOCK)
        mixed = attend(flat(qkv_out[:, at, :]), same, lambda head, probs: probs_out.__setitem__((block, head), probs))
        mixed_out[:, at, :] = mixed.reshape(FRAMES, BLOCK, half)
        return carry

    lax.fori_loop(0, BLOCKS, third, 0)

    def fourth(step, carry):
        at = pl.ds(step * PAIR, PAIR)
        part = dot(flat(mixed_out[at]), outproj[...]).astype(LOW)
        part_out[at] = part.reshape(PAIR, ROWS, part.shape[1])
        return carry

    lax.fori_loop(0, FRAMES // PAIR, fourth, 0)


def heads_low(linear, inbias, half):
    query = ((linear[:, :half] + inbias[0:1]) * HEAD ** (-0.5)).astype(LOW)
    keys = linear[:, half : 2 * half].astype(LOW)
    values = (linear[:, 2 * half :] + inbias[1:2]).astype(LOW)
    return jnp.concatenate([query, keys, values], axis=1)


def beside(field_t, head):
    own = field_t[HEAD * head : HEAD * (head + 1)]
    none = jnp.zeros_like(own)
    return jnp.concatenate([own, none] if head % 2 == 0 else [none, own], axis=0)


def pair_of(field, head):
    start = head // 2 * 2 * HEAD
    return field[:, start : start + 2 * HEAD]


def attend(qkv, allowed, keep):
    half = qkv.shape[1] // 3
    query_t = qkv[:, :half].T
    keys = qkv[:, half : 2 * half]
    values_t = qkv[:, 2 * half :].T
    mixed_t = []
    for head in range(half // HEAD):
        scores = dot(pair_of(keys, head), beside(query_t, head))
        scores = jnp.where(allowed, scores, -1e30)
        expon = jnp.exp(scores - jnp.max(scores, axis=0, keepdims=True))
        probs = (expon * (1.0 / column_sum(expon))).astype(LOW)
        keep(head, probs)
        mixed_t.append(dot(values_t[HEAD * head : HEAD * (head + 1)], probs))
    return jnp.concatenate(mixed_t, axis=0).T.astype(LOW)


def attend_back(qkv, probs_of, d_mixed):
    half = qkv.shape[1] // 3
    query = qkv[:, :half]
    keys = qkv[:, half : 2 * half]
    keys_t = keys.T
    values = qkv[:, 2 * half :]
    d_mixed_t = d_mixed.T
    rows = qkv.shape[0]
    lane = iota((rows, 2 * HEAD), 1) < HEAD
    d_query_t = []
    d_keys = []
    d_values = []
    for head in range(half // HEAD):
        probs_low = probs_of(head)
        probs = wide(probs_low)
        d_probs = dot(pair_of(values, head), beside(d_mixed_t, head))
        inner = column_sum(probs * d_probs)
        d_scores = (probs * (d_probs - inner)).astype(LOW)
        d_values.append(dot(probs_low, pair_of(d_mixed, head)))
        d_keys.append(dot(d_scores, pair_of(query, head)))
        d_query_t.append(dot(keys_t[HEAD * head : HEAD * (head + 1)], d_scores))

    def paired(fields):
        return [jnp.where(lane, fields[at], fields[at + 1]) for at in range(0, len(fields), 2)]

    d_query = (jnp.concatenate(d_query_t, axis=0).T).astype(LOW) * HEAD ** (-0.5)
    return jnp.concatenate([d_query] + [d.astype(LOW) for d in paired(d_keys) + paired(d_values)], axis=1)


def time_forward(clips, gain, shift, inproj, inbias, outproj):
    tokens, width = clips.shape
    half = outproj.shape[0]
    heads = half // HEAD
    count = FRAMES * BLOCK
    args = (clips, gain, shift, inproj, inbias, outproj)
    outs = [
        shape((FRAMES, ROWS, width)),
        shape((FRAMES, ROWS, width)),
        shape((FRAMES, ROWS, 3 * half)),
        shape((BLOCKS, heads, count, count)),
        shape((FRAMES, ROWS, half)),
        shape((FRAMES, ROWS, width)),
    ]
    rows = FRAMES * ROWS
    return call(
        time_forward_kernel,
        (1,),
        [whole(a) for a in args],
        [whole(o) for o in outs],
        outs,
        [pltpu.VMEM((BLOCKS * count + BLOCK, width), LOW)],
        2 * rows * width * half * 5,
        args,
    )


def cotangent_kernel(cotangent, live, out, total, source):
    fill_rows(source, cotangent)
    present = live[0, 0]
    class_row = wide(cotangent[0:1])

    def first(block, carry):
        rows = frame_rows(source, block, class_row, 1) * present
        at = pl.ds(pl.multiple_of(block * BLOCK, BLOCK), BLOCK)
        out[:, at, :] = rows.astype(LOW).reshape(FRAMES, BLOCK, rows.shape[1])
        return carry + column_sum(rows)

    total[...] = lax.fori_loop(0, BLOCKS, first, jnp.zeros(total.shape, jnp.float32))


def cotangent_frames(cotangent, live):
    tokens, width = cotangent.shape
    args = (cotangent, live)
    outs = [shape((FRAMES, ROWS, width)), shape((1, width), jnp.float32)]
    return call(
        cotangent_kernel,
        (1,),
        [whole(cotangent), pl.BlockSpec(memory_space=pltpu.SMEM)],
        [whole(o) for o in outs],
        outs,
        [pltpu.VMEM((BLOCKS * FRAMES * BLOCK + BLOCK, width), LOW)],
        2 * FRAMES * ROWS * 128 * width,
        args,
    )


def vector(ref):
    return ref[...].reshape(1, -1)


def place_of(shape_of):
    return iota(shape_of, 0) % ROWS


def space_forward_kernel(
    own, other, x, outbias, mixer, mixbias, gain, shift, inproj, inbias, outproj,
    mixer_out, after_out, norm_out, qkv_out, probs_out, mixed_out, part_out,
):
    half = outproj.shape[0]
    width = outproj.shape[1]

    def spread(field):
        return field.astype(LOW).reshape(PAIR, ROWS, field.shape[1])

    mixer_in = (wide(flat(own[...])) + wide(flat(other[...])) + vector(outbias)).astype(LOW)
    mixer_out[...] = spread(mixer_in)
    branch = dot(mixer_in, mixer[...]) + vector(mixbias)
    after = wide(flat(x[...])) + jnp.where(place_of((PAIR * ROWS, 1)) < PLACES, branch, 0.0)
    after_out[...] = spread(after)
    unit, _ = normed(after)
    norm = (unit * vector(gain) + vector(shift)).astype(LOW)
    norm_out[...] = spread(norm)
    qkv = heads_low(dot(norm, inproj[...]), inbias, half)
    qkv_out[...] = spread(qkv)
    allowed = iota((ROWS, ROWS), 0) <= PLACES
    for frame in range(PAIR):

        def keep(head, probs, frame=frame):
            probs_out[frame, head] = probs

        mixed_out[frame] = attend(qkv[frame * ROWS : (frame + 1) * ROWS], allowed, keep)
    part_out[...] = spread(dot(flat(mixed_out[...]), outproj[...]))


def pairs(array):
    rest = (0,) * (array.ndim - 1)
    return pl.BlockSpec((PAIR,) + array.shape[1:], lambda at: (at,) + rest)


def space_forward(own, other, x, outbias, mixer, mixbias, gain, shift, inproj, inbias, outproj):
    width = x.shape[2]
    half = outproj.shape[0]
    heads = half // HEAD
    args = (own, other, x, outbias, mixer, mixbias, gain, shift, inproj, inbias, outproj)
    outs = [
        shape((FRAMES, ROWS, width)),
        shape((FRAMES, ROWS, width)),
        shape((FRAMES, ROWS, width)),
        shape((FRAMES, ROWS, 3 * half)),
        shape((FRAMES, heads, ROWS, ROWS)),
        shape((FRAMES, ROWS, half)),
        shape((FRAMES, ROWS, width)),
    ]
    return call(
        space_forward_kernel,
        (FRAMES // PAIR,),
        [pairs(a) for a in args[:3]] + [whole(a) for a in args[3:]],
        [pairs(o) for o in outs],
        outs,
        [],
        2 * FRAMES * ROWS * width * half * 8,
        args,
    )


def last_block(count):
    return lambda array: pl.BlockSpec((count, BLOCK, array.shape[2]), lambda at: (0, BLOCKS - 1, 0))


CLASS_AT = PLACES - (BLOCKS - 1) * BLOCK


def feed_kernel(
    own, other, after, cot, own_last, other_last, after_last, outbias, gain, shift, upward, upbias, down,
    mid_out, norm_out, act_out, dpre_out, part_out, dnorm_out, upbias_out,
):
    step = pl.program_id(0)
    units = upward.shape[1]
    width = upward.shape[0]

    def spread(field):
        return field.astype(LOW).reshape(PAIR, ROWS, field.shape[1])

    class_branch = wide(own_last[...]) + wide(other_last[...])
    class_branch = jnp.sum(class_branch, axis=0)[CLASS_AT : CLASS_AT + 1] * (1.0 / FRAMES) + vector(outbias)
    at = iota((PAIR * ROWS, 1), 0)
    branch = wide(flat(own[...])) + wide(flat(other[...])) + vector(outbias)
    is_class = (at == PLACES) & (step == 0)
    mid = jnp.where(at % ROWS < PLACES, wide(flat(after[...])) + branch, 0.0)
    mid = mid + jnp.where(is_class, wide(after_last[0])[CLASS_AT : CLASS_AT + 1] + class_branch, 0.0)
    mid_out[...] = spread(mid)
    unit, _ = normed(mid)
    norm = (unit * vector(gain) + vector(shift)).astype(LOW)
    norm_out[...] = spread(norm)
    grad = flat(cot[...])
    part = jnp.zeros((PAIR * ROWS, width), jnp.float32)
    d_norm = jnp.zeros((PAIR * ROWS, width), jnp.float32)
    share = 512

    @pl.when(step == 0)
    def _():
        upbias_out[...] = jnp.zeros(upbias_out.shape, jnp.float32)

    for start in range(0, units, share):
        cols = slice(start, start + share)
        pre = dot(norm, upward[:, cols]) + vector(upbias)[:, cols]
        cumulative = 0.5 * (1.0 + lax.erf(pre * 0.5**0.5))
        slope = cumulative + pre * jnp.exp(-0.5 * pre * pre) * 0.3989422804014327
        act = (pre * cumulative).astype(LOW)
        act_out[:, :, cols] = spread(act)
        d_pre = (dot_last(grad, down[cols]) * slope).astype(LOW)
        dpre_out[:, :, cols] = spread(d_pre)
        upbias_out[:, cols] += column_sum(wide(d_pre))
        part = part + dot(act, down[cols])
        d_norm = d_norm + dot_last(d_pre, upward[:, cols])
    part_out[...] = spread(part)
    dnorm_out[...] = spread(d_norm)


def feed(own, other, after, cot, outbias, gain, shift, upward, upbias, down):
    width, units = upward.shape
    args = (own, other, after, cot, own, other, after, outbias, gain, shift, upward, upbias, down)
    outs = [
        shape((FRAMES, ROWS, width)),
        shape((FRAMES, ROWS, width)),
        shape((FRAMES, ROWS, units)),
        shape((FRAMES, ROWS, units)),
        shape((FRAMES, ROWS, width)),
        shape((FRAMES, ROWS, width)),
        shape((1, units), jnp.float32),
    ]
    tail = last_block(FRAMES)
    return call(
        feed_kernel,
        (FRAMES // PAIR,),
        [pairs(a) for a in args[:4]] + [tail(a) for a in args[4:7]] + [whole(a) for a in args[7:]],
        [pairs(o) for o in outs[:6]] + [whole(outs[6])],
        outs,
        [],
        2 * FRAMES * ROWS * width * units * 4,
        args,
    )


def space_backward_kernel(
    own, other, mid, cot, qkv, probs, own_last, other_last, mid_last, cot_last, gain, outproj, inproj,
    dspace_out, back_out, part_out, dclass_out, gain_out, shift_out, outbias_out, inbias_out,
):
    step = pl.program_id(0)
    half = outproj.shape[0]

    def spread(field):
        return field.astype(LOW).reshape(PAIR, ROWS, field.shape[1])

    def back(own_part, other_part, mid_part, cot_part):
        d_norm = wide(own_part) + wide(other_part)
        unit, inverse = normed(wide(mid_part))
        return wide(cot_part) + normed_back(unit, inverse, d_norm * vector(gain)), d_norm, d_norm * unit

    d_class = back(own_last[0], other_last[0], mid_last[0], cot_last[0])[0][CLASS_AT : CLASS_AT + 1]
    d_mid, d_shift, d_gain = back(flat(own[...]), flat(other[...]), flat(mid[...]), flat(cot[...]))
    place = place_of((PAIR * ROWS, 1))
    d_space = jnp.where(place < PLACES, d_mid, jnp.where(place == PLACES, d_class * (1.0 / FRAMES), 0.0))

    @pl.when(step == 0)
    def _():
        dclass_out[...] = d_class
        for ref in (gain_out, shift_out, outbias_out, inbias_out):
            ref[...] = jnp.zeros(ref.shape, jnp.float32)

    gain_out[...] += column_sum(d_gain)
    shift_out[...] += column_sum(d_shift)
    outbias_out[...] += column_sum(d_space)
    d_low = d_space.astype(LOW)
    dspace_out[...] = spread(d_low)
    d_mixed = dot_last(d_low, outproj[...]).astype(LOW)
    for frame in range(PAIR):
        rows = slice(frame * ROWS, (frame + 1) * ROWS)
        back_out[frame] = attend_back(qkv[frame], lambda head, frame=frame: probs[frame, head], d_mixed[rows])
    backs = flat(back_out[...])
    inbias_out[...] += column_sum(wide(backs))
    part_out[...] = spread(dot_last(backs, inproj[...]))


def space_backward(own, other, mid, cot, qkv, probs, gain, outproj, inproj):
    width = mid.shape[2]
    half = outproj.shape[0]
    args = (own, other, mid, cot, qkv, probs, own, other, mid, cot, gain, outproj, inproj)
    outs = [
        shape((FRAMES, ROWS, width)),
        shape((FRAMES, ROWS, 3 * half)),
        shape((FRAMES, ROWS, width)),
        shape((1, width), jnp.float32),
        shape((1, width), jnp.float32),
        shape((1, width), jnp.float32),
        shape((1, width), jnp.float32),
        shape((1, 3 * half), jnp.float32),
    ]
    tail = last_block(1)
    return call(
        space_backward_kernel,
        (FRAMES // PAIR,),
        [pairs(a) for a in args[:6]] + [tail(a) for a in args[6:10]] + [whole(a) for a in args[10:]],
        [pairs(o) for o in outs[:3]] + [whole(o) for o in outs[3:]],
        outs,
        [],
        2 * FRAMES * ROWS * width * half * 6,
        args,
    )


def mixer_backward_kernel(
    own, other, after, dspace, dclass, gain, mixer, outproj,
    dgrid_out, dmixer_out, dmixed_out, dsource_out, gain_out, shift_out, mixbias_out, outbias_out,
):
    @pl.when(pl.program_id(0) == 0)
    def _():
        dsource_out[...] = dclass[...]
        for ref in (gain_out, shift_out, mixbias_out, outbias_out):
            ref[...] = jnp.zeros(ref.shape, jnp.float32)

    def spread(field):
        return field.astype(LOW).reshape(PAIR, ROWS, field.shape[1])

    d_norm = wide(flat(own[...])) + wide(flat(other[...]))
    unit, inverse = normed(wide(flat(after[...])))
    gain_out[...] += column_sum(d_norm * unit)
    shift_out[...] += column_sum(d_norm)
    d_space_in = normed_back(unit, inverse, d_norm * vector(gain))
    place = place_of((PAIR * ROWS, 1))
    dsource_out[...] += column_sum(jnp.where(place == PLACES, d_space_in, 0.0))
    d_grid = jnp.where(place < PLACES, d_space_in + wide(flat(dspace[...])), 0.0)
    mixbias_out[...] += column_sum(d_grid)
    d_low = d_grid.astype(LOW)
    dgrid_out[...] = spread(d_low)
    d_mixer = dot_last(d_low, mixer[...]).astype(LOW)
    dmixer_out[...] = spread(d_mixer)
    outbias_out[...] += column_sum(wide(d_mixer))
    dmixed_out[...] = spread(dot_last(d_mixer, outproj[...]))


def mixer_backward(own, other, after, dspace, dclass, gain, mixer, outproj):
    width = after.shape[2]
    half = outproj.shape[0]
    args = (own, other, after, dspace, dclass, gain, mixer, outproj)
    outs = [
        shape((FRAMES, ROWS, width)),
        shape((FRAMES, ROWS, width)),
        shape((FRAMES, ROWS, half)),
    ] + [shape((1, width), jnp.float32)] * 5
    return call(
        mixer_backward_kernel,
        (FRAMES // PAIR,),
        [pairs(a) for a in args[:4]] + [whole(a) for a in args[4:]],
        [pairs(o) for o in outs[:3]] + [whole(o) for o in outs[3:]],
        outs,
        [],
        2 * FRAMES * ROWS * width * half * 3,
        args,
    )


def time_backward_kernel(d_mixed, qkv, probs, inproj, back_out, part_out, inbias_out):
    half = d_mixed.shape[2]
    width = inproj.shape[0]
    inbias_out[...] = jnp.zeros(inbias_out.shape, jnp.float32)

    def second(block, carry):
        at = pl.ds(pl.multiple_of(block * BLOCK, BLOCK), BLOCK)
        backs = attend_back(flat(qkv[:, at, :]), lambda head: probs[block, head], flat(d_mixed[:, at, :]))
        back_out[:, at, :] = backs.reshape(FRAMES, BLOCK, 3 * half)
        return carry

    lax.fori_loop(0, BLOCKS, second, 0)

    def third(step, carry):
        at = pl.ds(step * PAIR, PAIR)
        backs = flat(back_out[at])
        inbias_out[...] += column_sum(wide(backs))
        part_out[at] = dot_last(backs, inproj[...]).astype(LOW).reshape(PAIR, ROWS, width)
        return carry

    lax.fori_loop(0, FRAMES // PAIR, third, 0)


def time_backward(d_mixed, qkv, probs, inproj):
    width = inproj.shape[0]
    half = d_mixed.shape[2]
    args = (d_mixed, qkv, probs, inproj)
    outs = [
        shape((FRAMES, ROWS, 3 * half)),
        shape((FRAMES, ROWS, width)),
        shape((1, 3 * half), jnp.float32),
    ]
    return call(
        time_backward_kernel,
        (1,),
        [whole(a) for a in args],
        [whole(o) for o in outs],
        outs,
        [],
        2 * FRAMES * ROWS * width * half * 5,
        args,
    )


def blocks(array):
    return pl.BlockSpec((FRAMES, BLOCK, array.shape[2]), lambda at: (0, at, 0))


def put_tokens(out, rows, carry):
    low = rows.astype(LOW)
    moved = to_tokens(low)
    out[...] = jnp.where(iota((rows.shape[0], 1), 0) == 0, carry[...], moved).astype(out.dtype)
    carry[...] = rows[rows.shape[0] - 1 :].astype(LOW).astype(jnp.float32)


VECTORS = 16


def source_kernel(own, other, x, dgrid, dsource, gain, *rest):
    given = rest[:-3]
    out, packed, carry = rest[-3:]
    block = pl.program_id(0)
    width = packed.shape[1]

    @pl.when(block == 0)
    def _():
        carry[...] = dsource[...]
        packed[...] = jnp.zeros(packed.shape, jnp.float32)

    d_norm = wide(flat(own[...])) + wide(flat(other[...]))
    unit, inverse = normed(wide(flat(x[...])))
    packed[0:1] += column_sum(d_norm * unit)
    packed[1:2] += column_sum(d_norm)
    rows = wide(flat(dgrid[...])) + normed_back(unit, inverse, d_norm * vector(gain))
    put_tokens(out, rows, carry)

    @pl.when(block == BLOCKS - 1)
    def _():
        at = 2
        for ref in given:
            count = ref.shape[1]
            if count == 3 * width // 2:
                packed[at : at + 1] = jnp.concatenate([ref[:, : width // 2], ref[:, width:]], axis=1)
                at += 1
                continue
            for start in range(0, count, width):
                packed[at : at + 1] = ref[:, start : start + width]
                at += 1


def source_gradient(own, other, x, dgrid, dsource, gain, given, tokens):
    width = x.shape[2]
    args = (own, other, x, dgrid, dsource, gain) + tuple(given)
    outs = [shape((tokens, width)), shape((VECTORS, width), jnp.float32)]
    out_block = pl.BlockSpec((FRAMES * BLOCK, width), lambda at: (at, 0))
    return call(
        source_kernel,
        (BLOCKS,),
        [blocks(a) for a in args[:4]] + [whole(a) for a in args[4:]],
        [out_block, whole(outs[1])],
        outs,
        [pltpu.VMEM((1, width), jnp.float32)],
        2 * FRAMES * ROWS * 128 * width,
        args,
    )


def result_kernel(own, other, mid, own_last, other_last, mid_last, bias, live, out, carry):
    present = live[0, 0]

    def rows_of(own_part, other_part, mid_part):
        return (wide(mid_part) + wide(own_part) + wide(other_part) + vector(bias)) * present

    @pl.when(pl.program_id(0) == 0)
    def _():
        carry[...] = rows_of(own_last[0], other_last[0], mid_last[0])[CLASS_AT : CLASS_AT + 1]

    put_tokens(out, rows_of(flat(own[...]), flat(other[...]), flat(mid[...])), carry)


def result_tokens(own, other, mid, bias, live, tokens):
    width = mid.shape[2]
    args = (own, other, mid, own, other, mid, bias, live)
    tail = last_block(1)
    return call(
        result_kernel,
        (BLOCKS,),
        [blocks(a) for a in args[:3]] + [tail(a) for a in args[3:6]]
        + [whole(bias), pl.BlockSpec(memory_space=pltpu.SMEM)],
        [pl.BlockSpec((FRAMES * BLOCK, width), lambda at: (at, 0))],
        [shape((tokens, width))],
        [pltpu.VMEM((1, width), jnp.float32)],
        2 * FRAMES * ROWS * 128 * width,
        args,
    )[0]


def settle_kernel(place, total, *outs):
    width = total.shape[1]
    dests = width // outs[0].shape[0]
    share = width // dests
    at = place[0, 0]
    moved = pltpu.roll(total[...], (dests - at) % dests * share, 1)
    for row in range(10):
        outs[row][...] = moved[row, :share]
    small = share // 2
    moved = pltpu.roll(total[...], (2 * dests - at) % (2 * dests) * small, 1)
    for row in (10, 11):
        for part in range(2):
            start = part * (width // 2)
            outs[row][part : part + 1, :] = moved[row : row + 1, start : start + small]
    moved = pltpu.roll(total[...], (dests - 2 * at % dests) % dests * share, 1)
    outs[12][...] = jnp.where(2 * at < dests, moved[12, : 2 * share], moved[13, : 2 * share])


def settle(total, place, dests):
    width = total.shape[1]
    share = width // dests
    outs = [shape((share,), jnp.float32)] * 10
    outs += [shape((2, share // 2), jnp.float32)] * 2
    outs += [shape((2 * share,), jnp.float32)]
    args = (place, total)
    return call(
        settle_kernel,
        (1,),
        [pl.BlockSpec(memory_space=pltpu.SMEM), whole(total)],
        [whole(o) for o in outs],
        outs,
        [],
        0,
        args,
    )


def swap_tensor(field):
    size = lax.axis_size("tensor")
    return lax.ppermute(field, "tensor", [(i, i ^ 1) for i in range(size)])


def swap_dp(field, bits):
    return lax.ppermute(field, "dp", [(i, i ^ bits) for i in range(lax.axis_size("dp"))])


def pick(field, at, axis=0):
    return lax.dynamic_index_in_dim(field, at, axis, keepdims=False)


def add_low(left, right):
    return (wide(left) + wide(right)).astype(LOW)


def dp_reduction(first, second):
    size = lax.axis_size("dp")
    me = lax.axis_index("dp")
    share = first.shape[0] // size
    if size != 16:
        sums = []
        for field in (first, second):
            span = size // 2
            while span >= 1:
                field = field.reshape((2, span, share, -1))
                bit = (me // span) % 2
                field = add_low(pick(field, bit), swap_dp(pick(field, 1 - bit), span))
                span //= 2
            sums.append(wide(field[0]))
        for _ in range(3):
            yield ()
        yield tuple(sums)
        return
    first = first.reshape((4, 2, 2, share, -1))
    second = second.reshape((4, 2, 2, share, -1))
    x_bit = me % 2
    y_bit = me // 2 % 2
    got_first, got_second = yield (swap_dp(pick(first, 1 - x_bit, 2), 1), swap_dp(pick(second, 1 - y_bit, 1), 2))
    first = add_low(pick(first, x_bit, 2), got_first)
    second = add_low(pick(second, y_bit, 1), got_second)
    got_first, got_second = yield (swap_dp(pick(first, 1 - y_bit, 1), 2), swap_dp(pick(second, 1 - x_bit, 1), 1))
    first = add_low(pick(first, y_bit, 1), got_first)
    second = add_low(pick(second, x_bit, 1), got_second)
    both = jnp.concatenate([first, second], axis=2)
    z_at = me // 4
    gots = yield tuple(swap_dp(pick(both, z_at ^ step), 4 * step) for step in (1, 2, 3))
    total = wide(pick(both, z_at))
    for got in gots:
        total = total + wide(got)
    cut = first.shape[2]
    yield total[:, :cut], total[:, cut:]


def start(reduction):
    return next(reduction)


def after(reduction, moving, *done):
    moving, done = lax.optimization_barrier((moving, done))
    return (reduction.send(moving),) + tuple(done)


def dp_sum(field):
    span = 1
    while span < lax.axis_size("dp"):
        field = field + swap_dp(field, span)
        span *= 2
    return field


def grad_of(left, right):
    return lax.dot_general(
        left.reshape(-1, left.shape[2]),
        right.reshape(-1, right.shape[2]),
        (((0,), (0,)), ((), ())),
        preferred_element_type=jnp.float32,
    ).astype(LOW)


def local(
    clips,
    cotangent,
    live,
    time_gain,
    time_shift,
    time_inproj,
    time_inbias,
    time_outproj,
    time_outbias,
    time_mixer,
    time_mixbias,
    space_gain,
    space_shift,
    space_inproj,
    space_inbias,
    space_outproj,
    space_outbias,
    feed_gain,
    feed_shift,
    feed_upward,
    feed_upbias,
    feed_down,
    feed_downbias,
):
    tokens, width = clips.shape[1:]
    half = time_outproj.shape[0]
    dests = lax.axis_size("dp")
    share = width // dests
    tensor_rank = lax.axis_index("tensor")
    present = live.astype(jnp.float32).reshape(1, 1)
    time_in = time_inproj.reshape(width, 3 * half)
    space_in = space_inproj.reshape(width, 3 * half)
    mixer_other = swap_tensor(time_mixer)
    mixer = jnp.where(
        tensor_rank == 0,
        jnp.concatenate([time_mixer, mixer_other], axis=0),
        jnp.concatenate([mixer_other, time_mixer], axis=0),
    )
    x, t_norm, t_qkv, t_probs, t_mixed, t_part = time_forward(
        clips[0], time_gain, time_shift, time_in, time_inbias, time_outproj
    )
    cot, g_downbias = cotangent_frames(cotangent[0], present)
    mixer_in, after_time, s_norm, s_qkv, s_probs, s_mixed, s_part = space_forward(
        t_part, swap_tensor(t_part), x, time_outbias, mixer, time_mixbias, space_gain, space_shift, space_in,
        space_inbias, space_outproj,
    )
    mid, f_norm, act, d_pre, f_part, df_part, g_upbias = feed(
        s_part, swap_tensor(s_part), after_time, cot, space_outbias, feed_gain, feed_shift, feed_upward, feed_upbias,
        feed_down,
    )
    feed_sums = dp_reduction(grad_of(f_norm, d_pre), grad_of(cot, act))
    feed_moving = start(feed_sums)
    d_space, s_back, ds_part, d_class, g_feed_gain, g_feed_shift, g_space_outbias, g_space_inbias = space_backward(
        df_part, swap_tensor(df_part), mid, cot, s_qkv, s_probs, feed_gain, space_outproj, space_in
    )
    feed_moving, g_space_outbias = after(feed_sums, feed_moving, g_space_outbias)
    g_space_in = grad_of(s_norm, s_back)
    space_sums = dp_reduction(
        g_space_in[:, : 2 * half], jnp.concatenate([g_space_in[:, 2 * half :], grad_of(d_space, s_mixed)], axis=1)
    )
    space_moving = start(space_sums)
    d_grid, d_mixer, d_mixed, d_source, g_space_gain, g_space_shift, g_mixbias, g_outbias = mixer_backward(
        ds_part, swap_tensor(ds_part), after_time, d_space, d_class, space_gain, mixer, time_outproj
    )
    feed_moving, d_mixed = after(feed_sums, feed_moving, d_mixed)
    mixer_half = lax.dynamic_slice_in_dim(mixer_in, tensor_rank * half, half, 2)
    mixer_sums = dp_reduction(grad_of(d_mixer, t_mixed), grad_of(d_grid, mixer_half))
    mixer_moving = start(mixer_sums)
    t_back, dt_part, g_time_inbias = time_backward(d_mixed, t_qkv, t_probs, time_in)
    space_moving, mixer_moving, feed_moving, g_time_inbias = lax.optimization_barrier(
        (space_moving, mixer_moving, feed_moving, g_time_inbias)
    )
    space_moving = space_sums.send(space_moving)
    mixer_moving = mixer_sums.send(mixer_moving)
    up_sum, down_sum = feed_sums.send(feed_moving)
    g_time_in = grad_of(t_norm, t_back)
    time_sums = dp_reduction(g_time_in[:, : 3 * half // 2], g_time_in[:, 3 * half // 2 :])
    time_moving = start(time_sums)
    grad_clips, vectors = source_gradient(
        dt_part, swap_tensor(dt_part), x, d_grid, d_source, time_gain,
        (
            g_outbias, g_mixbias, g_space_gain, g_space_shift, g_space_outbias, g_feed_gain, g_feed_shift, g_downbias,
            g_time_inbias, g_space_inbias, g_upbias,
        ),
        tokens,
    )
    space_moving, mixer_moving, time_moving, vectors = lax.optimization_barrier(
        (space_moving, mixer_moving, time_moving, vectors)
    )
    time_moving = time_sums.send(time_moving)
    space_moving = space_sums.send(space_moving)
    mixer_moving = mixer_sums.send(mixer_moving)
    result = result_tokens(f_part, swap_tensor(f_part), mid, feed_downbias, present, tokens)
    space_moving, mixer_moving, time_moving, result = lax.optimization_barrier(
        (space_moving, mixer_moving, time_moving, result)
    )
    time_moving = time_sums.send(time_moving)
    space_a, space_b = space_sums.send(space_moving)
    out_sum, mixer_sum = mixer_sums.send(mixer_moving)
    time_a, time_b = time_sums.send(time_moving)
    small = settle(dp_sum(vectors), lax.axis_index("dp").astype(jnp.int32).reshape(1, 1), dests)
    settled = (
        small[0],
        small[1],
        jnp.concatenate([time_a, time_b], axis=1).reshape(share, 3, half),
        small[10],
        out_sum.T,
        small[2],
        mixer_sum.T,
        small[3],
        small[4],
        small[5],
        jnp.concatenate([space_a, space_b[:, :half]], axis=1).reshape(share, 3, half),
        small[11],
        space_b[:, half:].T,
        small[6],
        small[7],
        small[8],
        up_sum,
        small[12],
        down_sum.T,
        small[9],
    )
    return (result[None], grad_clips[None]) + settled


def solution(mesh):
    in_specs = (
        P("dp", None, None),
        P("dp", None, None),
        P("dp"),
        P(),
        P(),
        P(None, None, "tensor"),
        P(None, "tensor"),
        P("tensor", None),
        P(),
        P("tensor", None),
        P(),
        P(),
        P(),
        P(None, None, "tensor"),
        P(None, "tensor"),
        P("tensor", None),
        P(),
        P(),
        P(),
        P(None, "tensor"),
        P("tensor"),
        P("tensor", None),
        P(),
    )
    out_specs = (
        P("dp", None, None),
        P("dp", None, None),
        P("dp"),
        P("dp"),
        P("dp", None, "tensor"),
        P(None, ("tensor", "dp")),
        P("tensor", "dp"),
        P("dp"),
        P("tensor", "dp"),
        P("dp"),
        P("dp"),
        P("dp"),
        P("dp", None, "tensor"),
        P(None, ("tensor", "dp")),
        P("tensor", "dp"),
        P("dp"),
        P("dp"),
        P("dp"),
        P("dp", "tensor"),
        P(("tensor", "dp")),
        P("tensor", "dp"),
        P("dp"),
    )
    return jax.shard_map(local, mesh=mesh, in_specs=in_specs, out_specs=out_specs, check_vma=False)
```

```python
import functools

import jax
import jax.numpy as jnp
from jax import lax
from jax.experimental import pallas as pl
from jax.experimental.pallas import tpu as pltpu
from jax.sharding import PartitionSpec as P

HEAD = 64
FRAMES = 8
PLACES = 196
BLOCK = 16
ROWS = 208
BLOCKS = ROWS // BLOCK
PAIR = 2
UNROLL = BLOCKS
TIME_GROUP = 13
TIME_LAG = 1
SPACE_LAG = 6
EPS = 1e-06
LOW = jnp.bfloat16
VMEM_BYTES = 60 * 1024 * 1024
COST = 16


def dot(left, right):
    return jnp.dot(left, right, preferred_element_type=jnp.float32)


def dot_last(left, right):
    return lax.dot_general(left, right, (((1,), (1,)), ((), ())), preferred_element_type=jnp.float32)


def normed(field):
    center = field - jnp.mean(field, axis=-1, keepdims=True)
    spread_sq = jnp.mean(center * center, axis=-1, keepdims=True)
    inverse = lax.rsqrt(spread_sq + EPS)
    return center * inverse, inverse


def normed_back(unit, inverse, grad_unit):
    first = jnp.mean(grad_unit, axis=-1, keepdims=True)
    second = jnp.mean(grad_unit * unit, axis=-1, keepdims=True)
    return (grad_unit - first - unit * second) * inverse


def side_by_side(weights):
    return jnp.concatenate([weights[part] for part in range(weights.shape[0])], axis=1)


def flat(field):
    return field.reshape((field.shape[0] * field.shape[1],) + field.shape[2:])


def wide(field):
    return field.astype(jnp.float32)


def iota(shape, axis):
    return lax.broadcasted_iota(jnp.int32, shape, axis)


def column_sum(field):
    return jnp.sum(field, axis=0, keepdims=True)


def call(kernel, grid, in_specs, out_specs, out_shapes, scratch, flops, args):
    moved = sum(a.size * a.dtype.itemsize for a in args) + sum(o.size * o.dtype.itemsize for o in out_shapes)
    return pl.pallas_call(
        kernel,
        grid=grid,
        in_specs=in_specs,
        out_specs=out_specs,
        out_shape=out_shapes,
        scratch_shapes=scratch,
        compiler_params=pltpu.CompilerParams(vmem_limit_bytes=VMEM_BYTES),
        cost_estimate=pl.CostEstimate(flops=int(flops) // COST, bytes_accessed=int(moved) // COST, transcendentals=0),
    )(*args)


SCALAR = pl.BlockSpec(memory_space=pltpu.SMEM)


def whole(array):
    zeros = (0,) * array.ndim
    return pl.BlockSpec(array.shape, lambda *at: zeros)


def shape(dims, kind=LOW):
    return jax.ShapeDtypeStruct(dims, kind)


def to_frames(rows, block):
    count = FRAMES * BLOCK
    at = iota((count, count + BLOCK), 0)
    source = 1 + FRAMES * (at % BLOCK) + at // BLOCK
    pick = jnp.where(source == iota((count, count + BLOCK), 1), 1.0, 0.0).astype(LOW)
    return dot(pick, rows)


def to_tokens(rows):
    count = FRAMES * BLOCK
    at = iota((count, count), 1)
    target = 1 + FRAMES * (at % BLOCK) + at // BLOCK
    pick = jnp.where(target == iota((count, count), 0), 1.0, 0.0).astype(LOW)
    return dot(pick, rows)


def fill_rows(source, tokens):
    count = tokens.shape[0]
    even = count // BLOCK * BLOCK
    source[0:even] = tokens[0:even]
    source[even:] = jnp.zeros((source.shape[0] - even, source.shape[1]), source.dtype)
    left = wide(tokens[even:count])
    tail = jnp.zeros((BLOCK, source.shape[1]), jnp.float32)
    for row in range(count - even):
        tail = tail + jnp.where(iota(tail.shape, 0) == row, left[row : row + 1], 0.0)
    source[even : even + BLOCK] = tail.astype(source.dtype)


def frame_rows(source, block, class_row, class_frames):
    count = FRAMES * BLOCK
    rows = to_frames(source[pl.ds(pl.multiple_of(block * count, count), count + BLOCK), :], block)
    at = iota((count, 1), 0)
    is_class = (block * BLOCK + at % BLOCK == PLACES) & (at // BLOCK < class_frames)
    return rows + jnp.where(is_class, class_row, 0.0)


class Copies:
    def __init__(self, semaphores):
        self.semaphores = semaphores
        self.started = []

    def start(self, source, target):
        copy = pltpu.make_async_copy(source, target, self.semaphores.at[len(self.started)])
        copy.start()
        self.started.append(copy)
        return copy


def time_forward_kernel(
    clips, gain, shift, inproj_far, inbias, outproj_far, x_far, norm_far, qkv_far, probs_far, mixed_far, part_far,
    inproj, outproj, x_out, norm_out, qkv_out, probs_out, mixed_out, part_out, source, semaphores,
):
    half = outproj.shape[0]
    copies = Copies(semaphores)
    fetched = [copies.start(inproj_far, inproj), copies.start(outproj_far, outproj)]
    fill_rows(source, clips)
    class_row = wide(clips[0:1])

    def first(block, carry):
        rows = frame_rows(source, block, class_row, FRAMES)
        unit, _ = normed(rows)
        at = pl.ds(pl.multiple_of(block * BLOCK, BLOCK), BLOCK)
        x_out[:, at, :] = rows.astype(LOW).reshape(FRAMES, BLOCK, rows.shape[1])
        norm_out[:, at, :] = (unit * vector(gain) + vector(shift)).astype(LOW).reshape(FRAMES, BLOCK, rows.shape[1])
        return carry

    lax.fori_loop(0, BLOCKS, first, 0, unroll=UNROLL)
    sent = [copies.start(x_out, x_far), copies.start(norm_out, norm_far)]
    fetched[0].wait()
    weights = side_by_side(inproj)
    for step in range(FRAMES // PAIR):
        at = pl.ds(step * PAIR, PAIR)
        qkv = heads_low(dot(flat(norm_out[at]), weights), inbias, half)
        qkv_out[at] = qkv.reshape(PAIR, ROWS, 3 * half)
    sent.append(copies.start(qkv_out, qkv_far))
    count = FRAMES * BLOCK
    same = iota((count, 2 * count), 0) % BLOCK == iota((count, 2 * count), 1) % BLOCK

    def third(first_block, count):
        ats = [
            pl.ds(pl.multiple_of((first_block + step) * BLOCK, BLOCK), BLOCK) for step in range(count)
        ]

        def keep(step, head, probs):
            probs_out[first_block + step, head] = probs

        mixed = attend(
            [flat(qkv_out[:, at, :]) for at in ats], lambda scores: jnp.where(same, scores, -1e30), keep, 2, TIME_LAG
        )
        for at, part in zip(ats, mixed):
            mixed_out[:, at, :] = part.reshape(FRAMES, BLOCK, half)

    by_blocks(third)
    sent += [copies.start(probs_out, probs_far), copies.start(mixed_out, mixed_far)]
    fetched[1].wait()
    for step in range(FRAMES // PAIR):
        at = pl.ds(step * PAIR, PAIR)
        part = dot(flat(mixed_out[at]), outproj[...]).astype(LOW)
        part_out[at] = part.reshape(PAIR, ROWS, part.shape[1])
        sent.append(copies.start(part_out.at[at], part_far.at[at]))
    for copy in sent:
        copy.wait()


def by_blocks(run):
    def step(at, carry):
        run(at * TIME_GROUP, TIME_GROUP)
        return carry

    lax.fori_loop(0, BLOCKS // TIME_GROUP, step, 0)
    if BLOCKS % TIME_GROUP:
        run(BLOCKS // TIME_GROUP * TIME_GROUP, BLOCKS % TIME_GROUP)


def heads_low(linear, inbias, half):
    query = ((linear[:, :half] + inbias[0:1]) * HEAD ** (-0.5)).astype(LOW)
    keys = linear[:, half : 2 * half].astype(LOW)
    values = (linear[:, 2 * half :] + inbias[1:2]).astype(LOW)
    return jnp.concatenate([query, keys, values], axis=1)


def beside(field_t, head):
    own = field_t[HEAD * head : HEAD * (head + 1)]
    none = jnp.zeros_like(own)
    return jnp.concatenate([own, none] if head % 2 == 0 else [none, own], axis=0)


def beside_all(field_t, heads):
    return jnp.concatenate([beside(field_t, head) for head in heads], axis=1)


def pair_of(field, head):
    start = head // 2 * 2 * HEAD
    return field[:, start : start + 2 * HEAD]


def head_rows(field_t, head):
    return field_t[HEAD * head : HEAD * (head + 1)]


def staged(count, stages, lag):
    held = [None] * count
    for step in range(count + lag * (len(stages) - 1)):
        for depth, stage in enumerate(stages):
            item = step - lag * depth
            if 0 <= item < count:
                held[item] = stage(item, held[item])
    return held


def attend(inputs, block_allowed, keep, group, lag):
    half = inputs[0].shape[1] // 3
    rows = inputs[0].shape[0]
    query_t = [qkv[:, :half].T for qkv in inputs]
    values_t = [qkv[:, 2 * half :].T for qkv in inputs]
    groups = half // HEAD // group

    def heads_of(item):
        first = item % groups * group
        return range(first, first + group)

    def score(item, held):
        block = item // groups
        keys = inputs[block][:, half : 2 * half]
        return dot(pair_of(keys, heads_of(item)[0]), beside_all(query_t[block], heads_of(item)))

    def weigh(item, scores):
        scores = block_allowed(scores)
        expon = jnp.exp(scores - jnp.max(scores, axis=0, keepdims=True))
        probs = (expon * (1.0 / column_sum(expon))).astype(LOW)
        for at, head in enumerate(heads_of(item)):
            keep(item // groups, head, probs[:, at * rows : (at + 1) * rows])
        return probs

    def mix(item, probs):
        return [
            dot(head_rows(values_t[item // groups], head), probs[:, at * rows : (at + 1) * rows])
            for at, head in enumerate(heads_of(item))
        ]

    mixed_t = staged(len(inputs) * groups, [score, weigh, mix], lag)
    out = []
    for block in range(len(inputs)):
        parts = [part for item in mixed_t[block * groups : (block + 1) * groups] for part in item]
        out.append(jnp.concatenate(parts, axis=0).T.astype(LOW))
    return out


def attend_back(inputs, probs_of, d_mixeds, group, lag):
    half = inputs[0].shape[1] // 3
    rows = inputs[0].shape[0]
    keys_t = [qkv[:, half : 2 * half].T for qkv in inputs]
    d_mixed_t = [d_mixed.T for d_mixed in d_mixeds]
    lane = iota((rows, 2 * HEAD), 1) < HEAD
    groups = half // HEAD // group

    def heads_of(item):
        first = item % groups * group
        return range(first, first + group)

    def score(item, held):
        block = item // groups
        values = inputs[block][:, 2 * half :]
        return dot(pair_of(values, heads_of(item)[0]), beside_all(d_mixed_t[block], heads_of(item)))

    def weigh(item, d_probs):
        probs_low = jnp.concatenate([probs_of(item // groups, head) for head in heads_of(item)], axis=1)
        probs = wide(probs_low)
        scaled = probs * d_probs
        d_scores = scaled - probs * column_sum(scaled)
        return probs_low, d_scores.astype(LOW)

    def halves(field):
        none = jnp.zeros_like(field)
        return jnp.concatenate([jnp.where(lane, field, none), jnp.where(lane, none, field)], axis=0)

    def mix(item, held):
        block = item // groups
        probs_low, d_scores = held
        d_query_t = [
            dot(head_rows(keys_t[block], head), d_scores[:, at * rows : (at + 1) * rows])
            for at, head in enumerate(heads_of(item))
        ]
        d_mixed = pair_of(d_mixeds[block], heads_of(item)[0])
        query = pair_of(inputs[block][:, :half], heads_of(item)[0])
        if group == 2:
            d_mixed = halves(d_mixed)
            query = halves(query)
        return d_query_t, dot(d_scores, query), dot(probs_low, d_mixed)

    made = staged(len(inputs) * groups, [score, weigh, mix], lag)

    def paired(fields):
        if group == 2:
            return fields
        return [jnp.where(lane, fields[at], fields[at + 1]) for at in range(0, len(fields), 2)]

    out = []
    for block in range(len(inputs)):
        own = made[block * groups : (block + 1) * groups]
        d_query = jnp.concatenate([part for item in own for part in item[0]], axis=0).T.astype(LOW) * HEAD ** (-0.5)
        d_keys = paired([item[1] for item in own])
        d_values = paired([item[2] for item in own])
        out.append(jnp.concatenate([d_query] + [d.astype(LOW) for d in d_keys + d_values], axis=1))
    return out


def time_forward(clips, gain, shift, inproj, inbias, outproj):
    tokens, width = clips.shape
    half = outproj.shape[0]
    heads = half // HEAD
    count = FRAMES * BLOCK
    args = (clips, gain, shift, inproj, inbias, outproj)
    outs = [
        shape((FRAMES, ROWS, width)),
        shape((FRAMES, ROWS, width)),
        shape((FRAMES, ROWS, 3 * half)),
        shape((BLOCKS, heads, count, count)),
        shape((FRAMES, ROWS, half)),
        shape((FRAMES, ROWS, width)),
    ]
    rows = FRAMES * ROWS
    near = [pltpu.VMEM(a.shape, a.dtype) for a in (inproj, outproj)] + [pltpu.VMEM(o.shape, o.dtype) for o in outs]
    far = pl.BlockSpec(memory_space=pl.ANY)
    return call(
        time_forward_kernel,
        (1,),
        [whole(clips), whole(gain), whole(shift), far, whole(inbias), far],
        [far] * 6,
        outs,
        near + [pltpu.VMEM((BLOCKS * count + BLOCK, width), LOW), pltpu.SemaphoreType.DMA((16,))],
        2 * rows * width * half * 5,
        args,
    )


def cotangent_kernel(cotangent, live, out, total, source):
    fill_rows(source, cotangent)
    present = live[0, 0]
    class_row = wide(cotangent[0:1])

    def first(block, carry):
        rows = frame_rows(source, block, class_row, 1) * present
        at = pl.ds(pl.multiple_of(block * BLOCK, BLOCK), BLOCK)
        out[:, at, :] = rows.astype(LOW).reshape(FRAMES, BLOCK, rows.shape[1])
        return carry + column_sum(rows)

    total[...] = lax.fori_loop(0, BLOCKS, first, jnp.zeros(total.shape, jnp.float32), unroll=UNROLL)


def cotangent_frames(cotangent, live):
    tokens, width = cotangent.shape
    args = (cotangent, live)
    outs = [shape((FRAMES, ROWS, width)), shape((1, width), jnp.float32)]
    return call(
        cotangent_kernel,
        (1,),
        [whole(cotangent), SCALAR],
        [whole(o) for o in outs],
        outs,
        [pltpu.VMEM((BLOCKS * FRAMES * BLOCK + BLOCK, width), LOW)],
        2 * FRAMES * ROWS * 128 * width,
        args,
    )


def vector(ref):
    return ref[...].reshape(1, -1)


def place_of(shape_of):
    return iota(shape_of, 0) % ROWS


def gather_mixer(own, other, rank, mixer):
    half = own.shape[0]

    @pl.when(pl.program_id(0) == 0)
    def _():
        mixer[pl.ds(pl.multiple_of(rank[0, 0] * half, half), half), :] = own[...]
        mixer[pl.ds(pl.multiple_of((1 - rank[0, 0]) * half, half), half), :] = other[...]


def space_forward_kernel(
    own, other, x, outbias, mixer_own, mixer_other, rank, mixbias, gain, shift, inproj, inbias, outproj,
    mixer_out, after_out, norm_out, qkv_out, probs_out, mixed_out, part_out, mixer,
):
    gather_mixer(mixer_own, mixer_other, rank, mixer)
    half = outproj.shape[0]
    width = outproj.shape[1]

    def spread(field):
        return field.astype(LOW).reshape(PAIR, ROWS, field.shape[1])

    mixer_in = (wide(flat(own[...])) + wide(flat(other[...])) + vector(outbias)).astype(LOW)
    mixer_out[...] = spread(mixer_in)
    branch = dot(mixer_in, mixer[...]) + vector(mixbias)
    after = wide(flat(x[...])) + jnp.where(place_of((PAIR * ROWS, 1)) < PLACES, branch, 0.0)
    after_out[...] = spread(after)
    unit, _ = normed(after)
    norm = (unit * vector(gain) + vector(shift)).astype(LOW)
    norm_out[...] = spread(norm)
    qkv = heads_low(dot(norm, side_by_side(inproj)), inbias, half)
    qkv_out[...] = spread(qkv)

    def allowed(scores):
        even = ROWS - BLOCK
        last = jnp.where(iota((BLOCK, ROWS), 0) <= PLACES - even, scores[even:], -1e30)
        return jnp.concatenate([scores[:even], last], axis=0)

    def keep(frame, head, probs):
        probs_out[frame, head] = probs

    frames = [qkv[frame * ROWS : (frame + 1) * ROWS] for frame in range(PAIR)]
    for frame, mixed in enumerate(attend(frames, allowed, keep, 1, SPACE_LAG)):
        mixed_out[frame] = mixed
    part_out[...] = spread(dot(flat(mixed_out[...]), outproj[...]))


def pairs(array):
    rest = (0,) * (array.ndim - 1)
    return pl.BlockSpec((PAIR,) + array.shape[1:], lambda at: (at,) + rest)


def space_forward(own, other, x, outbias, mixers, mixbias, gain, shift, inproj, inbias, outproj):
    width = x.shape[2]
    half = outproj.shape[0]
    heads = half // HEAD
    args = (own, other, x, outbias) + mixers + (mixbias, gain, shift, inproj, inbias, outproj)
    outs = [
        shape((FRAMES, ROWS, width)),
        shape((FRAMES, ROWS, width)),
        shape((FRAMES, ROWS, width)),
        shape((FRAMES, ROWS, 3 * half)),
        shape((FRAMES, heads, ROWS, ROWS)),
        shape((FRAMES, ROWS, half)),
        shape((FRAMES, ROWS, width)),
    ]
    return call(
        space_forward_kernel,
        (FRAMES // PAIR,),
        [pairs(a) for a in args[:3]] + [whole(a) for a in args[3:6]] + [SCALAR] + [whole(a) for a in args[7:]],
        [pairs(o) for o in outs],
        outs,
        [pltpu.VMEM((width, width), LOW)],
        2 * FRAMES * ROWS * width * half * 8,
        args,
    )


def last_block(count):
    return lambda array: pl.BlockSpec((count, BLOCK, array.shape[2]), lambda at: (0, BLOCKS - 1, 0))


CLASS_AT = PLACES - (BLOCKS - 1) * BLOCK


def feed_kernel(
    own, other, after, cot, own_last, other_last, after_last, outbias, gain, shift, upward, upbias, down,
    mid_out, norm_out, act_out, dpre_out, part_out, dnorm_out, upbias_out,
):
    step = pl.program_id(0)
    units = upward.shape[1]
    width = upward.shape[0]

    def spread(field):
        return field.astype(LOW).reshape(PAIR, ROWS, field.shape[1])

    class_branch = wide(own_last[...]) + wide(other_last[...])
    class_branch = jnp.sum(class_branch, axis=0)[CLASS_AT : CLASS_AT + 1] * (1.0 / FRAMES) + vector(outbias)
    at = iota((PAIR * ROWS, 1), 0)
    branch = wide(flat(own[...])) + wide(flat(other[...])) + vector(outbias)
    is_class = (at == PLACES) & (step == 0)
    mid = jnp.where(at % ROWS < PLACES, wide(flat(after[...])) + branch, 0.0)
    mid = mid + jnp.where(is_class, wide(after_last[0])[CLASS_AT : CLASS_AT + 1] + class_branch, 0.0)
    mid_out[...] = spread(mid)
    unit, _ = normed(mid)
    norm = (unit * vector(gain) + vector(shift)).astype(LOW)
    norm_out[...] = spread(norm)
    grad = flat(cot[...])
    part = jnp.zeros((PAIR * ROWS, width), jnp.float32)
    d_norm = jnp.zeros((PAIR * ROWS, width), jnp.float32)
    share = 512

    @pl.when(step == 0)
    def _():
        upbias_out[...] = jnp.zeros(upbias_out.shape, jnp.float32)

    for start in range(0, units, share):
        cols = slice(start, start + share)
        pre = dot(norm, upward[:, cols]) + vector(upbias)[:, cols]
        cumulative = 0.5 * (1.0 + lax.erf(pre * 0.5**0.5))
        slope = cumulative + pre * jnp.exp(-0.5 * pre * pre) * 0.3989422804014327
        act = (pre * cumulative).astype(LOW)
        act_out[:, :, cols] = spread(act)
        d_pre = (dot_last(grad, down[cols]) * slope).astype(LOW)
        dpre_out[:, :, cols] = spread(d_pre)
        upbias_out[:, cols] += column_sum(wide(d_pre))
        part = part + dot(act, down[cols])
        d_norm = d_norm + dot_last(d_pre, upward[:, cols])
    part_out[...] = spread(part)
    dnorm_out[...] = spread(d_norm)


def feed(own, other, after, cot, outbias, gain, shift, upward, upbias, down):
    width, units = upward.shape
    args = (own, other, after, cot, own, other, after, outbias, gain, shift, upward, upbias, down)
    outs = [
        shape((FRAMES, ROWS, width)),
        shape((FRAMES, ROWS, width)),
        shape((FRAMES, ROWS, units)),
        shape((FRAMES, ROWS, units)),
        shape((FRAMES, ROWS, width)),
        shape((FRAMES, ROWS, width)),
        shape((1, units), jnp.float32),
    ]
    tail = last_block(FRAMES)
    return call(
        feed_kernel,
        (FRAMES // PAIR,),
        [pairs(a) for a in args[:4]] + [tail(a) for a in args[4:7]] + [whole(a) for a in args[7:]],
        [pairs(o) for o in outs[:6]] + [whole(outs[6])],
        outs,
        [],
        2 * FRAMES * ROWS * width * units * 4,
        args,
    )


def space_backward_kernel(
    own, other, mid, cot, qkv, probs, own_last, other_last, mid_last, cot_last, gain, outproj, inproj,
    dspace_out, back_out, part_out, dclass_out, gain_out, shift_out, outbias_out, inbias_out,
):
    step = pl.program_id(0)
    half = outproj.shape[0]

    def spread(field):
        return field.astype(LOW).reshape(PAIR, ROWS, field.shape[1])

    def back(own_part, other_part, mid_part, cot_part):
        d_norm = wide(own_part) + wide(other_part)
        unit, inverse = normed(wide(mid_part))
        return wide(cot_part) + normed_back(unit, inverse, d_norm * vector(gain)), d_norm, d_norm * unit

    d_class = back(own_last[0], other_last[0], mid_last[0], cot_last[0])[0][CLASS_AT : CLASS_AT + 1]
    d_mid, d_shift, d_gain = back(flat(own[...]), flat(other[...]), flat(mid[...]), flat(cot[...]))
    place = place_of((PAIR * ROWS, 1))
    d_space = jnp.where(place < PLACES, d_mid, jnp.where(place == PLACES, d_class * (1.0 / FRAMES), 0.0))

    @pl.when(step == 0)
    def _():
        dclass_out[...] = d_class
        for ref in (gain_out, shift_out, outbias_out, inbias_out):
            ref[...] = jnp.zeros(ref.shape, jnp.float32)

    gain_out[...] += column_sum(d_gain)
    shift_out[...] += column_sum(d_shift)
    outbias_out[...] += column_sum(d_space)
    d_low = d_space.astype(LOW)
    dspace_out[...] = spread(d_low)
    d_mixed = dot_last(d_low, outproj[...]).astype(LOW)
    made = attend_back(
        [qkv[frame] for frame in range(PAIR)],
        lambda frame, head: probs[frame, head],
        [d_mixed[frame * ROWS : (frame + 1) * ROWS] for frame in range(PAIR)],
        1,
        SPACE_LAG,
    )
    for frame, part in enumerate(made):
        back_out[frame] = part
    backs = flat(back_out[...])
    inbias_out[...] += column_sum(wide(backs))
    part_out[...] = spread(dot_last(backs, side_by_side(inproj)))


def space_backward(own, other, mid, cot, qkv, probs, gain, outproj, inproj):
    width = mid.shape[2]
    half = outproj.shape[0]
    args = (own, other, mid, cot, qkv, probs, own, other, mid, cot, gain, outproj, inproj)
    outs = [
        shape((FRAMES, ROWS, width)),
        shape((FRAMES, ROWS, 3 * half)),
        shape((FRAMES, ROWS, width)),
        shape((1, width), jnp.float32),
        shape((1, width), jnp.float32),
        shape((1, width), jnp.float32),
        shape((1, width), jnp.float32),
        shape((1, 3 * half), jnp.float32),
    ]
    tail = last_block(1)
    return call(
        space_backward_kernel,
        (FRAMES // PAIR,),
        [pairs(a) for a in args[:6]] + [tail(a) for a in args[6:10]] + [whole(a) for a in args[10:]],
        [pairs(o) for o in outs[:3]] + [whole(o) for o in outs[3:]],
        outs,
        [],
        2 * FRAMES * ROWS * width * half * 6,
        args,
    )


def mixer_backward_kernel(
    own, other, after, dspace, dclass, gain, mixer_own, mixer_other, rank, outproj,
    dgrid_out, dmixer_out, dmixed_out, dsource_out, gain_out, shift_out, mixbias_out, outbias_out, mixer,
):
    gather_mixer(mixer_own, mixer_other, rank, mixer)

    @pl.when(pl.program_id(0) == 0)
    def _():
        dsource_out[...] = dclass[...]
        for ref in (gain_out, shift_out, mixbias_out, outbias_out):
            ref[...] = jnp.zeros(ref.shape, jnp.float32)

    def spread(field):
        return field.astype(LOW).reshape(PAIR, ROWS, field.shape[1])

    d_norm = wide(flat(own[...])) + wide(flat(other[...]))
    unit, inverse = normed(wide(flat(after[...])))
    gain_out[...] += column_sum(d_norm * unit)
    shift_out[...] += column_sum(d_norm)
    d_space_in = normed_back(unit, inverse, d_norm * vector(gain))
    place = place_of((PAIR * ROWS, 1))
    dsource_out[...] += column_sum(jnp.where(place == PLACES, d_space_in, 0.0))
    d_grid = jnp.where(place < PLACES, d_space_in + wide(flat(dspace[...])), 0.0)
    mixbias_out[...] += column_sum(d_grid)
    d_low = d_grid.astype(LOW)
    dgrid_out[...] = spread(d_low)
    d_mixer = dot_last(d_low, mixer[...]).astype(LOW)
    dmixer_out[...] = spread(d_mixer)
    outbias_out[...] += column_sum(wide(d_mixer))
    dmixed_out[...] = spread(dot_last(d_mixer, outproj[...]))


def mixer_backward(own, other, after, dspace, dclass, gain, mixers, outproj):
    width = after.shape[2]
    half = outproj.shape[0]
    args = (own, other, after, dspace, dclass, gain) + mixers + (outproj,)
    outs = [
        shape((FRAMES, ROWS, width)),
        shape((FRAMES, ROWS, width)),
        shape((FRAMES, ROWS, half)),
    ] + [shape((1, width), jnp.float32)] * 5
    return call(
        mixer_backward_kernel,
        (FRAMES // PAIR,),
        [pairs(a) for a in args[:4]] + [whole(a) for a in args[4:8]] + [SCALAR, whole(outproj)],
        [pairs(o) for o in outs[:3]] + [whole(o) for o in outs[3:]],
        outs,
        [pltpu.VMEM((width, width), LOW)],
        2 * FRAMES * ROWS * width * half * 3,
        args,
    )


def time_backward_kernel(d_mixed, qkv, probs, inproj, back_out, part_out, inbias_out):
    half = d_mixed.shape[2]
    width = inproj.shape[1]
    inbias_out[...] = jnp.zeros(inbias_out.shape, jnp.float32)

    def second(first_block, count):
        ats = [
            pl.ds(pl.multiple_of((first_block + step) * BLOCK, BLOCK), BLOCK) for step in range(count)
        ]
        made = attend_back(
            [flat(qkv[:, at, :]) for at in ats],
            lambda step, head: probs[first_block + step, head],
            [flat(d_mixed[:, at, :]) for at in ats],
            2,
            TIME_LAG,
        )
        for at, part in zip(ats, made):
            back_out[:, at, :] = part.reshape(FRAMES, BLOCK, 3 * half)

    by_blocks(second)

    def third(step, carry):
        at = pl.ds(step * PAIR, PAIR)
        backs = flat(back_out[at])
        inbias_out[...] += column_sum(wide(backs))
        part_out[at] = dot_last(backs, side_by_side(inproj)).astype(LOW).reshape(PAIR, ROWS, width)
        return carry

    lax.fori_loop(0, FRAMES // PAIR, third, 0, unroll=True)


def time_backward(d_mixed, qkv, probs, inproj):
    width = inproj.shape[1]
    half = d_mixed.shape[2]
    args = (d_mixed, qkv, probs, inproj)
    outs = [
        shape((FRAMES, ROWS, 3 * half)),
        shape((FRAMES, ROWS, width)),
        shape((1, 3 * half), jnp.float32),
    ]
    return call(
        time_backward_kernel,
        (1,),
        [whole(a) for a in args],
        [whole(o) for o in outs],
        outs,
        [],
        2 * FRAMES * ROWS * width * half * 5,
        args,
    )


def put_tokens(out, block, low, carry):
    count = FRAMES * BLOCK
    moved = jnp.where(iota((count, 1), 0) == 0, carry, to_tokens(low))
    fits = min(out.shape[0] - block * count, count)
    out[block * count : block * count + fits] = moved[:fits].astype(out.dtype)
    return wide(low[count - BLOCK :])[BLOCK - 1 :]


def block_rows(ref, block):
    return wide(flat(ref[:, block * BLOCK : (block + 1) * BLOCK, :]))


VECTORS = 16


def source_kernel(own, other, x, dgrid, dsource, gain, *rest):
    given = rest[:-2]
    out, packed = rest[-2:]
    width = packed.shape[1]
    carry = dsource[...]
    d_gain = jnp.zeros((1, width), jnp.float32)
    d_shift = jnp.zeros((1, width), jnp.float32)
    for block in range(BLOCKS):
        d_norm = block_rows(own, block) + block_rows(other, block)
        unit, inverse = normed(block_rows(x, block))
        d_gain = d_gain + column_sum(d_norm * unit)
        d_shift = d_shift + column_sum(d_norm)
        rows = block_rows(dgrid, block) + normed_back(unit, inverse, d_norm * vector(gain))
        carry = put_tokens(out, block, rows.astype(LOW), carry)
    packed[...] = jnp.zeros(packed.shape, jnp.float32)
    packed[0:1] = d_gain
    packed[1:2] = d_shift
    at = 2
    for ref in given:
        count = ref.shape[1]
        if count == 3 * width // 2:
            packed[at : at + 1] = jnp.concatenate([ref[:, : width // 2], ref[:, width:]], axis=1)
            at += 1
            continue
        for start in range(0, count, width):
            packed[at : at + 1] = ref[:, start : start + width]
            at += 1


def source_gradient(own, other, x, dgrid, dsource, gain, given, tokens):
    width = x.shape[2]
    args = (own, other, x, dgrid, dsource, gain) + tuple(given)
    outs = [shape((tokens, width)), shape((VECTORS, width), jnp.float32)]
    return call(
        source_kernel,
        (1,),
        [whole(a) for a in args],
        [whole(o) for o in outs],
        outs,
        [],
        2 * FRAMES * ROWS * 128 * width,
        args,
    )


def result_kernel(own, other, mid, bias, live, out):
    present = live[0, 0]
    even = (BLOCKS - 1) * BLOCK

    def rows_of(take):
        return ((take(mid) + take(own) + take(other) + vector(bias)) * present).astype(LOW)

    carry = wide(rows_of(lambda ref: wide(ref[0, even:])))[PLACES - even : PLACES - even + 1]
    for block in range(BLOCKS):
        carry = put_tokens(out, block, rows_of(lambda ref: block_rows(ref, block)), carry)


def result_tokens(own, other, mid, bias, live, tokens):
    width = mid.shape[2]
    args = (own, other, mid, bias, live)
    outs = [shape((tokens, width))]
    return call(
        result_kernel,
        (1,),
        [whole(a) for a in args[:4]] + [SCALAR],
        [whole(outs[0])],
        outs,
        [],
        2 * FRAMES * ROWS * 128 * width,
        args,
    )[0]


def settle_kernel(place, total, *outs):
    width = total.shape[1]
    dests = width // outs[0].shape[0]
    share = width // dests
    at = place[0, 0]
    moved = pltpu.roll(total[...], (dests - at) % dests * share, 1)
    for row in range(10):
        outs[row][...] = moved[row, :share]
    small = share // 2
    moved = pltpu.roll(total[...], (2 * dests - at) % (2 * dests) * small, 1)
    for row in (10, 11):
        for part in range(2):
            start = part * (width // 2)
            outs[row][part : part + 1, :] = moved[row : row + 1, start : start + small]
    moved = pltpu.roll(total[...], (dests - 2 * at % dests) % dests * share, 1)
    outs[12][...] = jnp.where(2 * at < dests, moved[12, : 2 * share], moved[13, : 2 * share])


def settle(total, place, dests):
    width = total.shape[1]
    share = width // dests
    outs = [shape((share,), jnp.float32)] * 10
    outs += [shape((2, share // 2), jnp.float32)] * 2
    outs += [shape((2 * share,), jnp.float32)]
    args = (place, total)
    return call(
        settle_kernel,
        (1,),
        [SCALAR, whole(total)],
        [whole(o) for o in outs],
        outs,
        [],
        0,
        args,
    )


def swap_tensor(field):
    size = lax.axis_size("tensor")
    return lax.ppermute(field, "tensor", [(i, i ^ 1) for i in range(size)])


def swap_dp(field, bits):
    return lax.ppermute(field, "dp", [(i, i ^ bits) for i in range(lax.axis_size("dp"))])


def pick(field, at, axis=0):
    return lax.dynamic_index_in_dim(field, at, axis, keepdims=False)


def add_low(left, right):
    return (wide(left) + wide(right)).astype(LOW)


class Reduction:
    def __init__(self, fields, orders, direct=False):
        size = lax.axis_size("dp")
        me = lax.axis_index("dp")
        share = fields[0].shape[0] // size
        self.small = size == 16
        self.direct = direct
        self.ready = ()
        self.cuts = [field.shape[1] for field in fields]
        if not self.small:
            self.sums = []
            for field in fields:
                span = size // 2
                while span >= 1:
                    field = field.reshape((2, span, share, -1))
                    bit = (me // span) % 2
                    field = add_low(pick(field, bit), swap_dp(pick(field, 1 - bit), span))
                    span //= 2
                self.sums.append(wide(field[0]))
            return
        self.z_at = me // 4
        self.bits = {"x": me % 2, "y": me // 2 % 2, "near": self.z_at % 2, "far": self.z_at // 2}
        self.spans = {"x": 1, "y": 2, "near": 4, "far": 8}
        self.orders = [list(order) for order in orders]
        self.pieces = [[field.reshape((2, 2, 2, 2, share, -1))] for field in fields]
        self.prepare()

    def part(self, piece, name, bit):
        axis = {"far": 0, "near": 1, "y": 2, "x": 3}[name]
        return lax.dynamic_slice_in_dim(piece, bit, 1, axis)

    def total(self, pieces):
        if len(pieces) == 1:
            return pieces[0]
        return sum(wide(piece) for piece in pieces).astype(LOW)

    def prepare(self):
        if self.orders[0]:
            names = [order.pop(0) for order in self.orders]
        else:
            if len(self.pieces) > 1:
                joined = [self.total(pieces) for pieces in self.pieces]
                self.pieces = [[jnp.concatenate(joined, axis=5)]]
            if self.direct:
                whole_line = self.total(self.pieces[0])
                line = whole_line.reshape((4,) + whole_line.shape[4:])
                self.own = pick(line, self.z_at)
                self.ready = tuple(pick(line, self.z_at ^ step) for step in (1, 2, 3))
                self.sending = [4, 8, 12]
                return
            names = [self.z_steps.pop(0)]
        self.sending = [self.spans[name] for name in names]
        self.ready = tuple(
            self.total([self.part(piece, name, 1 - self.bits[name]) for piece in pieces])
            for name, pieces in zip(names, self.pieces)
        )
        self.pieces = [
            [self.part(piece, name, self.bits[name]) for piece in pieces] for name, pieces in zip(names, self.pieces)
        ]

    z_steps = ()

    def go(self):
        self.moving = tuple(swap_dp(field, span) for field, span in zip(self.ready, self.sending)) if self.small else ()

    def land(self):
        if not self.small:
            return
        if self.direct and len(self.moving) == 3:
            self.finish(sum(wide(got) for got in self.moving) + wide(self.own))
            return
        if self.z_steps == ():
            self.z_steps = ["near", "far"]
        self.pieces = [pieces + [got] for pieces, got in zip(self.pieces, self.moving)]
        if self.orders[0] or self.z_steps:
            self.prepare()
        else:
            last = sum(wide(piece) for piece in self.pieces[0])
            self.finish(last.reshape(last.shape[4:]))

    def finish(self, total):
        self.sums = []
        at = 0
        for cut in self.cuts:
            self.sums.append(total[:, at : at + cut])
            at += cut


def send(reductions, *before):
    ready, before = lax.optimization_barrier(([r.ready for r in reductions], before))
    for reduction, arrays in zip(reductions, ready):
        reduction.ready = arrays
        reduction.go()
    return before


def land(reductions, *done):
    moving, done = lax.optimization_barrier(([r.moving for r in reductions], done))
    for reduction, arrays in zip(reductions, moving):
        reduction.moving = arrays
        reduction.land()
    return done


def dp_sum(field):
    span = 1
    while span < lax.axis_size("dp"):
        steps = [step for step in (span, 2 * span, 3 * span) if step < lax.axis_size("dp")]
        field = field + sum(swap_dp(field, step) for step in steps)
        span *= 4
    return field


def grad_of(left, right):
    return lax.dot_general(
        left.reshape(-1, left.shape[2]),
        right.reshape(-1, right.shape[2]),
        (((0,), (0,)), ((), ())),
        preferred_element_type=jnp.float32,
    ).astype(LOW)


def local(
    clips,
    cotangent,
    live,
    time_gain,
    time_shift,
    time_inproj,
    time_inbias,
    time_outproj,
    time_outbias,
    time_mixer,
    time_mixbias,
    space_gain,
    space_shift,
    space_inproj,
    space_inbias,
    space_outproj,
    space_outbias,
    feed_gain,
    feed_shift,
    feed_upward,
    feed_upbias,
    feed_down,
    feed_downbias,
):
    tokens, width = clips.shape[1:]
    half = time_outproj.shape[0]
    dests = lax.axis_size("dp")
    share = width // dests
    tensor_rank = lax.axis_index("tensor")
    present = live.astype(jnp.float32).reshape(1, 1)
    time_in = jnp.transpose(time_inproj, (1, 0, 2))
    space_in = jnp.transpose(space_inproj, (1, 0, 2))
    mixers = (time_mixer, swap_tensor(time_mixer), tensor_rank.astype(jnp.int32).reshape(1, 1))
    x, t_norm, t_qkv, t_probs, t_mixed, t_part = time_forward(
        clips[0], time_gain, time_shift, time_in, time_inbias, time_outproj
    )
    cot, g_downbias = cotangent_frames(cotangent[0], present)
    mixer_in, after_time, s_norm, s_qkv, s_probs, s_mixed, s_part = space_forward(
        t_part, swap_tensor(t_part), x, time_outbias, mixers, time_mixbias, space_gain, space_shift, space_in,
        space_inbias, space_outproj,
    )
    mid, f_norm, act, d_pre, f_part, df_part, g_upbias = feed(
        s_part, swap_tensor(s_part), after_time, cot, space_outbias, feed_gain, feed_shift, feed_upward, feed_upbias,
        feed_down,
    )
    feed_sums = Reduction([grad_of(f_norm, d_pre), grad_of(cot, act)], ["xy", "yx"])
    (mid,) = send([feed_sums], mid)
    d_space, s_back, ds_part, d_class, g_feed_gain, g_feed_shift, g_space_outbias, g_space_inbias = space_backward(
        df_part, swap_tensor(df_part), mid, cot, s_qkv, s_probs, feed_gain, space_outproj, space_in
    )
    (g_space_outbias,) = land([feed_sums], g_space_outbias)
    (s_back,) = send([feed_sums], s_back)
    space_sums = Reduction(
        [jnp.concatenate([grad_of(s_norm, s_back), grad_of(d_space, s_mixed)], axis=1)], ["xy"]
    )
    (d_space,) = send([space_sums], d_space)
    result = result_tokens(f_part, swap_tensor(f_part), mid, feed_downbias, present, tokens)
    d_grid, d_mixer, d_mixed, d_source, g_space_gain, g_space_shift, g_mixbias, g_outbias = mixer_backward(
        ds_part, swap_tensor(ds_part), after_time, d_space, d_class, space_gain, mixers, time_outproj
    )
    (d_mixed,) = land([feed_sums], d_mixed)
    (d_grid,) = send([feed_sums], d_grid)
    mixer_half = lax.dynamic_slice_in_dim(mixer_in, tensor_rank * half, half, 2)
    mixer_sums = Reduction(
        [jnp.concatenate([grad_of(d_mixer, t_mixed), grad_of(d_grid, mixer_half)], axis=1)], ["yx"]
    )
    (d_mixed,) = send([mixer_sums], d_mixed)
    t_back, dt_part, g_time_inbias = time_backward(d_mixed, t_qkv, t_probs, time_in)
    (t_back,) = land([space_sums], t_back)
    (t_back,) = send([space_sums], t_back)
    g_time_in = grad_of(t_norm, t_back)
    time_sums = Reduction([g_time_in[:, : 3 * half // 2], g_time_in[:, 3 * half // 2 :]], ["xy", "yx"], direct=True)
    (d_source,) = send([time_sums], d_source)
    (d_source,) = land([feed_sums, mixer_sums], d_source)
    (d_source,) = send([feed_sums, mixer_sums], d_source)
    grad_clips, vectors = source_gradient(
        dt_part, swap_tensor(dt_part), x, d_grid, d_source, time_gain,
        (
            g_outbias, g_mixbias, g_space_gain, g_space_shift, g_space_outbias, g_feed_gain, g_feed_shift, g_downbias,
            g_time_inbias, g_space_inbias, g_upbias,
        ),
        tokens,
    )
    (vectors,) = land([time_sums, space_sums], vectors)
    (vectors,) = send([time_sums, space_sums], vectors)
    vectors = dp_sum(vectors)
    land([feed_sums, mixer_sums])
    send([mixer_sums])
    land([time_sums, space_sums])
    send([time_sums, space_sums])
    land([mixer_sums])
    send([mixer_sums])
    land([time_sums, space_sums, mixer_sums])
    up_sum, down_sum = feed_sums.sums
    (space_sum,) = space_sums.sums
    (mixer_sum,) = mixer_sums.sums
    time_sum = jnp.concatenate(time_sums.sums, axis=1)
    small = settle(vectors, lax.axis_index("dp").astype(jnp.int32).reshape(1, 1), dests)
    settled = (
        small[0],
        small[1],
        time_sum.reshape(share, 3, half),
        small[10],
        mixer_sum[:, :half].T,
        small[2],
        mixer_sum[:, half:].T,
        small[3],
        small[4],
        small[5],
        space_sum[:, : 3 * half].reshape(share, 3, half),
        small[11],
        space_sum[:, 3 * half :].T,
        small[6],
        small[7],
        small[8],
        up_sum,
        small[12],
        down_sum.T,
        small[9],
    )
    return (result[None], grad_clips[None]) + settled


def solution(mesh):
    in_specs = (
        P("dp", None, None),
        P("dp", None, None),
        P("dp"),
        P(),
        P(),
        P(None, None, "tensor"),
        P(None, "tensor"),
        P("tensor", None),
        P(),
        P("tensor", None),
        P(),
        P(),
        P(),
        P(None, None, "tensor"),
        P(None, "tensor"),
        P("tensor", None),
        P(),
        P(),
        P(),
        P(None, "tensor"),
        P("tensor"),
        P("tensor", None),
        P(),
    )
    out_specs = (
        P("dp", None, None),
        P("dp", None, None),
        P("dp"),
        P("dp"),
        P("dp", None, "tensor"),
        P(None, ("tensor", "dp")),
        P("tensor", "dp"),
        P("dp"),
        P("tensor", "dp"),
        P("dp"),
        P("dp"),
        P("dp"),
        P("dp", None, "tensor"),
        P(None, ("tensor", "dp")),
        P("tensor", "dp"),
        P("dp"),
        P("dp"),
        P("dp"),
        P("dp", "tensor"),
        P(("tensor", "dp")),
        P("tensor", "dp"),
        P("dp"),
    )
    return jax.shard_map(local, mesh=mesh, in_specs=in_specs, out_specs=out_specs, check_vma=False)
```

```python
import functools

import jax
import jax.numpy as jnp
from jax import lax
from jax.experimental import pallas as pl
from jax.experimental.pallas import tpu as pltpu
from jax.sharding import PartitionSpec as P

HEAD = 64
FRAMES = 8
PLACES = 196
BLOCK = 16
ROWS = 208
BLOCKS = ROWS // BLOCK
PAIR = 2
UNROLL = BLOCKS
TIME_GROUP = 13
TIME_LAG = 1
SPACE_LAG = 6
EPS = 1e-06
LOW = jnp.bfloat16
VMEM_BYTES = 62 * 1024 * 1024
COST = 1


def dot(left, right):
    return jnp.dot(left, right, preferred_element_type=jnp.float32)


def dot_last(left, right):
    return lax.dot_general(left, right, (((1,), (1,)), ((), ())), preferred_element_type=jnp.float32)


def normed(field):
    center = field - jnp.mean(field, axis=-1, keepdims=True)
    spread_sq = jnp.mean(center * center, axis=-1, keepdims=True)
    inverse = lax.rsqrt(spread_sq + EPS)
    return center * inverse, inverse


def normed_back(unit, inverse, grad_unit):
    first = jnp.mean(grad_unit, axis=-1, keepdims=True)
    second = jnp.mean(grad_unit * unit, axis=-1, keepdims=True)
    return (grad_unit - first - unit * second) * inverse


def side_by_side(weights):
    return jnp.concatenate([weights[part] for part in range(weights.shape[0])], axis=1)


def flat(field):
    return field.reshape((field.shape[0] * field.shape[1],) + field.shape[2:])


def wide(field):
    return field.astype(jnp.float32)


def iota(shape, axis):
    return lax.broadcasted_iota(jnp.int32, shape, axis)


def column_sum(field):
    return jnp.sum(field, axis=0, keepdims=True)


def call(kernel, grid, in_specs, out_specs, out_shapes, scratch, flops, args):
    moved = sum(a.size * a.dtype.itemsize for a in args) + sum(o.size * o.dtype.itemsize for o in out_shapes)
    return pl.pallas_call(
        kernel,
        grid=grid,
        in_specs=in_specs,
        out_specs=out_specs,
        out_shape=out_shapes,
        scratch_shapes=scratch,
        compiler_params=pltpu.CompilerParams(vmem_limit_bytes=VMEM_BYTES),
        cost_estimate=pl.CostEstimate(flops=int(flops) // COST, bytes_accessed=int(moved) // COST, transcendentals=0),
    )(*args)


SCALAR = pl.BlockSpec(memory_space=pltpu.SMEM)


def whole(array):
    zeros = (0,) * array.ndim
    return pl.BlockSpec(array.shape, lambda *at: zeros)


def shape(dims, kind=LOW):
    return jax.ShapeDtypeStruct(dims, kind)


def to_frames(rows, block):
    count = FRAMES * BLOCK
    at = iota((count, count + BLOCK), 0)
    source = 1 + FRAMES * (at % BLOCK) + at // BLOCK
    pick = jnp.where(source == iota((count, count + BLOCK), 1), 1.0, 0.0).astype(LOW)
    return dot(pick, rows)


def to_tokens(rows):
    count = FRAMES * BLOCK
    at = iota((count, count), 1)
    target = 1 + FRAMES * (at % BLOCK) + at // BLOCK
    pick = jnp.where(target == iota((count, count), 0), 1.0, 0.0).astype(LOW)
    return dot(pick, rows)


def fill_rows(source, tokens):
    count = tokens.shape[0]
    even = count // BLOCK * BLOCK
    source[0:even] = tokens[0:even]
    source[even:] = jnp.zeros((source.shape[0] - even, source.shape[1]), source.dtype)
    left = wide(tokens[even:count])
    tail = jnp.zeros((BLOCK, source.shape[1]), jnp.float32)
    for row in range(count - even):
        tail = tail + jnp.where(iota(tail.shape, 0) == row, left[row : row + 1], 0.0)
    source[even : even + BLOCK] = tail.astype(source.dtype)


def frame_rows(source, block, class_row, class_frames):
    count = FRAMES * BLOCK
    rows = to_frames(source[pl.ds(pl.multiple_of(block * count, count), count + BLOCK), :], block)
    at = iota((count, 1), 0)
    is_class = (block * BLOCK + at % BLOCK == PLACES) & (at // BLOCK < class_frames)
    return rows + jnp.where(is_class, class_row, 0.0)


class Copies:
    def __init__(self, semaphores):
        self.semaphores = semaphores
        self.started = []

    def start(self, source, target):
        copy = pltpu.make_async_copy(source, target, self.semaphores.at[len(self.started)])
        copy.start()
        self.started.append(copy)
        return copy


def time_forward_kernel(
    clips, gain, shift, inproj_far, inbias, outproj_far, x_far, norm_far, qkv_far, probs_far, mixed_far, part_far,
    inproj, outproj, x_out, norm_out, qkv_out, probs_out, mixed_out, part_out, source, semaphores,
):
    half = outproj.shape[0]
    copies = Copies(semaphores)
    fetched = [copies.start(inproj_far, inproj), copies.start(outproj_far, outproj)]
    fill_rows(source, clips)
    class_row = wide(clips[0:1])

    def first(block, carry):
        rows = frame_rows(source, block, class_row, FRAMES)
        unit, _ = normed(rows)
        at = pl.ds(pl.multiple_of(block * BLOCK, BLOCK), BLOCK)
        x_out[:, at, :] = rows.astype(LOW).reshape(FRAMES, BLOCK, rows.shape[1])
        norm_out[:, at, :] = (unit * vector(gain) + vector(shift)).astype(LOW).reshape(FRAMES, BLOCK, rows.shape[1])
        return carry

    lax.fori_loop(0, BLOCKS, first, 0, unroll=UNROLL)
    sent = [copies.start(x_out, x_far), copies.start(norm_out, norm_far)]
    fetched[0].wait()
    weights = side_by_side(inproj)
    for step in range(FRAMES // PAIR):
        at = pl.ds(step * PAIR, PAIR)
        qkv = heads_low(dot(flat(norm_out[at]), weights), inbias, half)
        qkv_out[at] = qkv.reshape(PAIR, ROWS, 3 * half)
    sent.append(copies.start(qkv_out, qkv_far))
    count = FRAMES * BLOCK
    same = iota((count, 2 * count), 0) % BLOCK == iota((count, 2 * count), 1) % BLOCK

    def third(first_block, count):
        ats = [
            pl.ds(pl.multiple_of((first_block + step) * BLOCK, BLOCK), BLOCK) for step in range(count)
        ]

        def keep(step, head, probs):
            probs_out[first_block + step, head] = probs

        mixed = attend(
            [flat(qkv_out[:, at, :]) for at in ats], lambda scores: jnp.where(same, scores, -1e30), keep, 2, TIME_LAG
        )
        for at, part in zip(ats, mixed):
            mixed_out[:, at, :] = part.reshape(FRAMES, BLOCK, half)

    by_blocks(third)
    sent += [copies.start(probs_out, probs_far), copies.start(mixed_out, mixed_far)]
    fetched[1].wait()
    for step in range(FRAMES // PAIR):
        at = pl.ds(step * PAIR, PAIR)
        part = dot(flat(mixed_out[at]), outproj[...]).astype(LOW)
        part_out[at] = part.reshape(PAIR, ROWS, part.shape[1])
        sent.append(copies.start(part_out.at[at], part_far.at[at]))
    for copy in sent:
        copy.wait()


def by_blocks(run):
    def step(at, carry):
        run(at * TIME_GROUP, TIME_GROUP)
        return carry

    lax.fori_loop(0, BLOCKS // TIME_GROUP, step, 0)
    if BLOCKS % TIME_GROUP:
        run(BLOCKS // TIME_GROUP * TIME_GROUP, BLOCKS % TIME_GROUP)


def heads_low(linear, inbias, half):
    query = ((linear[:, :half] + inbias[0:1]) * HEAD ** (-0.5)).astype(LOW)
    keys = linear[:, half : 2 * half].astype(LOW)
    values = (linear[:, 2 * half :] + inbias[1:2]).astype(LOW)
    return jnp.concatenate([query, keys, values], axis=1)


def beside(field_t, head):
    own = field_t[HEAD * head : HEAD * (head + 1)]
    none = jnp.zeros_like(own)
    return jnp.concatenate([own, none] if head % 2 == 0 else [none, own], axis=0)


def beside_all(field_t, heads):
    return jnp.concatenate([beside(field_t, head) for head in heads], axis=1)


def pair_of(field, head):
    start = head // 2 * 2 * HEAD
    return field[:, start : start + 2 * HEAD]


def head_rows(field_t, head):
    return field_t[HEAD * head : HEAD * (head + 1)]


def staged(count, stages, lag):
    held = [None] * count
    for step in range(count + lag * (len(stages) - 1)):
        for depth, stage in enumerate(stages):
            item = step - lag * depth
            if 0 <= item < count:
                held[item] = stage(item, held[item])
    return held


def attend(inputs, block_allowed, keep, group, lag):
    half = inputs[0].shape[1] // 3
    rows = inputs[0].shape[0]
    query_t = [qkv[:, :half].T for qkv in inputs]
    values_t = [qkv[:, 2 * half :].T for qkv in inputs]
    groups = half // HEAD // group

    def heads_of(item):
        first = item % groups * group
        return range(first, first + group)

    def score(item, held):
        block = item // groups
        keys = inputs[block][:, half : 2 * half]
        return dot(pair_of(keys, heads_of(item)[0]), beside_all(query_t[block], heads_of(item)))

    def weigh(item, scores):
        scores = block_allowed(scores)
        expon = jnp.exp(scores - jnp.max(scores, axis=0, keepdims=True))
        probs = (expon * (1.0 / column_sum(expon))).astype(LOW)
        for at, head in enumerate(heads_of(item)):
            keep(item // groups, head, probs[:, at * rows : (at + 1) * rows])
        return probs

    def mix(item, probs):
        return [
            dot(head_rows(values_t[item // groups], head), probs[:, at * rows : (at + 1) * rows])
            for at, head in enumerate(heads_of(item))
        ]

    mixed_t = staged(len(inputs) * groups, [score, weigh, mix], lag)
    out = []
    for block in range(len(inputs)):
        parts = [part for item in mixed_t[block * groups : (block + 1) * groups] for part in item]
        out.append(jnp.concatenate(parts, axis=0).T.astype(LOW))
    return out


def attend_back(inputs, probs_of, d_mixeds, group, lag):
    half = inputs[0].shape[1] // 3
    rows = inputs[0].shape[0]
    keys_t = [qkv[:, half : 2 * half].T for qkv in inputs]
    d_mixed_t = [d_mixed.T for d_mixed in d_mixeds]
    lane = iota((rows, 2 * HEAD), 1) < HEAD
    groups = half // HEAD // group

    def heads_of(item):
        first = item % groups * group
        return range(first, first + group)

    def score(item, held):
        block = item // groups
        values = inputs[block][:, 2 * half :]
        return dot(pair_of(values, heads_of(item)[0]), beside_all(d_mixed_t[block], heads_of(item)))

    def weigh(item, d_probs):
        probs_low = jnp.concatenate([probs_of(item // groups, head) for head in heads_of(item)], axis=1)
        probs = wide(probs_low)
        scaled = probs * d_probs
        d_scores = scaled - probs * column_sum(scaled)
        return probs_low, d_scores.astype(LOW)

    def halves(field):
        none = jnp.zeros_like(field)
        return jnp.concatenate([jnp.where(lane, field, none), jnp.where(lane, none, field)], axis=0)

    def mix(item, held):
        block = item // groups
        probs_low, d_scores = held
        d_query_t = [
            dot(head_rows(keys_t[block], head), d_scores[:, at * rows : (at + 1) * rows])
            for at, head in enumerate(heads_of(item))
        ]
        d_mixed = pair_of(d_mixeds[block], heads_of(item)[0])
        query = pair_of(inputs[block][:, :half], heads_of(item)[0])
        if group == 2:
            d_mixed = halves(d_mixed)
            query = halves(query)
        return d_query_t, dot(d_scores, query), dot(probs_low, d_mixed)

    made = staged(len(inputs) * groups, [score, weigh, mix], lag)

    def paired(fields):
        if group == 2:
            return fields
        return [jnp.where(lane, fields[at], fields[at + 1]) for at in range(0, len(fields), 2)]

    out = []
    for block in range(len(inputs)):
        own = made[block * groups : (block + 1) * groups]
        d_query = jnp.concatenate([part for item in own for part in item[0]], axis=0).T.astype(LOW) * HEAD ** (-0.5)
        d_keys = paired([item[1] for item in own])
        d_values = paired([item[2] for item in own])
        out.append(jnp.concatenate([d_query] + [d.astype(LOW) for d in d_keys + d_values], axis=1))
    return out


def time_forward(clips, gain, shift, inproj, inbias, outproj):
    tokens, width = clips.shape
    half = outproj.shape[0]
    heads = half // HEAD
    count = FRAMES * BLOCK
    args = (clips, gain, shift, inproj, inbias, outproj)
    outs = [
        shape((FRAMES, ROWS, width)),
        shape((FRAMES, ROWS, width)),
        shape((FRAMES, ROWS, 3 * half)),
        shape((BLOCKS, heads, count, count)),
        shape((FRAMES, ROWS, half)),
        shape((FRAMES, ROWS, width)),
    ]
    rows = FRAMES * ROWS
    near = [pltpu.VMEM(a.shape, a.dtype) for a in (inproj, outproj)] + [pltpu.VMEM(o.shape, o.dtype) for o in outs]
    far = pl.BlockSpec(memory_space=pl.ANY)
    return call(
        time_forward_kernel,
        (1,),
        [whole(clips), whole(gain), whole(shift), far, whole(inbias), far],
        [far] * 6,
        outs,
        near + [pltpu.VMEM((BLOCKS * count + BLOCK, width), LOW), pltpu.SemaphoreType.DMA((16,))],
        2 * rows * width * half * 5,
        args,
    )


def cotangent_kernel(cotangent, live, out, total, source):
    fill_rows(source, cotangent)
    present = live[0, 0]
    class_row = wide(cotangent[0:1])

    def first(block, carry):
        rows = frame_rows(source, block, class_row, 1) * present
        at = pl.ds(pl.multiple_of(block * BLOCK, BLOCK), BLOCK)
        out[:, at, :] = rows.astype(LOW).reshape(FRAMES, BLOCK, rows.shape[1])
        return carry + column_sum(rows)

    total[...] = lax.fori_loop(0, BLOCKS, first, jnp.zeros(total.shape, jnp.float32), unroll=UNROLL)


def cotangent_frames(cotangent, live):
    tokens, width = cotangent.shape
    args = (cotangent, live)
    outs = [shape((FRAMES, ROWS, width)), shape((1, width), jnp.float32)]
    return call(
        cotangent_kernel,
        (1,),
        [whole(cotangent), SCALAR],
        [whole(o) for o in outs],
        outs,
        [pltpu.VMEM((BLOCKS * FRAMES * BLOCK + BLOCK, width), LOW)],
        2 * FRAMES * ROWS * 128 * width,
        args,
    )


def vector(ref):
    return ref[...].reshape(1, -1)


def place_of(shape_of):
    return iota(shape_of, 0) % ROWS


def gather_mixer(own, other, rank, mixer):
    half = own.shape[0]

    @pl.when(pl.program_id(0) == 0)
    def _():
        mixer[pl.ds(pl.multiple_of(rank[0, 0] * half, half), half), :] = own[...]
        mixer[pl.ds(pl.multiple_of((1 - rank[0, 0]) * half, half), half), :] = other[...]


def space_forward_kernel(
    own, other, x, outbias, mixer_own, mixer_other, rank, mixbias, gain, shift, inproj, inbias, outproj,
    mixer_out, after_out, norm_out, qkv_out, probs_out, mixed_out, part_out, mixer,
):
    gather_mixer(mixer_own, mixer_other, rank, mixer)
    half = outproj.shape[0]
    width = outproj.shape[1]

    def spread(field):
        return field.astype(LOW).reshape(PAIR, ROWS, field.shape[1])

    mixer_in = (wide(flat(own[...])) + wide(flat(other[...])) + vector(outbias)).astype(LOW)
    mixer_out[...] = spread(mixer_in)
    branch = dot(mixer_in, mixer[...]) + vector(mixbias)
    after = wide(flat(x[...])) + jnp.where(place_of((PAIR * ROWS, 1)) < PLACES, branch, 0.0)
    after_out[...] = spread(after)
    unit, _ = normed(after)
    norm = (unit * vector(gain) + vector(shift)).astype(LOW)
    norm_out[...] = spread(norm)
    qkv = heads_low(dot(norm, side_by_side(inproj)), inbias, half)
    qkv_out[...] = spread(qkv)

    def allowed(scores):
        even = ROWS - BLOCK
        last = jnp.where(iota((BLOCK, ROWS), 0) <= PLACES - even, scores[even:], -1e30)
        return jnp.concatenate([scores[:even], last], axis=0)

    def keep(frame, head, probs):
        probs_out[frame, head] = probs

    frames = [qkv[frame * ROWS : (frame + 1) * ROWS] for frame in range(PAIR)]
    for frame, mixed in enumerate(attend(frames, allowed, keep, 1, SPACE_LAG)):
        mixed_out[frame] = mixed
    part_out[...] = spread(dot(flat(mixed_out[...]), outproj[...]))


def pairs(array):
    rest = (0,) * (array.ndim - 1)
    return pl.BlockSpec((PAIR,) + array.shape[1:], lambda at: (at,) + rest)


def space_forward(own, other, x, outbias, mixers, mixbias, gain, shift, inproj, inbias, outproj):
    width = x.shape[2]
    half = outproj.shape[0]
    heads = half // HEAD
    args = (own, other, x, outbias) + mixers + (mixbias, gain, shift, inproj, inbias, outproj)
    outs = [
        shape((FRAMES, ROWS, width)),
        shape((FRAMES, ROWS, width)),
        shape((FRAMES, ROWS, width)),
        shape((FRAMES, ROWS, 3 * half)),
        shape((FRAMES, heads, ROWS, ROWS)),
        shape((FRAMES, ROWS, half)),
        shape((FRAMES, ROWS, width)),
    ]
    return call(
        space_forward_kernel,
        (FRAMES // PAIR,),
        [pairs(a) for a in args[:3]] + [whole(a) for a in args[3:6]] + [SCALAR] + [whole(a) for a in args[7:]],
        [pairs(o) for o in outs],
        outs,
        [pltpu.VMEM((width, width), LOW)],
        2 * FRAMES * ROWS * width * half * 8,
        args,
    )


def last_block(count):
    return lambda array: pl.BlockSpec((count, BLOCK, array.shape[2]), lambda at: (0, BLOCKS - 1, 0))


CLASS_AT = PLACES - (BLOCKS - 1) * BLOCK


def feed_kernel(
    own, other, after, cot, own_last, other_last, after_last, outbias, gain, shift, upward, upbias, down,
    mid_out, norm_out, act_out, dpre_out, part_out, dnorm_out, upbias_out,
):
    step = pl.program_id(0)
    units = upward.shape[1]
    width = upward.shape[0]

    def spread(field):
        return field.astype(LOW).reshape(PAIR, ROWS, field.shape[1])

    class_branch = wide(own_last[...]) + wide(other_last[...])
    class_branch = jnp.sum(class_branch, axis=0)[CLASS_AT : CLASS_AT + 1] * (1.0 / FRAMES) + vector(outbias)
    at = iota((PAIR * ROWS, 1), 0)
    branch = wide(flat(own[...])) + wide(flat(other[...])) + vector(outbias)
    is_class = (at == PLACES) & (step == 0)
    mid = jnp.where(at % ROWS < PLACES, wide(flat(after[...])) + branch, 0.0)
    mid = mid + jnp.where(is_class, wide(after_last[0])[CLASS_AT : CLASS_AT + 1] + class_branch, 0.0)
    mid_out[...] = spread(mid)
    unit, _ = normed(mid)
    norm = (unit * vector(gain) + vector(shift)).astype(LOW)
    norm_out[...] = spread(norm)
    grad = flat(cot[...])
    part = jnp.zeros((PAIR * ROWS, width), jnp.float32)
    d_norm = jnp.zeros((PAIR * ROWS, width), jnp.float32)
    share = 512

    @pl.when(step == 0)
    def _():
        upbias_out[...] = jnp.zeros(upbias_out.shape, jnp.float32)

    for start in range(0, units, share):
        cols = slice(start, start + share)
        pre = dot(norm, upward[:, cols]) + vector(upbias)[:, cols]
        cumulative = 0.5 * (1.0 + lax.erf(pre * 0.5**0.5))
        slope = cumulative + pre * jnp.exp(-0.5 * pre * pre) * 0.3989422804014327
        act = (pre * cumulative).astype(LOW)
        act_out[:, :, cols] = spread(act)
        d_pre = (dot_last(grad, down[cols]) * slope).astype(LOW)
        dpre_out[:, :, cols] = spread(d_pre)
        upbias_out[:, cols] += column_sum(wide(d_pre))
        part = part + dot(act, down[cols])
        d_norm = d_norm + dot_last(d_pre, upward[:, cols])
    part_out[...] = spread(part)
    dnorm_out[...] = spread(d_norm)


def feed(own, other, after, cot, outbias, gain, shift, upward, upbias, down):
    width, units = upward.shape
    args = (own, other, after, cot, own, other, after, outbias, gain, shift, upward, upbias, down)
    outs = [
        shape((FRAMES, ROWS, width)),
        shape((FRAMES, ROWS, width)),
        shape((FRAMES, ROWS, units)),
        shape((FRAMES, ROWS, units)),
        shape((FRAMES, ROWS, width)),
        shape((FRAMES, ROWS, width)),
        shape((1, units), jnp.float32),
    ]
    tail = last_block(FRAMES)
    return call(
        feed_kernel,
        (FRAMES // PAIR,),
        [pairs(a) for a in args[:4]] + [tail(a) for a in args[4:7]] + [whole(a) for a in args[7:]],
        [pairs(o) for o in outs[:6]] + [whole(outs[6])],
        outs,
        [],
        2 * FRAMES * ROWS * width * units * 4,
        args,
    )


def space_backward_kernel(
    own, other, mid, cot, qkv, probs, own_last, other_last, mid_last, cot_last, gain, outproj, inproj,
    dspace_out, back_out, part_out, dclass_out, gain_out, shift_out, outbias_out, inbias_out,
):
    step = pl.program_id(0)
    half = outproj.shape[0]

    def spread(field):
        return field.astype(LOW).reshape(PAIR, ROWS, field.shape[1])

    def back(own_part, other_part, mid_part, cot_part):
        d_norm = wide(own_part) + wide(other_part)
        unit, inverse = normed(wide(mid_part))
        return wide(cot_part) + normed_back(unit, inverse, d_norm * vector(gain)), d_norm, d_norm * unit

    d_class = back(own_last[0], other_last[0], mid_last[0], cot_last[0])[0][CLASS_AT : CLASS_AT + 1]
    d_mid, d_shift, d_gain = back(flat(own[...]), flat(other[...]), flat(mid[...]), flat(cot[...]))
    place = place_of((PAIR * ROWS, 1))
    d_space = jnp.where(place < PLACES, d_mid, jnp.where(place == PLACES, d_class * (1.0 / FRAMES), 0.0))

    @pl.when(step == 0)
    def _():
        dclass_out[...] = d_class
        for ref in (gain_out, shift_out, outbias_out, inbias_out):
            ref[...] = jnp.zeros(ref.shape, jnp.float32)

    gain_out[...] += column_sum(d_gain)
    shift_out[...] += column_sum(d_shift)
    outbias_out[...] += column_sum(d_space)
    d_low = d_space.astype(LOW)
    dspace_out[...] = spread(d_low)
    d_mixed = dot_last(d_low, outproj[...]).astype(LOW)
    made = attend_back(
        [qkv[frame] for frame in range(PAIR)],
        lambda frame, head: probs[frame, head],
        [d_mixed[frame * ROWS : (frame + 1) * ROWS] for frame in range(PAIR)],
        1,
        SPACE_LAG,
    )
    for frame, part in enumerate(made):
        back_out[frame] = part
    backs = flat(back_out[...])
    inbias_out[...] += column_sum(wide(backs))
    part_out[...] = spread(dot_last(backs, side_by_side(inproj)))


def space_backward(own, other, mid, cot, qkv, probs, gain, outproj, inproj):
    width = mid.shape[2]
    half = outproj.shape[0]
    args = (own, other, mid, cot, qkv, probs, own, other, mid, cot, gain, outproj, inproj)
    outs = [
        shape((FRAMES, ROWS, width)),
        shape((FRAMES, ROWS, 3 * half)),
        shape((FRAMES, ROWS, width)),
        shape((1, width), jnp.float32),
        shape((1, width), jnp.float32),
        shape((1, width), jnp.float32),
        shape((1, width), jnp.float32),
        shape((1, 3 * half), jnp.float32),
    ]
    tail = last_block(1)
    return call(
        space_backward_kernel,
        (FRAMES // PAIR,),
        [pairs(a) for a in args[:6]] + [tail(a) for a in args[6:10]] + [whole(a) for a in args[10:]],
        [pairs(o) for o in outs[:3]] + [whole(o) for o in outs[3:]],
        outs,
        [],
        2 * FRAMES * ROWS * width * half * 6,
        args,
    )


def mixer_backward_kernel(
    own, other, after, dspace, dclass, gain, mixer_own, mixer_other, rank, outproj,
    dgrid_out, dmixer_out, dmixed_out, dsource_out, gain_out, shift_out, mixbias_out, outbias_out, mixer,
):
    gather_mixer(mixer_own, mixer_other, rank, mixer)

    @pl.when(pl.program_id(0) == 0)
    def _():
        dsource_out[...] = dclass[...]
        for ref in (gain_out, shift_out, mixbias_out, outbias_out):
            ref[...] = jnp.zeros(ref.shape, jnp.float32)

    def spread(field):
        return field.astype(LOW).reshape(PAIR, ROWS, field.shape[1])

    d_norm = wide(flat(own[...])) + wide(flat(other[...]))
    unit, inverse = normed(wide(flat(after[...])))
    gain_out[...] += column_sum(d_norm * unit)
    shift_out[...] += column_sum(d_norm)
    d_space_in = normed_back(unit, inverse, d_norm * vector(gain))
    place = place_of((PAIR * ROWS, 1))
    dsource_out[...] += column_sum(jnp.where(place == PLACES, d_space_in, 0.0))
    d_grid = jnp.where(place < PLACES, d_space_in + wide(flat(dspace[...])), 0.0)
    mixbias_out[...] += column_sum(d_grid)
    d_low = d_grid.astype(LOW)
    dgrid_out[...] = spread(d_low)
    d_mixer = dot_last(d_low, mixer[...]).astype(LOW)
    dmixer_out[...] = spread(d_mixer)
    outbias_out[...] += column_sum(wide(d_mixer))
    dmixed_out[...] = spread(dot_last(d_mixer, outproj[...]))


def mixer_backward(own, other, after, dspace, dclass, gain, mixers, outproj):
    width = after.shape[2]
    half = outproj.shape[0]
    args = (own, other, after, dspace, dclass, gain) + mixers + (outproj,)
    outs = [
        shape((FRAMES, ROWS, width)),
        shape((FRAMES, ROWS, width)),
        shape((FRAMES, ROWS, half)),
    ] + [shape((1, width), jnp.float32)] * 5
    return call(
        mixer_backward_kernel,
        (FRAMES // PAIR,),
        [pairs(a) for a in args[:4]] + [whole(a) for a in args[4:8]] + [SCALAR, whole(outproj)],
        [pairs(o) for o in outs[:3]] + [whole(o) for o in outs[3:]],
        outs,
        [pltpu.VMEM((width, width), LOW)],
        2 * FRAMES * ROWS * width * half * 3,
        args,
    )


def near_far(arrays):
    return [pltpu.VMEM(a.shape, a.dtype) for a in arrays], pl.BlockSpec(memory_space=pl.ANY)


def places(first, last):
    return pl.ds(first * BLOCK, (last - first) * BLOCK)


TIME_GROUPS = ((0, 3), (3, 8), (8, BLOCKS))


def time_backward_kernel(
    d_mixed_far, qkv_far, probs_far, inproj_far, back_far, part_far, inbias_out,
    d_mixed, qkv, probs, inproj, back_out, part_out, semaphores,
):
    half = d_mixed.shape[2]
    width = inproj.shape[1]
    copies = Copies(semaphores)
    coming = []
    for first, last in TIME_GROUPS:
        at = places(first, last)
        coming.append(
            [
                copies.start(d_mixed_far.at[:, at, :], d_mixed.at[:, at, :]),
                copies.start(qkv_far.at[:, at, :], qkv.at[:, at, :]),
                copies.start(probs_far.at[pl.ds(first, last - first)], probs.at[pl.ds(first, last - first)]),
            ]
        )
    weights_come = copies.start(inproj_far, inproj)
    sent = []
    for (first, last), arrivals in zip(TIME_GROUPS, coming):
        for arrival in arrivals:
            arrival.wait()
        ats = [places(block, block + 1) for block in range(first, last)]
        made = attend_back(
            [flat(qkv[:, at, :]) for at in ats],
            lambda step, head, first=first: probs[first + step, head],
            [flat(d_mixed[:, at, :]) for at in ats],
            2,
            TIME_LAG,
        )
        for at, part in zip(ats, made):
            back_out[:, at, :] = part.reshape(FRAMES, BLOCK, 3 * half)
        at = places(first, last)
        sent.append(copies.start(back_out.at[:, at, :], back_far.at[:, at, :]))
    weights_come.wait()
    inbias = jnp.zeros(inbias_out.shape, jnp.float32)
    for step in range(FRAMES // PAIR):
        at = pl.ds(step * PAIR, PAIR)
        backs = flat(back_out[at])
        inbias = inbias + column_sum(wide(backs))
        part_out[at] = dot_last(backs, side_by_side(inproj)).astype(LOW).reshape(PAIR, ROWS, width)
        sent.append(copies.start(part_out.at[at], part_far.at[at]))
    inbias_out[...] = inbias
    for copy in sent:
        copy.wait()


def time_backward(d_mixed, qkv, probs, inproj):
    width = inproj.shape[1]
    half = d_mixed.shape[2]
    args = (d_mixed, qkv, probs, inproj)
    outs = [
        shape((FRAMES, ROWS, 3 * half)),
        shape((FRAMES, ROWS, width)),
        shape((1, 3 * half), jnp.float32),
    ]
    near, far = near_far(args + tuple(outs[:2]))
    return call(
        time_backward_kernel,
        (1,),
        [far] * 4,
        [far, far, whole(outs[2])],
        outs,
        near + [pltpu.SemaphoreType.DMA((4 * len(TIME_GROUPS) + 1 + FRAMES // PAIR,))],
        2 * FRAMES * ROWS * width * half * 5,
        args,
    )


def fetch_places(copies, far, near, groups):
    return [
        [copies.start(f.at[:, places(*group), :], n.at[:, places(*group), :]) for f, n in zip(far, near)]
        for group in groups
    ]


def put_tokens(out, block, low, carry):
    count = FRAMES * BLOCK
    moved = jnp.where(iota((count, 1), 0) == 0, carry, to_tokens(low))
    fits = min(out.shape[0] - block * count, count)
    out[block * count : block * count + fits] = moved[:fits].astype(out.dtype)
    return wide(low[count - BLOCK :])[BLOCK - 1 :]


def block_rows(ref, block):
    return wide(flat(ref[:, block * BLOCK : (block + 1) * BLOCK, :]))


VECTORS = 16


SOURCE_GROUPS = ((0, 1), (1, 4), (4, 8), (8, BLOCKS))


def source_kernel(own_far, other_far, x_far, dgrid_far, dsource, gain, *rest):
    given = rest[:-7]
    out, packed, own, other, x, dgrid, semaphores = rest[-7:]
    width = packed.shape[1]
    coming = fetch_places(
        Copies(semaphores), (own_far, other_far, x_far, dgrid_far), (own, other, x, dgrid), SOURCE_GROUPS
    )
    carry = dsource[...]
    d_gain = jnp.zeros((1, width), jnp.float32)
    d_shift = jnp.zeros((1, width), jnp.float32)
    for (first, last), arrivals in zip(SOURCE_GROUPS, coming):
        for arrival in arrivals:
            arrival.wait()
        for block in range(first, last):
            d_norm = block_rows(own, block) + block_rows(other, block)
            unit, inverse = normed(block_rows(x, block))
            d_gain = d_gain + column_sum(d_norm * unit)
            d_shift = d_shift + column_sum(d_norm)
            rows = block_rows(dgrid, block) + normed_back(unit, inverse, d_norm * vector(gain))
            carry = put_tokens(out, block, rows.astype(LOW), carry)
    packed[...] = jnp.zeros(packed.shape, jnp.float32)
    packed[0:1] = d_gain
    packed[1:2] = d_shift
    at = 2
    for ref in given:
        count = ref.shape[1]
        if count == 3 * width // 2:
            packed[at : at + 1] = jnp.concatenate([ref[:, : width // 2], ref[:, width:]], axis=1)
            at += 1
            continue
        for start in range(0, count, width):
            packed[at : at + 1] = ref[:, start : start + width]
            at += 1


def source_gradient(own, other, x, dgrid, dsource, gain, given, tokens):
    width = x.shape[2]
    args = (own, other, x, dgrid, dsource, gain) + tuple(given)
    outs = [shape((tokens, width)), shape((VECTORS, width), jnp.float32)]
    near, far = near_far(args[:4])
    return call(
        source_kernel,
        (1,),
        [far] * 4 + [whole(a) for a in args[4:]],
        [whole(o) for o in outs],
        outs,
        near + [pltpu.SemaphoreType.DMA((4 * len(SOURCE_GROUPS),))],
        2 * FRAMES * ROWS * 128 * width,
        args,
    )


RESULT_GROUPS = ((BLOCKS - 1, BLOCKS), (0, 4), (4, 8), (8, BLOCKS - 1))


def result_kernel(own_far, other_far, mid_far, bias, live, out, own, other, mid, semaphores):
    present = live[0, 0]
    coming = fetch_places(Copies(semaphores), (own_far, other_far, mid_far), (own, other, mid), RESULT_GROUPS)

    def rows_of(block):
        total = block_rows(mid, block) + block_rows(own, block) + block_rows(other, block) + vector(bias)
        return (total * present).astype(LOW)

    for arrival in coming[0]:
        arrival.wait()
    last = rows_of(BLOCKS - 1)
    carry = wide(last[:BLOCK])[CLASS_AT : CLASS_AT + 1]
    for (first, end), arrivals in zip(RESULT_GROUPS[1:], coming[1:]):
        for arrival in arrivals:
            arrival.wait()
        for block in range(first, end):
            carry = put_tokens(out, block, rows_of(block), carry)
    put_tokens(out, BLOCKS - 1, last, carry)


def result_tokens(own, other, mid, bias, live, tokens):
    width = mid.shape[2]
    args = (own, other, mid, bias, live)
    outs = [shape((tokens, width))]
    near, far = near_far(args[:3])
    return call(
        result_kernel,
        (1,),
        [far] * 3 + [whole(bias), SCALAR],
        [whole(outs[0])],
        outs,
        near + [pltpu.SemaphoreType.DMA((3 * len(RESULT_GROUPS),))],
        2 * FRAMES * ROWS * 128 * width,
        args,
    )[0]


def settle_vectors(at, total, outs):
    width = total.shape[1]
    share = outs[0].shape[0]
    dests = width // share
    moved = pltpu.roll(total, (dests - at) % dests * share, 1)
    for row in range(10):
        outs[row][...] = moved[row, :share]
    small = share // 2
    moved = pltpu.roll(total, (2 * dests - at) % (2 * dests) * small, 1)
    for row in (10, 11):
        for part in range(2):
            start = part * (width // 2)
            outs[row][part : part + 1, :] = moved[row : row + 1, start : start + small]
    moved = pltpu.roll(total, (dests - 2 * at % dests) % dests * share, 1)
    outs[12][...] = jnp.where(2 * at < dests, moved[12, : 2 * share], moved[13, : 2 * share])


def small_shapes(share):
    outs = [shape((share,), jnp.float32)] * 10
    outs += [shape((2, share // 2), jnp.float32)] * 2
    return outs + [shape((2 * share,), jnp.float32)]


def settle_kernel(place, total, *outs):
    settle_vectors(place[0, 0], total[...], outs)


def settle(total, place, dests):
    outs = small_shapes(total.shape[1] // dests)
    return call(settle_kernel, (1,), [SCALAR, whole(total)], [whole(o) for o in outs], outs, [], 0, (place, total))


UNIT = 128


def bits_of(me):
    place = me[0, 0]
    return {"x": place % 2, "y": place // 2 % 2, "near": place // 4 % 2, "far": place // 8}


def pair_index(at, bit):
    return 2 * at + bit


def gap_index(at, bit):
    return at // 2 * 4 + 2 * bit + at % 2


def units_of(field):
    return [slice(at, at + UNIT) for at in range(0, field.shape[-1], UNIT)]


def split_gradient(field, axis, bits, message, start, keep):
    index = pair_index if axis == "x" else gap_index
    cols = units_of(field)
    for at in range(8):
        for unit, col in enumerate(cols):
            message[start + at * len(cols) + unit] = field[index(at, 1 - bits[axis]), :, col]
            keep[at, unit] = field[index(at, bits[axis]), :, col]


def split_total(held, got, got_start, bit, message, start, keep):
    units = held.shape[1]

    def total(at):
        return (wide(held[at]) + wide(got[pl.ds(got_start + at * units, units)])).astype(LOW)

    for at in range(held.shape[0] // 2):
        message[start + at * units : start + (at + 1) * units] = total(pair_index(at, 1 - bit))
        keep[at] = total(pair_index(at, bit))


def put_gradient(field, left, right, start=0):
    step = 768 if right.shape[1] % 768 == 0 else 384
    for at in range(0, right.shape[1], step):
        part = lax.dot_general(
            left, right[:, at : at + step], (((0,), (0,)), ((), ())), preferred_element_type=jnp.float32
        )
        field[:, :, start + at : start + at + step] = part.astype(LOW).reshape(field.shape[:2] + (step,))


def gradient_call(body, args, outs, scratch, flops):
    inputs, width = args[1:], len(args) - 1

    def kernel(me, *refs):
        far, near = refs[: width + len(outs)], refs[width + len(outs) : 2 * (width + len(outs))]
        copies = Copies(refs[-1])
        waiting = [copies.start(source, target) for source, target in zip(far[:width], near[:width])]
        sent = []

        def need(*wanted):
            for ref in wanted:
                waiting[[ref is one for one in near].index(True)].wait()

        def done(*made):
            for ref in made:
                sent.append(copies.start(ref, far[[ref is one for one in near].index(True)]))

        body(need, done, me, *near, *refs[2 * (width + len(outs)) : -1])
        for copy in sent:
            copy.wait()

    remote = pl.BlockSpec(memory_space=pl.ANY)
    return call(
        kernel,
        (1,),
        [SCALAR] + [remote] * width,
        [remote] * len(outs),
        outs,
        [pltpu.VMEM(a.shape, a.dtype) for a in list(inputs) + outs]
        + scratch
        + [pltpu.SemaphoreType.DMA((width + len(outs),))],
        flops,
        args,
    )


def plain_call(kernel, args, outs):
    return call(
        kernel,
        (1,),
        [SCALAR] + [whole(a) for a in args[1:]],
        [whole(o) for o in outs],
        outs,
        [],
        0,
        args,
    )


def feed_gradient_kernel(
    need, done, me, norm, d_pre, cot, act, message_x, message_y, keep_up, keep_down, up, down
):
    bits = bits_of(me)
    need(norm, d_pre)
    put_gradient(up, flat(norm[...]), flat(d_pre[...]))
    need(cot, act)
    put_gradient(down, flat(cot[...]), flat(act[...]))
    split_gradient(up, "x", bits, message_x, 0, keep_up)
    done(message_x, keep_up)
    split_gradient(down, "y", bits, message_y, 0, keep_down)
    done(message_y, keep_down)


def field_shape(dests, units, share):
    return shape((dests, units, share, UNIT))


def message_shape(blocks, share):
    return shape((blocks, share, UNIT))


def feed_gradient(me, norm, d_pre, cot, act):
    width = norm.shape[2]
    units = act.shape[2] // UNIT
    share = width // 16
    outs = [message_shape(8 * units, share)] * 2 + [field_shape(8, units, share)] * 2
    scratch = [pltpu.VMEM((16, share, act.shape[2]), LOW)] * 2
    return gradient_call(
        feed_gradient_kernel, (me, norm, d_pre, cot, act), outs, scratch, 4 * FRAMES * ROWS * width * act.shape[2]
    )


def space_gradient_kernel(
    need, done, me, norm, backs, d_space, mixed, up, got_x, down, got_y,
    message_x, message_y, keep_up, keep_down, keep_first, keep_second, first, second,
):
    bits = bits_of(me)
    count = 4 * up.shape[1]
    width = first.shape[2]
    need(norm, backs)
    rows = flat(norm[...])
    put_gradient(first, rows, flat(backs[...])[:, :width])
    put_gradient(second, rows, flat(backs[...])[:, width:])
    need(d_space, mixed)
    put_gradient(second, flat(d_space[...]), flat(mixed[...]), backs.shape[2] - width)
    need(up, got_x)
    split_total(up, got_x, 0, bits["y"], message_y, 0, keep_up)
    done(keep_up)
    split_gradient(first, "y", bits, message_y, count, keep_first)
    done(message_y, keep_first)
    need(down, got_y)
    split_total(down, got_y, 0, bits["x"], message_x, 0, keep_down)
    split_gradient(second, "x", bits, message_x, count, keep_second)
    done(message_x, keep_down, keep_second)


def space_gradient(me, norm, backs, d_space, mixed, up, down, got_x, got_y):
    width = norm.shape[2]
    half = mixed.shape[2]
    share = width // 16
    units = up.shape[1]
    own = 2 * half // UNIT
    outs = [message_shape(4 * units + 8 * own, share)] * 2
    outs += [field_shape(4, units, share)] * 2 + [field_shape(8, own, share)] * 2
    scratch = [pltpu.VMEM((16, share, 2 * half), LOW)] * 2
    return gradient_call(
        space_gradient_kernel,
        (me, norm, backs, d_space, mixed, up, got_x, down, got_y),
        outs,
        scratch,
        8 * FRAMES * ROWS * width * half,
    )


def mixer_gradient_kernel(
    need, done, me, d_mixer, mixed, d_grid, mixer_in, up, got_y, down, got_x, space_first, space_second,
    message_x, message_y, message_near, keep_up, keep_down, keep_first, keep_second, keep_out, keep_mixer, out, mixer,
):
    bits = bits_of(me)
    units = up.shape[1]
    feed = 4 * units
    own = space_first.shape[1]
    need(d_mixer, mixed)
    put_gradient(out, flat(d_mixer[...]), flat(mixed[...]))
    need(d_grid, mixer_in)
    put_gradient(mixer, flat(d_grid[...]), flat(mixer_in[...]))
    need(up, got_y)
    split_total(up, got_y, 0, bits["near"], message_near, 0, keep_up)
    need(down, got_x)
    split_total(down, got_x, 0, bits["near"], message_near, 2 * units, keep_down)
    done(message_near, keep_up, keep_down)
    need(space_first, space_second)
    split_total(space_first, got_y, feed, bits["x"], message_x, 0, keep_first)
    split_total(space_second, got_x, feed, bits["y"], message_y, 0, keep_second)
    split_gradient(out, "x", bits, message_x, 4 * own, keep_out)
    split_gradient(mixer, "y", bits, message_y, 4 * own, keep_mixer)
    done(message_x, message_y, keep_first, keep_second, keep_out, keep_mixer)


def mixer_gradient(me, d_mixer, mixed, d_grid, mixer_in, up, down, space_first, space_second, got_x, got_y):
    width = d_grid.shape[2]
    half = mixed.shape[2]
    share = width // 16
    units, own, new = up.shape[1], space_first.shape[1], half // UNIT
    outs = [message_shape(4 * own + 8 * new, share)] * 2 + [message_shape(4 * units, share)]
    outs += [field_shape(2, units, share)] * 2 + [field_shape(4, own, share)] * 2 + [field_shape(8, new, share)] * 2
    scratch = [pltpu.VMEM((16, share, half), LOW)] * 2
    return gradient_call(
        mixer_gradient_kernel,
        (me, d_mixer, mixed, d_grid, mixer_in, up, got_y, down, got_x, space_first, space_second),
        outs,
        scratch,
        4 * FRAMES * ROWS * width * half,
    )


TIME_FIRST = 5


def time_gradient_kernel(
    need, done, me, norm, backs, out, got_x, mixer, got_y, space_first, space_second, up, down, got_near,
    message_x, message_y, message_near, message_far,
    keep_up, keep_down, keep_space_first, keep_space_second, keep_out, keep_mixer, keep_first, keep_second, both,
):
    bits = bits_of(me)
    units, own, new = up.shape[1], space_first.shape[1], out.shape[1]
    need(norm, backs)
    put_gradient(both, flat(norm[...]), flat(backs[...]))
    need(out, got_x)
    split_total(out, got_x, 4 * own, bits["y"], message_y, 0, keep_out)
    need(mixer, got_y)
    split_total(mixer, got_y, 4 * own, bits["x"], message_x, 0, keep_mixer)
    cut = TIME_FIRST * UNIT
    split_gradient(both.at[:, :, :cut], "y", bits, message_y, 4 * new, keep_first)
    split_gradient(both.at[:, :, cut:], "x", bits, message_x, 4 * new, keep_second)
    done(message_y, message_x, keep_first, keep_second, keep_out, keep_mixer)
    need(space_first, space_second)
    split_total(space_first, got_x, 0, bits["near"], message_near, 0, keep_space_first)
    split_total(space_second, got_y, 0, bits["near"], message_near, 2 * own, keep_space_second)
    done(message_near, keep_space_first, keep_space_second)
    need(up, down, got_near)
    split_total(up, got_near, 0, bits["far"], message_far, 0, keep_up)
    split_total(down, got_near, 2 * units, bits["far"], message_far, units, keep_down)
    done(message_far, keep_up, keep_down)


def time_gradient(me, norm, backs, up, down, space_first, space_second, out, mixer, got_x, got_y, got_near):
    width = norm.shape[2]
    share = width // 16
    units, own, new = up.shape[1], space_first.shape[1], out.shape[1]
    last = backs.shape[2] // UNIT - TIME_FIRST
    outs = [
        message_shape(4 * new + 8 * last, share),
        message_shape(4 * new + 8 * TIME_FIRST, share),
        message_shape(4 * own, share),
        message_shape(2 * units, share),
    ]
    outs += [field_shape(1, units, share)] * 2 + [field_shape(2, own, share)] * 2 + [field_shape(4, new, share)] * 2
    outs += [field_shape(8, TIME_FIRST, share), field_shape(8, last, share)]
    return gradient_call(
        time_gradient_kernel,
        (me, norm, backs, out, got_x, mixer, got_y, space_first, space_second, up, down, got_near),
        outs,
        [pltpu.VMEM((16, share, backs.shape[2]), LOW)],
        2 * FRAMES * ROWS * width * backs.shape[2],
    )


def vector_blocks(vectors, share):
    parts = [vectors[:, col].astype(LOW) for col in units_of(vectors)]
    each = share // VECTORS
    return [jnp.concatenate(parts[at : at + each], axis=0) for at in range(0, len(parts), each)]


def second_kernel(
    me, vectors, space_first, space_second, out, mixer, first, second, got_x, got_y, got_near,
    message_x, message_y, message_xy, message_far,
    keep_space_first, keep_space_second, sum_out, sum_mixer, keep_first, keep_second,
):
    bits = bits_of(me)
    own, new = space_first.shape[1], out.shape[1]
    share = first.shape[2]
    split_total(first, got_y, 4 * new, bits["x"], message_x, 0, keep_first)
    split_total(second, got_x, 4 * new, bits["y"], message_y, 0, keep_second)
    for at, block in enumerate(vector_blocks(vectors[...], share)):
        message_x[4 * first.shape[1] + at] = block
        message_y[4 * second.shape[1] + at] = block
        message_xy[at] = block
    split_total(space_first, got_near, 0, bits["far"], message_far, 0, keep_space_first)
    split_total(space_second, got_near, 2 * own, bits["far"], message_far, own, keep_space_second)
    for ref, got, total in ((out, got_y, sum_out), (mixer, got_x, sum_mixer)):
        for at in range(4):
            total[at] = (wide(ref[at]) + wide(got[at * new : (at + 1) * new])).astype(LOW)


def second_step(me, vectors, space_first, space_second, out, mixer, first, second, got_x, got_y, got_near):
    own, new, share = space_first.shape[1], out.shape[1], first.shape[2]
    extra = vectors.size // (share * UNIT)
    outs = [
        message_shape(4 * first.shape[1] + extra, share),
        message_shape(4 * second.shape[1] + extra, share),
        message_shape(extra, share),
        message_shape(2 * own, share),
    ]
    outs += [field_shape(1, own, share)] * 2 + [field_shape(4, new, share)] * 2
    outs += [field_shape(4, first.shape[1], share), field_shape(4, second.shape[1], share)]
    return plain_call(
        second_kernel,
        (me, vectors, space_first, space_second, out, mixer, first, second, got_x, got_y, got_near),
        outs,
    )


def line_kernel(me, vectors, out, mixer, first, second, got_x, got_y, got_xy, message_1, message_2, message_3, own):
    bits = bits_of(me)
    share = first.shape[2]
    place = 2 * bits["far"] + bits["near"]
    messages = (own, message_1, message_2, message_3)
    start = 0
    for held, got in ((first, got_x), (second, got_y), (out, None), (mixer, None)):
        units = held.shape[1]
        for step, message in enumerate(messages):
            dest = place + step - 2 * (place & step)
            total = held[dest]
            if got is not None:
                total = (wide(total) + wide(got[pl.ds(dest * units, units)])).astype(LOW)
            message[start : start + units] = total
        start += units
    firsts, seconds = 4 * first.shape[1], 4 * second.shape[1]
    for at, block in enumerate(vector_blocks(vectors[...], share)):
        total = (wide(block) + wide(got_xy[at])) + (wide(got_x[firsts + at]) + wide(got_y[seconds + at]))
        for message in messages:
            message[start + at] = total.astype(LOW)


def line_step(me, vectors, out, mixer, first, second, got_x, got_y, got_xy):
    share = first.shape[2]
    blocks = first.shape[1] + second.shape[1] + out.shape[1] + mixer.shape[1] + vectors.size // (share * UNIT)
    return plain_call(
        line_kernel,
        (me, vectors, out, mixer, first, second, got_x, got_y, got_xy),
        [message_shape(blocks, share)] * 4,
    )


def final_kernel(
    me, own, got_1, got_2, got_3, up, down, got_feed, space_first, space_second, got_space,
    time_in, time_out, time_mixer, space_in, space_out, feed_up, feed_down, *small,
):
    units = up.shape[1]
    for unit, col in enumerate(units_of(feed_up)):
        feed_up[:, col] = wide(up[0, unit]) + wide(got_feed[unit])
        feed_down[:, col] = wide(down[0, unit]) + wide(got_feed[units + unit])
    mine = space_first.shape[1]
    half = space_out.shape[1]
    each = half // UNIT
    for unit in range(2 * mine):
        held = space_first[0, unit] if unit < mine else space_second[0, unit - mine]
        total = wide(held) + wide(got_space[unit])
        at = unit % each * UNIT
        if unit < 3 * each:
            space_in[unit // each, :, at : at + UNIT] = total
        else:
            space_out[:, at : at + UNIT] = total

    def line_total(at):
        return (wide(own[at]) + wide(got_1[at])) + (wide(got_2[at]) + wide(got_3[at]))

    for unit in range(5 * each):
        total = line_total(unit)
        at = unit % each * UNIT
        if unit < 3 * each:
            time_in[unit // each, :, at : at + UNIT] = total
        elif unit < 4 * each:
            time_out[:, at : at + UNIT] = total
        else:
            time_mixer[:, at : at + UNIT] = total
    share = feed_up.shape[0]
    parts = []
    for block in range(5 * each, own.shape[0]):
        total = line_total(block)
        parts += [total[at : at + VECTORS] for at in range(0, share, VECTORS)]
    settle_vectors(me[0, 0], jnp.concatenate(parts, axis=1), small)


def final_step(me, own, got_1, got_2, got_3, up, down, got_feed, space_first, space_second, got_space, width, half):
    share = width // 16
    units = up.shape[1] * UNIT
    outs = [
        shape(dims, jnp.float32)
        for dims in (
            (3, share, half), (share, half), (share, half), (3, share, half), (share, half), (share, units),
            (share, units),
        )
    ]
    return plain_call(
        final_kernel,
        (me, own, got_1, got_2, got_3, up, down, got_feed, space_first, space_second, got_space),
        outs + small_shapes(share),
    )


def swap_tensor(field):
    size = lax.axis_size("tensor")
    return lax.ppermute(field, "tensor", [(i, i ^ 1) for i in range(size)])


def swap_dp(field, bits):
    return lax.ppermute(field, "dp", [(i, i ^ bits) for i in range(lax.axis_size("dp"))])


def pick(field, at):
    return lax.dynamic_index_in_dim(field, at, 0, keepdims=False)


def reduce_rows(field):
    size = lax.axis_size("dp")
    me = lax.axis_index("dp")
    span = size // 2
    while span >= 1:
        field = field.reshape((2, span, -1) + field.shape[-1:])
        bit = me // span % 2
        field = (wide(pick(field, bit)) + wide(swap_dp(pick(field, 1 - bit), span))).astype(LOW)
        span //= 2
    return wide(field.reshape(-1, field.shape[-1]))


def dp_sum(field):
    span = 1
    while span < lax.axis_size("dp"):
        field = field + swap_dp(field, span)
        span *= 2
    return field


def in_order(first, then):
    return lax.optimization_barrier((first, then))


def grad_of(left, right):
    return lax.dot_general(
        left.reshape(-1, left.shape[2]),
        right.reshape(-1, right.shape[2]),
        (((0,), (0,)), ((), ())),
        preferred_element_type=jnp.float32,
    ).astype(LOW)


def local(
    clips,
    cotangent,
    live,
    time_gain,
    time_shift,
    time_inproj,
    time_inbias,
    time_outproj,
    time_outbias,
    time_mixer,
    time_mixbias,
    space_gain,
    space_shift,
    space_inproj,
    space_inbias,
    space_outproj,
    space_outbias,
    feed_gain,
    feed_shift,
    feed_upward,
    feed_upbias,
    feed_down,
    feed_downbias,
):
    tokens, width = clips.shape[1:]
    half = time_outproj.shape[0]
    dests = lax.axis_size("dp")
    tensor_rank = lax.axis_index("tensor")
    paired = dests == 16
    me = lax.axis_index("dp").astype(jnp.int32).reshape(1, 1)
    present = live.astype(jnp.float32).reshape(1, 1)
    time_in = jnp.transpose(time_inproj, (1, 0, 2))
    space_in = jnp.transpose(space_inproj, (1, 0, 2))
    mixers = (time_mixer, swap_tensor(time_mixer), tensor_rank.astype(jnp.int32).reshape(1, 1))
    x, t_norm, t_qkv, t_probs, t_mixed, t_part = time_forward(
        clips[0], time_gain, time_shift, time_in, time_inbias, time_outproj
    )
    cot, g_downbias = cotangent_frames(cotangent[0], present)
    mixer_in, after_time, s_norm, s_qkv, s_probs, s_mixed, s_part = space_forward(
        t_part, swap_tensor(t_part), x, time_outbias, mixers, time_mixbias, space_gain, space_shift, space_in,
        space_inbias, space_outproj,
    )
    mid, f_norm, act, d_pre, f_part, df_part, g_upbias = feed(
        s_part, swap_tensor(s_part), after_time, cot, space_outbias, feed_gain, feed_shift, feed_upward, feed_upbias,
        feed_down,
    )
    if paired:
        feed_x, feed_y, up, down = feed_gradient(me, f_norm, d_pre, cot, act)
        feed_x, mid = in_order(feed_x, mid)
        feed_x, feed_y = swap_dp(feed_x, 1), swap_dp(feed_y, 2)
    d_space, s_back, ds_part, d_class, g_feed_gain, g_feed_shift, g_space_outbias, g_space_inbias = space_backward(
        df_part, swap_tensor(df_part), mid, cot, s_qkv, s_probs, feed_gain, space_outproj, space_in
    )
    if paired:
        ds_part, feed_x, feed_y = lax.optimization_barrier((ds_part, feed_x, feed_y))
        space_x, space_y, up, down, s_first, s_second = space_gradient(
            me, s_norm, s_back, d_space, s_mixed, up, down, feed_x, feed_y
        )
        space_x, d_class = in_order(space_x, d_class)
        space_x, space_y = swap_dp(space_x, 1), swap_dp(space_y, 2)
    result = result_tokens(f_part, swap_tensor(f_part), mid, feed_downbias, present, tokens)
    result, d_class = in_order(result, d_class)
    d_grid, d_mixer, d_mixed, d_source, g_space_gain, g_space_shift, g_mixbias, g_outbias = mixer_backward(
        ds_part, swap_tensor(ds_part), after_time, d_space, d_class, space_gain, mixers, time_outproj
    )
    mixer_half = lax.dynamic_slice_in_dim(mixer_in, tensor_rank * half, half, 2)
    if paired:
        mixer_x, mixer_y, feed_near, up, down, s_first, s_second, t_out, t_mixer = mixer_gradient(
            me, d_mixer, t_mixed, d_grid, mixer_half, up, down, s_first, s_second, space_x, space_y
        )
        mixer_x, d_mixed = in_order(mixer_x, d_mixed)
        mixer_x, mixer_y, feed_near = swap_dp(mixer_x, 1), swap_dp(mixer_y, 2), swap_dp(feed_near, 4)
    t_back, dt_part, g_time_inbias = time_backward(d_mixed, t_qkv, t_probs, time_in)
    if paired:
        dt_part, mixer_x, mixer_y, feed_near = lax.optimization_barrier((dt_part, mixer_x, mixer_y, feed_near))
        time_x, time_y, space_near, feed_far, up, down, s_first, s_second, t_out, t_mixer, t_first, t_second = (
            time_gradient(
                me, t_norm, t_back, up, down, s_first, s_second, t_out, t_mixer, mixer_x, mixer_y, feed_near
            )
        )
        time_x, d_source = in_order(time_x, d_source)
        time_x, time_y = swap_dp(time_x, 1), swap_dp(time_y, 2)
        space_near, feed_far = swap_dp(space_near, 4), swap_dp(feed_far, 8)
    grad_clips, vectors = source_gradient(
        dt_part, swap_tensor(dt_part), x, d_grid, d_source, time_gain,
        (
            g_outbias, g_mixbias, g_space_gain, g_space_shift, g_space_outbias, g_feed_gain, g_feed_shift, g_downbias,
            g_time_inbias, g_space_inbias, g_upbias,
        ),
        tokens,
    )
    if paired:
        feed_far, space_near, vectors = lax.optimization_barrier((feed_far, space_near, vectors))
        last_x, last_y, last_xy, space_far, s_first, s_second, t_out, t_mixer, t_first, t_second = second_step(
            me, vectors, s_first, s_second, t_out, t_mixer, t_first, t_second, time_x, time_y, space_near
        )
        last_x, last_y, last_xy = swap_dp(last_x, 1), swap_dp(last_y, 2), swap_dp(last_xy, 3)
        space_far = swap_dp(space_far, 8)
        space_far, last_xy = lax.optimization_barrier((space_far, last_xy))
        line_1, line_2, line_3, line_own = line_step(
            me, vectors, t_out, t_mixer, t_first, t_second, last_x, last_y, last_xy
        )
        line_1, line_2, line_3 = swap_dp(line_1, 4), swap_dp(line_2, 8), swap_dp(line_3, 12)
        time_sum, out_sum, mixer_sum, space_sum, space_out, up_sum, down_sum, *small = final_step(
            me, line_own, line_1, line_2, line_3, up, down, feed_far, s_first, s_second, space_far, width, half
        )
    else:

        def parts(field):
            return jnp.stack([field[:, part * half : (part + 1) * half] for part in range(3)])

        up_sum = reduce_rows(grad_of(f_norm, d_pre))
        down_sum = reduce_rows(grad_of(cot, act))
        space_sum = parts(reduce_rows(grad_of(s_norm, s_back)))
        space_out = reduce_rows(grad_of(d_space, s_mixed))
        time_sum = parts(reduce_rows(grad_of(t_norm, t_back)))
        out_sum = reduce_rows(grad_of(d_mixer, t_mixed))
        mixer_sum = reduce_rows(grad_of(d_grid, mixer_half))
        small = settle(dp_sum(vectors), me, dests)
    settled = (
        small[0],
        small[1],
        jnp.transpose(time_sum, (1, 0, 2)),
        small[10],
        out_sum.T,
        small[2],
        mixer_sum.T,
        small[3],
        small[4],
        small[5],
        jnp.transpose(space_sum, (1, 0, 2)),
        small[11],
        space_out.T,
        small[6],
        small[7],
        small[8],
        up_sum,
        small[12],
        down_sum.T,
        small[9],
    )
    return (result[None], grad_clips[None]) + settled


def solution(mesh):
    in_specs = (
        P("dp", None, None),
        P("dp", None, None),
        P("dp"),
        P(),
        P(),
        P(None, None, "tensor"),
        P(None, "tensor"),
        P("tensor", None),
        P(),
        P("tensor", None),
        P(),
        P(),
        P(),
        P(None, None, "tensor"),
        P(None, "tensor"),
        P("tensor", None),
        P(),
        P(),
        P(),
        P(None, "tensor"),
        P("tensor"),
        P("tensor", None),
        P(),
    )
    out_specs = (
        P("dp", None, None),
        P("dp", None, None),
        P("dp"),
        P("dp"),
        P("dp", None, "tensor"),
        P(None, ("tensor", "dp")),
        P("tensor", "dp"),
        P("dp"),
        P("tensor", "dp"),
        P("dp"),
        P("dp"),
        P("dp"),
        P("dp", None, "tensor"),
        P(None, ("tensor", "dp")),
        P("tensor", "dp"),
        P("dp"),
        P("dp"),
        P("dp"),
        P("dp", "tensor"),
        P(("tensor", "dp")),
        P("tensor", "dp"),
        P("dp"),
    )
    return jax.shard_map(local, mesh=mesh, in_specs=in_specs, out_specs=out_specs, check_vma=False)
```

```python
import functools

import jax
import jax.numpy as jnp
from jax import lax
from jax.experimental import pallas as pl
from jax.experimental.pallas import tpu as pltpu
from jax.sharding import PartitionSpec as P

HEAD = 64
FRAMES = 8
PLACES = 196
BLOCK = 16
ROWS = 208
BLOCKS = ROWS // BLOCK
PAIR = 2
UNROLL = BLOCKS
TIME_GROUP = 13
TIME_LAG = 1
SPACE_LAG = 6
EPS = 1e-06
LOW = jnp.bfloat16
VMEM_BYTES = 62 * 1024 * 1024
COST = 1


def dot(left, right):
    return jnp.dot(left, right, preferred_element_type=jnp.float32)


def dot_last(left, right):
    return lax.dot_general(left, right, (((1,), (1,)), ((), ())), preferred_element_type=jnp.float32)


def normed(field):
    center = field - jnp.mean(field, axis=-1, keepdims=True)
    spread_sq = jnp.mean(center * center, axis=-1, keepdims=True)
    inverse = lax.rsqrt(spread_sq + EPS)
    return center * inverse, inverse


def normed_back(unit, inverse, grad_unit):
    first = jnp.mean(grad_unit, axis=-1, keepdims=True)
    second = jnp.mean(grad_unit * unit, axis=-1, keepdims=True)
    return (grad_unit - first - unit * second) * inverse


def side_by_side(weights):
    return jnp.concatenate([weights[part] for part in range(weights.shape[0])], axis=1)


def flat(field):
    return field.reshape((field.shape[0] * field.shape[1],) + field.shape[2:])


def wide(field):
    return field.astype(jnp.float32)


def iota(shape, axis):
    return lax.broadcasted_iota(jnp.int32, shape, axis)


def column_sum(field):
    return jnp.sum(field, axis=0, keepdims=True)


def call(kernel, grid, in_specs, out_specs, out_shapes, scratch, flops, args):
    moved = sum(a.size * a.dtype.itemsize for a in args) + sum(o.size * o.dtype.itemsize for o in out_shapes)
    return pl.pallas_call(
        kernel,
        grid=grid,
        in_specs=in_specs,
        out_specs=out_specs,
        out_shape=out_shapes,
        scratch_shapes=scratch,
        compiler_params=pltpu.CompilerParams(vmem_limit_bytes=VMEM_BYTES),
        cost_estimate=pl.CostEstimate(flops=int(flops) // COST, bytes_accessed=int(moved) // COST, transcendentals=0),
    )(*args)


SCALAR = pl.BlockSpec(memory_space=pltpu.SMEM)


def whole(array):
    zeros = (0,) * array.ndim
    return pl.BlockSpec(array.shape, lambda *at: zeros)


def shape(dims, kind=LOW):
    return jax.ShapeDtypeStruct(dims, kind)


def to_frames(rows, block):
    count = FRAMES * BLOCK
    at = iota((count, count + BLOCK), 0)
    source = 1 + FRAMES * (at % BLOCK) + at // BLOCK
    pick = jnp.where(source == iota((count, count + BLOCK), 1), 1.0, 0.0).astype(LOW)
    return dot(pick, rows)


def to_tokens(rows):
    count = FRAMES * BLOCK
    at = iota((count, count), 1)
    target = 1 + FRAMES * (at % BLOCK) + at // BLOCK
    pick = jnp.where(target == iota((count, count), 0), 1.0, 0.0).astype(LOW)
    return dot(pick, rows)


def fill_rows(source, tokens):
    count = tokens.shape[0]
    even = count // BLOCK * BLOCK
    source[0:even] = tokens[0:even]
    source[even:] = jnp.zeros((source.shape[0] - even, source.shape[1]), source.dtype)
    left = wide(tokens[even:count])
    tail = jnp.zeros((BLOCK, source.shape[1]), jnp.float32)
    for row in range(count - even):
        tail = tail + jnp.where(iota(tail.shape, 0) == row, left[row : row + 1], 0.0)
    source[even : even + BLOCK] = tail.astype(source.dtype)


def frame_rows(source, block, class_row, class_frames):
    count = FRAMES * BLOCK
    rows = to_frames(source[pl.ds(pl.multiple_of(block * count, count), count + BLOCK), :], block)
    at = iota((count, 1), 0)
    is_class = (block * BLOCK + at % BLOCK == PLACES) & (at // BLOCK < class_frames)
    return rows + jnp.where(is_class, class_row, 0.0)


class Copies:
    def __init__(self, semaphores):
        self.semaphores = semaphores
        self.started = []

    def start(self, source, target):
        copy = pltpu.make_async_copy(source, target, self.semaphores.at[len(self.started)])
        copy.start()
        self.started.append(copy)
        return copy


def time_forward_kernel(
    clips, gain, shift, inproj_far, inbias, outproj_far, x_far, norm_far, qkv_far, probs_far, mixed_far, part_far,
    inproj, outproj, x_out, norm_out, qkv_out, probs_out, mixed_out, part_out, source, semaphores,
):
    half = outproj.shape[0]
    copies = Copies(semaphores)
    fetched = [copies.start(inproj_far, inproj), copies.start(outproj_far, outproj)]
    fill_rows(source, clips)
    class_row = wide(clips[0:1])

    def first(block, carry):
        rows = frame_rows(source, block, class_row, FRAMES)
        unit, _ = normed(rows)
        at = pl.ds(pl.multiple_of(block * BLOCK, BLOCK), BLOCK)
        x_out[:, at, :] = rows.astype(LOW).reshape(FRAMES, BLOCK, rows.shape[1])
        norm_out[:, at, :] = (unit * vector(gain) + vector(shift)).astype(LOW).reshape(FRAMES, BLOCK, rows.shape[1])
        return carry

    lax.fori_loop(0, BLOCKS, first, 0, unroll=UNROLL)
    sent = [copies.start(x_out, x_far), copies.start(norm_out, norm_far)]
    fetched[0].wait()
    weights = side_by_side(inproj)
    for step in range(FRAMES // PAIR):
        at = pl.ds(step * PAIR, PAIR)
        qkv = heads_low(dot(flat(norm_out[at]), weights), inbias, half)
        qkv_out[at] = qkv.reshape(PAIR, ROWS, 3 * half)
    sent.append(copies.start(qkv_out, qkv_far))
    count = FRAMES * BLOCK
    same = iota((count, 2 * count), 0) % BLOCK == iota((count, 2 * count), 1) % BLOCK

    def third(first_block, count):
        ats = [
            pl.ds(pl.multiple_of((first_block + step) * BLOCK, BLOCK), BLOCK) for step in range(count)
        ]

        def keep(step, head, probs):
            probs_out[first_block + step, head] = probs

        mixed = attend(
            [flat(qkv_out[:, at, :]) for at in ats], lambda scores: jnp.where(same, scores, -1e30), keep, 2, TIME_LAG
        )
        for at, part in zip(ats, mixed):
            mixed_out[:, at, :] = part.reshape(FRAMES, BLOCK, half)

    by_blocks(third)
    sent += [copies.start(probs_out, probs_far), copies.start(mixed_out, mixed_far)]
    fetched[1].wait()
    for step in range(FRAMES // PAIR):
        at = pl.ds(step * PAIR, PAIR)
        part = dot(flat(mixed_out[at]), outproj[...]).astype(LOW)
        part_out[at] = part.reshape(PAIR, ROWS, part.shape[1])
        sent.append(copies.start(part_out.at[at], part_far.at[at]))
    for copy in sent:
        copy.wait()


def by_blocks(run):
    def step(at, carry):
        run(at * TIME_GROUP, TIME_GROUP)
        return carry

    lax.fori_loop(0, BLOCKS // TIME_GROUP, step, 0)
    if BLOCKS % TIME_GROUP:
        run(BLOCKS // TIME_GROUP * TIME_GROUP, BLOCKS % TIME_GROUP)


def heads_low(linear, inbias, half):
    query = ((linear[:, :half] + inbias[0:1]) * HEAD ** (-0.5)).astype(LOW)
    keys = linear[:, half : 2 * half].astype(LOW)
    values = (linear[:, 2 * half :] + inbias[1:2]).astype(LOW)
    return jnp.concatenate([query, keys, values], axis=1)


def beside(field_t, head):
    own = field_t[HEAD * head : HEAD * (head + 1)]
    none = jnp.zeros_like(own)
    return jnp.concatenate([own, none] if head % 2 == 0 else [none, own], axis=0)


def beside_all(field_t, heads):
    return jnp.concatenate([beside(field_t, head) for head in heads], axis=1)


def pair_of(field, head):
    start = head // 2 * 2 * HEAD
    return field[:, start : start + 2 * HEAD]


def head_rows(field_t, head):
    return field_t[HEAD * head : HEAD * (head + 1)]


def staged(count, stages, lag):
    held = [None] * count
    for step in range(count + lag * (len(stages) - 1)):
        for depth, stage in enumerate(stages):
            item = step - lag * depth
            if 0 <= item < count:
                held[item] = stage(item, held[item])
    return held


def attend(inputs, block_allowed, keep, group, lag):
    half = inputs[0].shape[1] // 3
    rows = inputs[0].shape[0]
    query_t = [qkv[:, :half].T for qkv in inputs]
    values_t = [qkv[:, 2 * half :].T for qkv in inputs]
    groups = half // HEAD // group

    def heads_of(item):
        first = item % groups * group
        return range(first, first + group)

    def score(item, held):
        block = item // groups
        keys = inputs[block][:, half : 2 * half]
        return dot(pair_of(keys, heads_of(item)[0]), beside_all(query_t[block], heads_of(item)))

    def weigh(item, scores):
        scores = block_allowed(scores)
        expon = jnp.exp(scores - jnp.max(scores, axis=0, keepdims=True))
        probs = (expon * (1.0 / column_sum(expon))).astype(LOW)
        for at, head in enumerate(heads_of(item)):
            keep(item // groups, head, probs[:, at * rows : (at + 1) * rows])
        return probs

    def mix(item, probs):
        return [
            dot(head_rows(values_t[item // groups], head), probs[:, at * rows : (at + 1) * rows])
            for at, head in enumerate(heads_of(item))
        ]

    mixed_t = staged(len(inputs) * groups, [score, weigh, mix], lag)
    out = []
    for block in range(len(inputs)):
        parts = [part for item in mixed_t[block * groups : (block + 1) * groups] for part in item]
        out.append(jnp.concatenate(parts, axis=0).T.astype(LOW))
    return out


def attend_back(inputs, probs_of, d_mixeds, group, lag):
    half = inputs[0].shape[1] // 3
    rows = inputs[0].shape[0]
    keys_t = [qkv[:, half : 2 * half].T for qkv in inputs]
    d_mixed_t = [d_mixed.T for d_mixed in d_mixeds]
    lane = iota((rows, 2 * HEAD), 1) < HEAD
    groups = half // HEAD // group

    def heads_of(item):
        first = item % groups * group
        return range(first, first + group)

    def score(item, held):
        block = item // groups
        values = inputs[block][:, 2 * half :]
        return dot(pair_of(values, heads_of(item)[0]), beside_all(d_mixed_t[block], heads_of(item)))

    def weigh(item, d_probs):
        probs_low = jnp.concatenate([probs_of(item // groups, head) for head in heads_of(item)], axis=1)
        probs = wide(probs_low)
        scaled = probs * d_probs
        d_scores = scaled - probs * column_sum(scaled)
        return probs_low, d_scores.astype(LOW)

    def halves(field):
        none = jnp.zeros_like(field)
        return jnp.concatenate([jnp.where(lane, field, none), jnp.where(lane, none, field)], axis=0)

    def mix(item, held):
        block = item // groups
        probs_low, d_scores = held
        d_query_t = [
            dot(head_rows(keys_t[block], head), d_scores[:, at * rows : (at + 1) * rows])
            for at, head in enumerate(heads_of(item))
        ]
        d_mixed = pair_of(d_mixeds[block], heads_of(item)[0])
        query = pair_of(inputs[block][:, :half], heads_of(item)[0])
        if group == 2:
            d_mixed = halves(d_mixed)
            query = halves(query)
        return d_query_t, dot(d_scores, query), dot(probs_low, d_mixed)

    made = staged(len(inputs) * groups, [score, weigh, mix], lag)

    def paired(fields):
        if group == 2:
            return fields
        return [jnp.where(lane, fields[at], fields[at + 1]) for at in range(0, len(fields), 2)]

    out = []
    for block in range(len(inputs)):
        own = made[block * groups : (block + 1) * groups]
        d_query = jnp.concatenate([part for item in own for part in item[0]], axis=0).T.astype(LOW) * HEAD ** (-0.5)
        d_keys = paired([item[1] for item in own])
        d_values = paired([item[2] for item in own])
        out.append(jnp.concatenate([d_query] + [d.astype(LOW) for d in d_keys + d_values], axis=1))
    return out


def time_forward(clips, gain, shift, inproj, inbias, outproj):
    tokens, width = clips.shape
    half = outproj.shape[0]
    heads = half // HEAD
    count = FRAMES * BLOCK
    args = (clips, gain, shift, inproj, inbias, outproj)
    outs = [
        shape((FRAMES, ROWS, width)),
        shape((FRAMES, ROWS, width)),
        shape((FRAMES, ROWS, 3 * half)),
        shape((BLOCKS, heads, count, count)),
        shape((FRAMES, ROWS, half)),
        shape((FRAMES, ROWS, width)),
    ]
    rows = FRAMES * ROWS
    near = [pltpu.VMEM(a.shape, a.dtype) for a in (inproj, outproj)] + [pltpu.VMEM(o.shape, o.dtype) for o in outs]
    far = pl.BlockSpec(memory_space=pl.ANY)
    return call(
        time_forward_kernel,
        (1,),
        [whole(clips), whole(gain), whole(shift), far, whole(inbias), far],
        [far] * 6,
        outs,
        near + [pltpu.VMEM((BLOCKS * count + BLOCK, width), LOW), pltpu.SemaphoreType.DMA((16,))],
        2 * rows * width * half * 5,
        args,
    )


def cotangent_kernel(cotangent, live, out, total, source):
    fill_rows(source, cotangent)
    present = live[0, 0]
    class_row = wide(cotangent[0:1])

    def first(block, carry):
        rows = frame_rows(source, block, class_row, 1) * present
        at = pl.ds(pl.multiple_of(block * BLOCK, BLOCK), BLOCK)
        out[:, at, :] = rows.astype(LOW).reshape(FRAMES, BLOCK, rows.shape[1])
        return carry + column_sum(rows)

    total[...] = lax.fori_loop(0, BLOCKS, first, jnp.zeros(total.shape, jnp.float32), unroll=UNROLL)


def cotangent_frames(cotangent, live):
    tokens, width = cotangent.shape
    args = (cotangent, live)
    outs = [shape((FRAMES, ROWS, width)), shape((1, width), jnp.float32)]
    return call(
        cotangent_kernel,
        (1,),
        [whole(cotangent), SCALAR],
        [whole(o) for o in outs],
        outs,
        [pltpu.VMEM((BLOCKS * FRAMES * BLOCK + BLOCK, width), LOW)],
        2 * FRAMES * ROWS * 128 * width,
        args,
    )


def vector(ref):
    return ref[...].reshape(1, -1)


def place_of(shape_of):
    return iota(shape_of, 0) % ROWS


def gather_mixer(own, other, rank, mixer):
    half = own.shape[0]

    @pl.when(pl.program_id(0) == 0)
    def _():
        mixer[pl.ds(pl.multiple_of(rank[0, 0] * half, half), half), :] = own[...]
        mixer[pl.ds(pl.multiple_of((1 - rank[0, 0]) * half, half), half), :] = other[...]


def space_forward_kernel(
    own, other, x, outbias, mixer_own, mixer_other, rank, mixbias, gain, shift, inproj, inbias, outproj,
    mixer_out, after_out, norm_out, qkv_out, probs_out, mixed_out, part_out, mixer,
):
    gather_mixer(mixer_own, mixer_other, rank, mixer)
    half = outproj.shape[0]
    width = outproj.shape[1]

    def spread(field):
        return field.astype(LOW).reshape(PAIR, ROWS, field.shape[1])

    mixer_in = (wide(flat(own[...])) + wide(flat(other[...])) + vector(outbias)).astype(LOW)
    mixer_out[...] = spread(jnp.where(rank[0, 0] == 0, mixer_in[:, :half], mixer_in[:, half:]))
    branch = dot(mixer_in, mixer[...]) + vector(mixbias)
    after = wide(flat(x[...])) + jnp.where(place_of((PAIR * ROWS, 1)) < PLACES, branch, 0.0)
    after_out[...] = spread(after)
    unit, _ = normed(after)
    norm = (unit * vector(gain) + vector(shift)).astype(LOW)
    norm_out[...] = spread(norm)
    qkv = heads_low(dot(norm, side_by_side(inproj)), inbias, half)
    qkv_out[...] = spread(qkv)

    def allowed(scores):
        even = ROWS - BLOCK
        last = jnp.where(iota((BLOCK, ROWS), 0) <= PLACES - even, scores[even:], -1e30)
        return jnp.concatenate([scores[:even], last], axis=0)

    def keep(frame, head, probs):
        probs_out[frame, head] = probs

    frames = [qkv[frame * ROWS : (frame + 1) * ROWS] for frame in range(PAIR)]
    for frame, mixed in enumerate(attend(frames, allowed, keep, 1, SPACE_LAG)):
        mixed_out[frame] = mixed
    part_out[...] = spread(dot(flat(mixed_out[...]), outproj[...]))


def pairs(array):
    rest = (0,) * (array.ndim - 1)
    return pl.BlockSpec((PAIR,) + array.shape[1:], lambda at: (at,) + rest)


def space_forward(own, other, x, outbias, mixers, mixbias, gain, shift, inproj, inbias, outproj):
    width = x.shape[2]
    half = outproj.shape[0]
    heads = half // HEAD
    args = (own, other, x, outbias) + mixers + (mixbias, gain, shift, inproj, inbias, outproj)
    outs = [
        shape((FRAMES, ROWS, half)),
        shape((FRAMES, ROWS, width)),
        shape((FRAMES, ROWS, width)),
        shape((FRAMES, ROWS, 3 * half)),
        shape((FRAMES, heads, ROWS, ROWS)),
        shape((FRAMES, ROWS, half)),
        shape((FRAMES, ROWS, width)),
    ]
    return call(
        space_forward_kernel,
        (FRAMES // PAIR,),
        [pairs(a) for a in args[:3]] + [whole(a) for a in args[3:6]] + [SCALAR] + [whole(a) for a in args[7:]],
        [pairs(o) for o in outs],
        outs,
        [pltpu.VMEM((width, width), LOW)],
        2 * FRAMES * ROWS * width * half * 8,
        args,
    )


def last_block(count):
    return lambda array: pl.BlockSpec((count, BLOCK, array.shape[2]), lambda at: (0, BLOCKS - 1, 0))


CLASS_AT = PLACES - (BLOCKS - 1) * BLOCK


def feed_kernel(
    own, other, after, cot, own_last, other_last, after_last, outbias, gain, shift, upward, upbias, down,
    mid_out, norm_out, act_out, dpre_out, part_out, dnorm_out, upbias_out,
):
    step = pl.program_id(0)
    units = upward.shape[1]
    width = upward.shape[0]

    def spread(field):
        return field.astype(LOW).reshape(PAIR, ROWS, field.shape[1])

    class_branch = wide(own_last[...]) + wide(other_last[...])
    class_branch = jnp.sum(class_branch, axis=0)[CLASS_AT : CLASS_AT + 1] * (1.0 / FRAMES) + vector(outbias)
    at = iota((PAIR * ROWS, 1), 0)
    branch = wide(flat(own[...])) + wide(flat(other[...])) + vector(outbias)
    is_class = (at == PLACES) & (step == 0)
    mid = jnp.where(at % ROWS < PLACES, wide(flat(after[...])) + branch, 0.0)
    mid = mid + jnp.where(is_class, wide(after_last[0])[CLASS_AT : CLASS_AT + 1] + class_branch, 0.0)
    mid_out[...] = spread(mid)
    unit, _ = normed(mid)
    norm = (unit * vector(gain) + vector(shift)).astype(LOW)
    norm_out[...] = spread(norm)
    grad = flat(cot[...])
    part = jnp.zeros((PAIR * ROWS, width), jnp.float32)
    d_norm = jnp.zeros((PAIR * ROWS, width), jnp.float32)
    share = units

    @pl.when(step == 0)
    def _():
        upbias_out[...] = jnp.zeros(upbias_out.shape, jnp.float32)

    for start in range(0, units, share):
        cols = slice(start, start + share)
        pre = dot(norm, upward[:, cols]) + vector(upbias)[:, cols]
        cumulative = 0.5 * (1.0 + lax.erf(pre * 0.5**0.5))
        slope = cumulative + pre * jnp.exp(-0.5 * pre * pre) * 0.3989422804014327
        act = (pre * cumulative).astype(LOW)
        act_out[:, :, cols] = spread(act)
        d_pre = (dot_last(grad, down[cols]) * slope).astype(LOW)
        dpre_out[:, :, cols] = spread(d_pre)
        upbias_out[:, cols] += column_sum(wide(d_pre))
        part = part + dot(act, down[cols])
        d_norm = d_norm + dot_last(d_pre, upward[:, cols])
    part_out[...] = spread(part)
    dnorm_out[...] = spread(d_norm)


def feed(own, other, after, cot, outbias, gain, shift, upward, upbias, down):
    width, units = upward.shape
    args = (own, other, after, cot, own, other, after, outbias, gain, shift, upward, upbias, down)
    outs = [
        shape((FRAMES, ROWS, width)),
        shape((FRAMES, ROWS, width)),
        shape((FRAMES, ROWS, units)),
        shape((FRAMES, ROWS, units)),
        shape((FRAMES, ROWS, width)),
        shape((FRAMES, ROWS, width)),
        shape((1, units), jnp.float32),
    ]
    tail = last_block(FRAMES)
    return call(
        feed_kernel,
        (FRAMES // PAIR,),
        [pairs(a) for a in args[:4]] + [tail(a) for a in args[4:7]] + [whole(a) for a in args[7:]],
        [pairs(o) for o in outs[:6]] + [whole(outs[6])],
        outs,
        [],
        2 * FRAMES * ROWS * width * units * 4,
        args,
    )


def space_backward_kernel(
    own, other, mid, cot, qkv, probs, own_last, other_last, mid_last, cot_last, gain, outproj, inproj,
    dspace_out, back_out, part_out, dclass_out, gain_out, shift_out, outbias_out, inbias_out,
):
    step = pl.program_id(0)
    half = outproj.shape[0]

    def spread(field):
        return field.astype(LOW).reshape(PAIR, ROWS, field.shape[1])

    def back(own_part, other_part, mid_part, cot_part):
        d_norm = wide(own_part) + wide(other_part)
        unit, inverse = normed(wide(mid_part))
        return wide(cot_part) + normed_back(unit, inverse, d_norm * vector(gain)), d_norm, d_norm * unit

    d_class = back(own_last[0], other_last[0], mid_last[0], cot_last[0])[0][CLASS_AT : CLASS_AT + 1]
    d_mid, d_shift, d_gain = back(flat(own[...]), flat(other[...]), flat(mid[...]), flat(cot[...]))
    place = place_of((PAIR * ROWS, 1))
    d_space = jnp.where(place < PLACES, d_mid, jnp.where(place == PLACES, d_class * (1.0 / FRAMES), 0.0))

    @pl.when(step == 0)
    def _():
        dclass_out[...] = d_class
        for ref in (gain_out, shift_out, outbias_out, inbias_out):
            ref[...] = jnp.zeros(ref.shape, jnp.float32)

    gain_out[...] += column_sum(d_gain)
    shift_out[...] += column_sum(d_shift)
    outbias_out[...] += column_sum(d_space)
    d_low = d_space.astype(LOW)
    dspace_out[...] = spread(d_low)
    d_mixed = dot_last(d_low, outproj[...]).astype(LOW)
    made = attend_back(
        [qkv[frame] for frame in range(PAIR)],
        lambda frame, head: probs[frame, head],
        [d_mixed[frame * ROWS : (frame + 1) * ROWS] for frame in range(PAIR)],
        1,
        SPACE_LAG,
    )
    for frame, part in enumerate(made):
        back_out[frame] = part
    backs = flat(back_out[...])
    inbias_out[...] += column_sum(wide(backs))
    part_out[...] = spread(dot_last(backs, side_by_side(inproj)))


def space_backward(own, other, mid, cot, qkv, probs, gain, outproj, inproj):
    width = mid.shape[2]
    half = outproj.shape[0]
    args = (own, other, mid, cot, qkv, probs, own, other, mid, cot, gain, outproj, inproj)
    outs = [
        shape((FRAMES, ROWS, width)),
        shape((FRAMES, ROWS, 3 * half)),
        shape((FRAMES, ROWS, width)),
        shape((1, width), jnp.float32),
        shape((1, width), jnp.float32),
        shape((1, width), jnp.float32),
        shape((1, width), jnp.float32),
        shape((1, 3 * half), jnp.float32),
    ]
    tail = last_block(1)
    return call(
        space_backward_kernel,
        (FRAMES // PAIR,),
        [pairs(a) for a in args[:6]] + [tail(a) for a in args[6:10]] + [whole(a) for a in args[10:]],
        [pairs(o) for o in outs[:3]] + [whole(o) for o in outs[3:]],
        outs,
        [],
        2 * FRAMES * ROWS * width * half * 6,
        args,
    )


def mixer_backward_kernel(
    own, other, after, dspace, dclass, gain, mixer_own, mixer_other, rank, outproj,
    dgrid_out, dmixer_out, dmixed_out, dsource_out, gain_out, shift_out, mixbias_out, outbias_out, mixer,
):
    gather_mixer(mixer_own, mixer_other, rank, mixer)

    @pl.when(pl.program_id(0) == 0)
    def _():
        dsource_out[...] = dclass[...]
        for ref in (gain_out, shift_out, mixbias_out, outbias_out):
            ref[...] = jnp.zeros(ref.shape, jnp.float32)

    def spread(field):
        return field.astype(LOW).reshape(PAIR, ROWS, field.shape[1])

    d_norm = wide(flat(own[...])) + wide(flat(other[...]))
    unit, inverse = normed(wide(flat(after[...])))
    gain_out[...] += column_sum(d_norm * unit)
    shift_out[...] += column_sum(d_norm)
    d_space_in = normed_back(unit, inverse, d_norm * vector(gain))
    place = place_of((PAIR * ROWS, 1))
    dsource_out[...] += column_sum(jnp.where(place == PLACES, d_space_in, 0.0))
    d_grid = jnp.where(place < PLACES, d_space_in + wide(flat(dspace[...])), 0.0)
    mixbias_out[...] += column_sum(d_grid)
    d_low = d_grid.astype(LOW)
    dgrid_out[...] = spread(d_low)
    d_mixer = dot_last(d_low, mixer[...]).astype(LOW)
    dmixer_out[...] = spread(d_mixer)
    outbias_out[...] += column_sum(wide(d_mixer))
    dmixed_out[...] = spread(dot_last(d_mixer, outproj[...]))


def mixer_backward(own, other, after, dspace, dclass, gain, mixers, outproj):
    width = after.shape[2]
    half = outproj.shape[0]
    args = (own, other, after, dspace, dclass, gain) + mixers + (outproj,)
    outs = [
        shape((FRAMES, ROWS, width)),
        shape((FRAMES, ROWS, width)),
        shape((FRAMES, ROWS, half)),
    ] + [shape((1, width), jnp.float32)] * 5
    return call(
        mixer_backward_kernel,
        (FRAMES // PAIR,),
        [pairs(a) for a in args[:4]] + [whole(a) for a in args[4:8]] + [SCALAR, whole(outproj)],
        [pairs(o) for o in outs[:3]] + [whole(o) for o in outs[3:]],
        outs,
        [pltpu.VMEM((width, width), LOW)],
        2 * FRAMES * ROWS * width * half * 3,
        args,
    )


def near_far(arrays):
    return [pltpu.VMEM(a.shape, a.dtype) for a in arrays], pl.BlockSpec(memory_space=pl.ANY)


def places(first, last):
    return pl.ds(first * BLOCK, (last - first) * BLOCK)


TIME_GROUPS = ((0, 3), (3, 8), (8, BLOCKS))


def time_backward_kernel(
    d_mixed_far, qkv_far, probs_far, inproj_far, back_far, part_far, inbias_out,
    d_mixed, qkv, probs, inproj, back_out, part_out, semaphores,
):
    half = d_mixed.shape[2]
    width = inproj.shape[1]
    copies = Copies(semaphores)
    coming = []
    for first, last in TIME_GROUPS:
        at = places(first, last)
        coming.append(
            [
                copies.start(d_mixed_far.at[:, at, :], d_mixed.at[:, at, :]),
                copies.start(qkv_far.at[:, at, :], qkv.at[:, at, :]),
                copies.start(probs_far.at[pl.ds(first, last - first)], probs.at[pl.ds(first, last - first)]),
            ]
        )
    weights_come = copies.start(inproj_far, inproj)
    sent = []
    for (first, last), arrivals in zip(TIME_GROUPS, coming):
        for arrival in arrivals:
            arrival.wait()
        ats = [places(block, block + 1) for block in range(first, last)]
        made = attend_back(
            [flat(qkv[:, at, :]) for at in ats],
            lambda step, head, first=first: probs[first + step, head],
            [flat(d_mixed[:, at, :]) for at in ats],
            2,
            TIME_LAG,
        )
        for at, part in zip(ats, made):
            back_out[:, at, :] = part.reshape(FRAMES, BLOCK, 3 * half)
        at = places(first, last)
        sent.append(copies.start(back_out.at[:, at, :], back_far.at[:, at, :]))
    weights_come.wait()
    inbias = jnp.zeros(inbias_out.shape, jnp.float32)
    for step in range(FRAMES // PAIR):
        at = pl.ds(step * PAIR, PAIR)
        backs = flat(back_out[at])
        inbias = inbias + column_sum(wide(backs))
        part_out[at] = dot_last(backs, side_by_side(inproj)).astype(LOW).reshape(PAIR, ROWS, width)
        sent.append(copies.start(part_out.at[at], part_far.at[at]))
    inbias_out[...] = inbias
    for copy in sent:
        copy.wait()


def time_backward(d_mixed, qkv, probs, inproj):
    width = inproj.shape[1]
    half = d_mixed.shape[2]
    args = (d_mixed, qkv, probs, inproj)
    outs = [
        shape((FRAMES, ROWS, 3 * half)),
        shape((FRAMES, ROWS, width)),
        shape((1, 3 * half), jnp.float32),
    ]
    near, far = near_far(args + tuple(outs[:2]))
    return call(
        time_backward_kernel,
        (1,),
        [far] * 4,
        [far, far, whole(outs[2])],
        outs,
        near + [pltpu.SemaphoreType.DMA((4 * len(TIME_GROUPS) + 1 + FRAMES // PAIR,))],
        2 * FRAMES * ROWS * width * half * 5,
        args,
    )


def fetch_places(copies, far, near, groups):
    return [
        [copies.start(f.at[:, places(*group), :], n.at[:, places(*group), :]) for f, n in zip(far, near)]
        for group in groups
    ]


def put_tokens(out, block, low, carry):
    count = FRAMES * BLOCK
    moved = jnp.where(iota((count, 1), 0) == 0, carry, to_tokens(low))
    fits = min(out.shape[0] - block * count, count)
    out[block * count : block * count + fits] = moved[:fits].astype(out.dtype)
    return wide(low[count - BLOCK :])[BLOCK - 1 :]


def block_rows(ref, block):
    return wide(flat(ref[:, block * BLOCK : (block + 1) * BLOCK, :]))


VECTORS = 16


SOURCE_GROUPS = ((0, 1), (1, 4), (4, 8), (8, BLOCKS))


def source_kernel(own_far, other_far, x_far, dgrid_far, dsource, gain, *rest):
    given = rest[:-7]
    out, packed, own, other, x, dgrid, semaphores = rest[-7:]
    width = packed.shape[1]
    coming = fetch_places(
        Copies(semaphores), (own_far, other_far, x_far, dgrid_far), (own, other, x, dgrid), SOURCE_GROUPS
    )
    carry = dsource[...]
    d_gain = jnp.zeros((1, width), jnp.float32)
    d_shift = jnp.zeros((1, width), jnp.float32)
    for (first, last), arrivals in zip(SOURCE_GROUPS, coming):
        for arrival in arrivals:
            arrival.wait()
        for block in range(first, last):
            d_norm = block_rows(own, block) + block_rows(other, block)
            unit, inverse = normed(block_rows(x, block))
            d_gain = d_gain + column_sum(d_norm * unit)
            d_shift = d_shift + column_sum(d_norm)
            rows = block_rows(dgrid, block) + normed_back(unit, inverse, d_norm * vector(gain))
            carry = put_tokens(out, block, rows.astype(LOW), carry)
    packed[...] = jnp.zeros(packed.shape, jnp.float32)
    packed[0:1] = d_gain
    packed[1:2] = d_shift
    at = 2
    for ref in given:
        count = ref.shape[1]
        if count == 3 * width // 2:
            packed[at : at + 1] = jnp.concatenate([ref[:, : width // 2], ref[:, width:]], axis=1)
            at += 1
            continue
        for start in range(0, count, width):
            packed[at : at + 1] = ref[:, start : start + width]
            at += 1


def source_gradient(own, other, x, dgrid, dsource, gain, given, tokens):
    width = x.shape[2]
    args = (own, other, x, dgrid, dsource, gain) + tuple(given)
    outs = [shape((tokens, width)), shape((VECTORS, width), jnp.float32)]
    near, far = near_far(args[:4])
    return call(
        source_kernel,
        (1,),
        [far] * 4 + [whole(a) for a in args[4:]],
        [whole(o) for o in outs],
        outs,
        near + [pltpu.SemaphoreType.DMA((4 * len(SOURCE_GROUPS),))],
        2 * FRAMES * ROWS * 128 * width,
        args,
    )


RESULT_GROUPS = ((BLOCKS - 1, BLOCKS), (0, 4), (4, 8), (8, BLOCKS - 1))


def result_kernel(own_far, other_far, mid_far, bias, live, out, own, other, mid, semaphores):
    present = live[0, 0]
    coming = fetch_places(Copies(semaphores), (own_far, other_far, mid_far), (own, other, mid), RESULT_GROUPS)

    def rows_of(block):
        total = block_rows(mid, block) + block_rows(own, block) + block_rows(other, block) + vector(bias)
        return (total * present).astype(LOW)

    for arrival in coming[0]:
        arrival.wait()
    last = rows_of(BLOCKS - 1)
    carry = wide(last[:BLOCK])[CLASS_AT : CLASS_AT + 1]
    for (first, end), arrivals in zip(RESULT_GROUPS[1:], coming[1:]):
        for arrival in arrivals:
            arrival.wait()
        for block in range(first, end):
            carry = put_tokens(out, block, rows_of(block), carry)
    put_tokens(out, BLOCKS - 1, last, carry)


def result_tokens(own, other, mid, bias, live, tokens):
    width = mid.shape[2]
    args = (own, other, mid, bias, live)
    outs = [shape((tokens, width))]
    near, far = near_far(args[:3])
    return call(
        result_kernel,
        (1,),
        [far] * 3 + [whole(bias), SCALAR],
        [whole(outs[0])],
        outs,
        near + [pltpu.SemaphoreType.DMA((3 * len(RESULT_GROUPS),))],
        2 * FRAMES * ROWS * 128 * width,
        args,
    )[0]


def settle_vectors(at, total, outs):
    width = total.shape[1]
    share = outs[0].shape[0]
    dests = width // share
    moved = pltpu.roll(total, (dests - at) % dests * share, 1)
    for row in range(10):
        outs[row][...] = moved[row, :share]
    small = share // 2
    moved = pltpu.roll(total, (2 * dests - at) % (2 * dests) * small, 1)
    for row in (10, 11):
        for part in range(2):
            start = part * (width // 2)
            outs[row][part : part + 1, :] = moved[row : row + 1, start : start + small]
    moved = pltpu.roll(total, (dests - 2 * at % dests) % dests * share, 1)
    outs[12][...] = jnp.where(2 * at < dests, moved[12, : 2 * share], moved[13, : 2 * share])


def small_shapes(share):
    outs = [shape((share,), jnp.float32)] * 10
    outs += [shape((2, share // 2), jnp.float32)] * 2
    return outs + [shape((2 * share,), jnp.float32)]


def settle_kernel(place, total, *outs):
    settle_vectors(place[0, 0], total[...], outs)


def settle(total, place, dests):
    outs = small_shapes(total.shape[1] // dests)
    return call(settle_kernel, (1,), [SCALAR, whole(total)], [whole(o) for o in outs], outs, [], 0, (place, total))


UNIT = 128


def bits_of(me):
    place = me[0, 0]
    return {"x": place % 2, "y": place // 2 % 2, "near": place // 4 % 2, "far": place // 8}


def pair_index(at, bit):
    return 2 * at + bit


def gap_index(at, bit):
    return at // 2 * 4 + 2 * bit + at % 2


def near_index(at, bit):
    return at // 4 * 8 + 4 * bit + at % 4


def top_index(half):
    return lambda at, bit: half * bit + at


def units_of(field):
    return [slice(at, at + UNIT) for at in range(0, field.shape[-1], UNIT)]


def split_gradient(field, axis, bits, message, start, keep):
    index = {"x": pair_index, "y": gap_index, "near": near_index}[axis]
    cols = units_of(field)
    for at in range(8):
        for unit, col in enumerate(cols):
            message[start + at * len(cols) + unit] = field[index(at, 1 - bits[axis]), :, col]
            keep[at, unit] = field[index(at, bits[axis]), :, col]


def split_total(held, got, got_start, bit, message, start, keep, index=pair_index):
    units = held.shape[1]

    def total(at):
        return (wide(held[at]) + wide(got[pl.ds(got_start + at * units, units)])).astype(LOW)

    for at in range(held.shape[0] // 2):
        message[start + at * units : start + (at + 1) * units] = total(index(at, 1 - bit))
        keep[at] = total(index(at, bit))


def put_gradient(field, left, right, start=0):
    step = 768 if right.shape[1] % 768 == 0 else 384
    for at in range(0, right.shape[1], step):
        part = lax.dot_general(
            left, right[:, at : at + step], (((0,), (0,)), ((), ())), preferred_element_type=jnp.float32
        )
        field[:, :, start + at : start + at + step] = part.astype(LOW).reshape(field.shape[:2] + (step,))


def gradient_call(body, args, outs, scratch, flops):
    inputs, width = args[1:], len(args) - 1

    def kernel(me, *refs):
        far, near = refs[: width + len(outs)], refs[width + len(outs) : 2 * (width + len(outs))]
        copies = Copies(refs[-1])
        waiting = [copies.start(source, target) for source, target in zip(far[:width], near[:width])]
        sent = []

        def need(*wanted):
            for ref in wanted:
                waiting[[ref is one for one in near].index(True)].wait()

        def done(*made):
            for ref in made:
                sent.append(copies.start(ref, far[[ref is one for one in near].index(True)]))

        body(need, done, me, *near, *refs[2 * (width + len(outs)) : -1])
        for copy in sent:
            copy.wait()

    remote = pl.BlockSpec(memory_space=pl.ANY)
    return call(
        kernel,
        (1,),
        [SCALAR] + [remote] * width,
        [remote] * len(outs),
        outs,
        [pltpu.VMEM(a.shape, a.dtype) for a in list(inputs) + outs]
        + scratch
        + [pltpu.SemaphoreType.DMA((width + len(outs),))],
        flops,
        args,
    )


def plain_call(kernel, args, outs):
    return call(
        kernel,
        (1,),
        [SCALAR] + [whole(a) for a in args[1:]],
        [whole(o) for o in outs],
        outs,
        [],
        0,
        args,
    )


LINE_UNITS = 4


def feed_gradient_kernel(
    need, done, me, norm, d_pre, cot, act,
    message_x, message_y, message_near, keep_up, keep_down, keep_line_up, keep_line_down, up, down,
):
    bits = bits_of(me)
    cut = keep_up.shape[1] * UNIT
    need(norm, d_pre)
    put_gradient(up, flat(norm[...]), flat(d_pre[...]))
    need(cot, act)
    put_gradient(down, flat(cot[...]), flat(act[...]))
    split_gradient(up.at[:, :, :cut], "x", bits, message_x, 0, keep_up)
    split_gradient(up.at[:, :, cut:], "near", bits, message_near, 0, keep_line_up)
    done(message_x, keep_up, keep_line_up)
    split_gradient(down.at[:, :, :cut], "y", bits, message_y, 0, keep_down)
    split_gradient(down.at[:, :, cut:], "near", bits, message_near, 8 * LINE_UNITS, keep_line_down)
    done(message_y, message_near, keep_down, keep_line_down)


def field_shape(dests, units, share):
    return shape((dests, units, share, UNIT))


def message_shape(blocks, share):
    return shape((blocks, share, UNIT))


def feed_gradient(me, norm, d_pre, cot, act):
    width = norm.shape[2]
    units = act.shape[2] // UNIT - LINE_UNITS
    share = width // 16
    outs = [message_shape(8 * units, share)] * 2 + [message_shape(16 * LINE_UNITS, share)]
    outs += [field_shape(8, units, share)] * 2 + [field_shape(8, LINE_UNITS, share)] * 2
    scratch = [pltpu.VMEM((16, share, act.shape[2]), LOW)] * 2
    return gradient_call(
        feed_gradient_kernel, (me, norm, d_pre, cot, act), outs, scratch, 4 * FRAMES * ROWS * width * act.shape[2]
    )


def space_gradient_kernel(
    need, done, me, norm, backs, d_space, mixed, up, got_x, down, got_y, line_up, line_down, got_near,
    message_x, message_y, message_far, keep_up, keep_down, keep_line_up, keep_line_down, keep_first, keep_second,
    first, second,
):
    bits = bits_of(me)
    count = 4 * up.shape[1]
    width = first.shape[2]
    need(norm, backs)
    rows = flat(norm[...])
    put_gradient(first, rows, flat(backs[...])[:, :width])
    put_gradient(second, rows, flat(backs[...])[:, width:])
    need(d_space, mixed)
    put_gradient(second, flat(d_space[...]), flat(mixed[...]), backs.shape[2] - width)
    need(up, got_x)
    split_total(up, got_x, 0, bits["y"], message_y, 0, keep_up)
    done(keep_up)
    split_gradient(first, "y", bits, message_y, count, keep_first)
    done(message_y, keep_first)
    need(down, got_y)
    split_total(down, got_y, 0, bits["x"], message_x, 0, keep_down)
    split_gradient(second, "x", bits, message_x, count, keep_second)
    done(message_x, keep_down, keep_second)
    need(line_up, line_down, got_near)
    split_total(line_up, got_near, 0, bits["far"], message_far, 0, keep_line_up, top_index(4))
    split_total(
        line_down, got_near, 8 * LINE_UNITS, bits["far"], message_far, 4 * LINE_UNITS, keep_line_down, top_index(4)
    )
    done(message_far, keep_line_up, keep_line_down)


def space_gradient(me, norm, backs, d_space, mixed, up, down, line_up, line_down, got_x, got_y, got_near):
    width = norm.shape[2]
    half = mixed.shape[2]
    share = width // 16
    units = up.shape[1]
    own = 2 * half // UNIT
    outs = [message_shape(4 * units + 8 * own, share)] * 2 + [message_shape(8 * LINE_UNITS, share)]
    outs += [field_shape(4, units, share)] * 2 + [field_shape(4, LINE_UNITS, share)] * 2
    outs += [field_shape(8, own, share)] * 2
    scratch = [pltpu.VMEM((16, share, 2 * half), LOW)] * 2
    return gradient_call(
        space_gradient_kernel,
        (me, norm, backs, d_space, mixed, up, got_x, down, got_y, line_up, line_down, got_near),
        outs,
        scratch,
        8 * FRAMES * ROWS * width * half,
    )


def mixer_gradient_kernel(
    need, done, me, d_mixer, mixed, d_grid, mixer_in, up, got_y, down, got_x, space_first, space_second,
    line_up, line_down, got_far,
    message_x, message_y, message_near, keep_up, keep_down, keep_line_up, keep_line_down, keep_first, keep_second,
    keep_out, keep_mixer, out, mixer,
):
    bits = bits_of(me)
    units = up.shape[1]
    feed = 4 * units
    own = space_first.shape[1]
    need(d_mixer, mixed)
    put_gradient(out, flat(d_mixer[...]), flat(mixed[...]))
    need(d_grid, mixer_in)
    put_gradient(mixer, flat(d_grid[...]), flat(mixer_in[...]))
    need(up, got_y)
    split_total(up, got_y, 0, bits["near"], message_near, 0, keep_up)
    need(down, got_x)
    split_total(down, got_x, 0, bits["near"], message_near, 2 * units, keep_down)
    done(message_near, keep_up, keep_down)
    need(space_first, space_second)
    split_total(space_first, got_y, feed, bits["x"], message_x, 0, keep_first)
    split_total(space_second, got_x, feed, bits["y"], message_y, 0, keep_second)
    split_gradient(out, "x", bits, message_x, 4 * own, keep_out)
    split_gradient(mixer, "y", bits, message_y, 4 * own, keep_mixer)
    need(line_up, line_down, got_far)
    line = 4 * own + 8 * keep_out.shape[1]
    split_total(line_up, got_far, 0, bits["x"], message_x, line, keep_line_up)
    split_total(line_down, got_far, 4 * LINE_UNITS, bits["y"], message_y, line, keep_line_down, top_index(2))
    done(message_x, message_y, keep_line_up, keep_line_down, keep_first, keep_second, keep_out, keep_mixer)


def mixer_gradient(
    me, d_mixer, mixed, d_grid, mixer_in, up, down, line_up, line_down, space_first, space_second, got_x, got_y, got_far
):
    width = d_grid.shape[2]
    half = mixed.shape[2]
    share = width // 16
    units, own, new = up.shape[1], space_first.shape[1], half // UNIT
    outs = [message_shape(4 * own + 8 * new + 2 * LINE_UNITS, share)] * 2 + [message_shape(4 * units, share)]
    outs += [field_shape(2, units, share)] * 2 + [field_shape(2, LINE_UNITS, share)] * 2
    outs += [field_shape(4, own, share)] * 2 + [field_shape(8, new, share)] * 2
    scratch = [pltpu.VMEM((16, share, half), LOW)] * 2
    return gradient_call(
        mixer_gradient_kernel,
        (
            me, d_mixer, mixed, d_grid, mixer_in, up, got_y, down, got_x, space_first, space_second,
            line_up, line_down, got_far,
        ),
        outs,
        scratch,
        4 * FRAMES * ROWS * width * half,
    )


TIME_FIRST = 5


def time_gradient_kernel(
    need, done, me, norm, backs, out, got_x, mixer, got_y, line_up, line_down, space_first, space_second,
    up, down, got_near,
    message_x, message_y, message_near, message_far, keep_up, keep_down, keep_line_up, keep_line_down,
    keep_space_first, keep_space_second, keep_out, keep_mixer, keep_first, keep_second, both,
):
    bits = bits_of(me)
    units, own, new = up.shape[1], space_first.shape[1], out.shape[1]
    need(norm, backs)
    put_gradient(both, flat(norm[...]), flat(backs[...]))
    need(out, got_x)
    split_total(out, got_x, 4 * own, bits["y"], message_y, 0, keep_out)
    need(mixer, got_y)
    split_total(mixer, got_y, 4 * own, bits["x"], message_x, 0, keep_mixer)
    cut = TIME_FIRST * UNIT
    split_gradient(both.at[:, :, :cut], "y", bits, message_y, 4 * new, keep_first)
    split_gradient(both.at[:, :, cut:], "x", bits, message_x, 4 * new, keep_second)
    need(line_up, line_down)
    line = 4 * own + 8 * new
    split_total(line_up, got_x, line, bits["y"], message_y, message_y.shape[0] - LINE_UNITS, keep_line_up)
    split_total(line_down, got_y, line, bits["x"], message_x, message_x.shape[0] - LINE_UNITS, keep_line_down)
    done(message_y, message_x, keep_line_up, keep_line_down, keep_first, keep_second, keep_out, keep_mixer)
    need(space_first, space_second)
    split_total(space_first, got_x, 0, bits["near"], message_near, 0, keep_space_first)
    split_total(space_second, got_y, 0, bits["near"], message_near, 2 * own, keep_space_second)
    done(message_near, keep_space_first, keep_space_second)
    need(up, down, got_near)
    split_total(up, got_near, 0, bits["far"], message_far, 0, keep_up)
    split_total(down, got_near, 2 * units, bits["far"], message_far, units, keep_down)
    done(message_far, keep_up, keep_down)


def time_gradient(
    me, norm, backs, up, down, line_up, line_down, space_first, space_second, out, mixer, got_x, got_y, got_near
):
    width = norm.shape[2]
    share = width // 16
    units, own, new = up.shape[1], space_first.shape[1], out.shape[1]
    last = backs.shape[2] // UNIT - TIME_FIRST
    outs = [
        message_shape(4 * new + 8 * last + LINE_UNITS, share),
        message_shape(4 * new + 8 * TIME_FIRST + LINE_UNITS, share),
        message_shape(4 * own, share),
        message_shape(2 * units, share),
    ]
    outs += [field_shape(1, units, share)] * 2 + [field_shape(1, LINE_UNITS, share)] * 2
    outs += [field_shape(2, own, share)] * 2 + [field_shape(4, new, share)] * 2
    outs += [field_shape(8, TIME_FIRST, share), field_shape(8, last, share)]
    return gradient_call(
        time_gradient_kernel,
        (
            me, norm, backs, out, got_x, mixer, got_y, line_up, line_down, space_first, space_second,
            up, down, got_near,
        ),
        outs,
        [pltpu.VMEM((16, share, backs.shape[2]), LOW)],
        2 * FRAMES * ROWS * width * backs.shape[2],
    )


def vector_blocks(vectors, share):
    parts = [vectors[:, col].astype(LOW) for col in units_of(vectors)]
    each = share // VECTORS
    return [jnp.concatenate(parts[at : at + each], axis=0) for at in range(0, len(parts), each)]


def second_kernel(
    me, vectors, space_first, space_second, out, mixer, first, second, line_up, line_down, got_x, got_y, got_near,
    message_x, message_y, message_xy, message_far,
    keep_space_first, keep_space_second, sum_out, sum_mixer, keep_first, keep_second, sum_line_up, sum_line_down,
):
    bits = bits_of(me)
    own, new = space_first.shape[1], out.shape[1]
    share = first.shape[2]
    split_total(first, got_y, 4 * new, bits["x"], message_x, 0, keep_first)
    split_total(second, got_x, 4 * new, bits["y"], message_y, 0, keep_second)
    for at, block in enumerate(vector_blocks(vectors[...], share)):
        message_x[4 * first.shape[1] + at] = block
        message_y[4 * second.shape[1] + at] = block
        message_xy[at] = block
    split_total(space_first, got_near, 0, bits["far"], message_far, 0, keep_space_first)
    split_total(space_second, got_near, 2 * own, bits["far"], message_far, own, keep_space_second)
    for ref, got, total in ((line_up, got_y, sum_line_up), (line_down, got_x, sum_line_down)):
        total[0] = (wide(ref[0]) + wide(got[got.shape[0] - LINE_UNITS :])).astype(LOW)
    for ref, got, total in ((out, got_y, sum_out), (mixer, got_x, sum_mixer)):
        for at in range(4):
            total[at] = (wide(ref[at]) + wide(got[at * new : (at + 1) * new])).astype(LOW)


def second_step(
    me, vectors, space_first, space_second, out, mixer, first, second, line_up, line_down, got_x, got_y, got_near
):
    own, new, share = space_first.shape[1], out.shape[1], first.shape[2]
    extra = vectors.size // (share * UNIT)
    outs = [
        message_shape(4 * first.shape[1] + extra, share),
        message_shape(4 * second.shape[1] + extra, share),
        message_shape(extra, share),
        message_shape(2 * own, share),
    ]
    outs += [field_shape(1, own, share)] * 2 + [field_shape(4, new, share)] * 2
    outs += [field_shape(4, first.shape[1], share), field_shape(4, second.shape[1], share)]
    outs += [field_shape(1, LINE_UNITS, share)] * 2
    return plain_call(
        second_kernel,
        (me, vectors, space_first, space_second, out, mixer, first, second, line_up, line_down, got_x, got_y, got_near),
        outs,
    )


def line_kernel(me, vectors, out, mixer, first, second, got_x, got_y, got_xy, message_1, message_2, message_3, own):
    bits = bits_of(me)
    share = first.shape[2]
    place = 2 * bits["far"] + bits["near"]
    messages = (own, message_1, message_2, message_3)
    start = 0
    for held, got in ((first, got_x), (second, got_y), (out, None), (mixer, None)):
        units = held.shape[1]
        for step, message in enumerate(messages):
            dest = place + step - 2 * (place & step)
            total = held[dest]
            if got is not None:
                total = (wide(total) + wide(got[pl.ds(dest * units, units)])).astype(LOW)
            message[start : start + units] = total
        start += units
    firsts, seconds = 4 * first.shape[1], 4 * second.shape[1]
    for at, block in enumerate(vector_blocks(vectors[...], share)):
        total = (wide(block) + wide(got_xy[at])) + (wide(got_x[firsts + at]) + wide(got_y[seconds + at]))
        for message in messages:
            message[start + at] = total.astype(LOW)


def line_step(me, vectors, out, mixer, first, second, got_x, got_y, got_xy):
    share = first.shape[2]
    blocks = first.shape[1] + second.shape[1] + out.shape[1] + mixer.shape[1] + vectors.size // (share * UNIT)
    return plain_call(
        line_kernel,
        (me, vectors, out, mixer, first, second, got_x, got_y, got_xy),
        [message_shape(blocks, share)] * 4,
    )


def final_kernel(
    me, own, got_1, got_2, got_3, up, down, got_feed, line_up, line_down, space_first, space_second, got_space,
    time_in, time_out, time_mixer, space_in, space_out, feed_up, feed_down, *small,
):
    units = up.shape[1]
    for unit, col in enumerate(units_of(feed_up)):
        if unit < units:
            feed_up[:, col] = wide(up[0, unit]) + wide(got_feed[unit])
            feed_down[:, col] = wide(down[0, unit]) + wide(got_feed[units + unit])
        else:
            feed_up[:, col] = wide(line_up[0, unit - units])
            feed_down[:, col] = wide(line_down[0, unit - units])
    mine = space_first.shape[1]
    half = space_out.shape[1]
    each = half // UNIT
    for unit in range(2 * mine):
        held = space_first[0, unit] if unit < mine else space_second[0, unit - mine]
        total = wide(held) + wide(got_space[unit])
        at = unit % each * UNIT
        if unit < 3 * each:
            space_in[unit // each, :, at : at + UNIT] = total
        else:
            space_out[:, at : at + UNIT] = total

    def line_total(at):
        return (wide(own[at]) + wide(got_1[at])) + (wide(got_2[at]) + wide(got_3[at]))

    for unit in range(5 * each):
        total = line_total(unit)
        at = unit % each * UNIT
        if unit < 3 * each:
            time_in[unit // each, :, at : at + UNIT] = total
        elif unit < 4 * each:
            time_out[:, at : at + UNIT] = total
        else:
            time_mixer[:, at : at + UNIT] = total
    share = feed_up.shape[0]
    parts = []
    for block in range(5 * each, own.shape[0]):
        total = line_total(block)
        parts += [total[at : at + VECTORS] for at in range(0, share, VECTORS)]
    settle_vectors(me[0, 0], jnp.concatenate(parts, axis=1), small)


def final_step(
    me, own, got_1, got_2, got_3, up, down, got_feed, line_up, line_down, space_first, space_second, got_space,
    width, half,
):
    share = width // 16
    units = (up.shape[1] + LINE_UNITS) * UNIT
    outs = [
        shape(dims, jnp.float32)
        for dims in (
            (3, share, half), (share, half), (share, half), (3, share, half), (share, half), (share, units),
            (share, units),
        )
    ]
    return plain_call(
        final_kernel,
        (
            me, own, got_1, got_2, got_3, up, down, got_feed, line_up, line_down, space_first, space_second,
            got_space,
        ),
        outs + small_shapes(share),
    )


def swap_tensor(field):
    size = lax.axis_size("tensor")
    return lax.ppermute(field, "tensor", [(i, i ^ 1) for i in range(size)])


def swap_dp(field, bits):
    return lax.ppermute(field, "dp", [(i, i ^ bits) for i in range(lax.axis_size("dp"))])


def pick(field, at):
    return lax.dynamic_index_in_dim(field, at, 0, keepdims=False)


def reduce_rows(field):
    size = lax.axis_size("dp")
    me = lax.axis_index("dp")
    span = size // 2
    while span >= 1:
        field = field.reshape((2, span, -1) + field.shape[-1:])
        bit = me // span % 2
        field = (wide(pick(field, bit)) + wide(swap_dp(pick(field, 1 - bit), span))).astype(LOW)
        span //= 2
    return wide(field.reshape(-1, field.shape[-1]))


def dp_sum(field):
    span = 1
    while span < lax.axis_size("dp"):
        field = field + swap_dp(field, span)
        span *= 2
    return field


def in_order(first, then):
    return lax.optimization_barrier((first, then))


def grad_of(left, right):
    return lax.dot_general(
        left.reshape(-1, left.shape[2]),
        right.reshape(-1, right.shape[2]),
        (((0,), (0,)), ((), ())),
        preferred_element_type=jnp.float32,
    ).astype(LOW)


def local(
    clips,
    cotangent,
    live,
    time_gain,
    time_shift,
    time_inproj,
    time_inbias,
    time_outproj,
    time_outbias,
    time_mixer,
    time_mixbias,
    space_gain,
    space_shift,
    space_inproj,
    space_inbias,
    space_outproj,
    space_outbias,
    feed_gain,
    feed_shift,
    feed_upward,
    feed_upbias,
    feed_down,
    feed_downbias,
):
    tokens, width = clips.shape[1:]
    half = time_outproj.shape[0]
    dests = lax.axis_size("dp")
    tensor_rank = lax.axis_index("tensor")
    paired = dests == 16
    me = lax.axis_index("dp").astype(jnp.int32).reshape(1, 1)
    present = live.astype(jnp.float32).reshape(1, 1)
    time_in = jnp.transpose(time_inproj, (1, 0, 2))
    space_in = jnp.transpose(space_inproj, (1, 0, 2))
    mixers = (time_mixer, swap_tensor(time_mixer), tensor_rank.astype(jnp.int32).reshape(1, 1))
    x, t_norm, t_qkv, t_probs, t_mixed, t_part = time_forward(
        clips[0], time_gain, time_shift, time_in, time_inbias, time_outproj
    )
    cot, g_downbias = cotangent_frames(cotangent[0], present)
    mixer_in, after_time, s_norm, s_qkv, s_probs, s_mixed, s_part = space_forward(
        t_part, swap_tensor(t_part), x, time_outbias, mixers, time_mixbias, space_gain, space_shift, space_in,
        space_inbias, space_outproj,
    )
    mid, f_norm, act, d_pre, f_part, df_part, g_upbias = feed(
        s_part, swap_tensor(s_part), after_time, cot, space_outbias, feed_gain, feed_shift, feed_upward, feed_upbias,
        feed_down,
    )
    if paired:
        feed_x, feed_y, feed_near, up, down, l_up, l_down = feed_gradient(me, f_norm, d_pre, cot, act)
        feed_x, mid = in_order(feed_x, mid)
        feed_x, feed_y, feed_near = swap_dp(feed_x, 1), swap_dp(feed_y, 2), swap_dp(feed_near, 4)
    d_space, s_back, ds_part, d_class, g_feed_gain, g_feed_shift, g_space_outbias, g_space_inbias = space_backward(
        df_part, swap_tensor(df_part), mid, cot, s_qkv, s_probs, feed_gain, space_outproj, space_in
    )
    if paired:
        ds_part, feed_x, feed_y, feed_near = lax.optimization_barrier((ds_part, feed_x, feed_y, feed_near))
        space_x, space_y, line_far, up, down, l_up, l_down, s_first, s_second = space_gradient(
            me, s_norm, s_back, d_space, s_mixed, up, down, l_up, l_down, feed_x, feed_y, feed_near
        )
        space_x, d_class = in_order(space_x, d_class)
        space_x, space_y, line_far = swap_dp(space_x, 1), swap_dp(space_y, 2), swap_dp(line_far, 8)
    result = result_tokens(f_part, swap_tensor(f_part), mid, feed_downbias, present, tokens)
    result, d_class = in_order(result, d_class)
    d_grid, d_mixer, d_mixed, d_source, g_space_gain, g_space_shift, g_mixbias, g_outbias = mixer_backward(
        ds_part, swap_tensor(ds_part), after_time, d_space, d_class, space_gain, mixers, time_outproj
    )
    if paired:
        mixer_x, mixer_y, feed_near, up, down, l_up, l_down, s_first, s_second, t_out, t_mixer = mixer_gradient(
            me, d_mixer, t_mixed, d_grid, mixer_in, up, down, l_up, l_down, s_first, s_second, space_x, space_y,
            line_far,
        )
        mixer_x, d_mixed = in_order(mixer_x, d_mixed)
        mixer_x, mixer_y, feed_near = swap_dp(mixer_x, 1), swap_dp(mixer_y, 2), swap_dp(feed_near, 4)
    t_back, dt_part, g_time_inbias = time_backward(d_mixed, t_qkv, t_probs, time_in)
    if paired:
        dt_part, mixer_x, mixer_y, feed_near = lax.optimization_barrier((dt_part, mixer_x, mixer_y, feed_near))
        time_x, time_y, space_near, feed_far, up, down, l_up, l_down, s_first, s_second, *t_held = time_gradient(
            me, t_norm, t_back, up, down, l_up, l_down, s_first, s_second, t_out, t_mixer, mixer_x, mixer_y, feed_near
        )
        time_x, d_source = in_order(time_x, d_source)
        time_x, time_y = swap_dp(time_x, 1), swap_dp(time_y, 2)
        space_near, feed_far = swap_dp(space_near, 4), swap_dp(feed_far, 8)
    grad_clips, vectors = source_gradient(
        dt_part, swap_tensor(dt_part), x, d_grid, d_source, time_gain,
        (
            g_outbias, g_mixbias, g_space_gain, g_space_shift, g_space_outbias, g_feed_gain, g_feed_shift, g_downbias,
            g_time_inbias, g_space_inbias, g_upbias,
        ),
        tokens,
    )
    if paired:
        feed_far, space_near, vectors = lax.optimization_barrier((feed_far, space_near, vectors))
        last_x, last_y, last_xy, space_far, s_first, s_second, *t_held, l_up, l_down = second_step(
            me, vectors, s_first, s_second, *t_held, l_up, l_down, time_x, time_y, space_near
        )
        last_x, last_y, last_xy = swap_dp(last_x, 1), swap_dp(last_y, 2), swap_dp(last_xy, 3)
        space_far = swap_dp(space_far, 8)
        space_far, last_xy = lax.optimization_barrier((space_far, last_xy))
        line_1, line_2, line_3, line_own = line_step(
            me, vectors, *t_held, last_x, last_y, last_xy
        )
        line_1, line_2, line_3 = swap_dp(line_1, 4), swap_dp(line_2, 8), swap_dp(line_3, 12)
        time_sum, out_sum, mixer_sum, space_sum, space_out, up_sum, down_sum, *small = final_step(
            me, line_own, line_1, line_2, line_3, up, down, feed_far, l_up, l_down, s_first, s_second, space_far,
            width, half,
        )
    else:

        def parts(field):
            return jnp.stack([field[:, part * half : (part + 1) * half] for part in range(3)])

        up_sum = reduce_rows(grad_of(f_norm, d_pre))
        down_sum = reduce_rows(grad_of(cot, act))
        space_sum = parts(reduce_rows(grad_of(s_norm, s_back)))
        space_out = reduce_rows(grad_of(d_space, s_mixed))
        time_sum = parts(reduce_rows(grad_of(t_norm, t_back)))
        out_sum = reduce_rows(grad_of(d_mixer, t_mixed))
        mixer_sum = reduce_rows(grad_of(d_grid, mixer_in))
        small = settle(dp_sum(vectors), me, dests)
    settled = (
        small[0],
        small[1],
        jnp.transpose(time_sum, (1, 0, 2)),
        small[10],
        out_sum.T,
        small[2],
        mixer_sum.T,
        small[3],
        small[4],
        small[5],
        jnp.transpose(space_sum, (1, 0, 2)),
        small[11],
        space_out.T,
        small[6],
        small[7],
        small[8],
        up_sum,
        small[12],
        down_sum.T,
        small[9],
    )
    return (result[None], grad_clips[None]) + settled


def solution(mesh):
    in_specs = (
        P("dp", None, None),
        P("dp", None, None),
        P("dp"),
        P(),
        P(),
        P(None, None, "tensor"),
        P(None, "tensor"),
        P("tensor", None),
        P(),
        P("tensor", None),
        P(),
        P(),
        P(),
        P(None, None, "tensor"),
        P(None, "tensor"),
        P("tensor", None),
        P(),
        P(),
        P(),
        P(None, "tensor"),
        P("tensor"),
        P("tensor", None),
        P(),
    )
    out_specs = (
        P("dp", None, None),
        P("dp", None, None),
        P("dp"),
        P("dp"),
        P("dp", None, "tensor"),
        P(None, ("tensor", "dp")),
        P("tensor", "dp"),
        P("dp"),
        P("tensor", "dp"),
        P("dp"),
        P("dp"),
        P("dp"),
        P("dp", None, "tensor"),
        P(None, ("tensor", "dp")),
        P("tensor", "dp"),
        P("dp"),
        P("dp"),
        P("dp"),
        P("dp", "tensor"),
        P(("tensor", "dp")),
        P("tensor", "dp"),
        P("dp"),
    )
    return jax.shard_map(local, mesh=mesh, in_specs=in_specs, out_specs=out_specs, check_vma=False)
```

```python
import functools

import jax
import jax.numpy as jnp
from jax import lax
from jax.experimental import pallas as pl
from jax.experimental.pallas import tpu as pltpu
from jax.sharding import PartitionSpec as P

HEAD = 64
FRAMES = 8
PLACES = 196
BLOCK = 16
ROWS = 208
BLOCKS = ROWS // BLOCK
PAIR = 2
UNROLL = BLOCKS
TIME_GROUP = 13
TIME_LAG = 1
SPACE_LAG = 6
EPS = 1e-06
LOW = jnp.bfloat16
VMEM_BYTES = 62 * 1024 * 1024
COST = 1


def dot(left, right):
    return jnp.dot(left, right, preferred_element_type=jnp.float32)


def dot_last(left, right):
    return lax.dot_general(left, right, (((1,), (1,)), ((), ())), preferred_element_type=jnp.float32)


def normed(field):
    center = field - jnp.mean(field, axis=-1, keepdims=True)
    spread_sq = jnp.mean(center * center, axis=-1, keepdims=True)
    inverse = lax.rsqrt(spread_sq + EPS)
    return center * inverse, inverse


def normed_back(unit, inverse, grad_unit):
    first = jnp.mean(grad_unit, axis=-1, keepdims=True)
    second = jnp.mean(grad_unit * unit, axis=-1, keepdims=True)
    return (grad_unit - first - unit * second) * inverse


def side_by_side(weights):
    return jnp.concatenate([weights[part] for part in range(weights.shape[0])], axis=1)


def flat(field):
    return field.reshape((field.shape[0] * field.shape[1],) + field.shape[2:])


def wide(field):
    return field.astype(jnp.float32)


def iota(shape, axis):
    return lax.broadcasted_iota(jnp.int32, shape, axis)


def column_sum(field):
    return jnp.sum(field, axis=0, keepdims=True)


def call(kernel, grid, in_specs, out_specs, out_shapes, scratch, flops, args):
    moved = sum(a.size * a.dtype.itemsize for a in args) + sum(o.size * o.dtype.itemsize for o in out_shapes)
    return pl.pallas_call(
        kernel,
        grid=grid,
        in_specs=in_specs,
        out_specs=out_specs,
        out_shape=out_shapes,
        scratch_shapes=scratch,
        compiler_params=pltpu.CompilerParams(vmem_limit_bytes=VMEM_BYTES),
        cost_estimate=pl.CostEstimate(flops=int(flops) // COST, bytes_accessed=int(moved) // COST, transcendentals=0),
    )(*args)


SCALAR = pl.BlockSpec(memory_space=pltpu.SMEM)


def whole(array):
    zeros = (0,) * array.ndim
    return pl.BlockSpec(array.shape, lambda *at: zeros)


def shape(dims, kind=LOW):
    return jax.ShapeDtypeStruct(dims, kind)


def to_frames(rows, block):
    count = FRAMES * BLOCK
    at = iota((count, count + BLOCK), 0)
    source = 1 + FRAMES * (at % BLOCK) + at // BLOCK
    pick = jnp.where(source == iota((count, count + BLOCK), 1), 1.0, 0.0).astype(LOW)
    return dot(pick, rows)


def to_tokens(rows):
    count = FRAMES * BLOCK
    at = iota((count, count), 1)
    target = 1 + FRAMES * (at % BLOCK) + at // BLOCK
    pick = jnp.where(target == iota((count, count), 0), 1.0, 0.0).astype(LOW)
    return dot(pick, rows)


def fill_rows(source, tokens):
    count = tokens.shape[0]
    even = count // BLOCK * BLOCK
    source[0:even] = tokens[0:even]
    source[even:] = jnp.zeros((source.shape[0] - even, source.shape[1]), source.dtype)
    left = wide(tokens[even:count])
    tail = jnp.zeros((BLOCK, source.shape[1]), jnp.float32)
    for row in range(count - even):
        tail = tail + jnp.where(iota(tail.shape, 0) == row, left[row : row + 1], 0.0)
    source[even : even + BLOCK] = tail.astype(source.dtype)


def frame_rows(source, block, class_row, class_frames):
    count = FRAMES * BLOCK
    rows = to_frames(source[pl.ds(pl.multiple_of(block * count, count), count + BLOCK), :], block)
    at = iota((count, 1), 0)
    is_class = (block * BLOCK + at % BLOCK == PLACES) & (at // BLOCK < class_frames)
    return rows + jnp.where(is_class, class_row, 0.0)


class Copies:
    def __init__(self, semaphores):
        self.semaphores = semaphores
        self.started = []

    def start(self, source, target):
        copy = pltpu.make_async_copy(source, target, self.semaphores.at[len(self.started)])
        copy.start()
        self.started.append(copy)
        return copy


def time_forward_kernel(
    clips, gain, shift, inproj_far, inbias, outproj_far, x_far, norm_far, qkv_far, probs_far, mixed_far, part_far,
    inproj, outproj, x_out, norm_out, qkv_out, probs_out, mixed_out, part_out, source, semaphores,
):
    half = outproj.shape[0]
    copies = Copies(semaphores)
    fetched = [copies.start(inproj_far, inproj), copies.start(outproj_far, outproj)]
    fill_rows(source, clips)
    class_row = wide(clips[0:1])

    def first(block, carry):
        rows = frame_rows(source, block, class_row, FRAMES)
        unit, _ = normed(rows)
        at = pl.ds(pl.multiple_of(block * BLOCK, BLOCK), BLOCK)
        x_out[:, at, :] = rows.astype(LOW).reshape(FRAMES, BLOCK, rows.shape[1])
        norm_out[:, at, :] = (unit * vector(gain) + vector(shift)).astype(LOW).reshape(FRAMES, BLOCK, rows.shape[1])
        return carry

    lax.fori_loop(0, BLOCKS, first, 0, unroll=UNROLL)
    sent = [copies.start(x_out, x_far), copies.start(norm_out, norm_far)]
    fetched[0].wait()
    weights = side_by_side(inproj)
    for step in range(FRAMES // PAIR):
        at = pl.ds(step * PAIR, PAIR)
        qkv = heads_low(dot(flat(norm_out[at]), weights), inbias, half)
        qkv_out[at] = qkv.reshape(PAIR, ROWS, 3 * half)
    sent.append(copies.start(qkv_out, qkv_far))
    count = FRAMES * BLOCK
    same = iota((count, 2 * count), 0) % BLOCK == iota((count, 2 * count), 1) % BLOCK

    def third(first_block, count):
        ats = [
            pl.ds(pl.multiple_of((first_block + step) * BLOCK, BLOCK), BLOCK) for step in range(count)
        ]

        def keep(step, head, probs):
            probs_out[first_block + step, head] = probs

        mixed = attend(
            [flat(qkv_out[:, at, :]) for at in ats], lambda scores: jnp.where(same, scores, -1e30), keep, 2, TIME_LAG
        )
        for at, part in zip(ats, mixed):
            mixed_out[:, at, :] = part.reshape(FRAMES, BLOCK, half)

    by_blocks(third)
    sent += [copies.start(probs_out, probs_far), copies.start(mixed_out, mixed_far)]
    fetched[1].wait()
    for step in range(FRAMES // PAIR):
        at = pl.ds(step * PAIR, PAIR)
        part = dot(flat(mixed_out[at]), outproj[...]).astype(LOW)
        part_out[at] = part.reshape(PAIR, ROWS, part.shape[1])
        sent.append(copies.start(part_out.at[at], part_far.at[at]))
    for copy in sent:
        copy.wait()


def by_blocks(run):
    def step(at, carry):
        run(at * TIME_GROUP, TIME_GROUP)
        return carry

    lax.fori_loop(0, BLOCKS // TIME_GROUP, step, 0)
    if BLOCKS % TIME_GROUP:
        run(BLOCKS // TIME_GROUP * TIME_GROUP, BLOCKS % TIME_GROUP)


def heads_low(linear, inbias, half):
    query = ((linear[:, :half] + inbias[0:1]) * HEAD ** (-0.5)).astype(LOW)
    keys = linear[:, half : 2 * half].astype(LOW)
    values = (linear[:, 2 * half :] + inbias[1:2]).astype(LOW)
    return jnp.concatenate([query, keys, values], axis=1)


def beside(field_t, head):
    own = field_t[HEAD * head : HEAD * (head + 1)]
    none = jnp.zeros_like(own)
    return jnp.concatenate([own, none] if head % 2 == 0 else [none, own], axis=0)


def beside_all(field_t, heads):
    return jnp.concatenate([beside(field_t, head) for head in heads], axis=1)


def pair_of(field, head):
    start = head // 2 * 2 * HEAD
    return field[:, start : start + 2 * HEAD]


def head_rows(field_t, head):
    return field_t[HEAD * head : HEAD * (head + 1)]


def staged(count, stages, lag):
    held = [None] * count
    for step in range(count + lag * (len(stages) - 1)):
        for depth, stage in enumerate(stages):
            item = step - lag * depth
            if 0 <= item < count:
                held[item] = stage(item, held[item])
    return held


def attend(inputs, block_allowed, keep, group, lag):
    half = inputs[0].shape[1] // 3
    rows = inputs[0].shape[0]
    query_t = [qkv[:, :half].T for qkv in inputs]
    values_t = [qkv[:, 2 * half :].T for qkv in inputs]
    groups = half // HEAD // group

    def heads_of(item):
        first = item % groups * group
        return range(first, first + group)

    def score(item, held):
        block = item // groups
        keys = inputs[block][:, half : 2 * half]
        return dot(pair_of(keys, heads_of(item)[0]), beside_all(query_t[block], heads_of(item)))

    def weigh(item, scores):
        scores = block_allowed(scores)
        expon = jnp.exp(scores - jnp.max(scores, axis=0, keepdims=True))
        probs = (expon * (1.0 / column_sum(expon))).astype(LOW)
        for at, head in enumerate(heads_of(item)):
            keep(item // groups, head, probs[:, at * rows : (at + 1) * rows])
        return probs

    def mix(item, probs):
        return [
            dot(head_rows(values_t[item // groups], head), probs[:, at * rows : (at + 1) * rows])
            for at, head in enumerate(heads_of(item))
        ]

    mixed_t = staged(len(inputs) * groups, [score, weigh, mix], lag)
    out = []
    for block in range(len(inputs)):
        parts = [part for item in mixed_t[block * groups : (block + 1) * groups] for part in item]
        out.append(jnp.concatenate(parts, axis=0).T.astype(LOW))
    return out


def attend_back(inputs, probs_of, d_mixeds, group, lag):
    half = inputs[0].shape[1] // 3
    rows = inputs[0].shape[0]
    keys_t = [qkv[:, half : 2 * half].T for qkv in inputs]
    d_mixed_t = [d_mixed.T for d_mixed in d_mixeds]
    lane = iota((rows, 2 * HEAD), 1) < HEAD
    groups = half // HEAD // group

    def heads_of(item):
        first = item % groups * group
        return range(first, first + group)

    def score(item, held):
        block = item // groups
        values = inputs[block][:, 2 * half :]
        return dot(pair_of(values, heads_of(item)[0]), beside_all(d_mixed_t[block], heads_of(item)))

    def weigh(item, d_probs):
        probs_low = jnp.concatenate([probs_of(item // groups, head) for head in heads_of(item)], axis=1)
        probs = wide(probs_low)
        scaled = probs * d_probs
        d_scores = scaled - probs * column_sum(scaled)
        return probs_low, d_scores.astype(LOW)

    def halves(field):
        none = jnp.zeros_like(field)
        return jnp.concatenate([jnp.where(lane, field, none), jnp.where(lane, none, field)], axis=0)

    def mix(item, held):
        block = item // groups
        probs_low, d_scores = held
        d_query_t = [
            dot(head_rows(keys_t[block], head), d_scores[:, at * rows : (at + 1) * rows])
            for at, head in enumerate(heads_of(item))
        ]
        d_mixed = pair_of(d_mixeds[block], heads_of(item)[0])
        query = pair_of(inputs[block][:, :half], heads_of(item)[0])
        if group == 2:
            d_mixed = halves(d_mixed)
            query = halves(query)
        return d_query_t, dot(d_scores, query), dot(probs_low, d_mixed)

    made = staged(len(inputs) * groups, [score, weigh, mix], lag)

    def paired(fields):
        if group == 2:
            return fields
        return [jnp.where(lane, fields[at], fields[at + 1]) for at in range(0, len(fields), 2)]

    out = []
    for block in range(len(inputs)):
        own = made[block * groups : (block + 1) * groups]
        d_query = jnp.concatenate([part for item in own for part in item[0]], axis=0).T.astype(LOW) * HEAD ** (-0.5)
        d_keys = paired([item[1] for item in own])
        d_values = paired([item[2] for item in own])
        out.append(jnp.concatenate([d_query] + [d.astype(LOW) for d in d_keys + d_values], axis=1))
    return out


def time_forward(clips, gain, shift, inproj, inbias, outproj):
    tokens, width = clips.shape
    half = outproj.shape[0]
    heads = half // HEAD
    count = FRAMES * BLOCK
    args = (clips, gain, shift, inproj, inbias, outproj)
    outs = [
        shape((FRAMES, ROWS, width)),
        shape((FRAMES, ROWS, width)),
        shape((FRAMES, ROWS, 3 * half)),
        shape((BLOCKS, heads, count, count)),
        shape((FRAMES, ROWS, half)),
        shape((FRAMES, ROWS, width)),
    ]
    rows = FRAMES * ROWS
    near = [pltpu.VMEM(a.shape, a.dtype) for a in (inproj, outproj)] + [pltpu.VMEM(o.shape, o.dtype) for o in outs]
    far = pl.BlockSpec(memory_space=pl.ANY)
    return call(
        time_forward_kernel,
        (1,),
        [whole(clips), whole(gain), whole(shift), far, whole(inbias), far],
        [far] * 6,
        outs,
        near + [pltpu.VMEM((BLOCKS * count + BLOCK, width), LOW), pltpu.SemaphoreType.DMA((16,))],
        2 * rows * width * half * 5,
        args,
    )


def cotangent_kernel(cotangent, live, out, total, source):
    fill_rows(source, cotangent)
    present = live[0, 0]
    class_row = wide(cotangent[0:1])

    def first(block, carry):
        rows = frame_rows(source, block, class_row, 1) * present
        at = pl.ds(pl.multiple_of(block * BLOCK, BLOCK), BLOCK)
        out[:, at, :] = rows.astype(LOW).reshape(FRAMES, BLOCK, rows.shape[1])
        return carry + column_sum(rows)

    total[...] = lax.fori_loop(0, BLOCKS, first, jnp.zeros(total.shape, jnp.float32), unroll=UNROLL)


def cotangent_frames(cotangent, live):
    tokens, width = cotangent.shape
    args = (cotangent, live)
    outs = [shape((FRAMES, ROWS, width)), shape((1, width), jnp.float32)]
    return call(
        cotangent_kernel,
        (1,),
        [whole(cotangent), SCALAR],
        [whole(o) for o in outs],
        outs,
        [pltpu.VMEM((BLOCKS * FRAMES * BLOCK + BLOCK, width), LOW)],
        2 * FRAMES * ROWS * 128 * width,
        args,
    )


def vector(ref):
    return ref[...].reshape(1, -1)


def place_of(shape_of):
    return iota(shape_of, 0) % ROWS


def gather_mixer(own, other, rank, mixer):
    half = own.shape[0]

    @pl.when(pl.program_id(0) == 0)
    def _():
        mixer[pl.ds(pl.multiple_of(rank[0, 0] * half, half), half), :] = own[...]
        mixer[pl.ds(pl.multiple_of((1 - rank[0, 0]) * half, half), half), :] = other[...]


def space_forward_kernel(
    own, other, x, outbias, mixer_own, mixer_other, rank, mixbias, gain, shift, inproj, inbias, outproj,
    mixer_out, after_out, norm_out, qkv_out, probs_out, mixed_out, part_out, mixer,
):
    gather_mixer(mixer_own, mixer_other, rank, mixer)
    half = outproj.shape[0]
    width = outproj.shape[1]

    def spread(field):
        return field.astype(LOW).reshape(PAIR, ROWS, field.shape[1])

    mixer_in = (wide(flat(own[...])) + wide(flat(other[...])) + vector(outbias)).astype(LOW)
    mixer_out[...] = spread(jnp.where(rank[0, 0] == 0, mixer_in[:, :half], mixer_in[:, half:]))
    branch = dot(mixer_in, mixer[...]) + vector(mixbias)
    after = wide(flat(x[...])) + jnp.where(place_of((PAIR * ROWS, 1)) < PLACES, branch, 0.0)
    after_out[...] = spread(after)
    unit, _ = normed(after)
    norm = (unit * vector(gain) + vector(shift)).astype(LOW)
    norm_out[...] = spread(norm)
    qkv = heads_low(dot(norm, side_by_side(inproj)), inbias, half)
    qkv_out[...] = spread(qkv)

    def allowed(scores):
        even = ROWS - BLOCK
        last = jnp.where(iota((BLOCK, ROWS), 0) <= PLACES - even, scores[even:], -1e30)
        return jnp.concatenate([scores[:even], last], axis=0)

    def keep(frame, head, probs):
        probs_out[frame, head] = probs

    frames = [qkv[frame * ROWS : (frame + 1) * ROWS] for frame in range(PAIR)]
    for frame, mixed in enumerate(attend(frames, allowed, keep, 1, SPACE_LAG)):
        mixed_out[frame] = mixed
    part_out[...] = spread(dot(flat(mixed_out[...]), outproj[...]))


def pairs(array):
    rest = (0,) * (array.ndim - 1)
    return pl.BlockSpec((PAIR,) + array.shape[1:], lambda at: (at,) + rest)


def space_forward(own, other, x, outbias, mixers, mixbias, gain, shift, inproj, inbias, outproj):
    width = x.shape[2]
    half = outproj.shape[0]
    heads = half // HEAD
    args = (own, other, x, outbias) + mixers + (mixbias, gain, shift, inproj, inbias, outproj)
    outs = [
        shape((FRAMES, ROWS, half)),
        shape((FRAMES, ROWS, width)),
        shape((FRAMES, ROWS, width)),
        shape((FRAMES, ROWS, 3 * half)),
        shape((FRAMES, heads, ROWS, ROWS)),
        shape((FRAMES, ROWS, half)),
        shape((FRAMES, ROWS, width)),
    ]
    return call(
        space_forward_kernel,
        (FRAMES // PAIR,),
        [pairs(a) for a in args[:3]] + [whole(a) for a in args[3:6]] + [SCALAR] + [whole(a) for a in args[7:]],
        [pairs(o) for o in outs],
        outs,
        [pltpu.VMEM((width, width), LOW)],
        2 * FRAMES * ROWS * width * half * 8,
        args,
    )


def last_block(count):
    return lambda array: pl.BlockSpec((count, BLOCK, array.shape[2]), lambda at: (0, BLOCKS - 1, 0))


CLASS_AT = PLACES - (BLOCKS - 1) * BLOCK


def feed_kernel(
    own, other, after, cot, own_last, other_last, after_last, outbias, gain, shift, upward, upbias, down,
    mid_out, norm_out, act_out, dpre_out, part_out, dnorm_out, upbias_out,
):
    step = pl.program_id(0)
    units = upward.shape[1]
    width = upward.shape[0]

    def spread(field):
        return field.astype(LOW).reshape(PAIR, ROWS, field.shape[1])

    class_branch = wide(own_last[...]) + wide(other_last[...])
    class_branch = jnp.sum(class_branch, axis=0)[CLASS_AT : CLASS_AT + 1] * (1.0 / FRAMES) + vector(outbias)
    at = iota((PAIR * ROWS, 1), 0)
    branch = wide(flat(own[...])) + wide(flat(other[...])) + vector(outbias)
    is_class = (at == PLACES) & (step == 0)
    mid = jnp.where(at % ROWS < PLACES, wide(flat(after[...])) + branch, 0.0)
    mid = mid + jnp.where(is_class, wide(after_last[0])[CLASS_AT : CLASS_AT + 1] + class_branch, 0.0)
    mid_out[...] = spread(mid)
    unit, _ = normed(mid)
    norm = (unit * vector(gain) + vector(shift)).astype(LOW)
    norm_out[...] = spread(norm)
    grad = flat(cot[...])
    part = jnp.zeros((PAIR * ROWS, width), jnp.float32)
    d_norm = jnp.zeros((PAIR * ROWS, width), jnp.float32)
    share = units

    @pl.when(step == 0)
    def _():
        upbias_out[...] = jnp.zeros(upbias_out.shape, jnp.float32)

    for start in range(0, units, share):
        cols = slice(start, start + share)
        pre = dot(norm, upward[:, cols]) + vector(upbias)[:, cols]
        cumulative = 0.5 * (1.0 + lax.erf(pre * 0.5**0.5))
        slope = cumulative + pre * jnp.exp(-0.5 * pre * pre) * 0.3989422804014327
        act = (pre * cumulative).astype(LOW)
        act_out[:, :, cols] = spread(act)
        d_pre = (dot_last(grad, down[cols]) * slope).astype(LOW)
        dpre_out[:, :, cols] = spread(d_pre)
        upbias_out[:, cols] += column_sum(wide(d_pre))
        part = part + dot(act, down[cols])
        d_norm = d_norm + dot_last(d_pre, upward[:, cols])
    part_out[...] = spread(part)
    dnorm_out[...] = spread(d_norm)


def feed(own, other, after, cot, outbias, gain, shift, upward, upbias, down):
    width, units = upward.shape
    args = (own, other, after, cot, own, other, after, outbias, gain, shift, upward, upbias, down)
    outs = [
        shape((FRAMES, ROWS, width)),
        shape((FRAMES, ROWS, width)),
        shape((FRAMES, ROWS, units)),
        shape((FRAMES, ROWS, units)),
        shape((FRAMES, ROWS, width)),
        shape((FRAMES, ROWS, width)),
        shape((1, units), jnp.float32),
    ]
    tail = last_block(FRAMES)
    return call(
        feed_kernel,
        (FRAMES // PAIR,),
        [pairs(a) for a in args[:4]] + [tail(a) for a in args[4:7]] + [whole(a) for a in args[7:]],
        [pairs(o) for o in outs[:6]] + [whole(outs[6])],
        outs,
        [],
        2 * FRAMES * ROWS * width * units * 4,
        args,
    )


def space_backward_kernel(
    own, other, mid, cot, qkv, probs, own_last, other_last, mid_last, cot_last, gain, outproj, inproj,
    dspace_out, back_out, part_out, dclass_out, gain_out, shift_out, outbias_out, inbias_out,
):
    step = pl.program_id(0)
    half = outproj.shape[0]

    def spread(field):
        return field.astype(LOW).reshape(PAIR, ROWS, field.shape[1])

    def back(own_part, other_part, mid_part, cot_part):
        d_norm = wide(own_part) + wide(other_part)
        unit, inverse = normed(wide(mid_part))
        return wide(cot_part) + normed_back(unit, inverse, d_norm * vector(gain)), d_norm, d_norm * unit

    d_class = back(own_last[0], other_last[0], mid_last[0], cot_last[0])[0][CLASS_AT : CLASS_AT + 1]
    d_mid, d_shift, d_gain = back(flat(own[...]), flat(other[...]), flat(mid[...]), flat(cot[...]))
    place = place_of((PAIR * ROWS, 1))
    d_space = jnp.where(place < PLACES, d_mid, jnp.where(place == PLACES, d_class * (1.0 / FRAMES), 0.0))

    @pl.when(step == 0)
    def _():
        dclass_out[...] = d_class
        for ref in (gain_out, shift_out, outbias_out, inbias_out):
            ref[...] = jnp.zeros(ref.shape, jnp.float32)

    gain_out[...] += column_sum(d_gain)
    shift_out[...] += column_sum(d_shift)
    outbias_out[...] += column_sum(d_space)
    d_low = d_space.astype(LOW)
    dspace_out[...] = spread(d_low)
    d_mixed = dot_last(d_low, outproj[...]).astype(LOW)
    made = attend_back(
        [qkv[frame] for frame in range(PAIR)],
        lambda frame, head: probs[frame, head],
        [d_mixed[frame * ROWS : (frame + 1) * ROWS] for frame in range(PAIR)],
        1,
        SPACE_LAG,
    )
    for frame, part in enumerate(made):
        back_out[frame] = part
    backs = flat(back_out[...])
    inbias_out[...] += column_sum(wide(backs))
    part_out[...] = spread(dot_last(backs, side_by_side(inproj)))


def space_backward(own, other, mid, cot, qkv, probs, gain, outproj, inproj):
    width = mid.shape[2]
    half = outproj.shape[0]
    args = (own, other, mid, cot, qkv, probs, own, other, mid, cot, gain, outproj, inproj)
    outs = [
        shape((FRAMES, ROWS, width)),
        shape((FRAMES, ROWS, 3 * half)),
        shape((FRAMES, ROWS, width)),
        shape((1, width), jnp.float32),
        shape((1, width), jnp.float32),
        shape((1, width), jnp.float32),
        shape((1, width), jnp.float32),
        shape((1, 3 * half), jnp.float32),
    ]
    tail = last_block(1)
    return call(
        space_backward_kernel,
        (FRAMES // PAIR,),
        [pairs(a) for a in args[:6]] + [tail(a) for a in args[6:10]] + [whole(a) for a in args[10:]],
        [pairs(o) for o in outs[:3]] + [whole(o) for o in outs[3:]],
        outs,
        [],
        2 * FRAMES * ROWS * width * half * 6,
        args,
    )


def mixer_backward_kernel(
    own, other, after, dspace, dclass, gain, mixer_own, mixer_other, rank, outproj,
    dgrid_out, dmixer_out, dmixed_out, dsource_out, gain_out, shift_out, mixbias_out, outbias_out, mixer,
):
    gather_mixer(mixer_own, mixer_other, rank, mixer)

    @pl.when(pl.program_id(0) == 0)
    def _():
        dsource_out[...] = dclass[...]
        for ref in (gain_out, shift_out, mixbias_out, outbias_out):
            ref[...] = jnp.zeros(ref.shape, jnp.float32)

    def spread(field):
        return field.astype(LOW).reshape(PAIR, ROWS, field.shape[1])

    d_norm = wide(flat(own[...])) + wide(flat(other[...]))
    unit, inverse = normed(wide(flat(after[...])))
    gain_out[...] += column_sum(d_norm * unit)
    shift_out[...] += column_sum(d_norm)
    d_space_in = normed_back(unit, inverse, d_norm * vector(gain))
    place = place_of((PAIR * ROWS, 1))
    dsource_out[...] += column_sum(jnp.where(place == PLACES, d_space_in, 0.0))
    d_grid = jnp.where(place < PLACES, d_space_in + wide(flat(dspace[...])), 0.0)
    mixbias_out[...] += column_sum(d_grid)
    d_low = d_grid.astype(LOW)
    dgrid_out[...] = spread(d_low)
    d_mixer = dot_last(d_low, mixer[...]).astype(LOW)
    dmixer_out[...] = spread(d_mixer)
    outbias_out[...] += column_sum(wide(d_mixer))
    dmixed_out[...] = spread(dot_last(d_mixer, outproj[...]))


def mixer_backward(own, other, after, dspace, dclass, gain, mixers, outproj):
    width = after.shape[2]
    half = outproj.shape[0]
    args = (own, other, after, dspace, dclass, gain) + mixers + (outproj,)
    outs = [
        shape((FRAMES, ROWS, width)),
        shape((FRAMES, ROWS, width)),
        shape((FRAMES, ROWS, half)),
    ] + [shape((1, width), jnp.float32)] * 5
    return call(
        mixer_backward_kernel,
        (FRAMES // PAIR,),
        [pairs(a) for a in args[:4]] + [whole(a) for a in args[4:8]] + [SCALAR, whole(outproj)],
        [pairs(o) for o in outs[:3]] + [whole(o) for o in outs[3:]],
        outs,
        [pltpu.VMEM((width, width), LOW)],
        2 * FRAMES * ROWS * width * half * 3,
        args,
    )


def near_far(arrays):
    return [pltpu.VMEM(a.shape, a.dtype) for a in arrays], pl.BlockSpec(memory_space=pl.ANY)


def places(first, last):
    return pl.ds(first * BLOCK, (last - first) * BLOCK)


TIME_GROUPS = ((0, 3), (3, 8), (8, BLOCKS))


def settle_copies(arrivals):
    for copy in arrivals:
        copy.wait()


def fetch_time(copies, far, near):
    coming = []
    for first, last in TIME_GROUPS:
        at = (places(first, last), pl.ds(first, last - first))
        arrivals = [copies.start(f.at[:, at[0], :], n.at[:, at[0], :]) for f, n in zip(far[:2], near[:2])]
        coming.append(arrivals + [copies.start(far[2].at[at[1]], near[2].at[at[1]])])
    return coming


def time_attention_back(group, d_mixed, qkv, probs, back_out):
    first, last = group
    ats = [places(block, block + 1) for block in range(first, last)]
    made = attend_back(
        [flat(qkv[:, at, :]) for at in ats],
        lambda step, head: probs[first + step, head],
        [flat(d_mixed[:, at, :]) for at in ats],
        2,
        TIME_LAG,
    )
    for at, part in zip(ats, made):
        back_out[:, at, :] = part.reshape(FRAMES, BLOCK, part.shape[1])


def time_part(copies, back_out, inproj, part_out, part_far, inbias_out):
    sent = []
    inbias = jnp.zeros(inbias_out.shape, jnp.float32)
    for step in range(FRAMES // PAIR):
        at = pl.ds(step * PAIR, PAIR)
        backs = flat(back_out[at])
        inbias = inbias + column_sum(wide(backs))
        part_out[at] = dot_last(backs, side_by_side(inproj)).astype(LOW).reshape(PAIR, ROWS, part_out.shape[2])
        sent.append(copies.start(part_out.at[at], part_far.at[at]))
    inbias_out[...] = inbias
    return sent


def time_backward_kernel(
    d_mixed_far, qkv_far, probs_far, inproj_far, back_far, part_far, inbias_out,
    d_mixed, qkv, probs, inproj, back_out, part_out, semaphores,
):
    copies = Copies(semaphores)
    coming = fetch_time(copies, (d_mixed_far, qkv_far, probs_far), (d_mixed, qkv, probs))
    weights = copies.start(inproj_far, inproj)
    for group, arrivals in zip(TIME_GROUPS, coming):
        settle_copies(arrivals)
        time_attention_back(group, d_mixed, qkv, probs, back_out)
    sent = [copies.start(back_out, back_far)]
    weights.wait()
    settle_copies(sent + time_part(copies, back_out, inproj, part_out, part_far, inbias_out))


def time_backward(d_mixed, qkv, probs, inproj):
    width = inproj.shape[1]
    half = d_mixed.shape[2]
    args = (d_mixed, qkv, probs, inproj)
    outs = [
        shape((FRAMES, ROWS, 3 * half)),
        shape((FRAMES, ROWS, width)),
        shape((1, 3 * half), jnp.float32),
    ]
    near, far = near_far(args + tuple(outs[:2]))
    return call(
        time_backward_kernel,
        (1,),
        [far] * 4,
        [far, far, whole(outs[2])],
        outs,
        near + [pltpu.SemaphoreType.DMA((3 * len(TIME_GROUPS) + 2 + FRAMES // PAIR,))],
        2 * FRAMES * ROWS * width * half * 5,
        args,
    )


def fetch_places(copies, far, near, groups):
    return [
        [copies.start(f.at[:, places(*group), :], n.at[:, places(*group), :]) for f, n in zip(far, near)]
        for group in groups
    ]


def put_tokens(out, block, low, carry):
    count = FRAMES * BLOCK
    moved = jnp.where(iota((count, 1), 0) == 0, carry, to_tokens(low))
    fits = min(out.shape[0] - block * count, count)
    out[block * count : block * count + fits] = moved[:fits].astype(out.dtype)
    return wide(low[count - BLOCK :])[BLOCK - 1 :]


def block_rows(ref, block):
    return wide(flat(ref[:, block * BLOCK : (block + 1) * BLOCK, :]))


VECTORS = 16


SOURCE_GROUPS = ((0, 1), (1, 4), (4, 8), (8, BLOCKS))


def source_kernel(own_far, other_far, x_far, dgrid_far, dsource, gain, *rest):
    given = rest[:-7]
    out, packed, own, other, x, dgrid, semaphores = rest[-7:]
    width = packed.shape[1]
    coming = fetch_places(
        Copies(semaphores), (own_far, other_far, x_far, dgrid_far), (own, other, x, dgrid), SOURCE_GROUPS
    )
    carry = dsource[...]
    d_gain = jnp.zeros((1, width), jnp.float32)
    d_shift = jnp.zeros((1, width), jnp.float32)
    for (first, last), arrivals in zip(SOURCE_GROUPS, coming):
        for arrival in arrivals:
            arrival.wait()
        for block in range(first, last):
            d_norm = block_rows(own, block) + block_rows(other, block)
            unit, inverse = normed(block_rows(x, block))
            d_gain = d_gain + column_sum(d_norm * unit)
            d_shift = d_shift + column_sum(d_norm)
            rows = block_rows(dgrid, block) + normed_back(unit, inverse, d_norm * vector(gain))
            carry = put_tokens(out, block, rows.astype(LOW), carry)
    packed[...] = jnp.zeros(packed.shape, jnp.float32)
    packed[0:1] = d_gain
    packed[1:2] = d_shift
    at = 2
    for ref in given:
        count = ref.shape[1]
        if count == 3 * width // 2:
            packed[at : at + 1] = jnp.concatenate([ref[:, : width // 2], ref[:, width:]], axis=1)
            at += 1
            continue
        for start in range(0, count, width):
            packed[at : at + 1] = ref[:, start : start + width]
            at += 1


def source_gradient(own, other, x, dgrid, dsource, gain, given, tokens):
    width = x.shape[2]
    args = (own, other, x, dgrid, dsource, gain) + tuple(given)
    outs = [shape((tokens, width)), shape((VECTORS, width), jnp.float32)]
    near, far = near_far(args[:4])
    return call(
        source_kernel,
        (1,),
        [far] * 4 + [whole(a) for a in args[4:]],
        [whole(o) for o in outs],
        outs,
        near + [pltpu.SemaphoreType.DMA((4 * len(SOURCE_GROUPS),))],
        2 * FRAMES * ROWS * 128 * width,
        args,
    )


RESULT_GROUPS = ((BLOCKS - 1, BLOCKS), (0, 4), (4, 8), (8, BLOCKS - 1))


def result_kernel(own_far, other_far, mid_far, bias, live, out, own, other, mid, semaphores):
    present = live[0, 0]
    coming = fetch_places(Copies(semaphores), (own_far, other_far, mid_far), (own, other, mid), RESULT_GROUPS)

    def rows_of(block):
        total = block_rows(mid, block) + block_rows(own, block) + block_rows(other, block) + vector(bias)
        return (total * present).astype(LOW)

    for arrival in coming[0]:
        arrival.wait()
    last = rows_of(BLOCKS - 1)
    carry = wide(last[:BLOCK])[CLASS_AT : CLASS_AT + 1]
    for (first, end), arrivals in zip(RESULT_GROUPS[1:], coming[1:]):
        for arrival in arrivals:
            arrival.wait()
        for block in range(first, end):
            carry = put_tokens(out, block, rows_of(block), carry)
    put_tokens(out, BLOCKS - 1, last, carry)


def result_tokens(own, other, mid, bias, live, tokens):
    width = mid.shape[2]
    args = (own, other, mid, bias, live)
    outs = [shape((tokens, width))]
    near, far = near_far(args[:3])
    return call(
        result_kernel,
        (1,),
        [far] * 3 + [whole(bias), SCALAR],
        [whole(outs[0])],
        outs,
        near + [pltpu.SemaphoreType.DMA((3 * len(RESULT_GROUPS),))],
        2 * FRAMES * ROWS * 128 * width,
        args,
    )[0]


def settle_vectors(at, total, outs):
    width = total.shape[1]
    share = outs[0].shape[0]
    dests = width // share
    moved = pltpu.roll(total, (dests - at) % dests * share, 1)
    for row in range(10):
        outs[row][...] = moved[row, :share]
    small = share // 2
    moved = pltpu.roll(total, (2 * dests - at) % (2 * dests) * small, 1)
    for row in (10, 11):
        for part in range(2):
            start = part * (width // 2)
            outs[row][part : part + 1, :] = moved[row : row + 1, start : start + small]
    moved = pltpu.roll(total, (dests - 2 * at % dests) % dests * share, 1)
    outs[12][...] = jnp.where(2 * at < dests, moved[12, : 2 * share], moved[13, : 2 * share])


def small_shapes(share):
    outs = [shape((share,), jnp.float32)] * 10
    outs += [shape((2, share // 2), jnp.float32)] * 2
    return outs + [shape((2 * share,), jnp.float32)]


def settle_kernel(place, total, *outs):
    settle_vectors(place[0, 0], total[...], outs)


def settle(total, place, dests):
    outs = small_shapes(total.shape[1] // dests)
    return call(settle_kernel, (1,), [SCALAR, whole(total)], [whole(o) for o in outs], outs, [], 0, (place, total))


UNIT = 128


def bits_of(me):
    place = me[0, 0]
    return {"x": place % 2, "y": place // 2 % 2, "near": place // 4 % 2, "far": place // 8}


def pair_index(at, bit):
    return 2 * at + bit


def gap_index(at, bit):
    return at // 2 * 4 + 2 * bit + at % 2


def near_index(at, bit):
    return at // 4 * 8 + 4 * bit + at % 4


def top_index(half):
    return lambda at, bit: half * bit + at


def units_of(field):
    return [slice(at, at + UNIT) for at in range(0, field.shape[-1], UNIT)]


def split_gradient(field, axis, bits, message, start, keep):
    index = {"x": pair_index, "y": gap_index, "near": near_index}[axis]
    cols = units_of(field)
    for at in range(8):
        for unit, col in enumerate(cols):
            message[start + at * len(cols) + unit] = field[index(at, 1 - bits[axis]), :, col]
            keep[at, unit] = field[index(at, bits[axis]), :, col]


def split_total(held, got, got_start, bit, message, start, keep, index=pair_index):
    units = held.shape[1]

    def total(at):
        return (wide(held[at]) + wide(got[pl.ds(got_start + at * units, units)])).astype(LOW)

    for at in range(held.shape[0] // 2):
        message[start + at * units : start + (at + 1) * units] = total(index(at, 1 - bit))
        keep[at] = total(index(at, bit))


def put_gradient(field, left, right, start=0):
    step = 768 if right.shape[1] % 768 == 0 else 384
    for at in range(0, right.shape[1], step):
        part = lax.dot_general(
            left, right[:, at : at + step], (((0,), (0,)), ((), ())), preferred_element_type=jnp.float32
        )
        field[:, :, start + at : start + at + step] = part.astype(LOW).reshape(field.shape[:2] + (step,))


def gradient_call(body, args, outs, scratch, flops):
    inputs, width = args[1:], len(args) - 1

    def kernel(me, *refs):
        far, near = refs[: width + len(outs)], refs[width + len(outs) : 2 * (width + len(outs))]
        copies = Copies(refs[-1])
        waiting = [copies.start(source, target) for source, target in zip(far[:width], near[:width])]
        sent = []

        def need(*wanted):
            for ref in wanted:
                waiting[[ref is one for one in near].index(True)].wait()

        def done(*made):
            for ref in made:
                sent.append(copies.start(ref, far[[ref is one for one in near].index(True)]))

        body(need, done, me, *near, *refs[2 * (width + len(outs)) : -1])
        for copy in sent:
            copy.wait()

    remote = pl.BlockSpec(memory_space=pl.ANY)
    return call(
        kernel,
        (1,),
        [SCALAR] + [remote] * width,
        [remote] * len(outs),
        outs,
        [pltpu.VMEM(a.shape, a.dtype) for a in list(inputs) + outs]
        + scratch
        + [pltpu.SemaphoreType.DMA((width + len(outs),))],
        flops,
        args,
    )


def plain_call(kernel, args, outs):
    return call(
        kernel,
        (1,),
        [SCALAR] + [whole(a) for a in args[1:]],
        [whole(o) for o in outs],
        outs,
        [],
        0,
        args,
    )


LINE_UNITS = 4


def feed_gradient_kernel(
    need, done, me, norm, d_pre, cot, act,
    message_x, message_y, message_near, keep_up, keep_down, keep_line_up, keep_line_down, up, down,
):
    bits = bits_of(me)
    cut = keep_up.shape[1] * UNIT
    need(norm, d_pre)
    put_gradient(up, flat(norm[...]), flat(d_pre[...]))
    need(cot, act)
    put_gradient(down, flat(cot[...]), flat(act[...]))
    split_gradient(up.at[:, :, :cut], "x", bits, message_x, 0, keep_up)
    split_gradient(up.at[:, :, cut:], "near", bits, message_near, 0, keep_line_up)
    done(message_x, keep_up, keep_line_up)
    split_gradient(down.at[:, :, :cut], "y", bits, message_y, 0, keep_down)
    split_gradient(down.at[:, :, cut:], "near", bits, message_near, 8 * LINE_UNITS, keep_line_down)
    done(message_y, message_near, keep_down, keep_line_down)


def field_shape(dests, units, share):
    return shape((dests, units, share, UNIT))


def message_shape(blocks, share):
    return shape((blocks, share, UNIT))


def feed_gradient(me, norm, d_pre, cot, act):
    width = norm.shape[2]
    units = act.shape[2] // UNIT - LINE_UNITS
    share = width // 16
    outs = [message_shape(8 * units, share)] * 2 + [message_shape(16 * LINE_UNITS, share)]
    outs += [field_shape(8, units, share)] * 2 + [field_shape(8, LINE_UNITS, share)] * 2
    scratch = [pltpu.VMEM((16, share, act.shape[2]), LOW)] * 2
    return gradient_call(
        feed_gradient_kernel, (me, norm, d_pre, cot, act), outs, scratch, 4 * FRAMES * ROWS * width * act.shape[2]
    )


def space_gradient_kernel(
    need, done, me, norm, backs, d_space, mixed, up, got_x, down, got_y, line_up, line_down, got_near,
    message_x, message_y, message_far, keep_up, keep_down, keep_line_up, keep_line_down, keep_first, keep_second,
    first, second,
):
    bits = bits_of(me)
    count = 4 * up.shape[1]
    width = first.shape[2]
    need(norm, backs)
    rows = flat(norm[...])
    put_gradient(first, rows, flat(backs[...])[:, :width])
    put_gradient(second, rows, flat(backs[...])[:, width:])
    need(d_space, mixed)
    put_gradient(second, flat(d_space[...]), flat(mixed[...]), backs.shape[2] - width)
    need(up, got_x)
    split_total(up, got_x, 0, bits["y"], message_y, 0, keep_up)
    done(keep_up)
    split_gradient(first, "y", bits, message_y, count, keep_first)
    done(message_y, keep_first)
    need(down, got_y)
    split_total(down, got_y, 0, bits["x"], message_x, 0, keep_down)
    split_gradient(second, "x", bits, message_x, count, keep_second)
    done(message_x, keep_down, keep_second)
    need(line_up, line_down, got_near)
    split_total(line_up, got_near, 0, bits["far"], message_far, 0, keep_line_up, top_index(4))
    split_total(
        line_down, got_near, 8 * LINE_UNITS, bits["far"], message_far, 4 * LINE_UNITS, keep_line_down, top_index(4)
    )
    done(message_far, keep_line_up, keep_line_down)


def space_gradient(me, norm, backs, d_space, mixed, up, down, line_up, line_down, got_x, got_y, got_near):
    width = norm.shape[2]
    half = mixed.shape[2]
    share = width // 16
    units = up.shape[1]
    own = 2 * half // UNIT
    outs = [message_shape(4 * units + 8 * own, share)] * 2 + [message_shape(8 * LINE_UNITS, share)]
    outs += [field_shape(4, units, share)] * 2 + [field_shape(4, LINE_UNITS, share)] * 2
    outs += [field_shape(8, own, share)] * 2
    scratch = [pltpu.VMEM((16, share, 2 * half), LOW)] * 2
    return gradient_call(
        space_gradient_kernel,
        (me, norm, backs, d_space, mixed, up, got_x, down, got_y, line_up, line_down, got_near),
        outs,
        scratch,
        8 * FRAMES * ROWS * width * half,
    )


def mixer_gradient_kernel(
    need, done, me, d_mixer, mixed, d_grid, mixer_in, up, got_y, down, got_x, space_first, space_second,
    line_up, line_down, got_far,
    message_x, message_y, message_near, keep_up, keep_down, keep_line_up, keep_line_down, keep_first, keep_second,
    keep_out, keep_mixer, out, mixer,
):
    bits = bits_of(me)
    units = up.shape[1]
    feed = 4 * units
    own = space_first.shape[1]
    need(d_mixer, mixed)
    put_gradient(out, flat(d_mixer[...]), flat(mixed[...]))
    need(d_grid, mixer_in)
    put_gradient(mixer, flat(d_grid[...]), flat(mixer_in[...]))
    need(up, got_y)
    split_total(up, got_y, 0, bits["near"], message_near, 0, keep_up)
    need(down, got_x)
    split_total(down, got_x, 0, bits["near"], message_near, 2 * units, keep_down)
    done(message_near, keep_up, keep_down)
    need(space_first, space_second)
    split_total(space_first, got_y, feed, bits["x"], message_x, 0, keep_first)
    split_total(space_second, got_x, feed, bits["y"], message_y, 0, keep_second)
    split_gradient(out, "x", bits, message_x, 4 * own, keep_out)
    split_gradient(mixer, "y", bits, message_y, 4 * own, keep_mixer)
    need(line_up, line_down, got_far)
    line = 4 * own + 8 * keep_out.shape[1]
    split_total(line_up, got_far, 0, bits["x"], message_x, line, keep_line_up)
    split_total(line_down, got_far, 4 * LINE_UNITS, bits["y"], message_y, line, keep_line_down, top_index(2))
    done(message_x, message_y, keep_line_up, keep_line_down, keep_first, keep_second, keep_out, keep_mixer)


def mixer_gradient(
    me, d_mixer, mixed, d_grid, mixer_in, up, down, line_up, line_down, space_first, space_second, got_x, got_y, got_far
):
    width = d_grid.shape[2]
    half = mixed.shape[2]
    share = width // 16
    units, own, new = up.shape[1], space_first.shape[1], half // UNIT
    outs = [message_shape(4 * own + 8 * new + 2 * LINE_UNITS, share)] * 2 + [message_shape(4 * units, share)]
    outs += [field_shape(2, units, share)] * 2 + [field_shape(2, LINE_UNITS, share)] * 2
    outs += [field_shape(4, own, share)] * 2 + [field_shape(8, new, share)] * 2
    scratch = [pltpu.VMEM((16, share, half), LOW)] * 2
    return gradient_call(
        mixer_gradient_kernel,
        (
            me, d_mixer, mixed, d_grid, mixer_in, up, got_y, down, got_x, space_first, space_second,
            line_up, line_down, got_far,
        ),
        outs,
        scratch,
        4 * FRAMES * ROWS * width * half,
    )


TIME_FIRST = 5


def time_gradient_kernel(
    me, d_mixed_far, qkv_far, probs_far, inproj_far, norm_far, *rest,
):
    outs_far, inbias_out = rest[:5], rest[5]
    d_mixed, qkv, probs, inproj, norm = rest[6:11]
    outs = rest[11:16]
    part_out, message_x, message_y, keep_first, keep_second = outs
    back_out, both, semaphores = rest[16:]
    copies = Copies(semaphores)
    coming = fetch_time(copies, (d_mixed_far, qkv_far, probs_far), (d_mixed, qkv, probs))
    weights = [copies.start(inproj_far, inproj), copies.start(norm_far, norm)]
    for group, arrivals in zip(TIME_GROUPS, coming):
        settle_copies(arrivals)
        time_attention_back(group, d_mixed, qkv, probs, back_out)
    settle_copies(weights)
    bits = bits_of(me)
    put_gradient(both, flat(norm[...]), flat(back_out[...]))
    cut = TIME_FIRST * UNIT
    split_gradient(both.at[:, :, :cut], "y", bits, message_y, 0, keep_first)
    split_gradient(both.at[:, :, cut:], "x", bits, message_x, 0, keep_second)
    sent = [copies.start(near, far) for near, far in zip(outs[1:], outs_far[1:])]
    sent += time_part(copies, back_out, inproj, part_out, outs_far[0], inbias_out)
    settle_copies(sent)


def time_gradient(me, d_mixed, qkv, probs, inproj, norm):
    width = norm.shape[2]
    half = d_mixed.shape[2]
    share = width // 16
    last = 3 * half // UNIT - TIME_FIRST
    args = (me, d_mixed, qkv, probs, inproj, norm)
    outs = [
        shape((FRAMES, ROWS, width)),
        message_shape(8 * last, share),
        message_shape(8 * TIME_FIRST, share),
        field_shape(8, TIME_FIRST, share),
        field_shape(8, last, share),
        shape((1, 3 * half), jnp.float32),
    ]
    near, far = near_far(args[1:] + tuple(outs[:5]))
    scratch = [pltpu.VMEM((FRAMES, ROWS, 3 * half), LOW), pltpu.VMEM((16, share, 3 * half), LOW)]
    return call(
        time_gradient_kernel,
        (1,),
        [SCALAR] + [far] * 5,
        [far] * 5 + [whole(outs[5])],
        outs,
        near + scratch + [pltpu.SemaphoreType.DMA((3 * len(TIME_GROUPS) + 6 + FRAMES // PAIR,))],
        2 * FRAMES * ROWS * width * half * 8,
        args,
    )


def depth_kernel(
    me, up, down, space_first, space_second, got_x, got_y, got_near,
    message_near, message_far, keep_up, keep_down, keep_first, keep_second,
):
    bits = bits_of(me)
    units, own = up.shape[1], space_first.shape[1]
    split_total(space_first, got_x, 0, bits["near"], message_near, 0, keep_first)
    split_total(space_second, got_y, 0, bits["near"], message_near, 2 * own, keep_second)
    split_total(up, got_near, 0, bits["far"], message_far, 0, keep_up)
    split_total(down, got_near, 2 * units, bits["far"], message_far, units, keep_down)


def depth_step(me, up, down, space_first, space_second, got_x, got_y, got_near):
    units, own, share = up.shape[1], space_first.shape[1], up.shape[2]
    outs = [message_shape(4 * own, share), message_shape(2 * units, share)]
    outs += [field_shape(1, units, share)] * 2 + [field_shape(2, own, share)] * 2
    return plain_call(depth_kernel, (me, up, down, space_first, space_second, got_x, got_y, got_near), outs)


def vector_blocks(vectors, share):
    parts = [vectors[:, col].astype(LOW) for col in units_of(vectors)]
    each = share // VECTORS
    return [jnp.concatenate(parts[at : at + each], axis=0) for at in range(0, len(parts), each)]


def second_kernel(
    me, vectors, space_first, space_second, out, mixer, line_up, line_down, first, second,
    old_x, old_y, got_x, got_y, got_near,
    message_x, message_y, message_xy, message_far,
    keep_space_first, keep_space_second, keep_out, keep_mixer, keep_line_up, keep_line_down, keep_first, keep_second,
):
    bits = bits_of(me)
    own, new = space_first.shape[1], out.shape[1]
    share = first.shape[2]
    split_total(first, got_y, 0, bits["x"], message_x, 0, keep_first)
    split_total(second, got_x, 0, bits["y"], message_y, 0, keep_second)
    start_x, start_y = 4 * first.shape[1], 4 * second.shape[1]
    for at, block in enumerate(vector_blocks(vectors[...], share)):
        message_x[start_x + at] = block
        message_y[start_y + at] = block
        message_xy[at] = block
    start_x, start_y = start_x + message_xy.shape[0], start_y + message_xy.shape[0]
    split_total(out, old_x, 4 * own, bits["y"], message_y, start_y, keep_out)
    split_total(mixer, old_y, 4 * own, bits["x"], message_x, start_x, keep_mixer)
    line = 4 * own + 8 * new
    split_total(line_up, old_x, line, bits["y"], message_y, start_y + 4 * new, keep_line_up)
    split_total(line_down, old_y, line, bits["x"], message_x, start_x + 4 * new, keep_line_down)
    split_total(space_first, got_near, 0, bits["far"], message_far, 0, keep_space_first)
    split_total(space_second, got_near, 2 * own, bits["far"], message_far, own, keep_space_second)


def second_step(
    me, vectors, space_first, space_second, out, mixer, line_up, line_down, first, second,
    old_x, old_y, got_x, got_y, got_near,
):
    own, new, share = space_first.shape[1], out.shape[1], first.shape[2]
    extra = vectors.size // (share * UNIT)
    more = extra + 4 * new + LINE_UNITS
    outs = [
        message_shape(4 * first.shape[1] + more, share),
        message_shape(4 * second.shape[1] + more, share),
        message_shape(extra, share),
        message_shape(2 * own, share),
    ]
    outs += [field_shape(1, own, share)] * 2 + [field_shape(4, new, share)] * 2 + [field_shape(1, LINE_UNITS, share)] * 2
    outs += [field_shape(4, first.shape[1], share), field_shape(4, second.shape[1], share)]
    return plain_call(
        second_kernel,
        (
            me, vectors, space_first, space_second, out, mixer, line_up, line_down, first, second,
            old_x, old_y, got_x, got_y, got_near,
        ),
        outs,
    )


def line_kernel(
    me, vectors, out, mixer, line_up, line_down, first, second, got_x, got_y, got_xy,
    message_1, message_2, message_3, own, sum_line_up, sum_line_down,
):
    bits = bits_of(me)
    share = first.shape[2]
    new, extra = out.shape[1], got_xy.shape[0]
    place = 2 * bits["far"] + bits["near"]
    messages = (own, message_1, message_2, message_3)
    firsts, seconds = 4 * first.shape[1], 4 * second.shape[1]
    start = 0
    for held, got, at in (
        (first, got_x, 0), (second, got_y, 0), (out, got_y, seconds + extra), (mixer, got_x, firsts + extra),
    ):
        units = held.shape[1]
        for step, message in enumerate(messages):
            dest = place + step - 2 * (place & step)
            total = wide(held[dest]) + wide(got[pl.ds(at + dest * units, units)])
            message[start : start + units] = total.astype(LOW)
        start += units
    for at, block in enumerate(vector_blocks(vectors[...], share)):
        total = (wide(block) + wide(got_xy[at])) + (wide(got_x[firsts + at]) + wide(got_y[seconds + at]))
        for message in messages:
            message[start + at] = total.astype(LOW)
    line_x, line_y = firsts + extra + 4 * new, seconds + extra + 4 * new
    sum_line_up[0] = (wide(line_up[0]) + wide(got_y[line_y:])).astype(LOW)
    sum_line_down[0] = (wide(line_down[0]) + wide(got_x[line_x:])).astype(LOW)


def line_step(me, vectors, out, mixer, line_up, line_down, first, second, got_x, got_y, got_xy):
    share = first.shape[2]
    blocks = first.shape[1] + second.shape[1] + out.shape[1] + mixer.shape[1] + vectors.size // (share * UNIT)
    return plain_call(
        line_kernel,
        (me, vectors, out, mixer, line_up, line_down, first, second, got_x, got_y, got_xy),
        [message_shape(blocks, share)] * 4 + [field_shape(1, LINE_UNITS, share)] * 2,
    )


def final_kernel(
    me, own, got_1, got_2, got_3, up, down, got_feed, line_up, line_down, space_first, space_second, got_space,
    time_in, time_out, time_mixer, space_in, space_out, feed_up, feed_down, *small,
):
    units = up.shape[1]
    for unit, col in enumerate(units_of(feed_up)):
        if unit < units:
            feed_up[:, col] = wide(up[0, unit]) + wide(got_feed[unit])
            feed_down[:, col] = wide(down[0, unit]) + wide(got_feed[units + unit])
        else:
            feed_up[:, col] = wide(line_up[0, unit - units])
            feed_down[:, col] = wide(line_down[0, unit - units])
    mine = space_first.shape[1]
    half = space_out.shape[1]
    each = half // UNIT
    for unit in range(2 * mine):
        held = space_first[0, unit] if unit < mine else space_second[0, unit - mine]
        total = wide(held) + wide(got_space[unit])
        at = unit % each * UNIT
        if unit < 3 * each:
            space_in[unit // each, :, at : at + UNIT] = total
        else:
            space_out[:, at : at + UNIT] = total

    def line_total(at):
        return (wide(own[at]) + wide(got_1[at])) + (wide(got_2[at]) + wide(got_3[at]))

    for unit in range(5 * each):
        total = line_total(unit)
        at = unit % each * UNIT
        if unit < 3 * each:
            time_in[unit // each, :, at : at + UNIT] = total
        elif unit < 4 * each:
            time_out[:, at : at + UNIT] = total
        else:
            time_mixer[:, at : at + UNIT] = total
    share = feed_up.shape[0]
    parts = []
    for block in range(5 * each, own.shape[0]):
        total = line_total(block)
        parts += [total[at : at + VECTORS] for at in range(0, share, VECTORS)]
    settle_vectors(me[0, 0], jnp.concatenate(parts, axis=1), small)


def final_step(
    me, own, got_1, got_2, got_3, up, down, got_feed, line_up, line_down, space_first, space_second, got_space,
    width, half,
):
    share = width // 16
    units = (up.shape[1] + LINE_UNITS) * UNIT
    outs = [
        shape(dims, jnp.float32)
        for dims in (
            (3, share, half), (share, half), (share, half), (3, share, half), (share, half), (share, units),
            (share, units),
        )
    ]
    return plain_call(
        final_kernel,
        (
            me, own, got_1, got_2, got_3, up, down, got_feed, line_up, line_down, space_first, space_second,
            got_space,
        ),
        outs + small_shapes(share),
    )


def swap_tensor(field):
    size = lax.axis_size("tensor")
    return lax.ppermute(field, "tensor", [(i, i ^ 1) for i in range(size)])


def swap_dp(field, bits):
    return lax.ppermute(field, "dp", [(i, i ^ bits) for i in range(lax.axis_size("dp"))])


def pick(field, at):
    return lax.dynamic_index_in_dim(field, at, 0, keepdims=False)


def reduce_rows(field):
    size = lax.axis_size("dp")
    me = lax.axis_index("dp")
    span = size // 2
    while span >= 1:
        field = field.reshape((2, span, -1) + field.shape[-1:])
        bit = me // span % 2
        field = (wide(pick(field, bit)) + wide(swap_dp(pick(field, 1 - bit), span))).astype(LOW)
        span //= 2
    return wide(field.reshape(-1, field.shape[-1]))


def dp_sum(field):
    span = 1
    while span < lax.axis_size("dp"):
        field = field + swap_dp(field, span)
        span *= 2
    return field


def in_order(first, then):
    return lax.optimization_barrier((first, then))


def grad_of(left, right):
    return lax.dot_general(
        left.reshape(-1, left.shape[2]),
        right.reshape(-1, right.shape[2]),
        (((0,), (0,)), ((), ())),
        preferred_element_type=jnp.float32,
    ).astype(LOW)


def local(
    clips,
    cotangent,
    live,
    time_gain,
    time_shift,
    time_inproj,
    time_inbias,
    time_outproj,
    time_outbias,
    time_mixer,
    time_mixbias,
    space_gain,
    space_shift,
    space_inproj,
    space_inbias,
    space_outproj,
    space_outbias,
    feed_gain,
    feed_shift,
    feed_upward,
    feed_upbias,
    feed_down,
    feed_downbias,
):
    tokens, width = clips.shape[1:]
    half = time_outproj.shape[0]
    dests = lax.axis_size("dp")
    tensor_rank = lax.axis_index("tensor")
    paired = dests == 16
    me = lax.axis_index("dp").astype(jnp.int32).reshape(1, 1)
    present = live.astype(jnp.float32).reshape(1, 1)
    time_in = jnp.transpose(time_inproj, (1, 0, 2))
    space_in = jnp.transpose(space_inproj, (1, 0, 2))
    mixers = (time_mixer, swap_tensor(time_mixer), tensor_rank.astype(jnp.int32).reshape(1, 1))
    x, t_norm, t_qkv, t_probs, t_mixed, t_part = time_forward(
        clips[0], time_gain, time_shift, time_in, time_inbias, time_outproj
    )
    cot, g_downbias = cotangent_frames(cotangent[0], present)
    mixer_in, after_time, s_norm, s_qkv, s_probs, s_mixed, s_part = space_forward(
        t_part, swap_tensor(t_part), x, time_outbias, mixers, time_mixbias, space_gain, space_shift, space_in,
        space_inbias, space_outproj,
    )
    mid, f_norm, act, d_pre, f_part, df_part, g_upbias = feed(
        s_part, swap_tensor(s_part), after_time, cot, space_outbias, feed_gain, feed_shift, feed_upward, feed_upbias,
        feed_down,
    )
    if paired:
        feed_x, feed_y, feed_near, up, down, l_up, l_down = feed_gradient(me, f_norm, d_pre, cot, act)
        feed_x, mid = in_order(feed_x, mid)
        feed_x, feed_y, feed_near = swap_dp(feed_x, 1), swap_dp(feed_y, 2), swap_dp(feed_near, 4)
    d_space, s_back, ds_part, d_class, g_feed_gain, g_feed_shift, g_space_outbias, g_space_inbias = space_backward(
        df_part, swap_tensor(df_part), mid, cot, s_qkv, s_probs, feed_gain, space_outproj, space_in
    )
    if paired:
        ds_part, feed_x, feed_y, feed_near = lax.optimization_barrier((ds_part, feed_x, feed_y, feed_near))
        space_x, space_y, line_far, up, down, l_up, l_down, s_first, s_second = space_gradient(
            me, s_norm, s_back, d_space, s_mixed, up, down, l_up, l_down, feed_x, feed_y, feed_near
        )
        space_x, d_class = in_order(space_x, d_class)
        space_x, space_y, line_far = swap_dp(space_x, 1), swap_dp(space_y, 2), swap_dp(line_far, 8)
    result = result_tokens(f_part, swap_tensor(f_part), mid, feed_downbias, present, tokens)
    result, d_class = in_order(result, d_class)
    d_grid, d_mixer, d_mixed, d_source, g_space_gain, g_space_shift, g_mixbias, g_outbias = mixer_backward(
        ds_part, swap_tensor(ds_part), after_time, d_space, d_class, space_gain, mixers, time_outproj
    )
    if paired:
        mixer_x, mixer_y, feed_near, up, down, l_up, l_down, s_first, s_second, t_out, t_mixer = mixer_gradient(
            me, d_mixer, t_mixed, d_grid, mixer_in, up, down, l_up, l_down, s_first, s_second, space_x, space_y,
            line_far,
        )
        mixer_x, d_mixed = in_order(mixer_x, d_mixed)
        mixer_x, mixer_y, feed_near = swap_dp(mixer_x, 1), swap_dp(mixer_y, 2), swap_dp(feed_near, 4)
    if paired:
        dt_part, time_x, time_y, t_first, t_second, g_time_inbias = time_gradient(
            me, d_mixed, t_qkv, t_probs, time_in, t_norm
        )
        time_x, dt_part = in_order(time_x, dt_part)
        time_x, time_y = swap_dp(time_x, 1), swap_dp(time_y, 2)
        dt_part, mixer_x, mixer_y, feed_near = lax.optimization_barrier((dt_part, mixer_x, mixer_y, feed_near))
        space_near, feed_far, up, down, s_first, s_second = depth_step(
            me, up, down, s_first, s_second, mixer_x, mixer_y, feed_near
        )
        space_near, d_source = in_order(space_near, d_source)
        space_near, feed_far = swap_dp(space_near, 4), swap_dp(feed_far, 8)
    else:
        t_back, dt_part, g_time_inbias = time_backward(d_mixed, t_qkv, t_probs, time_in)
    grad_clips, vectors = source_gradient(
        dt_part, swap_tensor(dt_part), x, d_grid, d_source, time_gain,
        (
            g_outbias, g_mixbias, g_space_gain, g_space_shift, g_space_outbias, g_feed_gain, g_feed_shift, g_downbias,
            g_time_inbias, g_space_inbias, g_upbias,
        ),
        tokens,
    )
    if paired:
        feed_far, space_near, vectors = lax.optimization_barrier((feed_far, space_near, vectors))
        last_x, last_y, last_xy, space_far, s_first, s_second, *held = second_step(
            me, vectors, s_first, s_second, t_out, t_mixer, l_up, l_down, t_first, t_second, mixer_x, mixer_y,
            time_x, time_y, space_near,
        )
        last_x, last_y, last_xy = swap_dp(last_x, 1), swap_dp(last_y, 2), swap_dp(last_xy, 3)
        space_far = swap_dp(space_far, 8)
        space_far, last_xy = lax.optimization_barrier((space_far, last_xy))
        line_1, line_2, line_3, line_own, l_up, l_down = line_step(
            me, vectors, *held, last_x, last_y, last_xy
        )
        line_1, line_2, line_3 = swap_dp(line_1, 4), swap_dp(line_2, 8), swap_dp(line_3, 12)
        time_sum, out_sum, mixer_sum, space_sum, space_out, up_sum, down_sum, *small = final_step(
            me, line_own, line_1, line_2, line_3, up, down, feed_far, l_up, l_down, s_first, s_second, space_far,
            width, half,
        )
    else:

        def parts(field):
            return jnp.stack([field[:, part * half : (part + 1) * half] for part in range(3)])

        up_sum = reduce_rows(grad_of(f_norm, d_pre))
        down_sum = reduce_rows(grad_of(cot, act))
        space_sum = parts(reduce_rows(grad_of(s_norm, s_back)))
        space_out = reduce_rows(grad_of(d_space, s_mixed))
        time_sum = parts(reduce_rows(grad_of(t_norm, t_back)))
        out_sum = reduce_rows(grad_of(d_mixer, t_mixed))
        mixer_sum = reduce_rows(grad_of(d_grid, mixer_in))
        small = settle(dp_sum(vectors), me, dests)
    settled = (
        small[0],
        small[1],
        jnp.transpose(time_sum, (1, 0, 2)),
        small[10],
        out_sum.T,
        small[2],
        mixer_sum.T,
        small[3],
        small[4],
        small[5],
        jnp.transpose(space_sum, (1, 0, 2)),
        small[11],
        space_out.T,
        small[6],
        small[7],
        small[8],
        up_sum,
        small[12],
        down_sum.T,
        small[9],
    )
    return (result[None], grad_clips[None]) + settled


def solution(mesh):
    in_specs = (
        P("dp", None, None),
        P("dp", None, None),
        P("dp"),
        P(),
        P(),
        P(None, None, "tensor"),
        P(None, "tensor"),
        P("tensor", None),
        P(),
        P("tensor", None),
        P(),
        P(),
        P(),
        P(None, None, "tensor"),
        P(None, "tensor"),
        P("tensor", None),
        P(),
        P(),
        P(),
        P(None, "tensor"),
        P("tensor"),
        P("tensor", None),
        P(),
    )
    out_specs = (
        P("dp", None, None),
        P("dp", None, None),
        P("dp"),
        P("dp"),
        P("dp", None, "tensor"),
        P(None, ("tensor", "dp")),
        P("tensor", "dp"),
        P("dp"),
        P("tensor", "dp"),
        P("dp"),
        P("dp"),
        P("dp"),
        P("dp", None, "tensor"),
        P(None, ("tensor", "dp")),
        P("tensor", "dp"),
        P("dp"),
        P("dp"),
        P("dp"),
        P("dp", "tensor"),
        P(("tensor", "dp")),
        P("tensor", "dp"),
        P("dp"),
    )
    return jax.shard_map(local, mesh=mesh, in_specs=in_specs, out_specs=out_specs, check_vma=False)
```

```python
import functools

import jax
import jax.numpy as jnp
from jax import lax
from jax.experimental import pallas as pl
from jax.experimental.pallas import tpu as pltpu
from jax.sharding import PartitionSpec as P

HEAD = 64
FRAMES = 8
PLACES = 196
BLOCK = 16
ROWS = 208
BLOCKS = ROWS // BLOCK
PAIR = 2
UNROLL = BLOCKS
TIME_GROUP = 13
TIME_LAG = 1
SPACE_LAG = 6
EPS = 1e-06
LOW = jnp.bfloat16
VMEM_BYTES = 63 * 1024 * 1024 + 512 * 1024
COST = 1


def dot(left, right):
    return jnp.dot(left, right, preferred_element_type=jnp.float32)


def dot_last(left, right):
    return lax.dot_general(left, right, (((1,), (1,)), ((), ())), preferred_element_type=jnp.float32)


def normed(field):
    center = field - jnp.mean(field, axis=-1, keepdims=True)
    spread_sq = jnp.mean(center * center, axis=-1, keepdims=True)
    inverse = lax.rsqrt(spread_sq + EPS)
    return center * inverse, inverse


def normed_back(unit, inverse, grad_unit):
    first = jnp.mean(grad_unit, axis=-1, keepdims=True)
    second = jnp.mean(grad_unit * unit, axis=-1, keepdims=True)
    return (grad_unit - first - unit * second) * inverse


def side_by_side(weights):
    return jnp.concatenate([weights[part] for part in range(weights.shape[0])], axis=1)


def flat(field):
    return field.reshape((field.shape[0] * field.shape[1],) + field.shape[2:])


def wide(field):
    return field.astype(jnp.float32)


def iota(shape, axis):
    return lax.broadcasted_iota(jnp.int32, shape, axis)


def column_sum(field):
    return jnp.sum(field, axis=0, keepdims=True)


def call(kernel, grid, in_specs, out_specs, out_shapes, scratch, flops, args):
    moved = sum(a.size * a.dtype.itemsize for a in args) + sum(o.size * o.dtype.itemsize for o in out_shapes)
    return pl.pallas_call(
        kernel,
        grid=grid,
        in_specs=in_specs,
        out_specs=out_specs,
        out_shape=out_shapes,
        scratch_shapes=scratch,
        compiler_params=pltpu.CompilerParams(vmem_limit_bytes=VMEM_BYTES),
        cost_estimate=pl.CostEstimate(flops=int(flops) // COST, bytes_accessed=int(moved) // COST, transcendentals=0),
    )(*args)


SCALAR = pl.BlockSpec(memory_space=pltpu.SMEM)


def whole(array):
    zeros = (0,) * array.ndim
    return pl.BlockSpec(array.shape, lambda *at: zeros)


def shape(dims, kind=LOW):
    return jax.ShapeDtypeStruct(dims, kind)


def to_frames(rows, block):
    count = FRAMES * BLOCK
    at = iota((count, count + BLOCK), 0)
    source = 1 + FRAMES * (at % BLOCK) + at // BLOCK
    pick = jnp.where(source == iota((count, count + BLOCK), 1), 1.0, 0.0).astype(LOW)
    return dot(pick, rows)


def to_tokens(rows):
    count = FRAMES * BLOCK
    at = iota((count, count), 1)
    target = 1 + FRAMES * (at % BLOCK) + at // BLOCK
    pick = jnp.where(target == iota((count, count), 0), 1.0, 0.0).astype(LOW)
    return dot(pick, rows)


def fill_rows(source, tokens):
    count = tokens.shape[0]
    even = count // BLOCK * BLOCK
    source[0:even] = tokens[0:even]
    source[even:] = jnp.zeros((source.shape[0] - even, source.shape[1]), source.dtype)
    left = wide(tokens[even:count])
    tail = jnp.zeros((BLOCK, source.shape[1]), jnp.float32)
    for row in range(count - even):
        tail = tail + jnp.where(iota(tail.shape, 0) == row, left[row : row + 1], 0.0)
    source[even : even + BLOCK] = tail.astype(source.dtype)


def frame_rows(source, block, class_row, class_frames):
    count = FRAMES * BLOCK
    rows = to_frames(source[pl.ds(pl.multiple_of(block * count, count), count + BLOCK), :], block)
    at = iota((count, 1), 0)
    is_class = (block * BLOCK + at % BLOCK == PLACES) & (at // BLOCK < class_frames)
    return rows + jnp.where(is_class, class_row, 0.0)


class Copies:
    def __init__(self, semaphores):
        self.semaphores = semaphores
        self.started = []

    def start(self, source, target):
        copy = pltpu.make_async_copy(source, target, self.semaphores.at[len(self.started)])
        copy.start()
        self.started.append(copy)
        return copy


def time_forward_kernel(
    clips, gain, shift, inproj_far, inbias, outproj_far, x_far, norm_far, qkv_far, probs_far, mixed_far, part_far,
    inproj, outproj, x_out, norm_out, qkv_out, probs_out, mixed_out, part_out, source, semaphores,
):
    half = outproj.shape[0]
    copies = Copies(semaphores)
    fetched = [copies.start(inproj_far, inproj), copies.start(outproj_far, outproj)]
    fill_rows(source, clips)
    class_row = wide(clips[0:1])

    def first(block, carry):
        rows = frame_rows(source, block, class_row, FRAMES)
        unit, _ = normed(rows)
        at = pl.ds(pl.multiple_of(block * BLOCK, BLOCK), BLOCK)
        x_out[:, at, :] = rows.astype(LOW).reshape(FRAMES, BLOCK, rows.shape[1])
        norm_out[:, at, :] = (unit * vector(gain) + vector(shift)).astype(LOW).reshape(FRAMES, BLOCK, rows.shape[1])
        return carry

    lax.fori_loop(0, BLOCKS, first, 0, unroll=UNROLL)
    sent = [copies.start(x_out, x_far), copies.start(norm_out, norm_far)]
    fetched[0].wait()
    weights = side_by_side(inproj)
    for step in range(FRAMES // PAIR):
        at = pl.ds(step * PAIR, PAIR)
        qkv = heads_low(dot(flat(norm_out[at]), weights), inbias, half)
        qkv_out[at] = qkv.reshape(PAIR, ROWS, 3 * half)
    sent.append(copies.start(qkv_out, qkv_far))
    count = FRAMES * BLOCK
    same = iota((count, 2 * count), 0) % BLOCK == iota((count, 2 * count), 1) % BLOCK

    def third(first_block, count):
        ats = [
            pl.ds(pl.multiple_of((first_block + step) * BLOCK, BLOCK), BLOCK) for step in range(count)
        ]

        def keep(step, head, probs):
            probs_out[first_block + step, head] = probs

        mixed = attend(
            [flat(qkv_out[:, at, :]) for at in ats], lambda scores: jnp.where(same, scores, -1e30), keep, 2, TIME_LAG
        )
        for at, part in zip(ats, mixed):
            mixed_out[:, at, :] = part.reshape(FRAMES, BLOCK, half)

    by_blocks(third)
    sent += [copies.start(probs_out, probs_far), copies.start(mixed_out, mixed_far)]
    fetched[1].wait()
    for step in range(FRAMES // PAIR):
        at = pl.ds(step * PAIR, PAIR)
        part = dot(flat(mixed_out[at]), outproj[...]).astype(LOW)
        part_out[at] = part.reshape(PAIR, ROWS, part.shape[1])
        sent.append(copies.start(part_out.at[at], part_far.at[at]))
    for copy in sent:
        copy.wait()


def by_blocks(run):
    def step(at, carry):
        run(at * TIME_GROUP, TIME_GROUP)
        return carry

    lax.fori_loop(0, BLOCKS // TIME_GROUP, step, 0)
    if BLOCKS % TIME_GROUP:
        run(BLOCKS // TIME_GROUP * TIME_GROUP, BLOCKS % TIME_GROUP)


def heads_low(linear, inbias, half):
    query = ((linear[:, :half] + inbias[0:1]) * HEAD ** (-0.5)).astype(LOW)
    keys = linear[:, half : 2 * half].astype(LOW)
    values = (linear[:, 2 * half :] + inbias[1:2]).astype(LOW)
    return jnp.concatenate([query, keys, values], axis=1)


def beside(field_t, head):
    own = field_t[HEAD * head : HEAD * (head + 1)]
    none = jnp.zeros_like(own)
    return jnp.concatenate([own, none] if head % 2 == 0 else [none, own], axis=0)


def beside_all(field_t, heads):
    return jnp.concatenate([beside(field_t, head) for head in heads], axis=1)


def pair_of(field, head):
    start = head // 2 * 2 * HEAD
    return field[:, start : start + 2 * HEAD]


def head_rows(field_t, head):
    return field_t[HEAD * head : HEAD * (head + 1)]


def staged(count, stages, lag):
    held = [None] * count
    for step in range(count + lag * (len(stages) - 1)):
        for depth, stage in enumerate(stages):
            item = step - lag * depth
            if 0 <= item < count:
                held[item] = stage(item, held[item])
    return held


def attend(inputs, block_allowed, keep, group, lag):
    half = inputs[0].shape[1] // 3
    rows = inputs[0].shape[0]
    query_t = [qkv[:, :half].T for qkv in inputs]
    values_t = [qkv[:, 2 * half :].T for qkv in inputs]
    groups = half // HEAD // group

    def heads_of(item):
        first = item % groups * group
        return range(first, first + group)

    def score(item, held):
        block = item // groups
        keys = inputs[block][:, half : 2 * half]
        return dot(pair_of(keys, heads_of(item)[0]), beside_all(query_t[block], heads_of(item)))

    def weigh(item, scores):
        scores = block_allowed(scores)
        expon = jnp.exp(scores - jnp.max(scores, axis=0, keepdims=True))
        probs = (expon * (1.0 / column_sum(expon))).astype(LOW)
        for at, head in enumerate(heads_of(item)):
            keep(item // groups, head, probs[:, at * rows : (at + 1) * rows])
        return probs

    def mix(item, probs):
        return [
            dot(head_rows(values_t[item // groups], head), probs[:, at * rows : (at + 1) * rows])
            for at, head in enumerate(heads_of(item))
        ]

    mixed_t = staged(len(inputs) * groups, [score, weigh, mix], lag)
    out = []
    for block in range(len(inputs)):
        parts = [part for item in mixed_t[block * groups : (block + 1) * groups] for part in item]
        out.append(jnp.concatenate(parts, axis=0).T.astype(LOW))
    return out


def attend_back(inputs, probs_of, d_mixeds, group, lag):
    half = inputs[0].shape[1] // 3
    rows = inputs[0].shape[0]
    keys_t = [qkv[:, half : 2 * half].T for qkv in inputs]
    d_mixed_t = [d_mixed.T for d_mixed in d_mixeds]
    lane = iota((rows, 2 * HEAD), 1) < HEAD
    groups = half // HEAD // group

    def heads_of(item):
        first = item % groups * group
        return range(first, first + group)

    def score(item, held):
        block = item // groups
        values = inputs[block][:, 2 * half :]
        return dot(pair_of(values, heads_of(item)[0]), beside_all(d_mixed_t[block], heads_of(item)))

    def weigh(item, d_probs):
        probs_low = jnp.concatenate([probs_of(item // groups, head) for head in heads_of(item)], axis=1)
        probs = wide(probs_low)
        scaled = probs * d_probs
        d_scores = scaled - probs * column_sum(scaled)
        return probs_low, d_scores.astype(LOW)

    def halves(field):
        none = jnp.zeros_like(field)
        return jnp.concatenate([jnp.where(lane, field, none), jnp.where(lane, none, field)], axis=0)

    def mix(item, held):
        block = item // groups
        probs_low, d_scores = held
        d_query_t = [
            dot(head_rows(keys_t[block], head), d_scores[:, at * rows : (at + 1) * rows])
            for at, head in enumerate(heads_of(item))
        ]
        d_mixed = pair_of(d_mixeds[block], heads_of(item)[0])
        query = pair_of(inputs[block][:, :half], heads_of(item)[0])
        if group == 2:
            d_mixed = halves(d_mixed)
            query = halves(query)
        return d_query_t, dot(d_scores, query), dot(probs_low, d_mixed)

    made = staged(len(inputs) * groups, [score, weigh, mix], lag)

    def paired(fields):
        if group == 2:
            return fields
        return [jnp.where(lane, fields[at], fields[at + 1]) for at in range(0, len(fields), 2)]

    out = []
    for block in range(len(inputs)):
        own = made[block * groups : (block + 1) * groups]
        d_query = jnp.concatenate([part for item in own for part in item[0]], axis=0).T.astype(LOW) * HEAD ** (-0.5)
        d_keys = paired([item[1] for item in own])
        d_values = paired([item[2] for item in own])
        out.append(jnp.concatenate([d_query] + [d.astype(LOW) for d in d_keys + d_values], axis=1))
    return out


def time_forward(clips, gain, shift, inproj, inbias, outproj):
    tokens, width = clips.shape
    half = outproj.shape[0]
    heads = half // HEAD
    count = FRAMES * BLOCK
    args = (clips, gain, shift, inproj, inbias, outproj)
    outs = [
        shape((FRAMES, ROWS, width)),
        shape((FRAMES, ROWS, width)),
        shape((FRAMES, ROWS, 3 * half)),
        shape((BLOCKS, heads, count, count)),
        shape((FRAMES, ROWS, half)),
        shape((FRAMES, ROWS, width)),
    ]
    rows = FRAMES * ROWS
    near = [pltpu.VMEM(a.shape, a.dtype) for a in (inproj, outproj)] + [pltpu.VMEM(o.shape, o.dtype) for o in outs]
    far = pl.BlockSpec(memory_space=pl.ANY)
    return call(
        time_forward_kernel,
        (1,),
        [whole(clips), whole(gain), whole(shift), far, whole(inbias), far],
        [far] * 6,
        outs,
        near + [pltpu.VMEM((BLOCKS * count + BLOCK, width), LOW), pltpu.SemaphoreType.DMA((16,))],
        2 * rows * width * half * 5,
        args,
    )


def cotangent_kernel(cotangent, live, out, total, source):
    fill_rows(source, cotangent)
    present = live[0, 0]
    class_row = wide(cotangent[0:1])

    def first(block, carry):
        rows = frame_rows(source, block, class_row, 1) * present
        at = pl.ds(pl.multiple_of(block * BLOCK, BLOCK), BLOCK)
        out[:, at, :] = rows.astype(LOW).reshape(FRAMES, BLOCK, rows.shape[1])
        return carry + column_sum(rows)

    total[...] = lax.fori_loop(0, BLOCKS, first, jnp.zeros(total.shape, jnp.float32), unroll=UNROLL)


def cotangent_frames(cotangent, live):
    tokens, width = cotangent.shape
    args = (cotangent, live)
    outs = [shape((FRAMES, ROWS, width)), shape((1, width), jnp.float32)]
    return call(
        cotangent_kernel,
        (1,),
        [whole(cotangent), SCALAR],
        [whole(o) for o in outs],
        outs,
        [pltpu.VMEM((BLOCKS * FRAMES * BLOCK + BLOCK, width), LOW)],
        2 * FRAMES * ROWS * 128 * width,
        args,
    )


def vector(ref):
    return ref[...].reshape(1, -1)


def place_of(shape_of):
    return iota(shape_of, 0) % ROWS


def gather_mixer(own, other, rank, mixer):
    half = own.shape[0]

    @pl.when(pl.program_id(0) == 0)
    def _():
        mixer[pl.ds(pl.multiple_of(rank[0, 0] * half, half), half), :] = own[...]
        mixer[pl.ds(pl.multiple_of((1 - rank[0, 0]) * half, half), half), :] = other[...]


def space_forward_kernel(
    own, other, x, outbias, mixer_own, mixer_other, rank, mixbias, gain, shift, inproj, inbias, outproj,
    mixer_out, after_out, norm_out, qkv_out, probs_out, mixed_out, part_out, mixer,
):
    gather_mixer(mixer_own, mixer_other, rank, mixer)
    half = outproj.shape[0]
    width = outproj.shape[1]

    def spread(field):
        return field.astype(LOW).reshape(PAIR, ROWS, field.shape[1])

    mixer_in = (wide(flat(own[...]) + flat(other[...])) + vector(outbias)).astype(LOW)
    mixer_out[...] = spread(jnp.where(rank[0, 0] == 0, mixer_in[:, :half], mixer_in[:, half:]))
    branch = dot(mixer_in, mixer[...]) + vector(mixbias)
    after = wide(flat(x[...])) + jnp.where(place_of((PAIR * ROWS, 1)) < PLACES, branch, 0.0)
    after_out[...] = spread(after)
    unit, _ = normed(after)
    norm = (unit * vector(gain) + vector(shift)).astype(LOW)
    norm_out[...] = spread(norm)
    qkv = heads_low(dot(norm, side_by_side(inproj)), inbias, half)
    qkv_out[...] = spread(qkv)

    def allowed(scores):
        even = ROWS - BLOCK
        last = jnp.where(iota((BLOCK, ROWS), 0) <= PLACES - even, scores[even:], -1e30)
        return jnp.concatenate([scores[:even], last], axis=0)

    def keep(frame, head, probs):
        probs_out[frame, head] = probs

    frames = [qkv[frame * ROWS : (frame + 1) * ROWS] for frame in range(PAIR)]
    for frame, mixed in enumerate(attend(frames, allowed, keep, 1, SPACE_LAG)):
        mixed_out[frame] = mixed
    part_out[...] = spread(dot(flat(mixed_out[...]), outproj[...]))


def pairs(array):
    rest = (0,) * (array.ndim - 1)
    return pl.BlockSpec((PAIR,) + array.shape[1:], lambda at: (at,) + rest)


def space_forward(own, other, x, outbias, mixers, mixbias, gain, shift, inproj, inbias, outproj):
    width = x.shape[2]
    half = outproj.shape[0]
    heads = half // HEAD
    args = (own, other, x, outbias) + mixers + (mixbias, gain, shift, inproj, inbias, outproj)
    outs = [
        shape((FRAMES, ROWS, half)),
        shape((FRAMES, ROWS, width)),
        shape((FRAMES, ROWS, width)),
        shape((FRAMES, ROWS, 3 * half)),
        shape((FRAMES, heads, ROWS, ROWS)),
        shape((FRAMES, ROWS, half)),
        shape((FRAMES, ROWS, width)),
    ]
    return call(
        space_forward_kernel,
        (FRAMES // PAIR,),
        [pairs(a) for a in args[:3]] + [whole(a) for a in args[3:6]] + [SCALAR] + [whole(a) for a in args[7:]],
        [pairs(o) for o in outs],
        outs,
        [pltpu.VMEM((width, width), LOW)],
        2 * FRAMES * ROWS * width * half * 8,
        args,
    )


def last_block(count):
    return lambda array: pl.BlockSpec((count, BLOCK, array.shape[2]), lambda at: (0, BLOCKS - 1, 0))


CLASS_AT = PLACES - (BLOCKS - 1) * BLOCK


def feed_kernel(
    own, other, after, cot, own_last, other_last, after_last, outbias, gain, shift, upward, upbias, down,
    mid_out, norm_out, act_out, dpre_out, part_out, dnorm_out, upbias_out,
):
    step = pl.program_id(0)
    units = upward.shape[1]
    width = upward.shape[0]

    def spread(field):
        return field.astype(LOW).reshape(PAIR, ROWS, field.shape[1])

    class_branch = wide(own_last[...]) + wide(other_last[...])
    class_branch = jnp.sum(class_branch, axis=0)[CLASS_AT : CLASS_AT + 1] * (1.0 / FRAMES) + vector(outbias)
    at = iota((PAIR * ROWS, 1), 0)
    branch = wide(flat(own[...]) + flat(other[...])) + vector(outbias)
    is_class = (at == PLACES) & (step == 0)
    mid = jnp.where(at % ROWS < PLACES, wide(flat(after[...])) + branch, 0.0)
    mid = mid + jnp.where(is_class, wide(after_last[0])[CLASS_AT : CLASS_AT + 1] + class_branch, 0.0)
    mid_out[...] = spread(mid)
    unit, _ = normed(mid)
    norm = (unit * vector(gain) + vector(shift)).astype(LOW)
    norm_out[...] = spread(norm)
    grad = flat(cot[...])
    part = jnp.zeros((PAIR * ROWS, width), jnp.float32)
    d_norm = jnp.zeros((PAIR * ROWS, width), jnp.float32)
    share = units

    @pl.when(step == 0)
    def _():
        upbias_out[...] = jnp.zeros(upbias_out.shape, jnp.float32)

    for start in range(0, units, share):
        cols = slice(start, start + share)
        pre = dot(norm, upward[:, cols]) + vector(upbias)[:, cols]
        cumulative = 0.5 * (1.0 + lax.erf(pre * 0.5**0.5))
        slope = cumulative + pre * jnp.exp(-0.5 * pre * pre) * 0.3989422804014327
        act = (pre * cumulative).astype(LOW)
        act_out[:, :, cols] = spread(act)
        d_pre = (dot_last(grad, down[cols]) * slope).astype(LOW)
        dpre_out[:, :, cols] = spread(d_pre)
        upbias_out[:, cols] += column_sum(wide(d_pre))
        part = part + dot(act, down[cols])
        d_norm = d_norm + dot_last(d_pre, upward[:, cols])
    part_out[...] = spread(part)
    dnorm_out[...] = spread(d_norm)


def feed(own, other, after, cot, outbias, gain, shift, upward, upbias, down):
    width, units = upward.shape
    args = (own, other, after, cot, own, other, after, outbias, gain, shift, upward, upbias, down)
    outs = [
        shape((FRAMES, ROWS, width)),
        shape((FRAMES, ROWS, width)),
        shape((FRAMES, ROWS, units)),
        shape((FRAMES, ROWS, units)),
        shape((FRAMES, ROWS, width)),
        shape((FRAMES, ROWS, width)),
        shape((1, units), jnp.float32),
    ]
    tail = last_block(FRAMES)
    return call(
        feed_kernel,
        (FRAMES // PAIR,),
        [pairs(a) for a in args[:4]] + [tail(a) for a in args[4:7]] + [whole(a) for a in args[7:]],
        [pairs(o) for o in outs[:6]] + [whole(outs[6])],
        outs,
        [],
        2 * FRAMES * ROWS * width * units * 4,
        args,
    )


def space_backward_kernel(
    own, other, mid, cot, qkv, probs, own_last, other_last, mid_last, cot_last, gain, outproj, inproj,
    dspace_out, back_out, part_out, dclass_out, gain_out, shift_out, outbias_out, inbias_out,
):
    step = pl.program_id(0)
    half = outproj.shape[0]

    def spread(field):
        return field.astype(LOW).reshape(PAIR, ROWS, field.shape[1])

    def back(own_part, other_part, mid_part, cot_part):
        d_norm = wide(own_part + other_part)
        unit, inverse = normed(wide(mid_part))
        return wide(cot_part) + normed_back(unit, inverse, d_norm * vector(gain)), d_norm, d_norm * unit

    d_class = back(own_last[0], other_last[0], mid_last[0], cot_last[0])[0][CLASS_AT : CLASS_AT + 1]
    d_mid, d_shift, d_gain = back(flat(own[...]), flat(other[...]), flat(mid[...]), flat(cot[...]))
    place = place_of((PAIR * ROWS, 1))
    d_space = jnp.where(place < PLACES, d_mid, jnp.where(place == PLACES, d_class * (1.0 / FRAMES), 0.0))

    @pl.when(step == 0)
    def _():
        dclass_out[...] = d_class
        for ref in (gain_out, shift_out, outbias_out, inbias_out):
            ref[...] = jnp.zeros(ref.shape, jnp.float32)

    gain_out[...] += column_sum(d_gain)
    shift_out[...] += column_sum(d_shift)
    outbias_out[...] += column_sum(d_space)
    d_low = d_space.astype(LOW)
    dspace_out[...] = spread(d_low)
    d_mixed = dot_last(d_low, outproj[...]).astype(LOW)
    made = attend_back(
        [qkv[frame] for frame in range(PAIR)],
        lambda frame, head: probs[frame, head],
        [d_mixed[frame * ROWS : (frame + 1) * ROWS] for frame in range(PAIR)],
        1,
        SPACE_LAG,
    )
    for frame, part in enumerate(made):
        back_out[frame] = part
    backs = flat(back_out[...])
    inbias_out[...] += column_sum(wide(backs))
    part_out[...] = spread(dot_last(backs, side_by_side(inproj)))


def space_backward(own, other, mid, cot, qkv, probs, gain, outproj, inproj):
    width = mid.shape[2]
    half = outproj.shape[0]
    args = (own, other, mid, cot, qkv, probs, own, other, mid, cot, gain, outproj, inproj)
    outs = [
        shape((FRAMES, ROWS, width)),
        shape((FRAMES, ROWS, 3 * half)),
        shape((FRAMES, ROWS, width)),
        shape((1, width), jnp.float32),
        shape((1, width), jnp.float32),
        shape((1, width), jnp.float32),
        shape((1, width), jnp.float32),
        shape((1, 3 * half), jnp.float32),
    ]
    tail = last_block(1)
    return call(
        space_backward_kernel,
        (FRAMES // PAIR,),
        [pairs(a) for a in args[:6]] + [tail(a) for a in args[6:10]] + [whole(a) for a in args[10:]],
        [pairs(o) for o in outs[:3]] + [whole(o) for o in outs[3:]],
        outs,
        [],
        2 * FRAMES * ROWS * width * half * 6,
        args,
    )


def mixer_backward_kernel(
    own, other, after, dspace, dclass, gain, mixer_own, mixer_other, rank, outproj,
    dgrid_out, dmixer_out, dmixed_out, dsource_out, gain_out, shift_out, mixbias_out, outbias_out, mixer,
):
    gather_mixer(mixer_own, mixer_other, rank, mixer)

    @pl.when(pl.program_id(0) == 0)
    def _():
        dsource_out[...] = dclass[...]
        for ref in (gain_out, shift_out, mixbias_out, outbias_out):
            ref[...] = jnp.zeros(ref.shape, jnp.float32)

    def spread(field):
        return field.astype(LOW).reshape(PAIR, ROWS, field.shape[1])

    d_norm = wide(flat(own[...]) + flat(other[...]))
    unit, inverse = normed(wide(flat(after[...])))
    gain_out[...] += column_sum(d_norm * unit)
    shift_out[...] += column_sum(d_norm)
    d_space_in = normed_back(unit, inverse, d_norm * vector(gain))
    place = place_of((PAIR * ROWS, 1))
    dsource_out[...] += column_sum(jnp.where(place == PLACES, d_space_in, 0.0))
    d_grid = jnp.where(place < PLACES, d_space_in + wide(flat(dspace[...])), 0.0)
    mixbias_out[...] += column_sum(d_grid)
    d_low = d_grid.astype(LOW)
    dgrid_out[...] = spread(d_low)
    d_mixer = dot_last(d_low, mixer[...]).astype(LOW)
    dmixer_out[...] = spread(d_mixer)
    outbias_out[...] += column_sum(wide(d_mixer))
    dmixed_out[...] = spread(dot_last(d_mixer, outproj[...]))


def mixer_backward(own, other, after, dspace, dclass, gain, mixers, outproj):
    width = after.shape[2]
    half = outproj.shape[0]
    args = (own, other, after, dspace, dclass, gain) + mixers + (outproj,)
    outs = [
        shape((FRAMES, ROWS, width)),
        shape((FRAMES, ROWS, width)),
        shape((FRAMES, ROWS, half)),
    ] + [shape((1, width), jnp.float32)] * 5
    return call(
        mixer_backward_kernel,
        (FRAMES // PAIR,),
        [pairs(a) for a in args[:4]] + [whole(a) for a in args[4:8]] + [SCALAR, whole(outproj)],
        [pairs(o) for o in outs[:3]] + [whole(o) for o in outs[3:]],
        outs,
        [pltpu.VMEM((width, width), LOW)],
        2 * FRAMES * ROWS * width * half * 3,
        args,
    )


def near_far(arrays):
    return [pltpu.VMEM(a.shape, a.dtype) for a in arrays], pl.BlockSpec(memory_space=pl.ANY)


def places(first, last):
    return pl.ds(first * BLOCK, (last - first) * BLOCK)


TIME_GROUPS = ((0, 3), (3, 8), (8, BLOCKS))


def settle_copies(arrivals):
    for copy in arrivals:
        copy.wait()


def fetch_time(copies, far, near):
    coming = []
    for first, last in TIME_GROUPS:
        at = (places(first, last), pl.ds(first, last - first))
        arrivals = [copies.start(f.at[:, at[0], :], n.at[:, at[0], :]) for f, n in zip(far[:2], near[:2])]
        coming.append(arrivals + [copies.start(far[2].at[at[1]], near[2].at[at[1]])])
    return coming


def time_attention_back(group, d_mixed, qkv, probs, back_out):
    first, last = group
    ats = [places(block, block + 1) for block in range(first, last)]
    made = attend_back(
        [flat(qkv[:, at, :]) for at in ats],
        lambda step, head: probs[first + step, head],
        [flat(d_mixed[:, at, :]) for at in ats],
        2,
        TIME_LAG,
    )
    for at, part in zip(ats, made):
        back_out[:, at, :] = part.reshape(FRAMES, BLOCK, part.shape[1])


def time_part(copies, back_out, inproj, part_out, part_far, inbias_out):
    sent = []
    inbias = jnp.zeros(inbias_out.shape, jnp.float32)
    for step in range(FRAMES // PAIR):
        at = pl.ds(step * PAIR, PAIR)
        backs = flat(back_out[at])
        inbias = inbias + column_sum(wide(backs))
        part_out[at] = dot_last(backs, side_by_side(inproj)).astype(LOW).reshape(PAIR, ROWS, part_out.shape[2])
        sent.append(copies.start(part_out.at[at], part_far.at[at]))
    inbias_out[...] = inbias
    return sent


def time_backward_kernel(
    d_mixed_far, qkv_far, probs_far, inproj_far, back_far, part_far, inbias_out,
    d_mixed, qkv, probs, inproj, back_out, part_out, semaphores,
):
    copies = Copies(semaphores)
    coming = fetch_time(copies, (d_mixed_far, qkv_far, probs_far), (d_mixed, qkv, probs))
    weights = copies.start(inproj_far, inproj)
    for group, arrivals in zip(TIME_GROUPS, coming):
        settle_copies(arrivals)
        time_attention_back(group, d_mixed, qkv, probs, back_out)
    sent = [copies.start(back_out, back_far)]
    weights.wait()
    settle_copies(sent + time_part(copies, back_out, inproj, part_out, part_far, inbias_out))


def time_backward(d_mixed, qkv, probs, inproj):
    width = inproj.shape[1]
    half = d_mixed.shape[2]
    args = (d_mixed, qkv, probs, inproj)
    outs = [
        shape((FRAMES, ROWS, 3 * half)),
        shape((FRAMES, ROWS, width)),
        shape((1, 3 * half), jnp.float32),
    ]
    near, far = near_far(args + tuple(outs[:2]))
    return call(
        time_backward_kernel,
        (1,),
        [far] * 4,
        [far, far, whole(outs[2])],
        outs,
        near + [pltpu.SemaphoreType.DMA((3 * len(TIME_GROUPS) + 2 + FRAMES // PAIR,))],
        2 * FRAMES * ROWS * width * half * 5,
        args,
    )


def fetch_places(copies, far, near, groups):
    return [
        [copies.start(f.at[:, places(*group), :], n.at[:, places(*group), :]) for f, n in zip(far, near)]
        for group in groups
    ]


def put_tokens(out, block, low, carry):
    count = FRAMES * BLOCK
    moved = jnp.where(iota((count, 1), 0) == 0, carry, to_tokens(low))
    fits = min(out.shape[0] - block * count, count)
    out[block * count : block * count + fits] = moved[:fits].astype(out.dtype)
    return wide(low[count - BLOCK :])[BLOCK - 1 :]


def block_rows(ref, block):
    return wide(flat(ref[:, block * BLOCK : (block + 1) * BLOCK, :]))


def block_sum(own, other, block):
    at = places(block, block + 1)
    return wide(flat(own[:, at, :]) + flat(other[:, at, :]))


VECTORS = 16


SOURCE_GROUPS = ((0, 1), (1, 4), (4, 8), (8, BLOCKS))


def source_kernel(own_far, other_far, x_far, dgrid_far, dsource, gain, *rest):
    given = rest[:-7]
    out, packed, own, other, x, dgrid, semaphores = rest[-7:]
    width = packed.shape[1]
    coming = fetch_places(
        Copies(semaphores), (own_far, other_far, x_far, dgrid_far), (own, other, x, dgrid), SOURCE_GROUPS
    )
    carry = dsource[...]
    d_gain = jnp.zeros((1, width), jnp.float32)
    d_shift = jnp.zeros((1, width), jnp.float32)
    for (first, last), arrivals in zip(SOURCE_GROUPS, coming):
        for arrival in arrivals:
            arrival.wait()
        for block in range(first, last):
            d_norm = block_sum(own, other, block)
            unit, inverse = normed(block_rows(x, block))
            d_gain = d_gain + column_sum(d_norm * unit)
            d_shift = d_shift + column_sum(d_norm)
            rows = block_rows(dgrid, block) + normed_back(unit, inverse, d_norm * vector(gain))
            carry = put_tokens(out, block, rows.astype(LOW), carry)
    packed[...] = jnp.zeros(packed.shape, jnp.float32)
    packed[0:1] = d_gain
    packed[1:2] = d_shift
    at = 2
    for ref in given:
        count = ref.shape[1]
        if count == 3 * width // 2:
            packed[at : at + 1] = jnp.concatenate([ref[:, : width // 2], ref[:, width:]], axis=1)
            at += 1
            continue
        for start in range(0, count, width):
            packed[at : at + 1] = ref[:, start : start + width]
            at += 1


def source_gradient(own, other, x, dgrid, dsource, gain, given, tokens):
    width = x.shape[2]
    args = (own, other, x, dgrid, dsource, gain) + tuple(given)
    outs = [shape((tokens, width)), shape((VECTORS, width), jnp.float32)]
    near, far = near_far(args[:4])
    return call(
        source_kernel,
        (1,),
        [far] * 4 + [whole(a) for a in args[4:]],
        [whole(o) for o in outs],
        outs,
        near + [pltpu.SemaphoreType.DMA((4 * len(SOURCE_GROUPS),))],
        2 * FRAMES * ROWS * 128 * width,
        args,
    )


RESULT_GROUPS = ((BLOCKS - 1, BLOCKS), (0, 4), (4, 8), (8, BLOCKS - 1))


def result_kernel(own_far, other_far, mid_far, bias, live, out, own, other, mid, semaphores):
    present = live[0, 0]
    coming = fetch_places(Copies(semaphores), (own_far, other_far, mid_far), (own, other, mid), RESULT_GROUPS)

    def rows_of(block):
        total = block_rows(mid, block) + block_sum(own, other, block) + vector(bias)
        return (total * present).astype(LOW)

    for arrival in coming[0]:
        arrival.wait()
    last = rows_of(BLOCKS - 1)
    carry = wide(last[:BLOCK])[CLASS_AT : CLASS_AT + 1]
    for (first, end), arrivals in zip(RESULT_GROUPS[1:], coming[1:]):
        for arrival in arrivals:
            arrival.wait()
        for block in range(first, end):
            carry = put_tokens(out, block, rows_of(block), carry)
    put_tokens(out, BLOCKS - 1, last, carry)


def result_tokens(own, other, mid, bias, live, tokens):
    width = mid.shape[2]
    args = (own, other, mid, bias, live)
    outs = [shape((tokens, width))]
    near, far = near_far(args[:3])
    return call(
        result_kernel,
        (1,),
        [far] * 3 + [whole(bias), SCALAR],
        [whole(outs[0])],
        outs,
        near + [pltpu.SemaphoreType.DMA((3 * len(RESULT_GROUPS),))],
        2 * FRAMES * ROWS * 128 * width,
        args,
    )[0]


def settle_vectors(at, total, outs):
    width = total.shape[1]
    share = outs[0].shape[0]
    dests = width // share
    moved = pltpu.roll(total, (dests - at) % dests * share, 1)
    for row in range(10):
        outs[row][...] = moved[row, :share]
    small = share // 2
    moved = pltpu.roll(total, (2 * dests - at) % (2 * dests) * small, 1)
    for row in (10, 11):
        for part in range(2):
            start = part * (width // 2)
            outs[row][part : part + 1, :] = moved[row : row + 1, start : start + small]
    moved = pltpu.roll(total, (dests - 2 * at % dests) % dests * share, 1)
    outs[12][...] = jnp.where(2 * at < dests, moved[12, : 2 * share], moved[13, : 2 * share])


def small_shapes(share):
    outs = [shape((share,), jnp.float32)] * 10
    outs += [shape((2, share // 2), jnp.float32)] * 2
    return outs + [shape((2 * share,), jnp.float32)]


def settle_kernel(place, total, *outs):
    settle_vectors(place[0, 0], total[...], outs)


def settle(total, place, dests):
    outs = small_shapes(total.shape[1] // dests)
    return call(settle_kernel, (1,), [SCALAR, whole(total)], [whole(o) for o in outs], outs, [], 0, (place, total))


UNIT = 128


def bits_of(me):
    place = me[0, 0]
    return {"x": place % 2, "y": place // 2 % 2, "near": place // 4 % 2, "far": place // 8}


def pair_index(at, bit):
    return 2 * at + bit


def gap_index(at, bit):
    return at // 2 * 4 + 2 * bit + at % 2


def near_index(at, bit):
    return at // 4 * 8 + 4 * bit + at % 4


def top_index(half):
    return lambda at, bit: half * bit + at


def units_of(field):
    return [slice(at, at + UNIT) for at in range(0, field.shape[-1], UNIT)]


def split_gradient(field, axis, bits, message, start, keep):
    index = {"x": pair_index, "y": gap_index, "near": near_index}[axis]
    cols = units_of(field)
    for at in range(8):
        for unit, col in enumerate(cols):
            message[start + at * len(cols) + unit] = field[index(at, 1 - bits[axis]), :, col]
            keep[at, unit] = field[index(at, bits[axis]), :, col]


def split_total(held, got, got_start, bit, message, start, keep, index=pair_index):
    units = held.shape[1]

    def total(at):
        return (wide(held[at]) + wide(got[pl.ds(got_start + at * units, units)])).astype(LOW)

    for at in range(held.shape[0] // 2):
        message[start + at * units : start + (at + 1) * units] = total(index(at, 1 - bit))
        keep[at] = total(index(at, bit))


def put_gradient(field, left, right, start=0):
    step = 768 if right.shape[1] % 768 == 0 else 384
    for at in range(0, right.shape[1], step):
        part = lax.dot_general(
            left, right[:, at : at + step], (((0,), (0,)), ((), ())), preferred_element_type=jnp.float32
        )
        field[:, :, start + at : start + at + step] = part.astype(LOW).reshape(field.shape[:2] + (step,))


def gradient_call(body, args, outs, scratch, flops):
    inputs, width = args[1:], len(args) - 1

    def kernel(me, *refs):
        far, near = refs[: width + len(outs)], refs[width + len(outs) : 2 * (width + len(outs))]
        copies = Copies(refs[-1])
        waiting = [copies.start(source, target) for source, target in zip(far[:width], near[:width])]
        sent = []

        def need(*wanted):
            for ref in wanted:
                waiting[[ref is one for one in near].index(True)].wait()

        def done(*made):
            for ref in made:
                sent.append(copies.start(ref, far[[ref is one for one in near].index(True)]))

        body(need, done, me, *near, *refs[2 * (width + len(outs)) : -1])
        for copy in sent:
            copy.wait()

    remote = pl.BlockSpec(memory_space=pl.ANY)
    return call(
        kernel,
        (1,),
        [SCALAR] + [remote] * width,
        [remote] * len(outs),
        outs,
        [pltpu.VMEM(a.shape, a.dtype) for a in list(inputs) + outs]
        + scratch
        + [pltpu.SemaphoreType.DMA((width + len(outs),))],
        flops,
        args,
    )


def plain_call(kernel, args, outs):
    return call(
        kernel,
        (1,),
        [SCALAR] + [whole(a) for a in args[1:]],
        [whole(o) for o in outs],
        outs,
        [],
        0,
        args,
    )


LINE_UNITS = 4


def feed_gradient_kernel(
    need, done, me, norm, d_pre, cot, act,
    message_x, message_y, message_near, keep_up, keep_down, keep_line_up, keep_line_down, up, down,
):
    bits = bits_of(me)
    cut = keep_up.shape[1] * UNIT
    need(norm, d_pre)
    put_gradient(up, flat(norm[...]), flat(d_pre[...]))
    need(cot, act)
    put_gradient(down, flat(cot[...]), flat(act[...]))
    split_gradient(up.at[:, :, :cut], "x", bits, message_x, 0, keep_up)
    split_gradient(up.at[:, :, cut:], "near", bits, message_near, 0, keep_line_up)
    done(message_x, keep_up, keep_line_up)
    split_gradient(down.at[:, :, :cut], "y", bits, message_y, 0, keep_down)
    split_gradient(down.at[:, :, cut:], "near", bits, message_near, 8 * LINE_UNITS, keep_line_down)
    done(message_y, message_near, keep_down, keep_line_down)


def field_shape(dests, units, share):
    return shape((dests, units, share, UNIT))


def message_shape(blocks, share):
    return shape((blocks, share, UNIT))


def feed_gradient(me, norm, d_pre, cot, act):
    width = norm.shape[2]
    units = act.shape[2] // UNIT - LINE_UNITS
    share = width // 16
    outs = [message_shape(8 * units, share)] * 2 + [message_shape(16 * LINE_UNITS, share)]
    outs += [field_shape(8, units, share)] * 2 + [field_shape(8, LINE_UNITS, share)] * 2
    scratch = [pltpu.VMEM((16, share, act.shape[2]), LOW)] * 2
    return gradient_call(
        feed_gradient_kernel, (me, norm, d_pre, cot, act), outs, scratch, 4 * FRAMES * ROWS * width * act.shape[2]
    )


def space_gradient_kernel(
    need, done, me, norm, backs, d_space, mixed, up, got_x, down, got_y, line_up, line_down, got_near,
    message_x, message_y, message_far, keep_up, keep_down, keep_line_up, keep_line_down, keep_first, keep_second,
    first, second,
):
    bits = bits_of(me)
    count = 4 * up.shape[1]
    width = first.shape[2]
    need(norm, backs)
    rows = flat(norm[...])
    put_gradient(first, rows, flat(backs[...])[:, :width])
    put_gradient(second, rows, flat(backs[...])[:, width:])
    need(d_space, mixed)
    put_gradient(second, flat(d_space[...]), flat(mixed[...]), backs.shape[2] - width)
    need(up, got_x)
    split_total(up, got_x, 0, bits["y"], message_y, 0, keep_up)
    done(keep_up)
    split_gradient(first, "y", bits, message_y, count, keep_first)
    done(message_y, keep_first)
    need(down, got_y)
    split_total(down, got_y, 0, bits["x"], message_x, 0, keep_down)
    split_gradient(second, "x", bits, message_x, count, keep_second)
    done(message_x, keep_down, keep_second)
    need(line_up, line_down, got_near)
    split_total(line_up, got_near, 0, bits["far"], message_far, 0, keep_line_up, top_index(4))
    split_total(
        line_down, got_near, 8 * LINE_UNITS, bits["far"], message_far, 4 * LINE_UNITS, keep_line_down, top_index(4)
    )
    done(message_far, keep_line_up, keep_line_down)


def space_gradient(me, norm, backs, d_space, mixed, up, down, line_up, line_down, got_x, got_y, got_near):
    width = norm.shape[2]
    half = mixed.shape[2]
    share = width // 16
    units = up.shape[1]
    own = 2 * half // UNIT
    outs = [message_shape(4 * units + 8 * own, share)] * 2 + [message_shape(8 * LINE_UNITS, share)]
    outs += [field_shape(4, units, share)] * 2 + [field_shape(4, LINE_UNITS, share)] * 2
    outs += [field_shape(8, own, share)] * 2
    scratch = [pltpu.VMEM((16, share, 2 * half), LOW)] * 2
    return gradient_call(
        space_gradient_kernel,
        (me, norm, backs, d_space, mixed, up, got_x, down, got_y, line_up, line_down, got_near),
        outs,
        scratch,
        8 * FRAMES * ROWS * width * half,
    )


def mixer_gradient_kernel(
    need, done, me, d_mixer, mixed, d_grid, mixer_in, up, got_y, down, got_x, space_first, space_second,
    line_up, line_down, got_far,
    message_x, message_y, message_near, keep_up, keep_down, keep_line_up, keep_line_down, keep_first, keep_second,
    keep_out, keep_mixer, out, mixer,
):
    bits = bits_of(me)
    units = up.shape[1]
    feed = 4 * units
    own = space_first.shape[1]
    need(d_mixer, mixed)
    put_gradient(out, flat(d_mixer[...]), flat(mixed[...]))
    need(d_grid, mixer_in)
    put_gradient(mixer, flat(d_grid[...]), flat(mixer_in[...]))
    need(up, got_y)
    split_total(up, got_y, 0, bits["near"], message_near, 0, keep_up)
    need(down, got_x)
    split_total(down, got_x, 0, bits["near"], message_near, 2 * units, keep_down)
    done(message_near, keep_up, keep_down)
    need(space_first, space_second)
    split_total(space_first, got_y, feed, bits["x"], message_x, 0, keep_first)
    split_total(space_second, got_x, feed, bits["y"], message_y, 0, keep_second)
    split_gradient(out, "x", bits, message_x, 4 * own, keep_out)
    split_gradient(mixer, "y", bits, message_y, 4 * own, keep_mixer)
    need(line_up, line_down, got_far)
    line = 4 * own + 8 * keep_out.shape[1]
    split_total(line_up, got_far, 0, bits["x"], message_x, line, keep_line_up)
    split_total(line_down, got_far, 4 * LINE_UNITS, bits["y"], message_y, line, keep_line_down, top_index(2))
    done(message_x, message_y, keep_line_up, keep_line_down, keep_first, keep_second, keep_out, keep_mixer)


def mixer_gradient(
    me, d_mixer, mixed, d_grid, mixer_in, up, down, line_up, line_down, space_first, space_second, got_x, got_y, got_far
):
    width = d_grid.shape[2]
    half = mixed.shape[2]
    share = width // 16
    units, own, new = up.shape[1], space_first.shape[1], half // UNIT
    outs = [message_shape(4 * own + 8 * new + 2 * LINE_UNITS, share)] * 2 + [message_shape(4 * units, share)]
    outs += [field_shape(2, units, share)] * 2 + [field_shape(2, LINE_UNITS, share)] * 2
    outs += [field_shape(4, own, share)] * 2 + [field_shape(8, new, share)] * 2
    scratch = [pltpu.VMEM((16, share, half), LOW)] * 2
    return gradient_call(
        mixer_gradient_kernel,
        (
            me, d_mixer, mixed, d_grid, mixer_in, up, got_y, down, got_x, space_first, space_second,
            line_up, line_down, got_far,
        ),
        outs,
        scratch,
        4 * FRAMES * ROWS * width * half,
    )


TIME_FIRST = 5


def time_gradient_kernel(
    me, d_mixed_far, qkv_far, probs_far, inproj_far, norm_far, *rest,
):
    outs_far, inbias_out = rest[:5], rest[5]
    d_mixed, qkv, probs, inproj, norm = rest[6:11]
    outs = rest[11:16]
    part_out, message_x, message_y, keep_first, keep_second = outs
    back_out, both, semaphores = rest[16:]
    copies = Copies(semaphores)
    coming = fetch_time(copies, (d_mixed_far, qkv_far, probs_far), (d_mixed, qkv, probs))
    weights = [copies.start(inproj_far, inproj), copies.start(norm_far, norm)]
    for group, arrivals in zip(TIME_GROUPS, coming):
        settle_copies(arrivals)
        time_attention_back(group, d_mixed, qkv, probs, back_out)
    settle_copies(weights)
    bits = bits_of(me)
    put_gradient(both, flat(norm[...]), flat(back_out[...]))
    cut = TIME_FIRST * UNIT
    split_gradient(both.at[:, :, :cut], "y", bits, message_y, 0, keep_first)
    split_gradient(both.at[:, :, cut:], "x", bits, message_x, 0, keep_second)
    sent = [copies.start(near, far) for near, far in zip(outs[1:], outs_far[1:])]
    sent += time_part(copies, back_out, inproj, part_out, outs_far[0], inbias_out)
    settle_copies(sent)


def time_gradient(me, d_mixed, qkv, probs, inproj, norm):
    width = norm.shape[2]
    half = d_mixed.shape[2]
    share = width // 16
    last = 3 * half // UNIT - TIME_FIRST
    args = (me, d_mixed, qkv, probs, inproj, norm)
    outs = [
        shape((FRAMES, ROWS, width)),
        message_shape(8 * last, share),
        message_shape(8 * TIME_FIRST, share),
        field_shape(8, TIME_FIRST, share),
        field_shape(8, last, share),
        shape((1, 3 * half), jnp.float32),
    ]
    near, far = near_far(args[1:] + tuple(outs[:5]))
    scratch = [pltpu.VMEM((FRAMES, ROWS, 3 * half), LOW), pltpu.VMEM((16, share, 3 * half), LOW)]
    return call(
        time_gradient_kernel,
        (1,),
        [SCALAR] + [far] * 5,
        [far] * 5 + [whole(outs[5])],
        outs,
        near + scratch + [pltpu.SemaphoreType.DMA((3 * len(TIME_GROUPS) + 6 + FRAMES // PAIR,))],
        2 * FRAMES * ROWS * width * half * 8,
        args,
    )


def depth_kernel(
    me, up, down, space_first, space_second, got_x, got_y, got_near,
    message_near, message_far, keep_up, keep_down, keep_first, keep_second,
):
    bits = bits_of(me)
    units, own = up.shape[1], space_first.shape[1]
    split_total(space_first, got_x, 0, bits["near"], message_near, 0, keep_first)
    split_total(space_second, got_y, 0, bits["near"], message_near, 2 * own, keep_second)
    split_total(up, got_near, 0, bits["far"], message_far, 0, keep_up)
    split_total(down, got_near, 2 * units, bits["far"], message_far, units, keep_down)


def depth_step(me, up, down, space_first, space_second, got_x, got_y, got_near):
    units, own, share = up.shape[1], space_first.shape[1], up.shape[2]
    outs = [message_shape(4 * own, share), message_shape(2 * units, share)]
    outs += [field_shape(1, units, share)] * 2 + [field_shape(2, own, share)] * 2
    return plain_call(depth_kernel, (me, up, down, space_first, space_second, got_x, got_y, got_near), outs)


def vector_blocks(vectors, share):
    parts = [vectors[:, col].astype(LOW) for col in units_of(vectors)]
    each = share // VECTORS
    return [jnp.concatenate(parts[at : at + each], axis=0) for at in range(0, len(parts), each)]


def second_kernel(
    me, vectors, space_first, space_second, out, mixer, line_up, line_down, first, second,
    old_x, old_y, got_x, got_y, got_near,
    message_x, message_y, message_xy, message_far,
    keep_space_first, keep_space_second, keep_out, keep_mixer, keep_line_up, keep_line_down, keep_first, keep_second,
):
    bits = bits_of(me)
    own, new = space_first.shape[1], out.shape[1]
    share = first.shape[2]
    split_total(first, got_y, 0, bits["x"], message_x, 0, keep_first)
    split_total(second, got_x, 0, bits["y"], message_y, 0, keep_second)
    start_x, start_y = 4 * first.shape[1], 4 * second.shape[1]
    for at, block in enumerate(vector_blocks(vectors[...], share)):
        message_x[start_x + at] = block
        message_y[start_y + at] = block
        message_xy[at] = block
    start_x, start_y = start_x + message_xy.shape[0], start_y + message_xy.shape[0]
    split_total(out, old_x, 4 * own, bits["y"], message_y, start_y, keep_out)
    split_total(mixer, old_y, 4 * own, bits["x"], message_x, start_x, keep_mixer)
    line = 4 * own + 8 * new
    split_total(line_up, old_x, line, bits["y"], message_y, start_y + 4 * new, keep_line_up)
    split_total(line_down, old_y, line, bits["x"], message_x, start_x + 4 * new, keep_line_down)
    split_total(space_first, got_near, 0, bits["far"], message_far, 0, keep_space_first)
    split_total(space_second, got_near, 2 * own, bits["far"], message_far, own, keep_space_second)


def second_step(
    me, vectors, space_first, space_second, out, mixer, line_up, line_down, first, second,
    old_x, old_y, got_x, got_y, got_near,
):
    own, new, share = space_first.shape[1], out.shape[1], first.shape[2]
    extra = vectors.size // (share * UNIT)
    more = extra + 4 * new + LINE_UNITS
    outs = [
        message_shape(4 * first.shape[1] + more, share),
        message_shape(4 * second.shape[1] + more, share),
        message_shape(extra, share),
        message_shape(2 * own, share),
    ]
    outs += [field_shape(1, own, share)] * 2 + [field_shape(4, new, share)] * 2 + [field_shape(1, LINE_UNITS, share)] * 2
    outs += [field_shape(4, first.shape[1], share), field_shape(4, second.shape[1], share)]
    return plain_call(
        second_kernel,
        (
            me, vectors, space_first, space_second, out, mixer, line_up, line_down, first, second,
            old_x, old_y, got_x, got_y, got_near,
        ),
        outs,
    )


def line_kernel(
    me, vectors, out, mixer, line_up, line_down, first, second, got_x, got_y, got_xy,
    message_1, message_2, message_3, own, sum_line_up, sum_line_down,
):
    bits = bits_of(me)
    share = first.shape[2]
    new, extra = out.shape[1], got_xy.shape[0]
    place = 2 * bits["far"] + bits["near"]
    messages = (own, message_1, message_2, message_3)
    firsts, seconds = 4 * first.shape[1], 4 * second.shape[1]
    start = 0
    for held, got, at in (
        (first, got_x, 0), (second, got_y, 0), (out, got_y, seconds + extra), (mixer, got_x, firsts + extra),
    ):
        units = held.shape[1]
        for step, message in enumerate(messages):
            dest = place + step - 2 * (place & step)
            total = wide(held[dest]) + wide(got[pl.ds(at + dest * units, units)])
            message[start : start + units] = total.astype(LOW)
        start += units
    for at, block in enumerate(vector_blocks(vectors[...], share)):
        total = (wide(block) + wide(got_xy[at])) + (wide(got_x[firsts + at]) + wide(got_y[seconds + at]))
        for message in messages:
            message[start + at] = total.astype(LOW)
    line_x, line_y = firsts + extra + 4 * new, seconds + extra + 4 * new
    sum_line_up[0] = (wide(line_up[0]) + wide(got_y[line_y:])).astype(LOW)
    sum_line_down[0] = (wide(line_down[0]) + wide(got_x[line_x:])).astype(LOW)


def line_step(me, vectors, out, mixer, line_up, line_down, first, second, got_x, got_y, got_xy):
    share = first.shape[2]
    blocks = first.shape[1] + second.shape[1] + out.shape[1] + mixer.shape[1] + vectors.size // (share * UNIT)
    return plain_call(
        line_kernel,
        (me, vectors, out, mixer, line_up, line_down, first, second, got_x, got_y, got_xy),
        [message_shape(blocks, share)] * 4 + [field_shape(1, LINE_UNITS, share)] * 2,
    )


def final_kernel(
    me, own, got_1, got_2, got_3, up, down, got_feed, line_up, line_down, space_first, space_second, got_space,
    time_in, time_out, time_mixer, space_in, space_out, feed_up, feed_down, *small,
):
    units = up.shape[1]
    for unit, col in enumerate(units_of(feed_up)):
        if unit < units:
            feed_up[:, col] = wide(up[0, unit]) + wide(got_feed[unit])
            feed_down[:, col] = wide(down[0, unit]) + wide(got_feed[units + unit])
        else:
            feed_up[:, col] = wide(line_up[0, unit - units])
            feed_down[:, col] = wide(line_down[0, unit - units])
    mine = space_first.shape[1]
    half = space_out.shape[1]
    each = half // UNIT
    for unit in range(2 * mine):
        held = space_first[0, unit] if unit < mine else space_second[0, unit - mine]
        total = wide(held) + wide(got_space[unit])
        at = unit % each * UNIT
        if unit < 3 * each:
            space_in[unit // each, :, at : at + UNIT] = total
        else:
            space_out[:, at : at + UNIT] = total

    def line_total(at):
        return (wide(own[at]) + wide(got_1[at])) + (wide(got_2[at]) + wide(got_3[at]))

    for unit in range(5 * each):
        total = line_total(unit)
        at = unit % each * UNIT
        if unit < 3 * each:
            time_in[unit // each, :, at : at + UNIT] = total
        elif unit < 4 * each:
            time_out[:, at : at + UNIT] = total
        else:
            time_mixer[:, at : at + UNIT] = total
    share = feed_up.shape[0]
    parts = []
    for block in range(5 * each, own.shape[0]):
        total = line_total(block)
        parts += [total[at : at + VECTORS] for at in range(0, share, VECTORS)]
    settle_vectors(me[0, 0], jnp.concatenate(parts, axis=1), small)


def final_step(
    me, own, got_1, got_2, got_3, up, down, got_feed, line_up, line_down, space_first, space_second, got_space,
    width, half,
):
    share = width // 16
    units = (up.shape[1] + LINE_UNITS) * UNIT
    outs = [
        shape(dims, jnp.float32)
        for dims in (
            (3, share, half), (share, half), (share, half), (3, share, half), (share, half), (share, units),
            (share, units),
        )
    ]
    return plain_call(
        final_kernel,
        (
            me, own, got_1, got_2, got_3, up, down, got_feed, line_up, line_down, space_first, space_second,
            got_space,
        ),
        outs + small_shapes(share),
    )


def swap_tensor(field):
    size = lax.axis_size("tensor")
    return lax.ppermute(field, "tensor", [(i, i ^ 1) for i in range(size)])


def swap_dp(field, bits):
    return lax.ppermute(field, "dp", [(i, i ^ bits) for i in range(lax.axis_size("dp"))])


def pick(field, at):
    return lax.dynamic_index_in_dim(field, at, 0, keepdims=False)


def reduce_rows(field):
    size = lax.axis_size("dp")
    me = lax.axis_index("dp")
    span = size // 2
    while span >= 1:
        field = field.reshape((2, span, -1) + field.shape[-1:])
        bit = me // span % 2
        field = (wide(pick(field, bit)) + wide(swap_dp(pick(field, 1 - bit), span))).astype(LOW)
        span //= 2
    return wide(field.reshape(-1, field.shape[-1]))


def dp_sum(field):
    span = 1
    while span < lax.axis_size("dp"):
        field = field + swap_dp(field, span)
        span *= 2
    return field


def in_order(first, then):
    return lax.optimization_barrier((first, then))


def grad_of(left, right):
    return lax.dot_general(
        left.reshape(-1, left.shape[2]),
        right.reshape(-1, right.shape[2]),
        (((0,), (0,)), ((), ())),
        preferred_element_type=jnp.float32,
    ).astype(LOW)


def local(
    clips,
    cotangent,
    live,
    time_gain,
    time_shift,
    time_inproj,
    time_inbias,
    time_outproj,
    time_outbias,
    time_mixer,
    time_mixbias,
    space_gain,
    space_shift,
    space_inproj,
    space_inbias,
    space_outproj,
    space_outbias,
    feed_gain,
    feed_shift,
    feed_upward,
    feed_upbias,
    feed_down,
    feed_downbias,
):
    tokens, width = clips.shape[1:]
    half = time_outproj.shape[0]
    dests = lax.axis_size("dp")
    tensor_rank = lax.axis_index("tensor")
    paired = dests == 16
    me = lax.axis_index("dp").astype(jnp.int32).reshape(1, 1)
    present = live.astype(jnp.float32).reshape(1, 1)
    time_in = jnp.transpose(time_inproj, (1, 0, 2))
    space_in = jnp.transpose(space_inproj, (1, 0, 2))
    mixers = (time_mixer, swap_tensor(time_mixer), tensor_rank.astype(jnp.int32).reshape(1, 1))
    x, t_norm, t_qkv, t_probs, t_mixed, t_part = time_forward(
        clips[0], time_gain, time_shift, time_in, time_inbias, time_outproj
    )
    cot, g_downbias = cotangent_frames(cotangent[0], present)
    mixer_in, after_time, s_norm, s_qkv, s_probs, s_mixed, s_part = space_forward(
        t_part, swap_tensor(t_part), x, time_outbias, mixers, time_mixbias, space_gain, space_shift, space_in,
        space_inbias, space_outproj,
    )
    mid, f_norm, act, d_pre, f_part, df_part, g_upbias = feed(
        s_part, swap_tensor(s_part), after_time, cot, space_outbias, feed_gain, feed_shift, feed_upward, feed_upbias,
        feed_down,
    )
    if paired:
        feed_x, feed_y, feed_near, up, down, l_up, l_down = feed_gradient(me, f_norm, d_pre, cot, act)
        feed_x, mid = in_order(feed_x, mid)
        feed_x, feed_y, feed_near = swap_dp(feed_x, 1), swap_dp(feed_y, 2), swap_dp(feed_near, 4)
    d_space, s_back, ds_part, d_class, g_feed_gain, g_feed_shift, g_space_outbias, g_space_inbias = space_backward(
        df_part, swap_tensor(df_part), mid, cot, s_qkv, s_probs, feed_gain, space_outproj, space_in
    )
    if paired:
        ds_part, feed_x, feed_y, feed_near = lax.optimization_barrier((ds_part, feed_x, feed_y, feed_near))
        space_x, space_y, line_far, up, down, l_up, l_down, s_first, s_second = space_gradient(
            me, s_norm, s_back, d_space, s_mixed, up, down, l_up, l_down, feed_x, feed_y, feed_near
        )
        space_x, d_class = in_order(space_x, d_class)
        space_x, space_y, line_far = swap_dp(space_x, 1), swap_dp(space_y, 2), swap_dp(line_far, 8)
    result = result_tokens(f_part, swap_tensor(f_part), mid, feed_downbias, present, tokens)
    result, d_class = in_order(result, d_class)
    d_grid, d_mixer, d_mixed, d_source, g_space_gain, g_space_shift, g_mixbias, g_outbias = mixer_backward(
        ds_part, swap_tensor(ds_part), after_time, d_space, d_class, space_gain, mixers, time_outproj
    )
    if paired:
        mixer_x, mixer_y, feed_near, up, down, l_up, l_down, s_first, s_second, t_out, t_mixer = mixer_gradient(
            me, d_mixer, t_mixed, d_grid, mixer_in, up, down, l_up, l_down, s_first, s_second, space_x, space_y,
            line_far,
        )
        mixer_x, d_mixed = in_order(mixer_x, d_mixed)
        mixer_x, mixer_y, feed_near = swap_dp(mixer_x, 1), swap_dp(mixer_y, 2), swap_dp(feed_near, 4)
    if paired:
        dt_part, time_x, time_y, t_first, t_second, g_time_inbias = time_gradient(
            me, d_mixed, t_qkv, t_probs, time_in, t_norm
        )
        time_x, dt_part = in_order(time_x, dt_part)
        time_x, time_y = swap_dp(time_x, 1), swap_dp(time_y, 2)
        dt_part, mixer_x, mixer_y, feed_near = lax.optimization_barrier((dt_part, mixer_x, mixer_y, feed_near))
        space_near, feed_far, up, down, s_first, s_second = depth_step(
            me, up, down, s_first, s_second, mixer_x, mixer_y, feed_near
        )
        space_near, d_source = in_order(space_near, d_source)
        space_near, feed_far = swap_dp(space_near, 4), swap_dp(feed_far, 8)
    else:
        t_back, dt_part, g_time_inbias = time_backward(d_mixed, t_qkv, t_probs, time_in)
    grad_clips, vectors = source_gradient(
        dt_part, swap_tensor(dt_part), x, d_grid, d_source, time_gain,
        (
            g_outbias, g_mixbias, g_space_gain, g_space_shift, g_space_outbias, g_feed_gain, g_feed_shift, g_downbias,
            g_time_inbias, g_space_inbias, g_upbias,
        ),
        tokens,
    )
    if paired:
        feed_far, space_near, vectors = lax.optimization_barrier((feed_far, space_near, vectors))
        last_x, last_y, last_xy, space_far, s_first, s_second, *held = second_step(
            me, vectors, s_first, s_second, t_out, t_mixer, l_up, l_down, t_first, t_second, mixer_x, mixer_y,
            time_x, time_y, space_near,
        )
        last_x, last_y, last_xy = swap_dp(last_x, 1), swap_dp(last_y, 2), swap_dp(last_xy, 3)
        space_far = swap_dp(space_far, 8)
        space_far, last_xy = lax.optimization_barrier((space_far, last_xy))
        line_1, line_2, line_3, line_own, l_up, l_down = line_step(
            me, vectors, *held, last_x, last_y, last_xy
        )
        line_1, line_2, line_3 = swap_dp(line_1, 4), swap_dp(line_2, 8), swap_dp(line_3, 12)
        time_sum, out_sum, mixer_sum, space_sum, space_out, up_sum, down_sum, *small = final_step(
            me, line_own, line_1, line_2, line_3, up, down, feed_far, l_up, l_down, s_first, s_second, space_far,
            width, half,
        )
    else:

        def parts(field):
            return jnp.stack([field[:, part * half : (part + 1) * half] for part in range(3)])

        up_sum = reduce_rows(grad_of(f_norm, d_pre))
        down_sum = reduce_rows(grad_of(cot, act))
        space_sum = parts(reduce_rows(grad_of(s_norm, s_back)))
        space_out = reduce_rows(grad_of(d_space, s_mixed))
        time_sum = parts(reduce_rows(grad_of(t_norm, t_back)))
        out_sum = reduce_rows(grad_of(d_mixer, t_mixed))
        mixer_sum = reduce_rows(grad_of(d_grid, mixer_in))
        small = settle(dp_sum(vectors), me, dests)
    settled = (
        small[0],
        small[1],
        jnp.transpose(time_sum, (1, 0, 2)),
        small[10],
        out_sum.T,
        small[2],
        mixer_sum.T,
        small[3],
        small[4],
        small[5],
        jnp.transpose(space_sum, (1, 0, 2)),
        small[11],
        space_out.T,
        small[6],
        small[7],
        small[8],
        up_sum,
        small[12],
        down_sum.T,
        small[9],
    )
    return (result[None], grad_clips[None]) + settled


def solution(mesh):
    in_specs = (
        P("dp", None, None),
        P("dp", None, None),
        P("dp"),
        P(),
        P(),
        P(None, None, "tensor"),
        P(None, "tensor"),
        P("tensor", None),
        P(),
        P("tensor", None),
        P(),
        P(),
        P(),
        P(None, None, "tensor"),
        P(None, "tensor"),
        P("tensor", None),
        P(),
        P(),
        P(),
        P(None, "tensor"),
        P("tensor"),
        P("tensor", None),
        P(),
    )
    out_specs = (
        P("dp", None, None),
        P("dp", None, None),
        P("dp"),
        P("dp"),
        P("dp", None, "tensor"),
        P(None, ("tensor", "dp")),
        P("tensor", "dp"),
        P("dp"),
        P("tensor", "dp"),
        P("dp"),
        P("dp"),
        P("dp"),
        P("dp", None, "tensor"),
        P(None, ("tensor", "dp")),
        P("tensor", "dp"),
        P("dp"),
        P("dp"),
        P("dp"),
        P("dp", "tensor"),
        P(("tensor", "dp")),
        P("tensor", "dp"),
        P("dp"),
    )
    return jax.shard_map(local, mesh=mesh, in_specs=in_specs, out_specs=out_specs, check_vma=False)
```

```python
import functools

import jax
import jax.numpy as jnp
from jax import lax
from jax.experimental import pallas as pl
from jax.experimental.pallas import tpu as pltpu
from jax.sharding import PartitionSpec as P

HEAD = 64
FRAMES = 8
PLACES = 196
BLOCK = 16
ROWS = 208
BLOCKS = ROWS // BLOCK
PAIR = 2
UNROLL = BLOCKS
TIME_GROUP = 13
TIME_LAG = 1
SPACE_LAG = 6
EPS = 1e-06
LOW = jnp.bfloat16
VMEM_BYTES = 64 * 1024 * 1024 - 64 * 1024
COST = 1


def dot(left, right):
    return jnp.dot(left, right, preferred_element_type=jnp.float32)


def dot_last(left, right):
    return lax.dot_general(left, right, (((1,), (1,)), ((), ())), preferred_element_type=jnp.float32)


def normed(field):
    center = field - jnp.mean(field, axis=-1, keepdims=True)
    spread_sq = jnp.mean(center * center, axis=-1, keepdims=True)
    inverse = lax.rsqrt(spread_sq + EPS)
    return center * inverse, inverse


def normed_back(unit, inverse, grad_unit):
    first = jnp.mean(grad_unit, axis=-1, keepdims=True)
    second = jnp.mean(grad_unit * unit, axis=-1, keepdims=True)
    return (grad_unit - first - unit * second) * inverse


def side_by_side(weights):
    return jnp.concatenate([weights[part] for part in range(weights.shape[0])], axis=1)


def flat(field):
    return field.reshape((field.shape[0] * field.shape[1],) + field.shape[2:])


def wide(field):
    return field.astype(jnp.float32)


def iota(shape, axis):
    return lax.broadcasted_iota(jnp.int32, shape, axis)


def column_sum(field):
    return jnp.sum(field, axis=0, keepdims=True)


def call(kernel, grid, in_specs, out_specs, out_shapes, scratch, flops, args):
    moved = sum(a.size * a.dtype.itemsize for a in args) + sum(o.size * o.dtype.itemsize for o in out_shapes)
    return pl.pallas_call(
        kernel,
        grid=grid,
        in_specs=in_specs,
        out_specs=out_specs,
        out_shape=out_shapes,
        scratch_shapes=scratch,
        compiler_params=pltpu.CompilerParams(vmem_limit_bytes=VMEM_BYTES),
        cost_estimate=pl.CostEstimate(flops=int(flops) // COST, bytes_accessed=int(moved) // COST, transcendentals=0),
    )(*args)


SCALAR = pl.BlockSpec(memory_space=pltpu.SMEM)


def whole(array):
    zeros = (0,) * array.ndim
    return pl.BlockSpec(array.shape, lambda *at: zeros)


def shape(dims, kind=LOW):
    return jax.ShapeDtypeStruct(dims, kind)


def to_frames(rows, block):
    count = FRAMES * BLOCK
    at = iota((count, count + BLOCK), 0)
    source = 1 + FRAMES * (at % BLOCK) + at // BLOCK
    pick = jnp.where(source == iota((count, count + BLOCK), 1), 1.0, 0.0).astype(LOW)
    return dot(pick, rows)


def to_tokens(rows):
    count = FRAMES * BLOCK
    at = iota((count, count), 1)
    target = 1 + FRAMES * (at % BLOCK) + at // BLOCK
    pick = jnp.where(target == iota((count, count), 0), 1.0, 0.0).astype(LOW)
    return dot(pick, rows)


def fill_rows(source, tokens):
    count = tokens.shape[0]
    even = count // BLOCK * BLOCK
    source[0:even] = tokens[0:even]
    source[even:] = jnp.zeros((source.shape[0] - even, source.shape[1]), source.dtype)
    left = wide(tokens[even:count])
    tail = jnp.zeros((BLOCK, source.shape[1]), jnp.float32)
    for row in range(count - even):
        tail = tail + jnp.where(iota(tail.shape, 0) == row, left[row : row + 1], 0.0)
    source[even : even + BLOCK] = tail.astype(source.dtype)


def frame_rows(source, block, class_row, class_frames):
    count = FRAMES * BLOCK
    rows = to_frames(source[pl.ds(pl.multiple_of(block * count, count), count + BLOCK), :], block)
    at = iota((count, 1), 0)
    is_class = (block * BLOCK + at % BLOCK == PLACES) & (at // BLOCK < class_frames)
    return rows + jnp.where(is_class, class_row, 0.0)


class Copies:
    def __init__(self, semaphores):
        self.semaphores = semaphores
        self.started = []

    def start(self, source, target):
        copy = pltpu.make_async_copy(source, target, self.semaphores.at[len(self.started)])
        copy.start()
        self.started.append(copy)
        return copy


def time_forward_kernel(
    clips, gain, shift, inproj_far, inbias, outproj_far, x_far, norm_far, qkv_far, probs_far, mixed_far, part_far,
    inproj, outproj, x_out, norm_out, qkv_out, probs_out, mixed_out, part_out, source, semaphores,
):
    half = outproj.shape[0]
    copies = Copies(semaphores)
    fetched = [copies.start(inproj_far, inproj), copies.start(outproj_far, outproj)]
    fill_rows(source, clips)
    class_row = wide(clips[0:1])

    def first(block, carry):
        rows = frame_rows(source, block, class_row, FRAMES)
        unit, _ = normed(rows)
        at = pl.ds(pl.multiple_of(block * BLOCK, BLOCK), BLOCK)
        x_out[:, at, :] = rows.astype(LOW).reshape(FRAMES, BLOCK, rows.shape[1])
        norm_out[:, at, :] = (unit * vector(gain) + vector(shift)).astype(LOW).reshape(FRAMES, BLOCK, rows.shape[1])
        return carry

    lax.fori_loop(0, BLOCKS, first, 0, unroll=UNROLL)
    sent = [copies.start(x_out, x_far), copies.start(norm_out, norm_far)]
    fetched[0].wait()
    weights = side_by_side(inproj)
    for step in range(FRAMES // PAIR):
        at = pl.ds(step * PAIR, PAIR)
        qkv = heads_low(dot(flat(norm_out[at]), weights), inbias, half)
        qkv_out[at] = qkv.reshape(PAIR, ROWS, 3 * half)
    sent.append(copies.start(qkv_out, qkv_far))
    count = FRAMES * BLOCK
    same = iota((count, 2 * count), 0) % BLOCK == iota((count, 2 * count), 1) % BLOCK

    def third(first_block, count):
        ats = [
            pl.ds(pl.multiple_of((first_block + step) * BLOCK, BLOCK), BLOCK) for step in range(count)
        ]

        def keep(step, head, probs):
            probs_out[first_block + step, head] = probs

        mixed = attend(
            [flat(qkv_out[:, at, :]) for at in ats], lambda scores: jnp.where(same, scores, -1e30), keep, 2, TIME_LAG
        )
        for at, part in zip(ats, mixed):
            mixed_out[:, at, :] = part.reshape(FRAMES, BLOCK, half)

    by_blocks(third)
    sent += [copies.start(probs_out, probs_far), copies.start(mixed_out, mixed_far)]
    fetched[1].wait()
    for step in range(FRAMES // PAIR):
        at = pl.ds(step * PAIR, PAIR)
        part = dot(flat(mixed_out[at]), outproj[...]).astype(LOW)
        part_out[at] = part.reshape(PAIR, ROWS, part.shape[1])
        sent.append(copies.start(part_out.at[at], part_far.at[at]))
    for copy in sent:
        copy.wait()


def by_blocks(run):
    def step(at, carry):
        run(at * TIME_GROUP, TIME_GROUP)
        return carry

    lax.fori_loop(0, BLOCKS // TIME_GROUP, step, 0)
    if BLOCKS % TIME_GROUP:
        run(BLOCKS // TIME_GROUP * TIME_GROUP, BLOCKS % TIME_GROUP)


def heads_low(linear, inbias, half):
    query = ((linear[:, :half] + inbias[0:1]) * HEAD ** (-0.5)).astype(LOW)
    keys = linear[:, half : 2 * half].astype(LOW)
    values = (linear[:, 2 * half :] + inbias[1:2]).astype(LOW)
    return jnp.concatenate([query, keys, values], axis=1)


def beside(field_t, head):
    own = field_t[HEAD * head : HEAD * (head + 1)]
    none = jnp.zeros_like(own)
    return jnp.concatenate([own, none] if head % 2 == 0 else [none, own], axis=0)


def beside_all(field_t, heads):
    return jnp.concatenate([beside(field_t, head) for head in heads], axis=1)


def pair_of(field, head):
    start = head // 2 * 2 * HEAD
    return field[:, start : start + 2 * HEAD]


def head_rows(field_t, head):
    return field_t[HEAD * head : HEAD * (head + 1)]


def staged(count, stages, lag):
    held = [None] * count
    for step in range(count + lag * (len(stages) - 1)):
        for depth, stage in enumerate(stages):
            item = step - lag * depth
            if 0 <= item < count:
                held[item] = stage(item, held[item])
    return held


def attend(inputs, block_allowed, keep, group, lag):
    half = inputs[0].shape[1] // 3
    rows = inputs[0].shape[0]
    query_t = [qkv[:, :half].T for qkv in inputs]
    values_t = [qkv[:, 2 * half :].T for qkv in inputs]
    groups = half // HEAD // group

    def heads_of(item):
        first = item % groups * group
        return range(first, first + group)

    def score(item, held):
        block = item // groups
        keys = inputs[block][:, half : 2 * half]
        return dot(pair_of(keys, heads_of(item)[0]), beside_all(query_t[block], heads_of(item)))

    def weigh(item, scores):
        scores = block_allowed(scores)
        expon = jnp.exp(scores - jnp.max(scores, axis=0, keepdims=True))
        probs = (expon * (1.0 / column_sum(expon))).astype(LOW)
        for at, head in enumerate(heads_of(item)):
            keep(item // groups, head, probs[:, at * rows : (at + 1) * rows])
        return probs

    def mix(item, probs):
        return [
            dot(head_rows(values_t[item // groups], head), probs[:, at * rows : (at + 1) * rows])
            for at, head in enumerate(heads_of(item))
        ]

    mixed_t = staged(len(inputs) * groups, [score, weigh, mix], lag)
    out = []
    for block in range(len(inputs)):
        parts = [part for item in mixed_t[block * groups : (block + 1) * groups] for part in item]
        out.append(jnp.concatenate(parts, axis=0).T.astype(LOW))
    return out


def attend_back(inputs, probs_of, d_mixeds, group, lag):
    half = inputs[0].shape[1] // 3
    rows = inputs[0].shape[0]
    keys_t = [qkv[:, half : 2 * half].T for qkv in inputs]
    d_mixed_t = [d_mixed.T for d_mixed in d_mixeds]
    lane = iota((rows, 2 * HEAD), 1) < HEAD
    groups = half // HEAD // group

    def heads_of(item):
        first = item % groups * group
        return range(first, first + group)

    def score(item, held):
        block = item // groups
        values = inputs[block][:, 2 * half :]
        return dot(pair_of(values, heads_of(item)[0]), beside_all(d_mixed_t[block], heads_of(item)))

    def weigh(item, d_probs):
        probs_low = jnp.concatenate([probs_of(item // groups, head) for head in heads_of(item)], axis=1)
        probs = wide(probs_low)
        scaled = probs * d_probs
        d_scores = scaled - probs * column_sum(scaled)
        return probs_low, d_scores.astype(LOW)

    def halves(field):
        none = jnp.zeros_like(field)
        return jnp.concatenate([jnp.where(lane, field, none), jnp.where(lane, none, field)], axis=0)

    def mix(item, held):
        block = item // groups
        probs_low, d_scores = held
        d_query_t = [
            dot(head_rows(keys_t[block], head), d_scores[:, at * rows : (at + 1) * rows])
            for at, head in enumerate(heads_of(item))
        ]
        d_mixed = pair_of(d_mixeds[block], heads_of(item)[0])
        query = pair_of(inputs[block][:, :half], heads_of(item)[0])
        if group == 2:
            d_mixed = halves(d_mixed)
            query = halves(query)
        return d_query_t, dot(d_scores, query), dot(probs_low, d_mixed)

    made = staged(len(inputs) * groups, [score, weigh, mix], lag)

    def paired(fields):
        if group == 2:
            return fields
        return [jnp.where(lane, fields[at], fields[at + 1]) for at in range(0, len(fields), 2)]

    out = []
    for block in range(len(inputs)):
        own = made[block * groups : (block + 1) * groups]
        d_query = jnp.concatenate([part for item in own for part in item[0]], axis=0).T.astype(LOW) * HEAD ** (-0.5)
        d_keys = paired([item[1] for item in own])
        d_values = paired([item[2] for item in own])
        out.append(jnp.concatenate([d_query] + [d.astype(LOW) for d in d_keys + d_values], axis=1))
    return out


def time_forward(clips, gain, shift, inproj, inbias, outproj):
    tokens, width = clips.shape
    half = outproj.shape[0]
    heads = half // HEAD
    count = FRAMES * BLOCK
    args = (clips, gain, shift, inproj, inbias, outproj)
    outs = [
        shape((FRAMES, ROWS, width)),
        shape((FRAMES, ROWS, width)),
        shape((FRAMES, ROWS, 3 * half)),
        shape((BLOCKS, heads, count, count)),
        shape((FRAMES, ROWS, half)),
        shape((FRAMES, ROWS, width)),
    ]
    rows = FRAMES * ROWS
    near = [pltpu.VMEM(a.shape, a.dtype) for a in (inproj, outproj)] + [pltpu.VMEM(o.shape, o.dtype) for o in outs]
    far = pl.BlockSpec(memory_space=pl.ANY)
    return call(
        time_forward_kernel,
        (1,),
        [whole(clips), whole(gain), whole(shift), far, whole(inbias), far],
        [far] * 6,
        outs,
        near + [pltpu.VMEM((BLOCKS * count + BLOCK, width), LOW), pltpu.SemaphoreType.DMA((16,))],
        2 * rows * width * half * 5,
        args,
    )


def cotangent_kernel(cotangent, live, out, total, source):
    fill_rows(source, cotangent)
    present = live[0, 0]
    class_row = wide(cotangent[0:1])

    def first(block, carry):
        rows = frame_rows(source, block, class_row, 1) * present
        at = pl.ds(pl.multiple_of(block * BLOCK, BLOCK), BLOCK)
        out[:, at, :] = rows.astype(LOW).reshape(FRAMES, BLOCK, rows.shape[1])
        return carry + column_sum(rows)

    total[...] = lax.fori_loop(0, BLOCKS, first, jnp.zeros(total.shape, jnp.float32), unroll=UNROLL)


def cotangent_frames(cotangent, live):
    tokens, width = cotangent.shape
    args = (cotangent, live)
    outs = [shape((FRAMES, ROWS, width)), shape((1, width), jnp.float32)]
    return call(
        cotangent_kernel,
        (1,),
        [whole(cotangent), SCALAR],
        [whole(o) for o in outs],
        outs,
        [pltpu.VMEM((BLOCKS * FRAMES * BLOCK + BLOCK, width), LOW)],
        2 * FRAMES * ROWS * 128 * width,
        args,
    )


def vector(ref):
    return ref[...].reshape(1, -1)


def place_of(shape_of):
    return iota(shape_of, 0) % ROWS


def gather_mixer(own, other, rank, mixer):
    half = own.shape[0]

    @pl.when(pl.program_id(0) == 0)
    def _():
        mixer[pl.ds(pl.multiple_of(rank[0, 0] * half, half), half), :] = own[...]
        mixer[pl.ds(pl.multiple_of((1 - rank[0, 0]) * half, half), half), :] = other[...]


def space_forward_kernel(
    own, other, x, outbias, mixer_own, mixer_other, rank, mixbias, gain, shift, inproj, inbias, outproj,
    mixer_out, after_out, norm_out, qkv_out, probs_out, mixed_out, part_out, mixer,
):
    gather_mixer(mixer_own, mixer_other, rank, mixer)
    half = outproj.shape[0]
    width = outproj.shape[1]

    def spread(field):
        return field.astype(LOW).reshape(PAIR, ROWS, field.shape[1])

    mixer_in = (wide(flat(own[...]) + flat(other[...])) + vector(outbias)).astype(LOW)
    mixer_out[...] = spread(jnp.where(rank[0, 0] == 0, mixer_in[:, :half], mixer_in[:, half:]))
    branch = dot(mixer_in, mixer[...]) + vector(mixbias)
    after = wide(flat(x[...])) + jnp.where(place_of((PAIR * ROWS, 1)) < PLACES, branch, 0.0)
    after_out[...] = spread(after)
    unit, _ = normed(after)
    norm = (unit * vector(gain) + vector(shift)).astype(LOW)
    norm_out[...] = spread(norm)
    qkv = heads_low(dot(norm, side_by_side(inproj)), inbias, half)
    qkv_out[...] = spread(qkv)

    def allowed(scores):
        even = ROWS - BLOCK
        last = jnp.where(iota((BLOCK, ROWS), 0) <= PLACES - even, scores[even:], -1e30)
        return jnp.concatenate([scores[:even], last], axis=0)

    def keep(frame, head, probs):
        probs_out[frame, head] = probs

    frames = [qkv[frame * ROWS : (frame + 1) * ROWS] for frame in range(PAIR)]
    for frame, mixed in enumerate(attend(frames, allowed, keep, 1, SPACE_LAG)):
        mixed_out[frame] = mixed
    part_out[...] = spread(dot(flat(mixed_out[...]), outproj[...]))


def pairs(array):
    rest = (0,) * (array.ndim - 1)
    return pl.BlockSpec((PAIR,) + array.shape[1:], lambda at: (at,) + rest)


def space_forward(own, other, x, outbias, mixers, mixbias, gain, shift, inproj, inbias, outproj):
    width = x.shape[2]
    half = outproj.shape[0]
    heads = half // HEAD
    args = (own, other, x, outbias) + mixers + (mixbias, gain, shift, inproj, inbias, outproj)
    outs = [
        shape((FRAMES, ROWS, half)),
        shape((FRAMES, ROWS, width)),
        shape((FRAMES, ROWS, width)),
        shape((FRAMES, ROWS, 3 * half)),
        shape((FRAMES, heads, ROWS, ROWS)),
        shape((FRAMES, ROWS, half)),
        shape((FRAMES, ROWS, width)),
    ]
    return call(
        space_forward_kernel,
        (FRAMES // PAIR,),
        [pairs(a) for a in args[:3]] + [whole(a) for a in args[3:6]] + [SCALAR] + [whole(a) for a in args[7:]],
        [pairs(o) for o in outs],
        outs,
        [pltpu.VMEM((width, width), LOW)],
        2 * FRAMES * ROWS * width * half * 8,
        args,
    )


def last_block(count):
    return lambda array: pl.BlockSpec((count, BLOCK, array.shape[2]), lambda at: (0, BLOCKS - 1, 0))


CLASS_AT = PLACES - (BLOCKS - 1) * BLOCK


def feed_kernel(
    own, other, after, cot, own_last, other_last, after_last, outbias, gain, shift, upward, upbias, down,
    mid_out, norm_out, act_out, dpre_out, part_out, dnorm_out, upbias_out,
):
    step = pl.program_id(0)
    units = upward.shape[1]
    width = upward.shape[0]

    def spread(field):
        return field.astype(LOW).reshape(PAIR, ROWS, field.shape[1])

    class_branch = wide(own_last[...]) + wide(other_last[...])
    class_branch = jnp.sum(class_branch, axis=0)[CLASS_AT : CLASS_AT + 1] * (1.0 / FRAMES) + vector(outbias)
    at = iota((PAIR * ROWS, 1), 0)
    branch = wide(flat(own[...]) + flat(other[...])) + vector(outbias)
    is_class = (at == PLACES) & (step == 0)
    mid = jnp.where(at % ROWS < PLACES, wide(flat(after[...])) + branch, 0.0)
    mid = mid + jnp.where(is_class, wide(after_last[0])[CLASS_AT : CLASS_AT + 1] + class_branch, 0.0)
    mid_out[...] = spread(mid)
    unit, _ = normed(mid)
    norm = (unit * vector(gain) + vector(shift)).astype(LOW)
    norm_out[...] = spread(norm)
    grad = flat(cot[...])
    part = jnp.zeros((PAIR * ROWS, width), jnp.float32)
    d_norm = jnp.zeros((PAIR * ROWS, width), jnp.float32)
    share = units

    @pl.when(step == 0)
    def _():
        upbias_out[...] = jnp.zeros(upbias_out.shape, jnp.float32)

    for start in range(0, units, share):
        cols = slice(start, start + share)
        pre = dot(norm, upward[:, cols]) + vector(upbias)[:, cols]
        cumulative = 0.5 * (1.0 + lax.erf(pre * 0.5**0.5))
        slope = cumulative + pre * jnp.exp(-0.5 * pre * pre) * 0.3989422804014327
        act = (pre * cumulative).astype(LOW)
        act_out[:, :, cols] = spread(act)
        d_pre = (dot_last(grad, down[cols]) * slope).astype(LOW)
        dpre_out[:, :, cols] = spread(d_pre)
        upbias_out[:, cols] += column_sum(wide(d_pre))
        part = part + dot(act, down[cols])
        d_norm = d_norm + dot_last(d_pre, upward[:, cols])
    part_out[...] = spread(part)
    dnorm_out[...] = spread(d_norm)


def feed(own, other, after, cot, outbias, gain, shift, upward, upbias, down):
    width, units = upward.shape
    args = (own, other, after, cot, own, other, after, outbias, gain, shift, upward, upbias, down)
    outs = [
        shape((FRAMES, ROWS, width)),
        shape((FRAMES, ROWS, width)),
        shape((FRAMES, ROWS, units)),
        shape((FRAMES, ROWS, units)),
        shape((FRAMES, ROWS, width)),
        shape((FRAMES, ROWS, width)),
        shape((1, units), jnp.float32),
    ]
    tail = last_block(FRAMES)
    return call(
        feed_kernel,
        (FRAMES // PAIR,),
        [pairs(a) for a in args[:4]] + [tail(a) for a in args[4:7]] + [whole(a) for a in args[7:]],
        [pairs(o) for o in outs[:6]] + [whole(outs[6])],
        outs,
        [],
        2 * FRAMES * ROWS * width * units * 4,
        args,
    )


def space_backward_kernel(
    own, other, mid, cot, qkv, probs, own_last, other_last, mid_last, cot_last, gain, outproj, inproj,
    dspace_out, back_out, part_out, dclass_out, gain_out, shift_out, outbias_out, inbias_out,
):
    step = pl.program_id(0)
    half = outproj.shape[0]

    def spread(field):
        return field.astype(LOW).reshape(PAIR, ROWS, field.shape[1])

    def back(own_part, other_part, mid_part, cot_part):
        d_norm = wide(own_part + other_part)
        unit, inverse = normed(wide(mid_part))
        return wide(cot_part) + normed_back(unit, inverse, d_norm * vector(gain)), d_norm, d_norm * unit

    d_class = back(own_last[0], other_last[0], mid_last[0], cot_last[0])[0][CLASS_AT : CLASS_AT + 1]
    d_mid, d_shift, d_gain = back(flat(own[...]), flat(other[...]), flat(mid[...]), flat(cot[...]))
    place = place_of((PAIR * ROWS, 1))
    d_space = jnp.where(place < PLACES, d_mid, jnp.where(place == PLACES, d_class * (1.0 / FRAMES), 0.0))

    @pl.when(step == 0)
    def _():
        dclass_out[...] = d_class
        for ref in (gain_out, shift_out, outbias_out, inbias_out):
            ref[...] = jnp.zeros(ref.shape, jnp.float32)

    gain_out[...] += column_sum(d_gain)
    shift_out[...] += column_sum(d_shift)
    outbias_out[...] += column_sum(d_space)
    d_low = d_space.astype(LOW)
    dspace_out[...] = spread(d_low)
    d_mixed = dot_last(d_low, outproj[...]).astype(LOW)
    made = attend_back(
        [qkv[frame] for frame in range(PAIR)],
        lambda frame, head: probs[frame, head],
        [d_mixed[frame * ROWS : (frame + 1) * ROWS] for frame in range(PAIR)],
        1,
        SPACE_LAG,
    )
    for frame, part in enumerate(made):
        back_out[frame] = part
    backs = flat(back_out[...])
    inbias_out[...] += column_sum(wide(backs))
    part_out[...] = spread(dot_last(backs, side_by_side(inproj)))


def space_backward(own, other, mid, cot, qkv, probs, gain, outproj, inproj):
    width = mid.shape[2]
    half = outproj.shape[0]
    args = (own, other, mid, cot, qkv, probs, own, other, mid, cot, gain, outproj, inproj)
    outs = [
        shape((FRAMES, ROWS, width)),
        shape((FRAMES, ROWS, 3 * half)),
        shape((FRAMES, ROWS, width)),
        shape((1, width), jnp.float32),
        shape((1, width), jnp.float32),
        shape((1, width), jnp.float32),
        shape((1, width), jnp.float32),
        shape((1, 3 * half), jnp.float32),
    ]
    tail = last_block(1)
    return call(
        space_backward_kernel,
        (FRAMES // PAIR,),
        [pairs(a) for a in args[:6]] + [tail(a) for a in args[6:10]] + [whole(a) for a in args[10:]],
        [pairs(o) for o in outs[:3]] + [whole(o) for o in outs[3:]],
        outs,
        [],
        2 * FRAMES * ROWS * width * half * 6,
        args,
    )


def mixer_backward_kernel(
    own, other, after, dspace, dclass, gain, mixer_own, mixer_other, rank, outproj,
    dgrid_out, dmixer_out, dmixed_out, dsource_out, gain_out, shift_out, mixbias_out, outbias_out, mixer,
):
    gather_mixer(mixer_own, mixer_other, rank, mixer)

    @pl.when(pl.program_id(0) == 0)
    def _():
        dsource_out[...] = dclass[...]
        for ref in (gain_out, shift_out, mixbias_out, outbias_out):
            ref[...] = jnp.zeros(ref.shape, jnp.float32)

    def spread(field):
        return field.astype(LOW).reshape(PAIR, ROWS, field.shape[1])

    d_norm = wide(flat(own[...]) + flat(other[...]))
    unit, inverse = normed(wide(flat(after[...])))
    gain_out[...] += column_sum(d_norm * unit)
    shift_out[...] += column_sum(d_norm)
    d_space_in = normed_back(unit, inverse, d_norm * vector(gain))
    place = place_of((PAIR * ROWS, 1))
    dsource_out[...] += column_sum(jnp.where(place == PLACES, d_space_in, 0.0))
    d_grid = jnp.where(place < PLACES, d_space_in + wide(flat(dspace[...])), 0.0)
    mixbias_out[...] += column_sum(d_grid)
    d_low = d_grid.astype(LOW)
    dgrid_out[...] = spread(d_low)
    d_mixer = dot_last(d_low, mixer[...]).astype(LOW)
    dmixer_out[...] = spread(d_mixer)
    outbias_out[...] += column_sum(wide(d_mixer))
    dmixed_out[...] = spread(dot_last(d_mixer, outproj[...]))


def mixer_backward(own, other, after, dspace, dclass, gain, mixers, outproj):
    width = after.shape[2]
    half = outproj.shape[0]
    args = (own, other, after, dspace, dclass, gain) + mixers + (outproj,)
    outs = [
        shape((FRAMES, ROWS, width)),
        shape((FRAMES, ROWS, width)),
        shape((FRAMES, ROWS, half)),
    ] + [shape((1, width), jnp.float32)] * 5
    return call(
        mixer_backward_kernel,
        (FRAMES // PAIR,),
        [pairs(a) for a in args[:4]] + [whole(a) for a in args[4:8]] + [SCALAR, whole(outproj)],
        [pairs(o) for o in outs[:3]] + [whole(o) for o in outs[3:]],
        outs,
        [pltpu.VMEM((width, width), LOW)],
        2 * FRAMES * ROWS * width * half * 3,
        args,
    )


def near_far(arrays):
    return [pltpu.VMEM(a.shape, a.dtype) for a in arrays], pl.BlockSpec(memory_space=pl.ANY)


def places(first, last):
    return pl.ds(first * BLOCK, (last - first) * BLOCK)


TIME_GROUPS = ((0, 3), (3, 8), (8, BLOCKS))


def settle_copies(arrivals):
    for copy in arrivals:
        copy.wait()


def fetch_time(copies, far, near):
    coming = []
    for first, last in TIME_GROUPS:
        at = (places(first, last), pl.ds(first, last - first))
        arrivals = [copies.start(f.at[:, at[0], :], n.at[:, at[0], :]) for f, n in zip(far[:2], near[:2])]
        coming.append(arrivals + [copies.start(far[2].at[at[1]], near[2].at[at[1]])])
    return coming


def time_attention_back(group, d_mixed, qkv, probs, back_out):
    first, last = group
    ats = [places(block, block + 1) for block in range(first, last)]
    made = attend_back(
        [flat(qkv[:, at, :]) for at in ats],
        lambda step, head: probs[first + step, head],
        [flat(d_mixed[:, at, :]) for at in ats],
        2,
        TIME_LAG,
    )
    for at, part in zip(ats, made):
        back_out[:, at, :] = part.reshape(FRAMES, BLOCK, part.shape[1])


def time_part(copies, back_out, inproj, part_out, part_far, inbias_out):
    sent = []
    inbias = jnp.zeros(inbias_out.shape, jnp.float32)
    for step in range(FRAMES // PAIR):
        at = pl.ds(step * PAIR, PAIR)
        backs = flat(back_out[at])
        inbias = inbias + column_sum(wide(backs))
        part_out[at] = dot_last(backs, side_by_side(inproj)).astype(LOW).reshape(PAIR, ROWS, part_out.shape[2])
        sent.append(copies.start(part_out.at[at], part_far.at[at]))
    inbias_out[...] = inbias
    return sent


def time_backward_kernel(
    d_mixed_far, qkv_far, probs_far, inproj_far, back_far, part_far, inbias_out,
    d_mixed, qkv, probs, inproj, back_out, part_out, semaphores,
):
    copies = Copies(semaphores)
    coming = fetch_time(copies, (d_mixed_far, qkv_far, probs_far), (d_mixed, qkv, probs))
    weights = copies.start(inproj_far, inproj)
    for group, arrivals in zip(TIME_GROUPS, coming):
        settle_copies(arrivals)
        time_attention_back(group, d_mixed, qkv, probs, back_out)
    sent = [copies.start(back_out, back_far)]
    weights.wait()
    settle_copies(sent + time_part(copies, back_out, inproj, part_out, part_far, inbias_out))


def time_backward(d_mixed, qkv, probs, inproj):
    width = inproj.shape[1]
    half = d_mixed.shape[2]
    args = (d_mixed, qkv, probs, inproj)
    outs = [
        shape((FRAMES, ROWS, 3 * half)),
        shape((FRAMES, ROWS, width)),
        shape((1, 3 * half), jnp.float32),
    ]
    near, far = near_far(args + tuple(outs[:2]))
    return call(
        time_backward_kernel,
        (1,),
        [far] * 4,
        [far, far, whole(outs[2])],
        outs,
        near + [pltpu.SemaphoreType.DMA((3 * len(TIME_GROUPS) + 2 + FRAMES // PAIR,))],
        2 * FRAMES * ROWS * width * half * 5,
        args,
    )


def fetch_places(copies, far, near, groups):
    return [
        [copies.start(f.at[:, places(*group), :], n.at[:, places(*group), :]) for f, n in zip(far, near)]
        for group in groups
    ]


def put_tokens(out, block, low, carry):
    count = FRAMES * BLOCK
    moved = jnp.where(iota((count, 1), 0) == 0, carry, to_tokens(low))
    fits = min(out.shape[0] - block * count, count)
    out[block * count : block * count + fits] = moved[:fits].astype(out.dtype)
    return wide(low[count - BLOCK :])[BLOCK - 1 :]


def block_rows(ref, block):
    return wide(flat(ref[:, block * BLOCK : (block + 1) * BLOCK, :]))


def block_sum(own, other, block):
    at = places(block, block + 1)
    return wide(flat(own[:, at, :]) + flat(other[:, at, :]))


VECTORS = 16


SOURCE_GROUPS = ((0, 1), (1, 4), (4, 8), (8, BLOCKS))


def source_kernel(own_far, other_far, x_far, dgrid_far, dsource, gain, *rest):
    given = rest[:-7]
    out, packed, own, other, x, dgrid, semaphores = rest[-7:]
    width = packed.shape[1]
    coming = fetch_places(
        Copies(semaphores), (own_far, other_far, x_far, dgrid_far), (own, other, x, dgrid), SOURCE_GROUPS
    )
    carry = dsource[...]
    d_gain = jnp.zeros((1, width), jnp.float32)
    d_shift = jnp.zeros((1, width), jnp.float32)
    for (first, last), arrivals in zip(SOURCE_GROUPS, coming):
        for arrival in arrivals:
            arrival.wait()
        for block in range(first, last):
            d_norm = block_sum(own, other, block)
            unit, inverse = normed(block_rows(x, block))
            d_gain = d_gain + column_sum(d_norm * unit)
            d_shift = d_shift + column_sum(d_norm)
            rows = block_rows(dgrid, block) + normed_back(unit, inverse, d_norm * vector(gain))
            carry = put_tokens(out, block, rows.astype(LOW), carry)
    packed[...] = jnp.zeros(packed.shape, jnp.float32)
    packed[0:1] = d_gain
    packed[1:2] = d_shift
    at = 2
    for ref in given:
        count = ref.shape[1]
        if count == 3 * width // 2:
            packed[at : at + 1] = jnp.concatenate([ref[:, : width // 2], ref[:, width:]], axis=1)
            at += 1
            continue
        for start in range(0, count, width):
            packed[at : at + 1] = ref[:, start : start + width]
            at += 1


def source_gradient(own, other, x, dgrid, dsource, gain, given, tokens):
    width = x.shape[2]
    args = (own, other, x, dgrid, dsource, gain) + tuple(given)
    outs = [shape((tokens, width)), shape((VECTORS, width), jnp.float32)]
    near, far = near_far(args[:4])
    return call(
        source_kernel,
        (1,),
        [far] * 4 + [whole(a) for a in args[4:]],
        [whole(o) for o in outs],
        outs,
        near + [pltpu.SemaphoreType.DMA((4 * len(SOURCE_GROUPS),))],
        2 * FRAMES * ROWS * 128 * width,
        args,
    )


RESULT_GROUPS = ((BLOCKS - 1, BLOCKS), (0, 4), (4, 8), (8, BLOCKS - 1))


def result_kernel(own_far, other_far, mid_far, bias, live, out, own, other, mid, semaphores):
    present = live[0, 0]
    coming = fetch_places(Copies(semaphores), (own_far, other_far, mid_far), (own, other, mid), RESULT_GROUPS)

    def rows_of(block):
        total = block_rows(mid, block) + block_sum(own, other, block) + vector(bias)
        return (total * present).astype(LOW)

    for arrival in coming[0]:
        arrival.wait()
    last = rows_of(BLOCKS - 1)
    carry = wide(last[:BLOCK])[CLASS_AT : CLASS_AT + 1]
    for (first, end), arrivals in zip(RESULT_GROUPS[1:], coming[1:]):
        for arrival in arrivals:
            arrival.wait()
        for block in range(first, end):
            carry = put_tokens(out, block, rows_of(block), carry)
    put_tokens(out, BLOCKS - 1, last, carry)


def result_tokens(own, other, mid, bias, live, tokens):
    width = mid.shape[2]
    args = (own, other, mid, bias, live)
    outs = [shape((tokens, width))]
    near, far = near_far(args[:3])
    return call(
        result_kernel,
        (1,),
        [far] * 3 + [whole(bias), SCALAR],
        [whole(outs[0])],
        outs,
        near + [pltpu.SemaphoreType.DMA((3 * len(RESULT_GROUPS),))],
        2 * FRAMES * ROWS * 128 * width,
        args,
    )[0]


def settle_vectors(at, total, outs):
    width = total.shape[1]
    share = outs[0].shape[0]
    dests = width // share
    moved = pltpu.roll(total, (dests - at) % dests * share, 1)
    for row in range(10):
        outs[row][...] = moved[row, :share]
    small = share // 2
    moved = pltpu.roll(total, (2 * dests - at) % (2 * dests) * small, 1)
    for row in (10, 11):
        for part in range(2):
            start = part * (width // 2)
            outs[row][part : part + 1, :] = moved[row : row + 1, start : start + small]
    moved = pltpu.roll(total, (dests - 2 * at % dests) % dests * share, 1)
    outs[12][...] = jnp.where(2 * at < dests, moved[12, : 2 * share], moved[13, : 2 * share])


def small_shapes(share):
    outs = [shape((share,), jnp.float32)] * 10
    outs += [shape((2, share // 2), jnp.float32)] * 2
    return outs + [shape((2 * share,), jnp.float32)]


def settle_kernel(place, total, *outs):
    settle_vectors(place[0, 0], total[...], outs)


def settle(total, place, dests):
    outs = small_shapes(total.shape[1] // dests)
    return call(settle_kernel, (1,), [SCALAR, whole(total)], [whole(o) for o in outs], outs, [], 0, (place, total))


UNIT = 128


def bits_of(me):
    place = me[0, 0]
    return {"x": place % 2, "y": place // 2 % 2, "near": place // 4 % 2, "far": place // 8}


def pair_index(at, bit):
    return 2 * at + bit


def gap_index(at, bit):
    return at // 2 * 4 + 2 * bit + at % 2


def near_index(at, bit):
    return at // 4 * 8 + 4 * bit + at % 4


def top_index(half):
    return lambda at, bit: half * bit + at


def units_of(field):
    return [slice(at, at + UNIT) for at in range(0, field.shape[-1], UNIT)]


def split_gradient(field, axis, bits, message, start, keep):
    index = {"x": pair_index, "y": gap_index, "near": near_index}[axis]
    cols = units_of(field)
    for at in range(8):
        for unit, col in enumerate(cols):
            message[start + at * len(cols) + unit] = field[index(at, 1 - bits[axis]), :, col]
            keep[at, unit] = field[index(at, bits[axis]), :, col]


def split_total(held, got, got_start, bit, message, start, keep, index=pair_index):
    units = held.shape[1]

    def total(at):
        return (wide(held[at]) + wide(got[pl.ds(got_start + at * units, units)])).astype(LOW)

    for at in range(held.shape[0] // 2):
        message[start + at * units : start + (at + 1) * units] = total(index(at, 1 - bit))
        keep[at] = total(index(at, bit))


def put_gradient(field, left, right, start=0):
    step = 768 if right.shape[1] % 768 == 0 else 384
    for at in range(0, right.shape[1], step):
        part = lax.dot_general(
            left, right[:, at : at + step], (((0,), (0,)), ((), ())), preferred_element_type=jnp.float32
        )
        field[:, :, start + at : start + at + step] = part.astype(LOW).reshape(field.shape[:2] + (step,))


def gradient_call(body, args, outs, scratch, flops):
    inputs, width = args[1:], len(args) - 1

    def kernel(me, *refs):
        far, near = refs[: width + len(outs)], refs[width + len(outs) : 2 * (width + len(outs))]
        copies = Copies(refs[-1])
        waiting = [copies.start(source, target) for source, target in zip(far[:width], near[:width])]
        sent = []

        def need(*wanted):
            for ref in wanted:
                waiting[[ref is one for one in near].index(True)].wait()

        def done(*made):
            for ref in made:
                sent.append(copies.start(ref, far[[ref is one for one in near].index(True)]))

        body(need, done, me, *near, *refs[2 * (width + len(outs)) : -1])
        for copy in sent:
            copy.wait()

    remote = pl.BlockSpec(memory_space=pl.ANY)
    return call(
        kernel,
        (1,),
        [SCALAR] + [remote] * width,
        [remote] * len(outs),
        outs,
        [pltpu.VMEM(a.shape, a.dtype) for a in list(inputs) + outs]
        + scratch
        + [pltpu.SemaphoreType.DMA((width + len(outs),))],
        flops,
        args,
    )


def plain_call(kernel, args, outs):
    return call(
        kernel,
        (1,),
        [SCALAR] + [whole(a) for a in args[1:]],
        [whole(o) for o in outs],
        outs,
        [],
        0,
        args,
    )


LINE_UNITS = 4


def feed_gradient_kernel(
    need, done, me, norm, d_pre, cot, act,
    message_x, message_y, message_near, keep_up, keep_down, keep_line_up, keep_line_down, up, down,
):
    bits = bits_of(me)
    cut = keep_up.shape[1] * UNIT
    need(norm, d_pre)
    put_gradient(up, flat(norm[...]), flat(d_pre[...]))
    need(cot, act)
    put_gradient(down, flat(cot[...]), flat(act[...]))
    split_gradient(up.at[:, :, :cut], "x", bits, message_x, 0, keep_up)
    split_gradient(up.at[:, :, cut:], "near", bits, message_near, 0, keep_line_up)
    done(message_x, keep_up, keep_line_up)
    split_gradient(down.at[:, :, :cut], "y", bits, message_y, 0, keep_down)
    split_gradient(down.at[:, :, cut:], "near", bits, message_near, 8 * LINE_UNITS, keep_line_down)
    done(message_y, message_near, keep_down, keep_line_down)


def field_shape(dests, units, share):
    return shape((dests, units, share, UNIT))


def message_shape(blocks, share):
    return shape((blocks, share, UNIT))


def feed_gradient(me, norm, d_pre, cot, act):
    width = norm.shape[2]
    units = act.shape[2] // UNIT - LINE_UNITS
    share = width // 16
    outs = [message_shape(8 * units, share)] * 2 + [message_shape(16 * LINE_UNITS, share)]
    outs += [field_shape(8, units, share)] * 2 + [field_shape(8, LINE_UNITS, share)] * 2
    scratch = [pltpu.VMEM((16, share, act.shape[2]), LOW)] * 2
    return gradient_call(
        feed_gradient_kernel, (me, norm, d_pre, cot, act), outs, scratch, 4 * FRAMES * ROWS * width * act.shape[2]
    )


def space_gradient_kernel(
    need, done, me, norm, backs, d_space, mixed, up, got_x, down, got_y, line_up, line_down, got_near,
    message_x, message_y, message_far, keep_up, keep_down, keep_line_up, keep_line_down, keep_first, keep_second,
    first, second,
):
    bits = bits_of(me)
    count = 4 * up.shape[1]
    width = first.shape[2]
    need(norm, backs)
    rows = flat(norm[...])
    put_gradient(first, rows, flat(backs[...])[:, :width])
    put_gradient(second, rows, flat(backs[...])[:, width:])
    need(d_space, mixed)
    put_gradient(second, flat(d_space[...]), flat(mixed[...]), backs.shape[2] - width)
    need(up, got_x)
    split_total(up, got_x, 0, bits["y"], message_y, 0, keep_up)
    done(keep_up)
    split_gradient(first, "y", bits, message_y, count, keep_first)
    done(message_y, keep_first)
    need(down, got_y)
    split_total(down, got_y, 0, bits["x"], message_x, 0, keep_down)
    split_gradient(second, "x", bits, message_x, count, keep_second)
    done(message_x, keep_down, keep_second)
    need(line_up, line_down, got_near)
    split_total(line_up, got_near, 0, bits["far"], message_far, 0, keep_line_up, top_index(4))
    split_total(
        line_down, got_near, 8 * LINE_UNITS, bits["far"], message_far, 4 * LINE_UNITS, keep_line_down, top_index(4)
    )
    done(message_far, keep_line_up, keep_line_down)


def space_gradient(me, norm, backs, d_space, mixed, up, down, line_up, line_down, got_x, got_y, got_near):
    width = norm.shape[2]
    half = mixed.shape[2]
    share = width // 16
    units = up.shape[1]
    own = 2 * half // UNIT
    outs = [message_shape(4 * units + 8 * own, share)] * 2 + [message_shape(8 * LINE_UNITS, share)]
    outs += [field_shape(4, units, share)] * 2 + [field_shape(4, LINE_UNITS, share)] * 2
    outs += [field_shape(8, own, share)] * 2
    scratch = [pltpu.VMEM((16, share, 2 * half), LOW)] * 2
    return gradient_call(
        space_gradient_kernel,
        (me, norm, backs, d_space, mixed, up, got_x, down, got_y, line_up, line_down, got_near),
        outs,
        scratch,
        8 * FRAMES * ROWS * width * half,
    )


def mixer_gradient_kernel(
    need, done, me, d_mixer, mixed, d_grid, mixer_in, up, got_y, down, got_x, space_first, space_second,
    line_up, line_down, got_far,
    message_x, message_y, message_near, keep_up, keep_down, keep_line_up, keep_line_down, keep_first, keep_second,
    keep_out, keep_mixer, out, mixer,
):
    bits = bits_of(me)
    units = up.shape[1]
    feed = 4 * units
    own = space_first.shape[1]
    need(d_mixer, mixed)
    put_gradient(out, flat(d_mixer[...]), flat(mixed[...]))
    need(d_grid, mixer_in)
    put_gradient(mixer, flat(d_grid[...]), flat(mixer_in[...]))
    need(up, got_y)
    split_total(up, got_y, 0, bits["near"], message_near, 0, keep_up)
    need(down, got_x)
    split_total(down, got_x, 0, bits["near"], message_near, 2 * units, keep_down)
    done(message_near, keep_up, keep_down)
    need(space_first, space_second)
    split_total(space_first, got_y, feed, bits["x"], message_x, 0, keep_first)
    split_total(space_second, got_x, feed, bits["y"], message_y, 0, keep_second)
    split_gradient(out, "x", bits, message_x, 4 * own, keep_out)
    split_gradient(mixer, "y", bits, message_y, 4 * own, keep_mixer)
    need(line_up, line_down, got_far)
    line = 4 * own + 8 * keep_out.shape[1]
    split_total(line_up, got_far, 0, bits["x"], message_x, line, keep_line_up)
    split_total(line_down, got_far, 4 * LINE_UNITS, bits["y"], message_y, line, keep_line_down, top_index(2))
    done(message_x, message_y, keep_line_up, keep_line_down, keep_first, keep_second, keep_out, keep_mixer)


def mixer_gradient(
    me, d_mixer, mixed, d_grid, mixer_in, up, down, line_up, line_down, space_first, space_second, got_x, got_y, got_far
):
    width = d_grid.shape[2]
    half = mixed.shape[2]
    share = width // 16
    units, own, new = up.shape[1], space_first.shape[1], half // UNIT
    outs = [message_shape(4 * own + 8 * new + 2 * LINE_UNITS, share)] * 2 + [message_shape(4 * units, share)]
    outs += [field_shape(2, units, share)] * 2 + [field_shape(2, LINE_UNITS, share)] * 2
    outs += [field_shape(4, own, share)] * 2 + [field_shape(8, new, share)] * 2
    scratch = [pltpu.VMEM((16, share, half), LOW)] * 2
    return gradient_call(
        mixer_gradient_kernel,
        (
            me, d_mixer, mixed, d_grid, mixer_in, up, got_y, down, got_x, space_first, space_second,
            line_up, line_down, got_far,
        ),
        outs,
        scratch,
        4 * FRAMES * ROWS * width * half,
    )


TIME_FIRST = 5


def time_gradient_kernel(
    me, d_mixed_far, qkv_far, probs_far, inproj_far, norm_far, *rest,
):
    outs_far, inbias_out = rest[:5], rest[5]
    d_mixed, qkv, probs, inproj, norm = rest[6:11]
    outs = rest[11:16]
    part_out, message_x, message_y, keep_first, keep_second = outs
    back_out, both, semaphores = rest[16:]
    copies = Copies(semaphores)
    coming = fetch_time(copies, (d_mixed_far, qkv_far, probs_far), (d_mixed, qkv, probs))
    weights = [copies.start(inproj_far, inproj), copies.start(norm_far, norm)]
    for group, arrivals in zip(TIME_GROUPS, coming):
        settle_copies(arrivals)
        time_attention_back(group, d_mixed, qkv, probs, back_out)
    settle_copies(weights)
    bits = bits_of(me)
    put_gradient(both, flat(norm[...]), flat(back_out[...]))
    cut = TIME_FIRST * UNIT
    split_gradient(both.at[:, :, :cut], "y", bits, message_y, 0, keep_first)
    split_gradient(both.at[:, :, cut:], "x", bits, message_x, 0, keep_second)
    sent = [copies.start(near, far) for near, far in zip(outs[1:], outs_far[1:])]
    sent += time_part(copies, back_out, inproj, part_out, outs_far[0], inbias_out)
    settle_copies(sent)


def time_gradient(me, d_mixed, qkv, probs, inproj, norm):
    width = norm.shape[2]
    half = d_mixed.shape[2]
    share = width // 16
    last = 3 * half // UNIT - TIME_FIRST
    args = (me, d_mixed, qkv, probs, inproj, norm)
    outs = [
        shape((FRAMES, ROWS, width)),
        message_shape(8 * last, share),
        message_shape(8 * TIME_FIRST, share),
        field_shape(8, TIME_FIRST, share),
        field_shape(8, last, share),
        shape((1, 3 * half), jnp.float32),
    ]
    near, far = near_far(args[1:] + tuple(outs[:5]))
    scratch = [pltpu.VMEM((FRAMES, ROWS, 3 * half), LOW), pltpu.VMEM((16, share, 3 * half), LOW)]
    return call(
        time_gradient_kernel,
        (1,),
        [SCALAR] + [far] * 5,
        [far] * 5 + [whole(outs[5])],
        outs,
        near + scratch + [pltpu.SemaphoreType.DMA((3 * len(TIME_GROUPS) + 6 + FRAMES // PAIR,))],
        2 * FRAMES * ROWS * width * half * 8,
        args,
    )


def depth_kernel(
    me, up, down, space_first, space_second, got_x, got_y, got_near,
    message_near, message_far, keep_up, keep_down, keep_first, keep_second,
):
    bits = bits_of(me)
    units, own = up.shape[1], space_first.shape[1]
    split_total(space_first, got_x, 0, bits["near"], message_near, 0, keep_first)
    split_total(space_second, got_y, 0, bits["near"], message_near, 2 * own, keep_second)
    split_total(up, got_near, 0, bits["far"], message_far, 0, keep_up)
    split_total(down, got_near, 2 * units, bits["far"], message_far, units, keep_down)


def depth_step(me, up, down, space_first, space_second, got_x, got_y, got_near):
    units, own, share = up.shape[1], space_first.shape[1], up.shape[2]
    outs = [message_shape(4 * own, share), message_shape(2 * units, share)]
    outs += [field_shape(1, units, share)] * 2 + [field_shape(2, own, share)] * 2
    return plain_call(depth_kernel, (me, up, down, space_first, space_second, got_x, got_y, got_near), outs)


def vector_blocks(vectors, share):
    parts = [vectors[:, col].astype(LOW) for col in units_of(vectors)]
    each = share // VECTORS
    return [jnp.concatenate(parts[at : at + each], axis=0) for at in range(0, len(parts), each)]


def second_kernel(
    me, vectors, space_first, space_second, out, mixer, line_up, line_down, first, second,
    old_x, old_y, got_x, got_y, got_near,
    message_x, message_y, message_xy, message_far,
    keep_space_first, keep_space_second, keep_out, keep_mixer, keep_line_up, keep_line_down, keep_first, keep_second,
):
    bits = bits_of(me)
    own, new = space_first.shape[1], out.shape[1]
    share = first.shape[2]
    split_total(first, got_y, 0, bits["x"], message_x, 0, keep_first)
    split_total(second, got_x, 0, bits["y"], message_y, 0, keep_second)
    start_x, start_y = 4 * first.shape[1], 4 * second.shape[1]
    for at, block in enumerate(vector_blocks(vectors[...], share)):
        message_x[start_x + at] = block
        message_y[start_y + at] = block
        message_xy[at] = block
    start_x, start_y = start_x + message_xy.shape[0], start_y + message_xy.shape[0]
    split_total(out, old_x, 4 * own, bits["y"], message_y, start_y, keep_out)
    split_total(mixer, old_y, 4 * own, bits["x"], message_x, start_x, keep_mixer)
    line = 4 * own + 8 * new
    split_total(line_up, old_x, line, bits["y"], message_y, start_y + 4 * new, keep_line_up)
    split_total(line_down, old_y, line, bits["x"], message_x, start_x + 4 * new, keep_line_down)
    split_total(space_first, got_near, 0, bits["far"], message_far, 0, keep_space_first)
    split_total(space_second, got_near, 2 * own, bits["far"], message_far, own, keep_space_second)


def second_step(
    me, vectors, space_first, space_second, out, mixer, line_up, line_down, first, second,
    old_x, old_y, got_x, got_y, got_near,
):
    own, new, share = space_first.shape[1], out.shape[1], first.shape[2]
    extra = vectors.size // (share * UNIT)
    more = extra + 4 * new + LINE_UNITS
    outs = [
        message_shape(4 * first.shape[1] + more, share),
        message_shape(4 * second.shape[1] + more, share),
        message_shape(extra, share),
        message_shape(2 * own, share),
    ]
    outs += [field_shape(1, own, share)] * 2 + [field_shape(4, new, share)] * 2 + [field_shape(1, LINE_UNITS, share)] * 2
    outs += [field_shape(4, first.shape[1], share), field_shape(4, second.shape[1], share)]
    return plain_call(
        second_kernel,
        (
            me, vectors, space_first, space_second, out, mixer, line_up, line_down, first, second,
            old_x, old_y, got_x, got_y, got_near,
        ),
        outs,
    )


def line_kernel(
    me, vectors, out, mixer, line_up, line_down, first, second, got_x, got_y, got_xy,
    message_1, message_2, message_3, own, sum_line_up, sum_line_down,
):
    bits = bits_of(me)
    share = first.shape[2]
    new, extra = out.shape[1], got_xy.shape[0]
    place = 2 * bits["far"] + bits["near"]
    messages = (own, message_1, message_2, message_3)
    firsts, seconds = 4 * first.shape[1], 4 * second.shape[1]
    start = 0
    for held, got, at in (
        (first, got_x, 0), (second, got_y, 0), (out, got_y, seconds + extra), (mixer, got_x, firsts + extra),
    ):
        units = held.shape[1]
        for step, message in enumerate(messages):
            dest = place + step - 2 * (place & step)
            total = wide(held[dest]) + wide(got[pl.ds(at + dest * units, units)])
            message[start : start + units] = total.astype(LOW)
        start += units
    for at, block in enumerate(vector_blocks(vectors[...], share)):
        total = (wide(block) + wide(got_xy[at])) + (wide(got_x[firsts + at]) + wide(got_y[seconds + at]))
        for message in messages:
            message[start + at] = total.astype(LOW)
    line_x, line_y = firsts + extra + 4 * new, seconds + extra + 4 * new
    sum_line_up[0] = (wide(line_up[0]) + wide(got_y[line_y:])).astype(LOW)
    sum_line_down[0] = (wide(line_down[0]) + wide(got_x[line_x:])).astype(LOW)


def line_step(me, vectors, out, mixer, line_up, line_down, first, second, got_x, got_y, got_xy):
    share = first.shape[2]
    blocks = first.shape[1] + second.shape[1] + out.shape[1] + mixer.shape[1] + vectors.size // (share * UNIT)
    return plain_call(
        line_kernel,
        (me, vectors, out, mixer, line_up, line_down, first, second, got_x, got_y, got_xy),
        [message_shape(blocks, share)] * 4 + [field_shape(1, LINE_UNITS, share)] * 2,
    )


def final_kernel(
    me, own, got_1, got_2, got_3, up, down, got_feed, line_up, line_down, space_first, space_second, got_space,
    time_in, time_out, time_mixer, space_in, space_out, feed_up, feed_down, *small,
):
    units = up.shape[1]
    for unit, col in enumerate(units_of(feed_up)):
        if unit < units:
            feed_up[:, col] = wide(up[0, unit]) + wide(got_feed[unit])
            feed_down[:, col] = wide(down[0, unit]) + wide(got_feed[units + unit])
        else:
            feed_up[:, col] = wide(line_up[0, unit - units])
            feed_down[:, col] = wide(line_down[0, unit - units])
    mine = space_first.shape[1]
    half = space_out.shape[1]
    each = half // UNIT
    for unit in range(2 * mine):
        held = space_first[0, unit] if unit < mine else space_second[0, unit - mine]
        total = wide(held) + wide(got_space[unit])
        at = unit % each * UNIT
        if unit < 3 * each:
            space_in[unit // each, :, at : at + UNIT] = total
        else:
            space_out[:, at : at + UNIT] = total

    def line_total(at):
        return (wide(own[at]) + wide(got_1[at])) + (wide(got_2[at]) + wide(got_3[at]))

    for unit in range(5 * each):
        total = line_total(unit)
        at = unit % each * UNIT
        if unit < 3 * each:
            time_in[unit // each, :, at : at + UNIT] = total
        elif unit < 4 * each:
            time_out[:, at : at + UNIT] = total
        else:
            time_mixer[:, at : at + UNIT] = total
    share = feed_up.shape[0]
    parts = []
    for block in range(5 * each, own.shape[0]):
        total = line_total(block)
        parts += [total[at : at + VECTORS] for at in range(0, share, VECTORS)]
    settle_vectors(me[0, 0], jnp.concatenate(parts, axis=1), small)


def final_step(
    me, own, got_1, got_2, got_3, up, down, got_feed, line_up, line_down, space_first, space_second, got_space,
    width, half,
):
    share = width // 16
    units = (up.shape[1] + LINE_UNITS) * UNIT
    outs = [
        shape(dims, jnp.float32)
        for dims in (
            (3, share, half), (share, half), (share, half), (3, share, half), (share, half), (share, units),
            (share, units),
        )
    ]
    return plain_call(
        final_kernel,
        (
            me, own, got_1, got_2, got_3, up, down, got_feed, line_up, line_down, space_first, space_second,
            got_space,
        ),
        outs + small_shapes(share),
    )


def swap_tensor(field):
    size = lax.axis_size("tensor")
    return lax.ppermute(field, "tensor", [(i, i ^ 1) for i in range(size)])


def swap_dp(field, bits):
    return lax.ppermute(field, "dp", [(i, i ^ bits) for i in range(lax.axis_size("dp"))])


def pick(field, at):
    return lax.dynamic_index_in_dim(field, at, 0, keepdims=False)


def reduce_rows(field):
    size = lax.axis_size("dp")
    me = lax.axis_index("dp")
    span = size // 2
    while span >= 1:
        field = field.reshape((2, span, -1) + field.shape[-1:])
        bit = me // span % 2
        field = (wide(pick(field, bit)) + wide(swap_dp(pick(field, 1 - bit), span))).astype(LOW)
        span //= 2
    return wide(field.reshape(-1, field.shape[-1]))


def dp_sum(field):
    span = 1
    while span < lax.axis_size("dp"):
        field = field + swap_dp(field, span)
        span *= 2
    return field


def in_order(first, then):
    return lax.optimization_barrier((first, then))


def grad_of(left, right):
    return lax.dot_general(
        left.reshape(-1, left.shape[2]),
        right.reshape(-1, right.shape[2]),
        (((0,), (0,)), ((), ())),
        preferred_element_type=jnp.float32,
    ).astype(LOW)


def local(
    clips,
    cotangent,
    live,
    time_gain,
    time_shift,
    time_inproj,
    time_inbias,
    time_outproj,
    time_outbias,
    time_mixer,
    time_mixbias,
    space_gain,
    space_shift,
    space_inproj,
    space_inbias,
    space_outproj,
    space_outbias,
    feed_gain,
    feed_shift,
    feed_upward,
    feed_upbias,
    feed_down,
    feed_downbias,
):
    tokens, width = clips.shape[1:]
    half = time_outproj.shape[0]
    dests = lax.axis_size("dp")
    tensor_rank = lax.axis_index("tensor")
    paired = dests == 16
    me = lax.axis_index("dp").astype(jnp.int32).reshape(1, 1)
    present = live.astype(jnp.float32).reshape(1, 1)
    time_in = jnp.transpose(time_inproj, (1, 0, 2))
    space_in = jnp.transpose(space_inproj, (1, 0, 2))
    mixers = (time_mixer, swap_tensor(time_mixer), tensor_rank.astype(jnp.int32).reshape(1, 1))
    x, t_norm, t_qkv, t_probs, t_mixed, t_part = time_forward(
        clips[0], time_gain, time_shift, time_in, time_inbias, time_outproj
    )
    cot, g_downbias = cotangent_frames(cotangent[0], present)
    mixer_in, after_time, s_norm, s_qkv, s_probs, s_mixed, s_part = space_forward(
        t_part, swap_tensor(t_part), x, time_outbias, mixers, time_mixbias, space_gain, space_shift, space_in,
        space_inbias, space_outproj,
    )
    mid, f_norm, act, d_pre, f_part, df_part, g_upbias = feed(
        s_part, swap_tensor(s_part), after_time, cot, space_outbias, feed_gain, feed_shift, feed_upward, feed_upbias,
        feed_down,
    )
    if paired:
        feed_x, feed_y, feed_near, up, down, l_up, l_down = feed_gradient(me, f_norm, d_pre, cot, act)
        feed_x, mid = in_order(feed_x, mid)
        feed_x, feed_y, feed_near = swap_dp(feed_x, 1), swap_dp(feed_y, 2), swap_dp(feed_near, 4)
    d_space, s_back, ds_part, d_class, g_feed_gain, g_feed_shift, g_space_outbias, g_space_inbias = space_backward(
        df_part, swap_tensor(df_part), mid, cot, s_qkv, s_probs, feed_gain, space_outproj, space_in
    )
    if paired:
        ds_part, feed_x, feed_y, feed_near = lax.optimization_barrier((ds_part, feed_x, feed_y, feed_near))
        space_x, space_y, line_far, up, down, l_up, l_down, s_first, s_second = space_gradient(
            me, s_norm, s_back, d_space, s_mixed, up, down, l_up, l_down, feed_x, feed_y, feed_near
        )
        space_x, d_class = in_order(space_x, d_class)
        space_x, space_y, line_far = swap_dp(space_x, 1), swap_dp(space_y, 2), swap_dp(line_far, 8)
    result = result_tokens(f_part, swap_tensor(f_part), mid, feed_downbias, present, tokens)
    result, d_class = in_order(result, d_class)
    d_grid, d_mixer, d_mixed, d_source, g_space_gain, g_space_shift, g_mixbias, g_outbias = mixer_backward(
        ds_part, swap_tensor(ds_part), after_time, d_space, d_class, space_gain, mixers, time_outproj
    )
    if paired:
        mixer_x, mixer_y, feed_near, up, down, l_up, l_down, s_first, s_second, t_out, t_mixer = mixer_gradient(
            me, d_mixer, t_mixed, d_grid, mixer_in, up, down, l_up, l_down, s_first, s_second, space_x, space_y,
            line_far,
        )
        mixer_x, d_mixed = in_order(mixer_x, d_mixed)
        mixer_x, mixer_y, feed_near = swap_dp(mixer_x, 1), swap_dp(mixer_y, 2), swap_dp(feed_near, 4)
    if paired:
        dt_part, time_x, time_y, t_first, t_second, g_time_inbias = time_gradient(
            me, d_mixed, t_qkv, t_probs, time_in, t_norm
        )
        time_x, dt_part = in_order(time_x, dt_part)
        time_x, time_y = swap_dp(time_x, 1), swap_dp(time_y, 2)
        dt_part, mixer_x, mixer_y, feed_near = lax.optimization_barrier((dt_part, mixer_x, mixer_y, feed_near))
        space_near, feed_far, up, down, s_first, s_second = depth_step(
            me, up, down, s_first, s_second, mixer_x, mixer_y, feed_near
        )
        space_near, d_source = in_order(space_near, d_source)
        space_near, feed_far = swap_dp(space_near, 4), swap_dp(feed_far, 8)
    else:
        t_back, dt_part, g_time_inbias = time_backward(d_mixed, t_qkv, t_probs, time_in)
    grad_clips, vectors = source_gradient(
        dt_part, swap_tensor(dt_part), x, d_grid, d_source, time_gain,
        (
            g_outbias, g_mixbias, g_space_gain, g_space_shift, g_space_outbias, g_feed_gain, g_feed_shift, g_downbias,
            g_time_inbias, g_space_inbias, g_upbias,
        ),
        tokens,
    )
    if paired:
        feed_far, space_near, vectors = lax.optimization_barrier((feed_far, space_near, vectors))
        last_x, last_y, last_xy, space_far, s_first, s_second, *held = second_step(
            me, vectors, s_first, s_second, t_out, t_mixer, l_up, l_down, t_first, t_second, mixer_x, mixer_y,
            time_x, time_y, space_near,
        )
        last_x, last_y, last_xy = swap_dp(last_x, 1), swap_dp(last_y, 2), swap_dp(last_xy, 3)
        space_far = swap_dp(space_far, 8)
        space_far, last_xy = lax.optimization_barrier((space_far, last_xy))
        line_1, line_2, line_3, line_own, l_up, l_down = line_step(
            me, vectors, *held, last_x, last_y, last_xy
        )
        line_1, line_2, line_3 = swap_dp(line_1, 4), swap_dp(line_2, 8), swap_dp(line_3, 12)
        time_sum, out_sum, mixer_sum, space_sum, space_out, up_sum, down_sum, *small = final_step(
            me, line_own, line_1, line_2, line_3, up, down, feed_far, l_up, l_down, s_first, s_second, space_far,
            width, half,
        )
    else:

        def parts(field):
            return jnp.stack([field[:, part * half : (part + 1) * half] for part in range(3)])

        up_sum = reduce_rows(grad_of(f_norm, d_pre))
        down_sum = reduce_rows(grad_of(cot, act))
        space_sum = parts(reduce_rows(grad_of(s_norm, s_back)))
        space_out = reduce_rows(grad_of(d_space, s_mixed))
        time_sum = parts(reduce_rows(grad_of(t_norm, t_back)))
        out_sum = reduce_rows(grad_of(d_mixer, t_mixed))
        mixer_sum = reduce_rows(grad_of(d_grid, mixer_in))
        small = settle(dp_sum(vectors), me, dests)
    settled = (
        small[0],
        small[1],
        jnp.transpose(time_sum, (1, 0, 2)),
        small[10],
        out_sum.T,
        small[2],
        mixer_sum.T,
        small[3],
        small[4],
        small[5],
        jnp.transpose(space_sum, (1, 0, 2)),
        small[11],
        space_out.T,
        small[6],
        small[7],
        small[8],
        up_sum,
        small[12],
        down_sum.T,
        small[9],
    )
    return (result[None], grad_clips[None]) + settled


def solution(mesh):
    in_specs = (
        P("dp", None, None),
        P("dp", None, None),
        P("dp"),
        P(),
        P(),
        P(None, None, "tensor"),
        P(None, "tensor"),
        P("tensor", None),
        P(),
        P("tensor", None),
        P(),
        P(),
        P(),
        P(None, None, "tensor"),
        P(None, "tensor"),
        P("tensor", None),
        P(),
        P(),
        P(),
        P(None, "tensor"),
        P("tensor"),
        P("tensor", None),
        P(),
    )
    out_specs = (
        P("dp", None, None),
        P("dp", None, None),
        P("dp"),
        P("dp"),
        P("dp", None, "tensor"),
        P(None, ("tensor", "dp")),
        P("tensor", "dp"),
        P("dp"),
        P("tensor", "dp"),
        P("dp"),
        P("dp"),
        P("dp"),
        P("dp", None, "tensor"),
        P(None, ("tensor", "dp")),
        P("tensor", "dp"),
        P("dp"),
        P("dp"),
        P("dp"),
        P("dp", "tensor"),
        P(("tensor", "dp")),
        P("tensor", "dp"),
        P("dp"),
    )
    return jax.shard_map(local, mesh=mesh, in_specs=in_specs, out_specs=out_specs, check_vma=False)
```

```python
import functools

import jax
import jax.numpy as jnp
from jax import lax
from jax.experimental import pallas as pl
from jax.experimental.pallas import tpu as pltpu
from jax.sharding import PartitionSpec as P

HEAD = 64
FRAMES = 8
PLACES = 196
BLOCK = 16
ROWS = 208
BLOCKS = ROWS // BLOCK
PAIR = 2
UNROLL = BLOCKS
TIME_GROUP = 13
TIME_LAG = 1
SPACE_LAG = 6
EPS = 1e-06
LOW = jnp.bfloat16
VMEM_BYTES = 64 * 1024 * 1024 - 64 * 1024
COST = 1


def dot(left, right):
    return jnp.dot(left, right, preferred_element_type=jnp.float32)


def dot_last(left, right):
    return lax.dot_general(left, right, (((1,), (1,)), ((), ())), preferred_element_type=jnp.float32)


def normed(field):
    center = field - jnp.mean(field, axis=-1, keepdims=True)
    spread_sq = jnp.mean(center * center, axis=-1, keepdims=True)
    inverse = lax.rsqrt(spread_sq + EPS)
    return center * inverse, inverse


def normed_back(unit, inverse, grad_unit):
    first = jnp.mean(grad_unit, axis=-1, keepdims=True)
    second = jnp.mean(grad_unit * unit, axis=-1, keepdims=True)
    return (grad_unit - first - unit * second) * inverse


def side_by_side(weights):
    return jnp.concatenate([weights[part] for part in range(weights.shape[0])], axis=1)


def flat(field):
    return field.reshape((field.shape[0] * field.shape[1],) + field.shape[2:])


def wide(field):
    return field.astype(jnp.float32)


def iota(shape, axis):
    return lax.broadcasted_iota(jnp.int32, shape, axis)


def column_sum(field):
    return jnp.sum(field, axis=0, keepdims=True)


def call(kernel, grid, in_specs, out_specs, out_shapes, scratch, flops, args):
    moved = sum(a.size * a.dtype.itemsize for a in args) + sum(o.size * o.dtype.itemsize for o in out_shapes)
    return pl.pallas_call(
        kernel,
        grid=grid,
        in_specs=in_specs,
        out_specs=out_specs,
        out_shape=out_shapes,
        scratch_shapes=scratch,
        compiler_params=pltpu.CompilerParams(vmem_limit_bytes=VMEM_BYTES),
        cost_estimate=pl.CostEstimate(flops=int(flops) // COST, bytes_accessed=int(moved) // COST, transcendentals=0),
    )(*args)


SCALAR = pl.BlockSpec(memory_space=pltpu.SMEM)


def whole(array):
    zeros = (0,) * array.ndim
    return pl.BlockSpec(array.shape, lambda *at: zeros)


def shape(dims, kind=LOW):
    return jax.ShapeDtypeStruct(dims, kind)


def to_frames(rows, block):
    count = FRAMES * BLOCK
    at = iota((count, count + BLOCK), 0)
    source = 1 + FRAMES * (at % BLOCK) + at // BLOCK
    pick = jnp.where(source == iota((count, count + BLOCK), 1), 1.0, 0.0).astype(LOW)
    return dot(pick, rows)


def to_tokens(rows):
    count = FRAMES * BLOCK
    at = iota((count, count), 1)
    target = 1 + FRAMES * (at % BLOCK) + at // BLOCK
    pick = jnp.where(target == iota((count, count), 0), 1.0, 0.0).astype(LOW)
    return dot(pick, rows)


def fill_rows(source, tokens):
    count = tokens.shape[0]
    even = count // BLOCK * BLOCK
    source[0:even] = tokens[0:even]
    source[even:] = jnp.zeros((source.shape[0] - even, source.shape[1]), source.dtype)
    left = wide(tokens[even:count])
    tail = jnp.zeros((BLOCK, source.shape[1]), jnp.float32)
    for row in range(count - even):
        tail = tail + jnp.where(iota(tail.shape, 0) == row, left[row : row + 1], 0.0)
    source[even : even + BLOCK] = tail.astype(source.dtype)


def frame_rows(source, block, class_row, class_frames):
    count = FRAMES * BLOCK
    rows = to_frames(source[pl.ds(pl.multiple_of(block * count, count), count + BLOCK), :], block)
    at = iota((count, 1), 0)
    is_class = (block * BLOCK + at % BLOCK == PLACES) & (at // BLOCK < class_frames)
    return rows + jnp.where(is_class, class_row, 0.0)


class Copies:
    def __init__(self, semaphores):
        self.semaphores = semaphores
        self.started = []

    def start(self, source, target):
        copy = pltpu.make_async_copy(source, target, self.semaphores.at[len(self.started)])
        copy.start()
        self.started.append(copy)
        return copy


def time_forward_kernel(
    clips, gain, shift, inproj_far, inbias, outproj_far, x_far, norm_far, qkv_far, probs_far, mixed_far, part_far,
    inproj, outproj, x_out, norm_out, qkv_out, probs_out, mixed_out, part_out, source, semaphores,
):
    half = outproj.shape[0]
    copies = Copies(semaphores)
    fetched = [copies.start(inproj_far, inproj), copies.start(outproj_far, outproj)]
    fill_rows(source, clips)
    class_row = wide(clips[0:1])

    def first(block, carry):
        rows = frame_rows(source, block, class_row, FRAMES)
        unit, _ = normed(rows)
        at = pl.ds(pl.multiple_of(block * BLOCK, BLOCK), BLOCK)
        x_out[:, at, :] = rows.astype(LOW).reshape(FRAMES, BLOCK, rows.shape[1])
        norm_out[:, at, :] = (unit * vector(gain) + vector(shift)).astype(LOW).reshape(FRAMES, BLOCK, rows.shape[1])
        return carry

    lax.fori_loop(0, BLOCKS, first, 0, unroll=UNROLL)
    sent = [copies.start(x_out, x_far), copies.start(norm_out, norm_far)]
    fetched[0].wait()
    weights = side_by_side(inproj)
    for step in range(FRAMES // PAIR):
        at = pl.ds(step * PAIR, PAIR)
        qkv = heads_low(dot(flat(norm_out[at]), weights), inbias, half)
        qkv_out[at] = qkv.reshape(PAIR, ROWS, 3 * half)
    sent.append(copies.start(qkv_out, qkv_far))
    count = FRAMES * BLOCK
    same = iota((count, 2 * count), 0) % BLOCK == iota((count, 2 * count), 1) % BLOCK

    def third(first_block, count):
        ats = [
            pl.ds(pl.multiple_of((first_block + step) * BLOCK, BLOCK), BLOCK) for step in range(count)
        ]

        def keep(step, head, probs):
            probs_out[first_block + step, head] = probs

        mixed = attend(
            [flat(qkv_out[:, at, :]) for at in ats], lambda scores: jnp.where(same, scores, -1e30), keep, 2, TIME_LAG
        )
        for at, part in zip(ats, mixed):
            mixed_out[:, at, :] = part.reshape(FRAMES, BLOCK, half)

    by_blocks(third)
    sent += [copies.start(probs_out, probs_far), copies.start(mixed_out, mixed_far)]
    fetched[1].wait()
    for step in range(FRAMES // PAIR):
        at = pl.ds(step * PAIR, PAIR)
        part = dot(flat(mixed_out[at]), outproj[...]).astype(LOW)
        part_out[at] = part.reshape(PAIR, ROWS, part.shape[1])
        sent.append(copies.start(part_out.at[at], part_far.at[at]))
    for copy in sent:
        copy.wait()


def by_blocks(run):
    def step(at, carry):
        run(at * TIME_GROUP, TIME_GROUP)
        return carry

    lax.fori_loop(0, BLOCKS // TIME_GROUP, step, 0)
    if BLOCKS % TIME_GROUP:
        run(BLOCKS // TIME_GROUP * TIME_GROUP, BLOCKS % TIME_GROUP)


def heads_low(linear, inbias, half):
    query = ((linear[:, :half] + inbias[0:1]) * HEAD ** (-0.5)).astype(LOW)
    keys = linear[:, half : 2 * half].astype(LOW)
    values = (linear[:, 2 * half :] + inbias[1:2]).astype(LOW)
    return jnp.concatenate([query, keys, values], axis=1)


def beside(field_t, head):
    own = field_t[HEAD * head : HEAD * (head + 1)]
    none = jnp.zeros_like(own)
    return jnp.concatenate([own, none] if head % 2 == 0 else [none, own], axis=0)


def beside_all(field_t, heads):
    return jnp.concatenate([beside(field_t, head) for head in heads], axis=1)


def pair_of(field, head):
    start = head // 2 * 2 * HEAD
    return field[:, start : start + 2 * HEAD]


def head_rows(field_t, head):
    return field_t[HEAD * head : HEAD * (head + 1)]


def staged(count, stages, lag):
    held = [None] * count
    for step in range(count + lag * (len(stages) - 1)):
        for depth, stage in enumerate(stages):
            item = step - lag * depth
            if 0 <= item < count:
                held[item] = stage(item, held[item])
    return held


def attend(inputs, block_allowed, keep, group, lag):
    half = inputs[0].shape[1] // 3
    rows = inputs[0].shape[0]
    query_t = [qkv[:, :half].T for qkv in inputs]
    values_t = [qkv[:, 2 * half :].T for qkv in inputs]
    groups = half // HEAD // group

    def heads_of(item):
        first = item % groups * group
        return range(first, first + group)

    def score(item, held):
        block = item // groups
        keys = inputs[block][:, half : 2 * half]
        return dot(pair_of(keys, heads_of(item)[0]), beside_all(query_t[block], heads_of(item)))

    def weigh(item, scores):
        scores = block_allowed(scores)
        expon = jnp.exp(scores - jnp.max(scores, axis=0, keepdims=True))
        probs = (expon * (1.0 / column_sum(expon))).astype(LOW)
        for at, head in enumerate(heads_of(item)):
            keep(item // groups, head, probs[:, at * rows : (at + 1) * rows])
        return probs

    def mix(item, probs):
        return [
            dot(head_rows(values_t[item // groups], head), probs[:, at * rows : (at + 1) * rows])
            for at, head in enumerate(heads_of(item))
        ]

    mixed_t = staged(len(inputs) * groups, [score, weigh, mix], lag)
    out = []
    for block in range(len(inputs)):
        parts = [part for item in mixed_t[block * groups : (block + 1) * groups] for part in item]
        out.append(jnp.concatenate(parts, axis=0).T.astype(LOW))
    return out


def attend_back(inputs, probs_of, d_mixeds, group, lag):
    half = inputs[0].shape[1] // 3
    rows = inputs[0].shape[0]
    keys_t = [qkv[:, half : 2 * half].T for qkv in inputs]
    d_mixed_t = [d_mixed.T for d_mixed in d_mixeds]
    lane = iota((rows, 2 * HEAD), 1) < HEAD
    groups = half // HEAD // group

    def heads_of(item):
        first = item % groups * group
        return range(first, first + group)

    def score(item, held):
        block = item // groups
        values = inputs[block][:, 2 * half :]
        return dot(pair_of(values, heads_of(item)[0]), beside_all(d_mixed_t[block], heads_of(item)))

    def weigh(item, d_probs):
        probs_low = jnp.concatenate([probs_of(item // groups, head) for head in heads_of(item)], axis=1)
        probs = wide(probs_low)
        scaled = probs * d_probs
        d_scores = scaled - probs * column_sum(scaled)
        return probs_low, d_scores.astype(LOW)

    def halves(field):
        none = jnp.zeros_like(field)
        return jnp.concatenate([jnp.where(lane, field, none), jnp.where(lane, none, field)], axis=0)

    def mix(item, held):
        block = item // groups
        probs_low, d_scores = held
        d_query_t = [
            dot(head_rows(keys_t[block], head), d_scores[:, at * rows : (at + 1) * rows])
            for at, head in enumerate(heads_of(item))
        ]
        d_mixed = pair_of(d_mixeds[block], heads_of(item)[0])
        query = pair_of(inputs[block][:, :half], heads_of(item)[0])
        if group == 2:
            d_mixed = halves(d_mixed)
            query = halves(query)
        return d_query_t, dot(d_scores, query), dot(probs_low, d_mixed)

    made = staged(len(inputs) * groups, [score, weigh, mix], lag)

    def paired(fields):
        if group == 2:
            return fields
        return [jnp.where(lane, fields[at], fields[at + 1]) for at in range(0, len(fields), 2)]

    out = []
    for block in range(len(inputs)):
        own = made[block * groups : (block + 1) * groups]
        d_query = jnp.concatenate([part for item in own for part in item[0]], axis=0).T.astype(LOW) * HEAD ** (-0.5)
        d_keys = paired([item[1] for item in own])
        d_values = paired([item[2] for item in own])
        out.append(jnp.concatenate([d_query] + [d.astype(LOW) for d in d_keys + d_values], axis=1))
    return out


def time_forward(clips, gain, shift, inproj, inbias, outproj):
    tokens, width = clips.shape
    half = outproj.shape[0]
    heads = half // HEAD
    count = FRAMES * BLOCK
    args = (clips, gain, shift, inproj, inbias, outproj)
    outs = [
        shape((FRAMES, ROWS, width)),
        shape((FRAMES, ROWS, width)),
        shape((FRAMES, ROWS, 3 * half)),
        shape((BLOCKS, heads, count, count)),
        shape((FRAMES, ROWS, half)),
        shape((FRAMES, ROWS, width)),
    ]
    rows = FRAMES * ROWS
    near = [pltpu.VMEM(a.shape, a.dtype) for a in (inproj, outproj)] + [pltpu.VMEM(o.shape, o.dtype) for o in outs]
    far = pl.BlockSpec(memory_space=pl.ANY)
    return call(
        time_forward_kernel,
        (1,),
        [whole(clips), whole(gain), whole(shift), far, whole(inbias), far],
        [far] * 6,
        outs,
        near + [pltpu.VMEM((BLOCKS * count + BLOCK, width), LOW), pltpu.SemaphoreType.DMA((16,))],
        2 * rows * width * half * 5,
        args,
    )


def cotangent_kernel(cotangent, live, out, total, source):
    fill_rows(source, cotangent)
    present = live[0, 0]
    class_row = wide(cotangent[0:1])

    def first(block, carry):
        rows = frame_rows(source, block, class_row, 1) * present
        at = pl.ds(pl.multiple_of(block * BLOCK, BLOCK), BLOCK)
        out[:, at, :] = rows.astype(LOW).reshape(FRAMES, BLOCK, rows.shape[1])
        return carry + column_sum(rows)

    total[...] = lax.fori_loop(0, BLOCKS, first, jnp.zeros(total.shape, jnp.float32), unroll=UNROLL)


def cotangent_frames(cotangent, live):
    tokens, width = cotangent.shape
    args = (cotangent, live)
    outs = [shape((FRAMES, ROWS, width)), shape((1, width), jnp.float32)]
    return call(
        cotangent_kernel,
        (1,),
        [whole(cotangent), SCALAR],
        [whole(o) for o in outs],
        outs,
        [pltpu.VMEM((BLOCKS * FRAMES * BLOCK + BLOCK, width), LOW)],
        2 * FRAMES * ROWS * 128 * width,
        args,
    )


def vector(ref):
    return ref[...].reshape(1, -1)


def place_of(shape_of):
    return iota(shape_of, 0) % ROWS


def gather_mixer(own, other, rank, mixer):
    half = own.shape[0]

    @pl.when(pl.program_id(0) == 0)
    def _():
        mixer[pl.ds(pl.multiple_of(rank[0, 0] * half, half), half), :] = own[...]
        mixer[pl.ds(pl.multiple_of((1 - rank[0, 0]) * half, half), half), :] = other[...]


def space_forward_kernel(
    own, other, x, outbias, mixer_own, mixer_other, rank, mixbias, gain, shift, inproj, inbias, outproj,
    mixer_out, after_out, norm_out, qkv_out, probs_out, mixed_out, part_out, mixer,
):
    gather_mixer(mixer_own, mixer_other, rank, mixer)
    half = outproj.shape[0]
    width = outproj.shape[1]

    def spread(field):
        return field.astype(LOW).reshape(PAIR, ROWS, field.shape[1])

    mixer_in = (wide(flat(own[...]) + flat(other[...])) + vector(outbias)).astype(LOW)
    mixer_out[...] = spread(jnp.where(rank[0, 0] == 0, mixer_in[:, :half], mixer_in[:, half:]))
    branch = dot(mixer_in, mixer[...]) + vector(mixbias)
    after = wide(flat(x[...])) + jnp.where(place_of((PAIR * ROWS, 1)) < PLACES, branch, 0.0)
    after_out[...] = spread(after)
    unit, _ = normed(after)
    norm = (unit * vector(gain) + vector(shift)).astype(LOW)
    norm_out[...] = spread(norm)
    qkv = heads_low(dot(norm, side_by_side(inproj)), inbias, half)
    qkv_out[...] = spread(qkv)

    def allowed(scores):
        even = ROWS - BLOCK
        last = jnp.where(iota((BLOCK, ROWS), 0) <= PLACES - even, scores[even:], -1e30)
        return jnp.concatenate([scores[:even], last], axis=0)

    def keep(frame, head, probs):
        probs_out[frame, head] = probs

    frames = [qkv[frame * ROWS : (frame + 1) * ROWS] for frame in range(PAIR)]
    for frame, mixed in enumerate(attend(frames, allowed, keep, 1, SPACE_LAG)):
        mixed_out[frame] = mixed
    part_out[...] = spread(dot(flat(mixed_out[...]), outproj[...]))


def pairs(array):
    rest = (0,) * (array.ndim - 1)
    return pl.BlockSpec((PAIR,) + array.shape[1:], lambda at: (at,) + rest)


def space_forward(own, other, x, outbias, mixers, mixbias, gain, shift, inproj, inbias, outproj):
    width = x.shape[2]
    half = outproj.shape[0]
    heads = half // HEAD
    args = (own, other, x, outbias) + mixers + (mixbias, gain, shift, inproj, inbias, outproj)
    outs = [
        shape((FRAMES, ROWS, half)),
        shape((FRAMES, ROWS, width)),
        shape((FRAMES, ROWS, width)),
        shape((FRAMES, ROWS, 3 * half)),
        shape((FRAMES, heads, ROWS, ROWS)),
        shape((FRAMES, ROWS, half)),
        shape((FRAMES, ROWS, width)),
    ]
    return call(
        space_forward_kernel,
        (FRAMES // PAIR,),
        [pairs(a) for a in args[:3]] + [whole(a) for a in args[3:6]] + [SCALAR] + [whole(a) for a in args[7:]],
        [pairs(o) for o in outs],
        outs,
        [pltpu.VMEM((width, width), LOW)],
        2 * FRAMES * ROWS * width * half * 8,
        args,
    )


def last_block(count):
    return lambda array: pl.BlockSpec((count, BLOCK, array.shape[2]), lambda at: (0, BLOCKS - 1, 0))


CLASS_AT = PLACES - (BLOCKS - 1) * BLOCK


def feed_kernel(
    own, other, after, cot, own_last, other_last, after_last, outbias, gain, shift, upward, upbias, down,
    mid_out, norm_out, act_out, dpre_out, part_out, dnorm_out, upbias_out,
):
    step = pl.program_id(0)
    units = upward.shape[1]
    width = upward.shape[0]

    def spread(field):
        return field.astype(LOW).reshape(PAIR, ROWS, field.shape[1])

    class_branch = wide(own_last[...]) + wide(other_last[...])
    class_branch = jnp.sum(class_branch, axis=0)[CLASS_AT : CLASS_AT + 1] * (1.0 / FRAMES) + vector(outbias)
    at = iota((PAIR * ROWS, 1), 0)
    branch = wide(flat(own[...]) + flat(other[...])) + vector(outbias)
    is_class = (at == PLACES) & (step == 0)
    mid = jnp.where(at % ROWS < PLACES, wide(flat(after[...])) + branch, 0.0)
    mid = mid + jnp.where(is_class, wide(after_last[0])[CLASS_AT : CLASS_AT + 1] + class_branch, 0.0)
    mid_out[...] = spread(mid)
    unit, _ = normed(mid)
    norm = (unit * vector(gain) + vector(shift)).astype(LOW)
    norm_out[...] = spread(norm)
    grad = flat(cot[...])
    part = jnp.zeros((PAIR * ROWS, width), jnp.float32)
    d_norm = jnp.zeros((PAIR * ROWS, width), jnp.float32)
    share = units

    @pl.when(step == 0)
    def _():
        upbias_out[...] = jnp.zeros(upbias_out.shape, jnp.float32)

    for start in range(0, units, share):
        cols = slice(start, start + share)
        pre = dot(norm, upward[:, cols]) + vector(upbias)[:, cols]
        cumulative = 0.5 * (1.0 + lax.erf(pre * 0.5**0.5))
        slope = cumulative + pre * jnp.exp(-0.5 * pre * pre) * 0.3989422804014327
        act = (pre * cumulative).astype(LOW)
        act_out[:, :, cols] = spread(act)
        d_pre = (dot_last(grad, down[cols]) * slope).astype(LOW)
        dpre_out[:, :, cols] = spread(d_pre)
        upbias_out[:, cols] += column_sum(wide(d_pre))
        part = part + dot(act, down[cols])
        d_norm = d_norm + dot_last(d_pre, upward[:, cols])
    part_out[...] = spread(part)
    dnorm_out[...] = spread(d_norm)


def feed(own, other, after, cot, outbias, gain, shift, upward, upbias, down):
    width, units = upward.shape
    args = (own, other, after, cot, own, other, after, outbias, gain, shift, upward, upbias, down)
    outs = [
        shape((FRAMES, ROWS, width)),
        shape((FRAMES, ROWS, width)),
        shape((FRAMES, ROWS, units)),
        shape((FRAMES, ROWS, units)),
        shape((FRAMES, ROWS, width)),
        shape((FRAMES, ROWS, width)),
        shape((1, units), jnp.float32),
    ]
    tail = last_block(FRAMES)
    return call(
        feed_kernel,
        (FRAMES // PAIR,),
        [pairs(a) for a in args[:4]] + [tail(a) for a in args[4:7]] + [whole(a) for a in args[7:]],
        [pairs(o) for o in outs[:6]] + [whole(outs[6])],
        outs,
        [],
        2 * FRAMES * ROWS * width * units * 4,
        args,
    )


def space_backward_kernel(
    own, other, mid, cot, qkv, probs, own_last, other_last, mid_last, cot_last, gain, outproj, inproj,
    dspace_out, back_out, part_out, dclass_out, gain_out, shift_out, outbias_out, inbias_out,
):
    step = pl.program_id(0)
    half = outproj.shape[0]

    def spread(field):
        return field.astype(LOW).reshape(PAIR, ROWS, field.shape[1])

    def back(own_part, other_part, mid_part, cot_part):
        d_norm = wide(own_part + other_part)
        unit, inverse = normed(wide(mid_part))
        return wide(cot_part) + normed_back(unit, inverse, d_norm * vector(gain)), d_norm, d_norm * unit

    d_class = back(own_last[0], other_last[0], mid_last[0], cot_last[0])[0][CLASS_AT : CLASS_AT + 1]
    d_mid, d_shift, d_gain = back(flat(own[...]), flat(other[...]), flat(mid[...]), flat(cot[...]))
    place = place_of((PAIR * ROWS, 1))
    d_space = jnp.where(place < PLACES, d_mid, jnp.where(place == PLACES, d_class * (1.0 / FRAMES), 0.0))

    @pl.when(step == 0)
    def _():
        dclass_out[...] = d_class
        for ref in (gain_out, shift_out, outbias_out, inbias_out):
            ref[...] = jnp.zeros(ref.shape, jnp.float32)

    gain_out[...] += column_sum(d_gain)
    shift_out[...] += column_sum(d_shift)
    outbias_out[...] += column_sum(d_space)
    d_low = d_space.astype(LOW)
    dspace_out[...] = spread(d_low)
    d_mixed = dot_last(d_low, outproj[...]).astype(LOW)
    made = attend_back(
        [qkv[frame] for frame in range(PAIR)],
        lambda frame, head: probs[frame, head],
        [d_mixed[frame * ROWS : (frame + 1) * ROWS] for frame in range(PAIR)],
        1,
        SPACE_LAG,
    )
    for frame, part in enumerate(made):
        back_out[frame] = part
    backs = flat(back_out[...])
    inbias_out[...] += column_sum(wide(backs))
    part_out[...] = spread(dot_last(backs, side_by_side(inproj)))


def space_backward(own, other, mid, cot, qkv, probs, gain, outproj, inproj):
    width = mid.shape[2]
    half = outproj.shape[0]
    args = (own, other, mid, cot, qkv, probs, own, other, mid, cot, gain, outproj, inproj)
    outs = [
        shape((FRAMES, ROWS, width)),
        shape((FRAMES, ROWS, 3 * half)),
        shape((FRAMES, ROWS, width)),
        shape((1, width), jnp.float32),
        shape((1, width), jnp.float32),
        shape((1, width), jnp.float32),
        shape((1, width), jnp.float32),
        shape((1, 3 * half), jnp.float32),
    ]
    tail = last_block(1)
    return call(
        space_backward_kernel,
        (FRAMES // PAIR,),
        [pairs(a) for a in args[:6]] + [tail(a) for a in args[6:10]] + [whole(a) for a in args[10:]],
        [pairs(o) for o in outs[:3]] + [whole(o) for o in outs[3:]],
        outs,
        [],
        2 * FRAMES * ROWS * width * half * 6,
        args,
    )


def mixer_backward_kernel(
    own, other, after, dspace, dclass, gain, mixer_own, mixer_other, rank, outproj,
    dgrid_out, dmixer_out, dmixed_out, dsource_out, gain_out, shift_out, mixbias_out, outbias_out, mixer,
):
    gather_mixer(mixer_own, mixer_other, rank, mixer)

    @pl.when(pl.program_id(0) == 0)
    def _():
        dsource_out[...] = dclass[...]
        for ref in (gain_out, shift_out, mixbias_out, outbias_out):
            ref[...] = jnp.zeros(ref.shape, jnp.float32)

    def spread(field):
        return field.astype(LOW).reshape(PAIR, ROWS, field.shape[1])

    d_norm = wide(flat(own[...]) + flat(other[...]))
    unit, inverse = normed(wide(flat(after[...])))
    gain_out[...] += column_sum(d_norm * unit)
    shift_out[...] += column_sum(d_norm)
    d_space_in = normed_back(unit, inverse, d_norm * vector(gain))
    place = place_of((PAIR * ROWS, 1))
    dsource_out[...] += column_sum(jnp.where(place == PLACES, d_space_in, 0.0))
    d_grid = jnp.where(place < PLACES, d_space_in + wide(flat(dspace[...])), 0.0)
    mixbias_out[...] += column_sum(d_grid)
    d_low = d_grid.astype(LOW)
    dgrid_out[...] = spread(d_low)
    d_mixer = dot_last(d_low, mixer[...]).astype(LOW)
    dmixer_out[...] = spread(d_mixer)
    outbias_out[...] += column_sum(wide(d_mixer))
    dmixed_out[...] = spread(dot_last(d_mixer, outproj[...]))


def mixer_backward(own, other, after, dspace, dclass, gain, mixers, outproj):
    width = after.shape[2]
    half = outproj.shape[0]
    args = (own, other, after, dspace, dclass, gain) + mixers + (outproj,)
    outs = [
        shape((FRAMES, ROWS, width)),
        shape((FRAMES, ROWS, width)),
        shape((FRAMES, ROWS, half)),
    ] + [shape((1, width), jnp.float32)] * 5
    return call(
        mixer_backward_kernel,
        (FRAMES // PAIR,),
        [pairs(a) for a in args[:4]] + [whole(a) for a in args[4:8]] + [SCALAR, whole(outproj)],
        [pairs(o) for o in outs[:3]] + [whole(o) for o in outs[3:]],
        outs,
        [pltpu.VMEM((width, width), LOW)],
        2 * FRAMES * ROWS * width * half * 3,
        args,
    )


def near_far(arrays):
    return [pltpu.VMEM(a.shape, a.dtype) for a in arrays], pl.BlockSpec(memory_space=pl.ANY)


def places(first, last):
    return pl.ds(first * BLOCK, (last - first) * BLOCK)


TIME_GROUPS = ((0, 2), (2, 7), (7, BLOCKS))


def settle_copies(arrivals):
    for copy in arrivals:
        copy.wait()


def fetch_time(copies, far, near):
    coming = []
    for first, last in TIME_GROUPS:
        at = (places(first, last), pl.ds(first, last - first))
        arrivals = [copies.start(f.at[:, at[0], :], n.at[:, at[0], :]) for f, n in zip(far[:2], near[:2])]
        coming.append(arrivals + [copies.start(far[2].at[at[1]], near[2].at[at[1]])])
    return coming


def time_attention_back(group, d_mixed, qkv, probs, back_out):
    first, last = group
    ats = [places(block, block + 1) for block in range(first, last)]
    made = attend_back(
        [flat(qkv[:, at, :]) for at in ats],
        lambda step, head: probs[first + step, head],
        [flat(d_mixed[:, at, :]) for at in ats],
        2,
        TIME_LAG,
    )
    for at, part in zip(ats, made):
        back_out[:, at, :] = part.reshape(FRAMES, BLOCK, part.shape[1])


def time_part(copies, back_out, inproj, part_out, part_far, inbias_out):
    sent = []
    inbias = jnp.zeros(inbias_out.shape, jnp.float32)
    for step in range(FRAMES // PAIR):
        at = pl.ds(step * PAIR, PAIR)
        backs = flat(back_out[at])
        inbias = inbias + column_sum(wide(backs))
        part_out[at] = dot_last(backs, side_by_side(inproj)).astype(LOW).reshape(PAIR, ROWS, part_out.shape[2])
        sent.append(copies.start(part_out.at[at], part_far.at[at]))
    inbias_out[...] = inbias
    return sent


def time_backward_kernel(
    d_mixed_far, qkv_far, probs_far, inproj_far, back_far, part_far, inbias_out,
    d_mixed, qkv, probs, inproj, back_out, part_out, semaphores,
):
    copies = Copies(semaphores)
    coming = fetch_time(copies, (d_mixed_far, qkv_far, probs_far), (d_mixed, qkv, probs))
    weights = copies.start(inproj_far, inproj)
    for group, arrivals in zip(TIME_GROUPS, coming):
        settle_copies(arrivals)
        time_attention_back(group, d_mixed, qkv, probs, back_out)
    sent = [copies.start(back_out, back_far)]
    weights.wait()
    settle_copies(sent + time_part(copies, back_out, inproj, part_out, part_far, inbias_out))


def time_backward(d_mixed, qkv, probs, inproj):
    width = inproj.shape[1]
    half = d_mixed.shape[2]
    args = (d_mixed, qkv, probs, inproj)
    outs = [
        shape((FRAMES, ROWS, 3 * half)),
        shape((FRAMES, ROWS, width)),
        shape((1, 3 * half), jnp.float32),
    ]
    near, far = near_far(args + tuple(outs[:2]))
    return call(
        time_backward_kernel,
        (1,),
        [far] * 4,
        [far, far, whole(outs[2])],
        outs,
        near + [pltpu.SemaphoreType.DMA((3 * len(TIME_GROUPS) + 2 + FRAMES // PAIR,))],
        2 * FRAMES * ROWS * width * half * 5,
        args,
    )


def fetch_places(copies, far, near, groups):
    return [
        [copies.start(f.at[:, places(*group), :], n.at[:, places(*group), :]) for f, n in zip(far, near)]
        for group in groups
    ]


def put_tokens(out, block, low, carry):
    count = FRAMES * BLOCK
    moved = jnp.where(iota((count, 1), 0) == 0, carry, to_tokens(low))
    fits = min(out.shape[0] - block * count, count)
    out[block * count : block * count + fits] = moved[:fits].astype(out.dtype)
    return wide(low[count - BLOCK :])[BLOCK - 1 :]


def block_rows(ref, block):
    return wide(flat(ref[:, block * BLOCK : (block + 1) * BLOCK, :]))


def block_sum(own, other, block):
    at = places(block, block + 1)
    return wide(flat(own[:, at, :]) + flat(other[:, at, :]))


VECTORS = 16


SOURCE_GROUPS = ((0, 1), (1, 4), (4, 8), (8, BLOCKS))


def source_kernel(own_far, other_far, x_far, dgrid_far, dsource, gain, *rest):
    given = rest[:-7]
    out, packed, own, other, x, dgrid, semaphores = rest[-7:]
    width = packed.shape[1]
    coming = fetch_places(
        Copies(semaphores), (own_far, other_far, x_far, dgrid_far), (own, other, x, dgrid), SOURCE_GROUPS
    )
    carry = dsource[...]
    d_gain = jnp.zeros((1, width), jnp.float32)
    d_shift = jnp.zeros((1, width), jnp.float32)
    for (first, last), arrivals in zip(SOURCE_GROUPS, coming):
        for arrival in arrivals:
            arrival.wait()
        for block in range(first, last):
            d_norm = block_sum(own, other, block)
            unit, inverse = normed(block_rows(x, block))
            d_gain = d_gain + column_sum(d_norm * unit)
            d_shift = d_shift + column_sum(d_norm)
            rows = block_rows(dgrid, block) + normed_back(unit, inverse, d_norm * vector(gain))
            carry = put_tokens(out, block, rows.astype(LOW), carry)
    packed[...] = jnp.zeros(packed.shape, jnp.float32)
    packed[0:1] = d_gain
    packed[1:2] = d_shift
    at = 2
    for ref in given:
        count = ref.shape[1]
        if count == 3 * width // 2:
            packed[at : at + 1] = jnp.concatenate([ref[:, : width // 2], ref[:, width:]], axis=1)
            at += 1
            continue
        for start in range(0, count, width):
            packed[at : at + 1] = ref[:, start : start + width]
            at += 1


def source_gradient(own, other, x, dgrid, dsource, gain, given, tokens):
    width = x.shape[2]
    args = (own, other, x, dgrid, dsource, gain) + tuple(given)
    outs = [shape((tokens, width)), shape((VECTORS, width), jnp.float32)]
    near, far = near_far(args[:4])
    return call(
        source_kernel,
        (1,),
        [far] * 4 + [whole(a) for a in args[4:]],
        [whole(o) for o in outs],
        outs,
        near + [pltpu.SemaphoreType.DMA((4 * len(SOURCE_GROUPS),))],
        2 * FRAMES * ROWS * 128 * width,
        args,
    )


RESULT_GROUPS = ((BLOCKS - 1, BLOCKS), (0, 4), (4, 8), (8, BLOCKS - 1))


def result_kernel(own_far, other_far, mid_far, bias, live, out, own, other, mid, semaphores):
    present = live[0, 0]
    coming = fetch_places(Copies(semaphores), (own_far, other_far, mid_far), (own, other, mid), RESULT_GROUPS)

    def rows_of(block):
        total = block_rows(mid, block) + block_sum(own, other, block) + vector(bias)
        return (total * present).astype(LOW)

    for arrival in coming[0]:
        arrival.wait()
    last = rows_of(BLOCKS - 1)
    carry = wide(last[:BLOCK])[CLASS_AT : CLASS_AT + 1]
    for (first, end), arrivals in zip(RESULT_GROUPS[1:], coming[1:]):
        for arrival in arrivals:
            arrival.wait()
        for block in range(first, end):
            carry = put_tokens(out, block, rows_of(block), carry)
    put_tokens(out, BLOCKS - 1, last, carry)


def result_tokens(own, other, mid, bias, live, tokens):
    width = mid.shape[2]
    args = (own, other, mid, bias, live)
    outs = [shape((tokens, width))]
    near, far = near_far(args[:3])
    return call(
        result_kernel,
        (1,),
        [far] * 3 + [whole(bias), SCALAR],
        [whole(outs[0])],
        outs,
        near + [pltpu.SemaphoreType.DMA((3 * len(RESULT_GROUPS),))],
        2 * FRAMES * ROWS * 128 * width,
        args,
    )[0]


def settle_vectors(at, total, outs):
    width = total.shape[1]
    share = outs[0].shape[0]
    dests = width // share
    moved = pltpu.roll(total, (dests - at) % dests * share, 1)
    for row in range(10):
        outs[row][...] = moved[row, :share]
    small = share // 2
    moved = pltpu.roll(total, (2 * dests - at) % (2 * dests) * small, 1)
    for row in (10, 11):
        for part in range(2):
            start = part * (width // 2)
            outs[row][part : part + 1, :] = moved[row : row + 1, start : start + small]
    moved = pltpu.roll(total, (dests - 2 * at % dests) % dests * share, 1)
    outs[12][...] = jnp.where(2 * at < dests, moved[12, : 2 * share], moved[13, : 2 * share])


def small_shapes(share):
    outs = [shape((share,), jnp.float32)] * 10
    outs += [shape((2, share // 2), jnp.float32)] * 2
    return outs + [shape((2 * share,), jnp.float32)]


def settle_kernel(place, total, *outs):
    settle_vectors(place[0, 0], total[...], outs)


def settle(total, place, dests):
    outs = small_shapes(total.shape[1] // dests)
    return call(settle_kernel, (1,), [SCALAR, whole(total)], [whole(o) for o in outs], outs, [], 0, (place, total))


UNIT = 128


def bits_of(me):
    place = me[0, 0]
    return {"x": place % 2, "y": place // 2 % 2, "near": place // 4 % 2, "far": place // 8}


def pair_index(at, bit):
    return 2 * at + bit


def gap_index(at, bit):
    return at // 2 * 4 + 2 * bit + at % 2


def near_index(at, bit):
    return at // 4 * 8 + 4 * bit + at % 4


def top_index(half):
    return lambda at, bit: half * bit + at


def units_of(field):
    return [slice(at, at + UNIT) for at in range(0, field.shape[-1], UNIT)]


def split_gradient(field, axis, bits, message, start, keep):
    index = {"x": pair_index, "y": gap_index, "near": near_index}[axis]
    cols = units_of(field)
    for at in range(8):
        for unit, col in enumerate(cols):
            message[start + at * len(cols) + unit] = field[index(at, 1 - bits[axis]), :, col]
            keep[at, unit] = field[index(at, bits[axis]), :, col]


def split_total(held, got, got_start, bit, message, start, keep, index=pair_index):
    units = held.shape[1]

    def total(at):
        return (wide(held[at]) + wide(got[pl.ds(got_start + at * units, units)])).astype(LOW)

    for at in range(held.shape[0] // 2):
        message[start + at * units : start + (at + 1) * units] = total(index(at, 1 - bit))
        keep[at] = total(index(at, bit))


def put_gradient(field, left, right, start=0):
    step = 768 if right.shape[1] % 768 == 0 else 384
    for at in range(0, right.shape[1], step):
        part = lax.dot_general(
            left, right[:, at : at + step], (((0,), (0,)), ((), ())), preferred_element_type=jnp.float32
        )
        field[:, :, start + at : start + at + step] = part.astype(LOW).reshape(field.shape[:2] + (step,))


def gradient_call(body, args, outs, scratch, flops):
    inputs, width = args[1:], len(args) - 1

    def kernel(me, *refs):
        far, near = refs[: width + len(outs)], refs[width + len(outs) : 2 * (width + len(outs))]
        copies = Copies(refs[-1])
        waiting = [copies.start(source, target) for source, target in zip(far[:width], near[:width])]
        sent = []

        def need(*wanted):
            for ref in wanted:
                waiting[[ref is one for one in near].index(True)].wait()

        def done(*made):
            for ref in made:
                sent.append(copies.start(ref, far[[ref is one for one in near].index(True)]))

        body(need, done, me, *near, *refs[2 * (width + len(outs)) : -1])
        for copy in sent:
            copy.wait()

    remote = pl.BlockSpec(memory_space=pl.ANY)
    return call(
        kernel,
        (1,),
        [SCALAR] + [remote] * width,
        [remote] * len(outs),
        outs,
        [pltpu.VMEM(a.shape, a.dtype) for a in list(inputs) + outs]
        + scratch
        + [pltpu.SemaphoreType.DMA((width + len(outs),))],
        flops,
        args,
    )


def plain_call(kernel, args, outs):
    return call(
        kernel,
        (1,),
        [SCALAR] + [whole(a) for a in args[1:]],
        [whole(o) for o in outs],
        outs,
        [],
        0,
        args,
    )


LINE_UNITS = 4


def feed_gradient_kernel(
    need, done, me, norm, d_pre, cot, act,
    message_x, message_y, message_near, keep_up, keep_down, keep_line_up, keep_line_down, up, down,
):
    bits = bits_of(me)
    cut = keep_up.shape[1] * UNIT
    need(norm, d_pre)
    put_gradient(up, flat(norm[...]), flat(d_pre[...]))
    need(cot, act)
    put_gradient(down, flat(cot[...]), flat(act[...]))
    split_gradient(up.at[:, :, :cut], "x", bits, message_x, 0, keep_up)
    split_gradient(up.at[:, :, cut:], "near", bits, message_near, 0, keep_line_up)
    done(message_x, keep_up, keep_line_up)
    split_gradient(down.at[:, :, :cut], "y", bits, message_y, 0, keep_down)
    split_gradient(down.at[:, :, cut:], "near", bits, message_near, 8 * LINE_UNITS, keep_line_down)
    done(message_y, message_near, keep_down, keep_line_down)


def field_shape(dests, units, share):
    return shape((dests, units, share, UNIT))


def message_shape(blocks, share):
    return shape((blocks, share, UNIT))


def feed_gradient(me, norm, d_pre, cot, act):
    width = norm.shape[2]
    units = act.shape[2] // UNIT - LINE_UNITS
    share = width // 16
    outs = [message_shape(8 * units, share)] * 2 + [message_shape(16 * LINE_UNITS, share)]
    outs += [field_shape(8, units, share)] * 2 + [field_shape(8, LINE_UNITS, share)] * 2
    scratch = [pltpu.VMEM((16, share, act.shape[2]), LOW)] * 2
    return gradient_call(
        feed_gradient_kernel, (me, norm, d_pre, cot, act), outs, scratch, 4 * FRAMES * ROWS * width * act.shape[2]
    )


def space_gradient_kernel(
    need, done, me, norm, backs, d_space, mixed, up, got_x, down, got_y, line_up, line_down, got_near,
    message_x, message_y, message_far, keep_up, keep_down, keep_line_up, keep_line_down, keep_first, keep_second,
    first, second,
):
    bits = bits_of(me)
    count = 4 * up.shape[1]
    width = first.shape[2]
    need(norm, backs)
    rows = flat(norm[...])
    put_gradient(first, rows, flat(backs[...])[:, :width])
    put_gradient(second, rows, flat(backs[...])[:, width:])
    need(d_space, mixed)
    put_gradient(second, flat(d_space[...]), flat(mixed[...]), backs.shape[2] - width)
    need(up, got_x)
    split_total(up, got_x, 0, bits["y"], message_y, 0, keep_up)
    done(keep_up)
    split_gradient(first, "y", bits, message_y, count, keep_first)
    done(message_y, keep_first)
    need(down, got_y)
    split_total(down, got_y, 0, bits["x"], message_x, 0, keep_down)
    split_gradient(second, "x", bits, message_x, count, keep_second)
    done(message_x, keep_down, keep_second)
    need(line_up, line_down, got_near)
    split_total(line_up, got_near, 0, bits["far"], message_far, 0, keep_line_up, top_index(4))
    split_total(
        line_down, got_near, 8 * LINE_UNITS, bits["far"], message_far, 4 * LINE_UNITS, keep_line_down, top_index(4)
    )
    done(message_far, keep_line_up, keep_line_down)


def space_gradient(me, norm, backs, d_space, mixed, up, down, line_up, line_down, got_x, got_y, got_near):
    width = norm.shape[2]
    half = mixed.shape[2]
    share = width // 16
    units = up.shape[1]
    own = 2 * half // UNIT
    outs = [message_shape(4 * units + 8 * own, share)] * 2 + [message_shape(8 * LINE_UNITS, share)]
    outs += [field_shape(4, units, share)] * 2 + [field_shape(4, LINE_UNITS, share)] * 2
    outs += [field_shape(8, own, share)] * 2
    scratch = [pltpu.VMEM((16, share, 2 * half), LOW)] * 2
    return gradient_call(
        space_gradient_kernel,
        (me, norm, backs, d_space, mixed, up, got_x, down, got_y, line_up, line_down, got_near),
        outs,
        scratch,
        8 * FRAMES * ROWS * width * half,
    )


def mixer_gradient_kernel(
    need, done, me, d_mixer, mixed, d_grid, mixer_in, up, got_y, down, got_x, space_first, space_second,
    line_up, line_down, got_far,
    message_x, message_y, message_near, keep_up, keep_down, keep_line_up, keep_line_down, keep_first, keep_second,
    keep_out, keep_mixer, out, mixer,
):
    bits = bits_of(me)
    units = up.shape[1]
    feed = 4 * units
    own = space_first.shape[1]
    need(d_mixer, mixed)
    put_gradient(out, flat(d_mixer[...]), flat(mixed[...]))
    need(d_grid, mixer_in)
    put_gradient(mixer, flat(d_grid[...]), flat(mixer_in[...]))
    need(up, got_y)
    split_total(up, got_y, 0, bits["near"], message_near, 0, keep_up)
    need(down, got_x)
    split_total(down, got_x, 0, bits["near"], message_near, 2 * units, keep_down)
    done(message_near, keep_up, keep_down)
    need(space_first, space_second)
    split_total(space_first, got_y, feed, bits["x"], message_x, 0, keep_first)
    split_total(space_second, got_x, feed, bits["y"], message_y, 0, keep_second)
    split_gradient(out, "x", bits, message_x, 4 * own, keep_out)
    split_gradient(mixer, "y", bits, message_y, 4 * own, keep_mixer)
    need(line_up, line_down, got_far)
    line = 4 * own + 8 * keep_out.shape[1]
    split_total(line_up, got_far, 0, bits["x"], message_x, line, keep_line_up)
    split_total(line_down, got_far, 4 * LINE_UNITS, bits["y"], message_y, line, keep_line_down, top_index(2))
    done(message_x, message_y, keep_line_up, keep_line_down, keep_first, keep_second, keep_out, keep_mixer)


def mixer_gradient(
    me, d_mixer, mixed, d_grid, mixer_in, up, down, line_up, line_down, space_first, space_second, got_x, got_y, got_far
):
    width = d_grid.shape[2]
    half = mixed.shape[2]
    share = width // 16
    units, own, new = up.shape[1], space_first.shape[1], half // UNIT
    outs = [message_shape(4 * own + 8 * new + 2 * LINE_UNITS, share)] * 2 + [message_shape(4 * units, share)]
    outs += [field_shape(2, units, share)] * 2 + [field_shape(2, LINE_UNITS, share)] * 2
    outs += [field_shape(4, own, share)] * 2 + [field_shape(8, new, share)] * 2
    scratch = [pltpu.VMEM((16, share, half), LOW)] * 2
    return gradient_call(
        mixer_gradient_kernel,
        (
            me, d_mixer, mixed, d_grid, mixer_in, up, got_y, down, got_x, space_first, space_second,
            line_up, line_down, got_far,
        ),
        outs,
        scratch,
        4 * FRAMES * ROWS * width * half,
    )


TIME_FIRST = 5


def time_gradient_kernel(
    me, d_mixed_far, qkv_far, probs_far, inproj_far, norm_far, *rest,
):
    outs_far, inbias_out = rest[:5], rest[5]
    d_mixed, qkv, probs, inproj, norm = rest[6:11]
    outs = rest[11:16]
    part_out, message_x, message_y, keep_first, keep_second = outs
    back_out, both, semaphores = rest[16:]
    copies = Copies(semaphores)
    coming = fetch_time(copies, (d_mixed_far, qkv_far, probs_far), (d_mixed, qkv, probs))
    weights = [copies.start(inproj_far, inproj), copies.start(norm_far, norm)]
    for group, arrivals in zip(TIME_GROUPS, coming):
        settle_copies(arrivals)
        time_attention_back(group, d_mixed, qkv, probs, back_out)
    settle_copies(weights)
    bits = bits_of(me)
    put_gradient(both, flat(norm[...]), flat(back_out[...]))
    cut = TIME_FIRST * UNIT
    split_gradient(both.at[:, :, :cut], "y", bits, message_y, 0, keep_first)
    split_gradient(both.at[:, :, cut:], "x", bits, message_x, 0, keep_second)
    sent = [copies.start(near, far) for near, far in zip(outs[1:], outs_far[1:])]
    sent += time_part(copies, back_out, inproj, part_out, outs_far[0], inbias_out)
    settle_copies(sent)


def time_gradient(me, d_mixed, qkv, probs, inproj, norm):
    width = norm.shape[2]
    half = d_mixed.shape[2]
    share = width // 16
    last = 3 * half // UNIT - TIME_FIRST
    args = (me, d_mixed, qkv, probs, inproj, norm)
    outs = [
        shape((FRAMES, ROWS, width)),
        message_shape(8 * last, share),
        message_shape(8 * TIME_FIRST, share),
        field_shape(8, TIME_FIRST, share),
        field_shape(8, last, share),
        shape((1, 3 * half), jnp.float32),
    ]
    near, far = near_far(args[1:] + tuple(outs[:5]))
    scratch = [pltpu.VMEM((FRAMES, ROWS, 3 * half), LOW), pltpu.VMEM((16, share, 3 * half), LOW)]
    return call(
        time_gradient_kernel,
        (1,),
        [SCALAR] + [far] * 5,
        [far] * 5 + [whole(outs[5])],
        outs,
        near + scratch + [pltpu.SemaphoreType.DMA((3 * len(TIME_GROUPS) + 6 + FRAMES // PAIR,))],
        2 * FRAMES * ROWS * width * half * 8,
        args,
    )


def depth_kernel(
    me, up, down, space_first, space_second, got_x, got_y, got_near,
    message_near, message_far, keep_up, keep_down, keep_first, keep_second,
):
    bits = bits_of(me)
    units, own = up.shape[1], space_first.shape[1]
    split_total(space_first, got_x, 0, bits["near"], message_near, 0, keep_first)
    split_total(space_second, got_y, 0, bits["near"], message_near, 2 * own, keep_second)
    split_total(up, got_near, 0, bits["far"], message_far, 0, keep_up)
    split_total(down, got_near, 2 * units, bits["far"], message_far, units, keep_down)


def depth_step(me, up, down, space_first, space_second, got_x, got_y, got_near):
    units, own, share = up.shape[1], space_first.shape[1], up.shape[2]
    outs = [message_shape(4 * own, share), message_shape(2 * units, share)]
    outs += [field_shape(1, units, share)] * 2 + [field_shape(2, own, share)] * 2
    return plain_call(depth_kernel, (me, up, down, space_first, space_second, got_x, got_y, got_near), outs)


def vector_blocks(vectors, share):
    parts = [vectors[:, col].astype(LOW) for col in units_of(vectors)]
    each = share // VECTORS
    return [jnp.concatenate(parts[at : at + each], axis=0) for at in range(0, len(parts), each)]


def second_kernel(
    me, vectors, space_first, space_second, out, mixer, line_up, line_down, first, second,
    old_x, old_y, got_x, got_y, got_near,
    message_x, message_y, message_xy, message_far,
    keep_space_first, keep_space_second, keep_out, keep_mixer, keep_line_up, keep_line_down, keep_first, keep_second,
):
    bits = bits_of(me)
    own, new = space_first.shape[1], out.shape[1]
    share = first.shape[2]
    split_total(first, got_y, 0, bits["x"], message_x, 0, keep_first)
    split_total(second, got_x, 0, bits["y"], message_y, 0, keep_second)
    start_x, start_y = 4 * first.shape[1], 4 * second.shape[1]
    for at, block in enumerate(vector_blocks(vectors[...], share)):
        message_x[start_x + at] = block
        message_y[start_y + at] = block
        message_xy[at] = block
    start_x, start_y = start_x + message_xy.shape[0], start_y + message_xy.shape[0]
    split_total(out, old_x, 4 * own, bits["y"], message_y, start_y, keep_out)
    split_total(mixer, old_y, 4 * own, bits["x"], message_x, start_x, keep_mixer)
    line = 4 * own + 8 * new
    split_total(line_up, old_x, line, bits["y"], message_y, start_y + 4 * new, keep_line_up)
    split_total(line_down, old_y, line, bits["x"], message_x, start_x + 4 * new, keep_line_down)
    split_total(space_first, got_near, 0, bits["far"], message_far, 0, keep_space_first)
    split_total(space_second, got_near, 2 * own, bits["far"], message_far, own, keep_space_second)


def second_step(
    me, vectors, space_first, space_second, out, mixer, line_up, line_down, first, second,
    old_x, old_y, got_x, got_y, got_near,
):
    own, new, share = space_first.shape[1], out.shape[1], first.shape[2]
    extra = vectors.size // (share * UNIT)
    more = extra + 4 * new + LINE_UNITS
    outs = [
        message_shape(4 * first.shape[1] + more, share),
        message_shape(4 * second.shape[1] + more, share),
        message_shape(extra, share),
        message_shape(2 * own, share),
    ]
    outs += [field_shape(1, own, share)] * 2 + [field_shape(4, new, share)] * 2 + [field_shape(1, LINE_UNITS, share)] * 2
    outs += [field_shape(4, first.shape[1], share), field_shape(4, second.shape[1], share)]
    return plain_call(
        second_kernel,
        (
            me, vectors, space_first, space_second, out, mixer, line_up, line_down, first, second,
            old_x, old_y, got_x, got_y, got_near,
        ),
        outs,
    )


def line_kernel(
    me, vectors, out, mixer, line_up, line_down, first, second, got_x, got_y, got_xy,
    message_1, message_2, message_3, own, sum_line_up, sum_line_down,
):
    bits = bits_of(me)
    share = first.shape[2]
    new, extra = out.shape[1], got_xy.shape[0]
    place = 2 * bits["far"] + bits["near"]
    messages = (own, message_1, message_2, message_3)
    firsts, seconds = 4 * first.shape[1], 4 * second.shape[1]
    start = 0
    for held, got, at in (
        (first, got_x, 0), (second, got_y, 0), (out, got_y, seconds + extra), (mixer, got_x, firsts + extra),
    ):
        units = held.shape[1]
        for step, message in enumerate(messages):
            dest = place + step - 2 * (place & step)
            total = wide(held[dest]) + wide(got[pl.ds(at + dest * units, units)])
            message[start : start + units] = total.astype(LOW)
        start += units
    for at, block in enumerate(vector_blocks(vectors[...], share)):
        total = (wide(block) + wide(got_xy[at])) + (wide(got_x[firsts + at]) + wide(got_y[seconds + at]))
        for message in messages:
            message[start + at] = total.astype(LOW)
    line_x, line_y = firsts + extra + 4 * new, seconds + extra + 4 * new
    sum_line_up[0] = (wide(line_up[0]) + wide(got_y[line_y:])).astype(LOW)
    sum_line_down[0] = (wide(line_down[0]) + wide(got_x[line_x:])).astype(LOW)


def line_step(me, vectors, out, mixer, line_up, line_down, first, second, got_x, got_y, got_xy):
    share = first.shape[2]
    blocks = first.shape[1] + second.shape[1] + out.shape[1] + mixer.shape[1] + vectors.size // (share * UNIT)
    return plain_call(
        line_kernel,
        (me, vectors, out, mixer, line_up, line_down, first, second, got_x, got_y, got_xy),
        [message_shape(blocks, share)] * 4 + [field_shape(1, LINE_UNITS, share)] * 2,
    )


def final_kernel(
    me, own, got_1, got_2, got_3, up, down, got_feed, line_up, line_down, space_first, space_second, got_space,
    time_in, time_out, time_mixer, space_in, space_out, feed_up, feed_down, *small,
):
    units = up.shape[1]
    for unit, col in enumerate(units_of(feed_up)):
        if unit < units:
            feed_up[:, col] = wide(up[0, unit]) + wide(got_feed[unit])
            feed_down[:, col] = wide(down[0, unit]) + wide(got_feed[units + unit])
        else:
            feed_up[:, col] = wide(line_up[0, unit - units])
            feed_down[:, col] = wide(line_down[0, unit - units])
    mine = space_first.shape[1]
    half = space_out.shape[1]
    each = half // UNIT
    for unit in range(2 * mine):
        held = space_first[0, unit] if unit < mine else space_second[0, unit - mine]
        total = wide(held) + wide(got_space[unit])
        at = unit % each * UNIT
        if unit < 3 * each:
            space_in[unit // each, :, at : at + UNIT] = total
        else:
            space_out[:, at : at + UNIT] = total

    def line_total(at):
        return (wide(own[at]) + wide(got_1[at])) + (wide(got_2[at]) + wide(got_3[at]))

    for unit in range(5 * each):
        total = line_total(unit)
        at = unit % each * UNIT
        if unit < 3 * each:
            time_in[unit // each, :, at : at + UNIT] = total
        elif unit < 4 * each:
            time_out[:, at : at + UNIT] = total
        else:
            time_mixer[:, at : at + UNIT] = total
    share = feed_up.shape[0]
    parts = []
    for block in range(5 * each, own.shape[0]):
        total = line_total(block)
        parts += [total[at : at + VECTORS] for at in range(0, share, VECTORS)]
    settle_vectors(me[0, 0], jnp.concatenate(parts, axis=1), small)


def final_step(
    me, own, got_1, got_2, got_3, up, down, got_feed, line_up, line_down, space_first, space_second, got_space,
    width, half,
):
    share = width // 16
    units = (up.shape[1] + LINE_UNITS) * UNIT
    outs = [
        shape(dims, jnp.float32)
        for dims in (
            (3, share, half), (share, half), (share, half), (3, share, half), (share, half), (share, units),
            (share, units),
        )
    ]
    return plain_call(
        final_kernel,
        (
            me, own, got_1, got_2, got_3, up, down, got_feed, line_up, line_down, space_first, space_second,
            got_space,
        ),
        outs + small_shapes(share),
    )


def swap_tensor(field):
    size = lax.axis_size("tensor")
    return lax.ppermute(field, "tensor", [(i, i ^ 1) for i in range(size)])


def swap_dp(field, bits):
    return lax.ppermute(field, "dp", [(i, i ^ bits) for i in range(lax.axis_size("dp"))])


def pick(field, at):
    return lax.dynamic_index_in_dim(field, at, 0, keepdims=False)


def reduce_rows(field):
    size = lax.axis_size("dp")
    me = lax.axis_index("dp")
    span = size // 2
    while span >= 1:
        field = field.reshape((2, span, -1) + field.shape[-1:])
        bit = me // span % 2
        field = (wide(pick(field, bit)) + wide(swap_dp(pick(field, 1 - bit), span))).astype(LOW)
        span //= 2
    return wide(field.reshape(-1, field.shape[-1]))


def dp_sum(field):
    span = 1
    while span < lax.axis_size("dp"):
        field = field + swap_dp(field, span)
        span *= 2
    return field


def in_order(first, then):
    return lax.optimization_barrier((first, then))


def grad_of(left, right):
    return lax.dot_general(
        left.reshape(-1, left.shape[2]),
        right.reshape(-1, right.shape[2]),
        (((0,), (0,)), ((), ())),
        preferred_element_type=jnp.float32,
    ).astype(LOW)


def local(
    clips,
    cotangent,
    live,
    time_gain,
    time_shift,
    time_inproj,
    time_inbias,
    time_outproj,
    time_outbias,
    time_mixer,
    time_mixbias,
    space_gain,
    space_shift,
    space_inproj,
    space_inbias,
    space_outproj,
    space_outbias,
    feed_gain,
    feed_shift,
    feed_upward,
    feed_upbias,
    feed_down,
    feed_downbias,
):
    tokens, width = clips.shape[1:]
    half = time_outproj.shape[0]
    dests = lax.axis_size("dp")
    tensor_rank = lax.axis_index("tensor")
    paired = dests == 16
    me = lax.axis_index("dp").astype(jnp.int32).reshape(1, 1)
    present = live.astype(jnp.float32).reshape(1, 1)
    time_in = jnp.transpose(time_inproj, (1, 0, 2))
    space_in = jnp.transpose(space_inproj, (1, 0, 2))
    mixers = (time_mixer, swap_tensor(time_mixer), tensor_rank.astype(jnp.int32).reshape(1, 1))
    x, t_norm, t_qkv, t_probs, t_mixed, t_part = time_forward(
        clips[0], time_gain, time_shift, time_in, time_inbias, time_outproj
    )
    cot, g_downbias = cotangent_frames(cotangent[0], present)
    mixer_in, after_time, s_norm, s_qkv, s_probs, s_mixed, s_part = space_forward(
        t_part, swap_tensor(t_part), x, time_outbias, mixers, time_mixbias, space_gain, space_shift, space_in,
        space_inbias, space_outproj,
    )
    mid, f_norm, act, d_pre, f_part, df_part, g_upbias = feed(
        s_part, swap_tensor(s_part), after_time, cot, space_outbias, feed_gain, feed_shift, feed_upward, feed_upbias,
        feed_down,
    )
    if paired:
        feed_x, feed_y, feed_near, up, down, l_up, l_down = feed_gradient(me, f_norm, d_pre, cot, act)
        feed_x, mid = in_order(feed_x, mid)
        feed_x, feed_y, feed_near = swap_dp(feed_x, 1), swap_dp(feed_y, 2), swap_dp(feed_near, 4)
    d_space, s_back, ds_part, d_class, g_feed_gain, g_feed_shift, g_space_outbias, g_space_inbias = space_backward(
        df_part, swap_tensor(df_part), mid, cot, s_qkv, s_probs, feed_gain, space_outproj, space_in
    )
    if paired:
        ds_part, feed_x, feed_y, feed_near = lax.optimization_barrier((ds_part, feed_x, feed_y, feed_near))
        space_x, space_y, line_far, up, down, l_up, l_down, s_first, s_second = space_gradient(
            me, s_norm, s_back, d_space, s_mixed, up, down, l_up, l_down, feed_x, feed_y, feed_near
        )
        space_x, d_class = in_order(space_x, d_class)
        space_x, space_y, line_far = swap_dp(space_x, 1), swap_dp(space_y, 2), swap_dp(line_far, 8)
    result = result_tokens(f_part, swap_tensor(f_part), mid, feed_downbias, present, tokens)
    result, d_class = in_order(result, d_class)
    d_grid, d_mixer, d_mixed, d_source, g_space_gain, g_space_shift, g_mixbias, g_outbias = mixer_backward(
        ds_part, swap_tensor(ds_part), after_time, d_space, d_class, space_gain, mixers, time_outproj
    )
    if paired:
        mixer_x, mixer_y, feed_near, up, down, l_up, l_down, s_first, s_second, t_out, t_mixer = mixer_gradient(
            me, d_mixer, t_mixed, d_grid, mixer_in, up, down, l_up, l_down, s_first, s_second, space_x, space_y,
            line_far,
        )
        mixer_x, d_mixed = in_order(mixer_x, d_mixed)
        mixer_x, mixer_y, feed_near = swap_dp(mixer_x, 1), swap_dp(mixer_y, 2), swap_dp(feed_near, 4)
    if paired:
        dt_part, time_x, time_y, t_first, t_second, g_time_inbias = time_gradient(
            me, d_mixed, t_qkv, t_probs, time_in, t_norm
        )
        time_x, dt_part = in_order(time_x, dt_part)
        time_x, time_y = swap_dp(time_x, 1), swap_dp(time_y, 2)
        dt_part, mixer_x, mixer_y, feed_near = lax.optimization_barrier((dt_part, mixer_x, mixer_y, feed_near))
        space_near, feed_far, up, down, s_first, s_second = depth_step(
            me, up, down, s_first, s_second, mixer_x, mixer_y, feed_near
        )
        space_near, d_source = in_order(space_near, d_source)
        space_near, feed_far = swap_dp(space_near, 4), swap_dp(feed_far, 8)
    else:
        t_back, dt_part, g_time_inbias = time_backward(d_mixed, t_qkv, t_probs, time_in)
    grad_clips, vectors = source_gradient(
        dt_part, swap_tensor(dt_part), x, d_grid, d_source, time_gain,
        (
            g_outbias, g_mixbias, g_space_gain, g_space_shift, g_space_outbias, g_feed_gain, g_feed_shift, g_downbias,
            g_time_inbias, g_space_inbias, g_upbias,
        ),
        tokens,
    )
    if paired:
        feed_far, space_near, vectors = lax.optimization_barrier((feed_far, space_near, vectors))
        last_x, last_y, last_xy, space_far, s_first, s_second, *held = second_step(
            me, vectors, s_first, s_second, t_out, t_mixer, l_up, l_down, t_first, t_second, mixer_x, mixer_y,
            time_x, time_y, space_near,
        )
        last_x, last_y, last_xy = swap_dp(last_x, 1), swap_dp(last_y, 2), swap_dp(last_xy, 3)
        space_far = swap_dp(space_far, 8)
        space_far, last_xy = lax.optimization_barrier((space_far, last_xy))
        line_1, line_2, line_3, line_own, l_up, l_down = line_step(
            me, vectors, *held, last_x, last_y, last_xy
        )
        line_1, line_2, line_3 = swap_dp(line_1, 4), swap_dp(line_2, 8), swap_dp(line_3, 12)
        time_sum, out_sum, mixer_sum, space_sum, space_out, up_sum, down_sum, *small = final_step(
            me, line_own, line_1, line_2, line_3, up, down, feed_far, l_up, l_down, s_first, s_second, space_far,
            width, half,
        )
    else:

        def parts(field):
            return jnp.stack([field[:, part * half : (part + 1) * half] for part in range(3)])

        up_sum = reduce_rows(grad_of(f_norm, d_pre))
        down_sum = reduce_rows(grad_of(cot, act))
        space_sum = parts(reduce_rows(grad_of(s_norm, s_back)))
        space_out = reduce_rows(grad_of(d_space, s_mixed))
        time_sum = parts(reduce_rows(grad_of(t_norm, t_back)))
        out_sum = reduce_rows(grad_of(d_mixer, t_mixed))
        mixer_sum = reduce_rows(grad_of(d_grid, mixer_in))
        small = settle(dp_sum(vectors), me, dests)
    settled = (
        small[0],
        small[1],
        jnp.transpose(time_sum, (1, 0, 2)),
        small[10],
        out_sum.T,
        small[2],
        mixer_sum.T,
        small[3],
        small[4],
        small[5],
        jnp.transpose(space_sum, (1, 0, 2)),
        small[11],
        space_out.T,
        small[6],
        small[7],
        small[8],
        up_sum,
        small[12],
        down_sum.T,
        small[9],
    )
    return (result[None], grad_clips[None]) + settled


def solution(mesh):
    in_specs = (
        P("dp", None, None),
        P("dp", None, None),
        P("dp"),
        P(),
        P(),
        P(None, None, "tensor"),
        P(None, "tensor"),
        P("tensor", None),
        P(),
        P("tensor", None),
        P(),
        P(),
        P(),
        P(None, None, "tensor"),
        P(None, "tensor"),
        P("tensor", None),
        P(),
        P(),
        P(),
        P(None, "tensor"),
        P("tensor"),
        P("tensor", None),
        P(),
    )
    out_specs = (
        P("dp", None, None),
        P("dp", None, None),
        P("dp"),
        P("dp"),
        P("dp", None, "tensor"),
        P(None, ("tensor", "dp")),
        P("tensor", "dp"),
        P("dp"),
        P("tensor", "dp"),
        P("dp"),
        P("dp"),
        P("dp"),
        P("dp", None, "tensor"),
        P(None, ("tensor", "dp")),
        P("tensor", "dp"),
        P("dp"),
        P("dp"),
        P("dp"),
        P("dp", "tensor"),
        P(("tensor", "dp")),
        P("tensor", "dp"),
        P("dp"),
    )
    return jax.shard_map(local, mesh=mesh, in_specs=in_specs, out_specs=out_specs, check_vma=False)
```
